32 devices in a mesh: groups: 2 (over y), chan: 4 (over z), sub: 2 (over x), rep: 2 (over core).
Axes of the slice: x: 2, y: 2, z: 4, core: 2. Of those that a mesh axis runs over, the one named last changes fastest.
Arguments:
- traces: bfloat16 [512, 128, 512], P(('groups', 'sub', 'rep'), 'chan'), parts along dimension 0, may hold values from -6 to 6
- channel_slot: int32 [512], P(('groups', 'sub', 'rep')), parts along dimension 0, may hold values from 0 to 63, as said below
Outputs:
- correlations: float32 [3, 8, 64, 64, 128], P(None, ('groups', 'chan'), 'sub', 'rep'), parts along dimension 1
The draws below stay inside these ranges and needn't reach their ends.
There are 2 independent parts, one for each index of `groups`. The reference program is written for one: setup_inputs(seed, part) draws one part's arguments, and reference() takes and returns one part's arrays. A program takes and returns all parts, laid end to end along the dimension named above; each array names one. Nothing has to cross between parts.
Inputs may be any that keep to these rules, and one draw needn't show every extreme that they name: `channel_slot`: each aligned run of 64 entries is a permutation of 0 .. 63.
All inputs are finite; a program needn't handle non-finite values.
Results may differ from the reference program's by a relative error of at most 0.0052.
Values may be sent and summed in bfloat16 or wider, within the bound.
No kernel may reach another device: no remote copies, remote signals or barrier semaphores. Data moves between devices by JAX's collectives and lax.ppermute only.
A program may use at most 64 MiB of HBM per device.

```python
import math
import jax
import jax.numpy as jnp
from jax import lax

CB = 64
WINDOWS = 128
BINS = 256
LAGS = 128
ROUNDS = 3
T_SAMP = 512
BLOCKS = 4
CHANNELS = 256
GROUPS_IN = 4
CH_GRP = 64
PIECE = 16
N_SUB = 2
N_REP = 2


def draw_channel_slot(key, part):
    key = jax.random.fold_in(key, 7)
    keys = jax.random.split(key, GROUPS_IN)
    orders = jax.vmap(lambda single: jax.random.permutation(single, CH_GRP))(keys)
    return orders.reshape(-1).astype(jnp.int32)


def block_scale(key, dims, cuts, smallest, top_value):
    factor_of, own = 1.0, jax.random.fold_in(key, 6)
    for axis_at, shards_of in cuts:
        steps = jnp.exp(jax.random.uniform(jax.random.fold_in(own, axis_at), (shards_of,), jnp.float32, smallest / len(cuts), top_value / len(cuts)))
        factor_of = factor_of * jnp.repeat(steps, dims[axis_at] // shards_of).reshape([-1 if axis == axis_at else 1 for axis in range(len(dims))])
    return factor_of


def noise(stream_key, dims, width, reach, cuts=(), kind=jnp.bfloat16):
    result = jax.random.normal(stream_key, dims, jnp.float32) * width
    if len(cuts) > 0:
        result = block_scale(stream_key, dims, cuts, -0.22, 0.18) * result
    return jnp.clip(result, min=-reach, max=reach).astype(kind)


def setup_inputs(seed: int = 0, part: int = 0) -> dict:
    key_of = jax.random.split(jax.random.key(seed), 3)
    part_splits = jax.random.split(jax.random.fold_in(key_of[2], part), 3)
    traces = noise(part_splits[0], (CHANNELS, WINDOWS, T_SAMP), 1.0, 6.0, ((0, 4), (1, 4)))
    channel_slot = draw_channel_slot(jax.random.fold_in(jax.random.fold_in(key_of[2], part), 71), part)
    return {"traces": traces, "channel_slot": channel_slot}


def dft_columns(samples, parts, sub_bins):
    shape = (samples, parts, 2, sub_bins)
    time_pos = lax.broadcasted_iota(jnp.int32, shape, 0)
    range_pos = lax.broadcasted_iota(jnp.int32, shape, 1)
    part_pos = lax.broadcasted_iota(jnp.int32, shape, 2)
    bin_pos = lax.broadcasted_iota(jnp.int32, shape, 3)
    frequency = range_pos * sub_bins + bin_pos
    angles = jnp.mod(time_pos * frequency, samples).astype(jnp.float32) * (2.0 * math.pi / samples)
    entries = jnp.where(part_pos == 0, jnp.cos(angles), -jnp.sin(angles))
    return entries.reshape(samples, parts * 2 * sub_bins).astype(jnp.bfloat16)

def lag_table(sub_bins, first_bin, lag_count, samples):
    frequency = first_bin + lax.broadcasted_iota(jnp.int32, (sub_bins, lag_count), 0)
    lag_offset = lax.broadcasted_iota(jnp.int32, (sub_bins, lag_count), 1) - lag_count // 2
    angles = jnp.mod(frequency * lag_offset, samples).astype(jnp.float32) * (2.0 * math.pi / samples)
    return jnp.stack([jnp.cos(angles), -jnp.sin(angles)], axis=1)

def reference(traces, channel_slot):
    dft_rows = dft_columns(T_SAMP, 1, BINS)
    grouped = traces.reshape(GROUPS_IN, CH_GRP, WINDOWS, T_SAMP)
    slots = channel_slot.reshape(GROUPS_IN, CH_GRP)

    def whiten(pair):
        rows, order = pair
        picked = jnp.take(rows, order, axis=0)
        spectrum = jnp.dot(picked.reshape(-1, T_SAMP), dft_rows, preferred_element_type=jnp.float32)
        energy = lax.optimization_barrier(jnp.sum(spectrum * spectrum, axis=1, keepdims=True)) / BINS
        whitened = (spectrum * lax.rsqrt(energy + 1e-05)).astype(jnp.bfloat16)
        return whitened.reshape(CH_GRP, WINDOWS, 2 * BINS)
    whitened = lax.map(whiten, (grouped, slots))
    blocks = whitened.reshape(N_SUB, N_REP, BLOCKS, PIECE, WINDOWS, 2, BINS)
    blocks = blocks.transpose(2, 1, 0, 3, 4, 5, 6).reshape(BLOCKS, CB, WINDOWS, 2, BINS)
    lag_rows = lag_table(BINS, 0, LAGS, T_SAMP)
    lag_scale = (2.0 / (WINDOWS * BINS)) ** 0.5

    def one_round(step):

        def one_block(block):
            own_rows = blocks[block].astype(jnp.float32)
            partner = blocks[(block + step) % BLOCKS].astype(jnp.float32)
            turned = jnp.stack([-partner[:, :, 1], partner[:, :, 0]], axis=2)
            partner_pair = jnp.stack([partner, turned], axis=0)
            cross_spec = jnp.einsum('iwpf,qjwpf->fqij', own_rows, partner_pair, precision=lax.Precision.HIGHEST)
            summed = jnp.einsum('fqij,fql->ijl', cross_spec, lag_rows, precision=lax.Precision.HIGHEST)
            return lag_scale * summed
        return lax.map(one_block, jnp.arange(BLOCKS, dtype=jnp.int32))
    results = [one_round(step) for step in range(1, ROUNDS + 1)]
    return jnp.stack(results)
```

```python
import math

import jax
import jax.numpy as jnp
import numpy as np
from jax import lax
from jax.experimental import pallas as pl
from jax.experimental.pallas import tpu as pltpu
from jax.sharding import PartitionSpec as P

LAGS = 128
ROUNDS = 3
LANES = 128
VMEM_BYTES = 48 * 1024 * 1024
NT = (((1,), (1,)), ((), ()))
TN = (((0,), (0,)), ((), ()))


def params(**more):
    return pltpu.CompilerParams(vmem_limit_bytes=VMEM_BYTES, **more)


def dft_rows_table(samples):
    bins = samples // 2
    turns = (np.arange(bins)[:, None] * np.arange(samples)[None, :]) % samples
    angles = turns.astype(np.float32) * np.float32(2.0 * math.pi / samples)
    table = np.concatenate([np.cos(angles), -np.sin(angles)], axis=0)
    return jnp.asarray(table.astype(np.float32)).astype(jnp.bfloat16)


def lag_rows_table(samples, scale):
    bins = samples // 2
    offsets = np.arange(LAGS) - LAGS // 2
    turns = (offsets[:, None] * np.arange(bins)[None, :]) % samples
    angles = turns.astype(np.float32) * np.float32(2.0 * math.pi / samples)
    table = np.concatenate([np.cos(angles), -np.sin(angles)], axis=1) * np.float32(scale)
    return jnp.asarray(table.astype(np.float32)).astype(jnp.bfloat16)


def order_rows(traces, slots, first_win, wins):
    rows, _, samples = traces.shape
    tiles = samples // LANES

    def kernel(slot_ref, in_ref, out_ref, wide):
        def move(n, carry):
            picked = in_ref[slot_ref[n]].astype(jnp.float32)
            for tile in range(tiles):
                wide[tile, pl.ds(n, wins, stride=rows), :] = picked[:, tile * LANES : (tile + 1) * LANES]
            return carry

        lax.fori_loop(0, rows, move, 0, unroll=4)

        def pack(w, carry):
            start = pl.multiple_of(w * rows, rows)
            for tile in range(tiles):
                out_ref[w, :, tile * LANES : (tile + 1) * LANES] = wide[tile, pl.ds(start, rows), :].astype(jnp.bfloat16)
            return carry

        lax.fori_loop(0, wins, pack, 0, unroll=2)

    return pl.pallas_call(
        kernel,
        out_shape=jax.ShapeDtypeStruct((wins, rows, samples), jnp.bfloat16),
        grid_spec=pltpu.PrefetchScalarGridSpec(
            num_scalar_prefetch=1,
            grid=(1,),
            in_specs=[pl.BlockSpec((rows, wins, samples), lambda g, s: (0, first_win // wins, 0))],
            out_specs=pl.BlockSpec((wins, rows, samples), lambda g, s: (0, 0, 0)),
            scratch_shapes=[pltpu.VMEM((tiles, wins * rows, LANES), jnp.float32)],
        ),
        compiler_params=params(),
        name="order_rows",
    )(slots, traces)


def spectra(own, other, own_sub, table, pieces):
    wins, rows, samples = own.shape
    bins = samples // 2
    piece = rows // pieces
    depth = 2 * wins

    def kernel(sub_ref, own_ref, other_ref, table_ref, out_ref, wide):
        own_first = sub_ref[0] == 0

        def one_pair(pair, carry):
            stacked = []
            for half in range(2):
                mine = own_ref[2 * pair + half]
                theirs = other_ref[2 * pair + half]
                first = jnp.where(own_first, mine, theirs)
                second = jnp.where(own_first, theirs, mine)
                for at in range(pieces):
                    stacked.append(first[at * piece : (at + 1) * piece])
                    stacked.append(second[at * piece : (at + 1) * piece])
            wave = jnp.concatenate(stacked, axis=0)
            spectrum = lax.dot_general(table_ref[...], wave, NT, preferred_element_type=jnp.float32)
            energy = jnp.sum(spectrum * spectrum, axis=0, keepdims=True) / bins
            white = spectrum * lax.rsqrt(energy + 1e-05)
            for half in range(2):
                for part in range(2):
                    wide[pl.ds(part * wins + 2 * pair + half, bins, stride=depth), :] = white[
                        part * bins : (part + 1) * bins, half * LANES : (half + 1) * LANES
                    ]
            return carry

        lax.fori_loop(0, wins // 2, one_pair, 0)

        def pack(f, carry):
            start = pl.multiple_of(f * depth, depth)
            out_ref[f] = wide[pl.ds(start, depth), :].astype(jnp.bfloat16)
            return carry

        lax.fori_loop(0, bins, pack, 0, unroll=8)

    whole = pl.BlockSpec(memory_space=pltpu.VMEM)
    return pl.pallas_call(
        kernel,
        out_shape=jax.ShapeDtypeStruct((bins, depth, LANES), jnp.bfloat16),
        in_specs=[pl.BlockSpec(memory_space=pltpu.SMEM), whole, whole, whole],
        out_specs=whole,
        scratch_shapes=[pltpu.VMEM((bins * depth, LANES), jnp.float32)],
        compiler_params=params(),
        name="spectra",
    )(own_sub, own, other, table)


def partial_correlations(scalars, own, other, lag_rows, at, blocks, out_type):
    bins, depth, _ = own[0].shape
    wins = depth // 2
    chunks = len(own)
    width = LANES // blocks
    step_bins = 32
    steps = bins // step_bins
    line = 2 * bins

    def kernel(scalar_ref, *refs):
        own_refs = refs[:chunks]
        other_refs = refs[chunks : 2 * chunks]
        lag_ref, out_ref, cross = refs[2 * chunks :]
        same = scalar_ref[0] == 1
        step = pl.program_id(0)

        def one_bin(f, carry):
            ys = [ref[f] for ref in own_refs]
            xs = [jnp.where(same, y, ref[f]) for y, ref in zip(ys, other_refs)]
            turned = []
            for y in ys:
                turned += [-y[wins:], y[:wins]]
            y = jnp.concatenate(ys, axis=0)
            rhs = jnp.concatenate([y, jnp.concatenate(turned, axis=0)], axis=1)
            x = jnp.concatenate(xs, axis=0)[:, at * width : (at + 1) * width]
            product = lax.dot_general(x, rhs, TN, preferred_element_type=jnp.float32)
            for part in range(2):
                cross[pl.ds(part * bins + step * step_bins + f, width, stride=line), :] = product[
                    :, part * LANES : (part + 1) * LANES
                ]
            return carry

        lax.fori_loop(0, step_bins, one_bin, 0, unroll=4)

        @pl.when(step == steps - 1)
        def _():
            def one_channel(i, carry):
                start = pl.multiple_of(i * line, line)
                values = cross[pl.ds(start, line), :].astype(jnp.bfloat16)
                lagged = jnp.dot(lag_ref[...], values, preferred_element_type=jnp.float32)
                turned = lagged.T.astype(out_type)
                for p in range(blocks):
                    if p != at:
                        out_ref[scalar_ref[1 + p], i] = turned[p * width : (p + 1) * width]
                return carry

            lax.fori_loop(0, width, one_channel, 0, unroll=2)

    spectra_spec = pl.BlockSpec((step_bins, depth, LANES), lambda g, s: (g, 0, 0))
    return pl.pallas_call(
        kernel,
        out_shape=jax.ShapeDtypeStruct((blocks - 1, width, width, LAGS), out_type),
        grid_spec=pltpu.PrefetchScalarGridSpec(
            num_scalar_prefetch=1,
            grid=(steps,),
            in_specs=[spectra_spec] * (2 * chunks) + [pl.BlockSpec((LAGS, line), lambda g, s: (0, 0))],
            out_specs=pl.BlockSpec((blocks - 1, width, width, LAGS), lambda g, s: (0, 0, 0, 0)),
            scratch_shapes=[pltpu.VMEM((width * line, LANES), jnp.float32)],
        ),
        compiler_params=params(dimension_semantics=("arbitrary",)),
        name="partial_correlations",
    )(scalars, *own, *other, lag_rows)


def send_order(chan_count):
    far = chan_count - 1
    orders = []
    for z in range(chan_count):
        right = list(range(far, z, -1))
        left = list(range(0, z))
        order = (right + left) if len(right) >= len(left) else (left + right)
        orders.append(order + [z])
    return np.asarray(orders, np.int32)


def shift(piece, by, first, last):
    return lax.ppermute(piece, "chan", [(z, z + by) for z in range(first, last + 1)])


def summed_in_place(traces, channel_slot):
    chan_count = lax.axis_size("chan")
    group_rows, win_here, samples = traces.shape
    piece_len = group_rows // chan_count
    z = lax.axis_index("chan")
    sub = lax.axis_index("sub")
    rep = lax.axis_index("rep")
    order = jnp.asarray(send_order(chan_count))[z]
    slots = channel_slot.reshape(chan_count, piece_len)[order].reshape(-1)
    scale = (2.0 / (win_here * chan_count * (samples // 2))) ** 0.5
    dft_rows = dft_rows_table(samples)
    lag_rows = lag_rows_table(samples, scale)
    swap = [(0, 1), (1, 0)]
    own, other = [], []
    chunk = 16
    for first in range(0, win_here, chunk):
        mine = order_rows(traces, slots, first, chunk)
        theirs = lax.ppermute(mine, "sub", swap)
        here = spectra(mine, theirs, sub[None].astype(jnp.int32), dft_rows, chan_count)
        own.append(here)
        other.append(lax.ppermute(here, ("sub", "rep"), [(0, 1), (3, 2)]))
    same = (sub == rep).astype(jnp.int32)[None]

    def part(at, out_type):
        rounds = jnp.mod(order - order[at] - 1, chan_count)
        scalars = jnp.concatenate([same, rounds]).astype(jnp.int32)
        return partial_correlations(scalars, own, other, lag_rows, at, chan_count, out_type)

    sends = [part(at, jnp.bfloat16) for at in range(chan_count - 1)]
    kept = part(chan_count - 1, jnp.float32)
    far = chan_count - 1
    wide = jnp.float32
    right = shift(sends[0], 1, 0, 0)
    left = shift(sends[0], -1, far, far)
    ends = (z == 0) | (z == far)
    second = jnp.where(ends, sends[1], sends[0]).astype(wide)
    right = shift((second + right.astype(wide)).astype(jnp.bfloat16), 1, 0, 1)
    left = shift((second + left.astype(wide)).astype(jnp.bfloat16), -1, far - 1, far)
    third_right = jnp.where(z == 1, sends[1], sends[2]).astype(wide)
    third_left = jnp.where(z == 2, sends[1], sends[2]).astype(wide)
    right = shift((third_right + right.astype(wide)).astype(jnp.bfloat16), 1, 0, 2)
    left = shift((third_left + left.astype(wide)).astype(jnp.bfloat16), -1, 1, far)
    return (kept + right.astype(wide) + left.astype(wide))[:, None]


def from_behind(shard, axis, by):
    count = lax.axis_size(axis)
    return lax.ppermute(shard, axis, [(i, (i + by) % count) for i in range(count)])


def dft_columns(samples, parts, sub_bins):
    shape = (samples, parts, 2, sub_bins)
    time_pos = lax.broadcasted_iota(jnp.int32, shape, 0)
    range_pos = lax.broadcasted_iota(jnp.int32, shape, 1)
    part_pos = lax.broadcasted_iota(jnp.int32, shape, 2)
    bin_pos = lax.broadcasted_iota(jnp.int32, shape, 3)
    frequency = range_pos * sub_bins + bin_pos
    angles = jnp.mod(time_pos * frequency, samples).astype(jnp.float32) * (2.0 * math.pi / samples)
    entries = jnp.where(part_pos == 0, jnp.cos(angles), -jnp.sin(angles))
    return entries.reshape(samples, parts * 2 * sub_bins).astype(jnp.bfloat16)


def lag_table(sub_bins, first_bin, lag_count, samples):
    frequency = first_bin + lax.broadcasted_iota(jnp.int32, (sub_bins, lag_count), 0)
    lag_offset = lax.broadcasted_iota(jnp.int32, (sub_bins, lag_count), 1) - lag_count // 2
    angles = jnp.mod(frequency * lag_offset, samples).astype(jnp.float32) * (2.0 * math.pi / samples)
    return jnp.stack([jnp.cos(angles), -jnp.sin(angles)], axis=1)


def moved_spectra(traces, channel_slot):
    chan_count = lax.axis_size("chan")
    sub_count = lax.axis_size("sub")
    group_rows, win_here, samples = traces.shape
    bin_count = samples // 2
    sub_bins = bin_count // sub_count
    bin_width = 2 * sub_bins
    piece_len = group_rows // chan_count
    picked = jnp.take(traces, channel_slot, axis=0)
    dft_rows = dft_columns(samples, sub_count, sub_bins)
    spectrum = jnp.dot(picked.reshape(-1, samples), dft_rows, preferred_element_type=jnp.float32)
    energy = jnp.sum(spectrum * spectrum, axis=1, keepdims=True) / bin_count
    whitened = (spectrum * lax.rsqrt(energy + 1e-05)).astype(jnp.bfloat16)
    whitened = whitened.reshape(chan_count, piece_len, win_here, sub_count, bin_width)
    regrouped = lax.all_to_all(whitened, "chan", split_axis=0, concat_axis=0, tiled=True)
    regrouped = lax.all_to_all(regrouped, "sub", split_axis=3, concat_axis=3, tiled=True)
    own_half = regrouped.transpose(3, 1, 0, 2, 4).reshape(sub_count * piece_len, chan_count * win_here, bin_width)
    own_block = lax.all_gather(own_half, "rep", axis=0, tiled=True)
    windows = own_block.shape[1]
    own_split = own_block.reshape(own_block.shape[0], windows, 2, sub_bins)
    lag_rows = lag_table(sub_bins, lax.axis_index("sub") * sub_bins, LAGS, samples)
    lag_scale = (2.0 / (windows * bin_count)) ** 0.5
    results = []
    for step in range(1, ROUNDS + 1):
        partner = from_behind(own_half, "chan", -step)
        partner_split = partner.reshape(partner.shape[0], windows, 2, sub_bins)
        turned = jnp.stack([-partner_split[:, :, 1], partner_split[:, :, 0]], axis=2)
        partner_pair = jnp.stack([partner_split, turned], axis=0)
        cross_spec = jnp.einsum("iwpf,qjwpf->fqij", own_split, partner_pair, preferred_element_type=jnp.float32)
        summed = jnp.einsum("fqij,fql->ijl", cross_spec, lag_rows, precision=lax.Precision.HIGHEST)
        results.append(lax.psum_scatter(lag_scale * summed, "sub", scatter_dimension=0, tiled=True))
    return jnp.stack(results)[:, None]


def solution(mesh):
    sizes = mesh.shape
    in_place = sizes["chan"] == ROUNDS + 1 and sizes["sub"] == 2 and sizes["rep"] == 2
    return jax.shard_map(
        summed_in_place if in_place else moved_spectra,
        mesh=mesh,
        in_specs=(P(("groups", "sub", "rep"), "chan", None), P(("groups", "sub", "rep"))),
        out_specs=P(None, ("groups", "chan"), "sub", "rep", None),
        check_vma=False,
    )
```

```python
import math

import jax
import jax.numpy as jnp
import numpy as np
from jax import lax
from jax.experimental import pallas as pl
from jax.experimental.pallas import tpu as pltpu
from jax.sharding import PartitionSpec as P

LAGS = 128
ROUNDS = 3
LANES = 128
VMEM_BYTES = 48 * 1024 * 1024
NT = (((1,), (1,)), ((), ()))
TN = (((0,), (0,)), ((), ()))


def params(**more):
    return pltpu.CompilerParams(vmem_limit_bytes=VMEM_BYTES, **more)


def dft_rows_table(samples):
    bins = samples // 2
    turns = (np.arange(bins)[:, None] * np.arange(samples)[None, :]) % samples
    angles = turns.astype(np.float32) * np.float32(2.0 * math.pi / samples)
    table = np.concatenate([np.cos(angles), -np.sin(angles)], axis=0)
    return jnp.asarray(table.astype(np.float32)).astype(jnp.bfloat16)


def lag_rows_table(samples, scale):
    bins = samples // 2
    offsets = np.arange(LAGS) - LAGS // 2
    turns = (offsets[:, None] * np.arange(bins)[None, :]) % samples
    angles = turns.astype(np.float32) * np.float32(2.0 * math.pi / samples)
    table = np.concatenate([np.cos(angles), -np.sin(angles)], axis=1) * np.float32(scale)
    return jnp.asarray(table.astype(np.float32)).astype(jnp.bfloat16)


def order_rows(traces, slots, first_win, wins):
    rows, _, samples = traces.shape
    tiles = samples // LANES

    def kernel(slot_ref, in_ref, out_ref, wide):
        def move(n, carry):
            picked = in_ref[slot_ref[n]].astype(jnp.float32)
            for tile in range(tiles):
                wide[tile, pl.ds(n, wins, stride=rows + 1), :] = picked[:, tile * LANES : (tile + 1) * LANES]
            return carry

        lax.fori_loop(0, rows, move, 0, unroll=4)

        def pack(w, carry):
            start = w * (rows + 1)
            for tile in range(tiles):
                out_ref[w, :, tile * LANES : (tile + 1) * LANES] = wide[tile, pl.ds(start, rows), :].astype(jnp.bfloat16)
            return carry

        lax.fori_loop(0, wins, pack, 0, unroll=2)

    return pl.pallas_call(
        kernel,
        out_shape=jax.ShapeDtypeStruct((wins, rows, samples), jnp.bfloat16),
        grid_spec=pltpu.PrefetchScalarGridSpec(
            num_scalar_prefetch=1,
            grid=(1,),
            in_specs=[pl.BlockSpec((rows, wins, samples), lambda g, s: (0, first_win // wins, 0))],
            out_specs=pl.BlockSpec((wins, rows, samples), lambda g, s: (0, 0, 0)),
            scratch_shapes=[pltpu.VMEM((tiles, (wins + 1) * (rows + 1), LANES), jnp.float32)],
        ),
        compiler_params=params(),
        name="order_rows",
    )(slots, traces)


def spectra(own, other, own_sub, table, pieces):
    wins, rows, samples = own.shape
    bins = samples // 2
    piece = rows // pieces
    depth = 2 * wins

    def kernel(sub_ref, own_ref, other_ref, table_ref, out_ref, wide):
        own_first = sub_ref[0] == 0

        def one_pair(pair, carry):
            stacked = []
            for half in range(2):
                mine = own_ref[2 * pair + half]
                theirs = other_ref[2 * pair + half]
                first = jnp.where(own_first, mine, theirs)
                second = jnp.where(own_first, theirs, mine)
                for at in range(pieces):
                    stacked.append(first[at * piece : (at + 1) * piece])
                    stacked.append(second[at * piece : (at + 1) * piece])
            wave = jnp.concatenate(stacked, axis=0)
            spectrum = lax.dot_general(table_ref[...], wave, NT, preferred_element_type=jnp.float32)
            energy = jnp.sum(spectrum * spectrum, axis=0, keepdims=True) / bins
            white = spectrum * lax.rsqrt(energy + 1e-05)
            for half in range(2):
                for part in range(2):
                    wide[pl.ds(part * wins + 2 * pair + half, bins, stride=depth + 1), :] = white[
                        part * bins : (part + 1) * bins, half * LANES : (half + 1) * LANES
                    ]
            return carry

        lax.fori_loop(0, wins // 2, one_pair, 0)

        def pack(f, carry):
            start = f * (depth + 1)
            out_ref[f] = wide[pl.ds(start, depth), :].astype(jnp.bfloat16)
            return carry

        lax.fori_loop(0, bins, pack, 0, unroll=8)

    whole = pl.BlockSpec(memory_space=pltpu.VMEM)
    return pl.pallas_call(
        kernel,
        out_shape=jax.ShapeDtypeStruct((bins, depth, LANES), jnp.bfloat16),
        in_specs=[pl.BlockSpec(memory_space=pltpu.SMEM), whole, whole, whole],
        out_specs=whole,
        scratch_shapes=[pltpu.VMEM(((bins + 1) * (depth + 1), LANES), jnp.float32)],
        compiler_params=params(),
        name="spectra",
    )(own_sub, own, other, table)


def partial_correlations(scalars, own, other, lag_rows, at, blocks, out_type):
    bins, depth, _ = own[0].shape
    wins = depth // 2
    chunks = len(own)
    width = LANES // blocks
    step_bins = 32
    steps = bins // step_bins
    line = 2 * bins

    def kernel(scalar_ref, *refs):
        own_refs = refs[:chunks]
        other_refs = refs[chunks : 2 * chunks]
        lag_ref, out_ref, cross = refs[2 * chunks :]
        same = scalar_ref[0] == 1
        step = pl.program_id(0)

        def one_bin(f, carry):
            ys = [ref[f] for ref in own_refs]
            xs = [jnp.where(same, y, ref[f]) for y, ref in zip(ys, other_refs)]
            turned = []
            for y in ys:
                turned += [-y[wins:], y[:wins]]
            y = jnp.concatenate(ys, axis=0)
            rhs = jnp.concatenate([y, jnp.concatenate(turned, axis=0)], axis=1)
            x = jnp.concatenate(xs, axis=0)[:, at * width : (at + 1) * width]
            product = lax.dot_general(x, rhs, TN, preferred_element_type=jnp.float32)
            for part in range(2):
                cross[pl.ds(part * bins + step * step_bins + f, width, stride=line + 1), :] = product[
                    :, part * LANES : (part + 1) * LANES
                ]
            return carry

        lax.fori_loop(0, step_bins, one_bin, 0, unroll=8)

        @pl.when(step == steps - 1)
        def _():
            def one_channel(i, carry):
                start = i * (line + 1)
                values = cross[pl.ds(start, line), :].astype(jnp.bfloat16)
                lagged = jnp.dot(lag_ref[...], values, preferred_element_type=jnp.float32)
                turned = lagged.T.astype(out_type)
                for p in range(blocks):
                    if p != at:
                        out_ref[scalar_ref[1 + p], i] = turned[p * width : (p + 1) * width]
                return carry

            lax.fori_loop(0, width, one_channel, 0, unroll=2)

    spectra_spec = pl.BlockSpec((step_bins, depth, LANES), lambda g, s: (g, 0, 0))
    return pl.pallas_call(
        kernel,
        out_shape=jax.ShapeDtypeStruct((blocks - 1, width, width, LAGS), out_type),
        grid_spec=pltpu.PrefetchScalarGridSpec(
            num_scalar_prefetch=1,
            grid=(steps,),
            in_specs=[spectra_spec] * (2 * chunks) + [pl.BlockSpec((LAGS, line), lambda g, s: (0, 0))],
            out_specs=pl.BlockSpec((blocks - 1, width, width, LAGS), lambda g, s: (0, 0, 0, 0)),
            scratch_shapes=[pltpu.VMEM(((width + 1) * (line + 1), LANES), jnp.float32)],
        ),
        compiler_params=params(dimension_semantics=("arbitrary",)),
        name="partial_correlations",
    )(scalars, *own, *other, lag_rows)


def send_order(chan_count):
    far = chan_count - 1
    orders = []
    for z in range(chan_count):
        right = list(range(far, z, -1))
        left = list(range(0, z))
        order = (right + left) if len(right) >= len(left) else (left + right)
        orders.append(order + [z])
    return np.asarray(orders, np.int32)


def shift(piece, by, first, last):
    return lax.ppermute(piece, "chan", [(z, z + by) for z in range(first, last + 1)])


def summed_in_place(traces, channel_slot):
    chan_count = lax.axis_size("chan")
    group_rows, win_here, samples = traces.shape
    piece_len = group_rows // chan_count
    z = lax.axis_index("chan")
    sub = lax.axis_index("sub")
    rep = lax.axis_index("rep")
    order = jnp.asarray(send_order(chan_count))[z]
    slots = channel_slot.reshape(chan_count, piece_len)[order].reshape(-1)
    scale = (2.0 / (win_here * chan_count * (samples // 2))) ** 0.5
    dft_rows = dft_rows_table(samples)
    lag_rows = lag_rows_table(samples, scale)
    swap = [(0, 1), (1, 0)]
    own, other = [], []
    chunk = 16
    for first in range(0, win_here, chunk):
        mine = order_rows(traces, slots, first, chunk)
        theirs = lax.ppermute(mine, "sub", swap)
        here = spectra(mine, theirs, sub[None].astype(jnp.int32), dft_rows, chan_count)
        own.append(here)
        other.append(lax.ppermute(here, ("sub", "rep"), [(0, 1), (3, 2)]))
    same = (sub == rep).astype(jnp.int32)[None]

    def part(at, out_type):
        rounds = jnp.mod(order - order[at] - 1, chan_count)
        scalars = jnp.concatenate([same, rounds]).astype(jnp.int32)
        return partial_correlations(scalars, own, other, lag_rows, at, chan_count, out_type)

    sends = [part(at, jnp.bfloat16) for at in range(chan_count - 1)]
    kept = part(chan_count - 1, jnp.float32)
    far = chan_count - 1
    wide = jnp.float32
    right = shift(sends[0], 1, 0, 0)
    left = shift(sends[0], -1, far, far)
    ends = (z == 0) | (z == far)
    second = jnp.where(ends, sends[1], sends[0]).astype(wide)
    right = shift((second + right.astype(wide)).astype(jnp.bfloat16), 1, 0, 1)
    left = shift((second + left.astype(wide)).astype(jnp.bfloat16), -1, far - 1, far)
    third_right = jnp.where(z == 1, sends[1], sends[2]).astype(wide)
    third_left = jnp.where(z == 2, sends[1], sends[2]).astype(wide)
    right = shift((third_right + right.astype(wide)).astype(jnp.bfloat16), 1, 0, 2)
    left = shift((third_left + left.astype(wide)).astype(jnp.bfloat16), -1, 1, far)
    return (kept + right.astype(wide) + left.astype(wide))[:, None]


def from_behind(shard, axis, by):
    count = lax.axis_size(axis)
    return lax.ppermute(shard, axis, [(i, (i + by) % count) for i in range(count)])


def dft_columns(samples, parts, sub_bins):
    shape = (samples, parts, 2, sub_bins)
    time_pos = lax.broadcasted_iota(jnp.int32, shape, 0)
    range_pos = lax.broadcasted_iota(jnp.int32, shape, 1)
    part_pos = lax.broadcasted_iota(jnp.int32, shape, 2)
    bin_pos = lax.broadcasted_iota(jnp.int32, shape, 3)
    frequency = range_pos * sub_bins + bin_pos
    angles = jnp.mod(time_pos * frequency, samples).astype(jnp.float32) * (2.0 * math.pi / samples)
    entries = jnp.where(part_pos == 0, jnp.cos(angles), -jnp.sin(angles))
    return entries.reshape(samples, parts * 2 * sub_bins).astype(jnp.bfloat16)


def lag_table(sub_bins, first_bin, lag_count, samples):
    frequency = first_bin + lax.broadcasted_iota(jnp.int32, (sub_bins, lag_count), 0)
    lag_offset = lax.broadcasted_iota(jnp.int32, (sub_bins, lag_count), 1) - lag_count // 2
    angles = jnp.mod(frequency * lag_offset, samples).astype(jnp.float32) * (2.0 * math.pi / samples)
    return jnp.stack([jnp.cos(angles), -jnp.sin(angles)], axis=1)


def moved_spectra(traces, channel_slot):
    chan_count = lax.axis_size("chan")
    sub_count = lax.axis_size("sub")
    group_rows, win_here, samples = traces.shape
    bin_count = samples // 2
    sub_bins = bin_count // sub_count
    bin_width = 2 * sub_bins
    piece_len = group_rows // chan_count
    picked = jnp.take(traces, channel_slot, axis=0)
    dft_rows = dft_columns(samples, sub_count, sub_bins)
    spectrum = jnp.dot(picked.reshape(-1, samples), dft_rows, preferred_element_type=jnp.float32)
    energy = jnp.sum(spectrum * spectrum, axis=1, keepdims=True) / bin_count
    whitened = (spectrum * lax.rsqrt(energy + 1e-05)).astype(jnp.bfloat16)
    whitened = whitened.reshape(chan_count, piece_len, win_here, sub_count, bin_width)
    regrouped = lax.all_to_all(whitened, "chan", split_axis=0, concat_axis=0, tiled=True)
    regrouped = lax.all_to_all(regrouped, "sub", split_axis=3, concat_axis=3, tiled=True)
    own_half = regrouped.transpose(3, 1, 0, 2, 4).reshape(sub_count * piece_len, chan_count * win_here, bin_width)
    own_block = lax.all_gather(own_half, "rep", axis=0, tiled=True)
    windows = own_block.shape[1]
    own_split = own_block.reshape(own_block.shape[0], windows, 2, sub_bins)
    lag_rows = lag_table(sub_bins, lax.axis_index("sub") * sub_bins, LAGS, samples)
    lag_scale = (2.0 / (windows * bin_count)) ** 0.5
    results = []
    for step in range(1, ROUNDS + 1):
        partner = from_behind(own_half, "chan", -step)
        partner_split = partner.reshape(partner.shape[0], windows, 2, sub_bins)
        turned = jnp.stack([-partner_split[:, :, 1], partner_split[:, :, 0]], axis=2)
        partner_pair = jnp.stack([partner_split, turned], axis=0)
        cross_spec = jnp.einsum("iwpf,qjwpf->fqij", own_split, partner_pair, preferred_element_type=jnp.float32)
        summed = jnp.einsum("fqij,fql->ijl", cross_spec, lag_rows, precision=lax.Precision.HIGHEST)
        results.append(lax.psum_scatter(lag_scale * summed, "sub", scatter_dimension=0, tiled=True))
    return jnp.stack(results)[:, None]


def solution(mesh):
    sizes = mesh.shape
    in_place = sizes["chan"] == ROUNDS + 1 and sizes["sub"] == 2 and sizes["rep"] == 2
    return jax.shard_map(
        summed_in_place if in_place else moved_spectra,
        mesh=mesh,
        in_specs=(P(("groups", "sub", "rep"), "chan", None), P(("groups", "sub", "rep"))),
        out_specs=P(None, ("groups", "chan"), "sub", "rep", None),
        check_vma=False,
    )
```

```python
import functools
import math

import jax
import jax.numpy as jnp
import numpy as np
from jax import lax
from jax.experimental import pallas as pl
from jax.experimental.pallas import tpu as pltpu
from jax.sharding import PartitionSpec as P

LAGS = 128
ROUNDS = 3
LANES = 128
HALF = LANES // 2
VMEM_BYTES = 56 * 1024 * 1024
NT = (((1,), (1,)), ((), ()))
AHEAD = (2, 1, 3, 0)
BLOCKS = len(AHEAD)
FAR = (0, 1)
NEAR = (2, 3)
OWN_AT = 3


def kernel_call(kernel, name, flops, bytes_accessed, **more):
    return pl.pallas_call(
        kernel,
        name=name,
        compiler_params=pltpu.CompilerParams(vmem_limit_bytes=VMEM_BYTES),
        cost_estimate=pl.CostEstimate(flops=flops, bytes_accessed=bytes_accessed, transcendentals=0),
        **more,
    )


def whole(shape):
    return pl.BlockSpec(shape, lambda g: (0,) * len(shape))


def dft_rows_table(samples):
    bins = samples // 2
    turns = (np.arange(bins)[:, None] * np.arange(samples)[None, :]) % samples
    angles = turns.astype(np.float32) * np.float32(2.0 * math.pi / samples)
    table = np.concatenate([np.cos(angles), -np.sin(angles)], axis=0)
    return jnp.asarray(table.astype(np.float32)).astype(jnp.bfloat16)


def lag_rows_table(samples, scale):
    bins = samples // 2
    offsets = np.arange(LAGS) - LAGS // 2
    turns = (offsets[:, None] * np.arange(bins)[None, :]) % samples
    angles = turns.astype(np.float32) * np.float32(2.0 * math.pi / samples)
    table = np.concatenate([np.cos(angles), -np.sin(angles)], axis=0) * np.float32(scale)
    return jnp.asarray(table.astype(np.float32)).astype(jnp.bfloat16)


def order_rows(traces, slots):
    rows, wins, samples = traces.shape
    tiles = samples // LANES
    piece = rows // BLOCKS
    step_wins = 16
    pitch = rows + 1

    def kernel(slot_ref, in_ref, all_ref, far_ref, near_ref, wide):
        z = lax.axis_index("chan")
        for at, ahead in enumerate(AHEAD):
            first = lax.rem(z + ahead, BLOCKS) * piece

            def move(j, carry, at=at, first=first):
                picked = in_ref[slot_ref[first + j]].astype(jnp.float32)
                for tile in range(tiles):
                    wide[tile, pl.ds(at * piece + j, step_wins, stride=pitch), :] = picked[
                        :, tile * LANES : (tile + 1) * LANES
                    ]
                return carry

            lax.fori_loop(0, piece, move, 0, unroll=4)

        def pack(w, carry):
            for tile in range(tiles):
                block = wide[tile, pl.ds(w * pitch, rows), :].astype(jnp.bfloat16)
                here = slice(tile * LANES, (tile + 1) * LANES)
                all_ref[w, :, here] = block
                far_ref[w, :, here] = block[: rows // 2]
                near_ref[w, :, here] = block[rows // 2 :]
            return carry

        lax.fori_loop(0, step_wins, pack, 0, unroll=2)

    def out(count):
        return jax.ShapeDtypeStruct((wins, count, samples), jnp.bfloat16)

    def out_spec(count):
        return pl.BlockSpec((step_wins, count, samples), lambda g: (g, 0, 0))

    half = rows // 2
    return kernel_call(
        kernel,
        "order_rows",
        0,
        3 * traces.size * 2,
        out_shape=(out(rows), out(half), out(half)),
        grid=(wins // step_wins,),
        in_specs=[
            pl.BlockSpec(memory_space=pltpu.SMEM),
            pl.BlockSpec((rows, step_wins, samples), lambda g: (0, g, 0)),
        ],
        out_specs=(out_spec(rows), out_spec(half), out_spec(half)),
        scratch_shapes=[pltpu.VMEM((tiles, (step_wins + 1) * pitch, LANES), jnp.float32)],
    )(slots, traces)


def spectra(rows_j, rows_i, table, with_j):
    count = len(rows_j)
    wins, _, samples = rows_j[0].shape
    given = sum(rows.shape[1] for rows in rows_j)
    bins = samples // 2
    depth = 2 * wins
    pitch = depth + 1
    step_wins = 8
    steps = wins // step_wins

    def kernel(*refs):
        j_refs, i_refs, table_ref = refs[:count], refs[count : 2 * count], refs[2 * count]
        i_out, j_out, wide = refs[2 * count + 1], refs[-2], refs[-1]
        same = lax.axis_index("sub") == lax.axis_index("rep")
        step = pl.program_id(0)
        blank = [jnp.zeros((HALF - given, samples), jnp.bfloat16)] if given < HALF else []

        def one_pair(pair, carry):
            stacked = []
            for half in range(2):
                js = [ref[2 * pair + half] for ref in j_refs]
                others = [ref[2 * pair + half] for ref in i_refs]
                stacked += js + blank + [jnp.where(same, a, b) for a, b in zip(js, others)] + blank
            wave = jnp.concatenate(stacked, axis=0)
            spectrum = lax.dot_general(table_ref[...], wave, NT, preferred_element_type=jnp.float32)
            energy = jnp.sum(spectrum * spectrum, axis=0, keepdims=True) / bins
            white = spectrum * lax.rsqrt(energy + 1e-05)
            win = step * step_wins + 2 * pair
            for half in range(2):
                for part in range(2):
                    wide[pl.ds(part * wins + win + half, bins, stride=pitch), :] = white[
                        part * bins : (part + 1) * bins, half * LANES : (half + 1) * LANES
                    ]
            return carry

        lax.fori_loop(0, step_wins // 2, one_pair, 0, unroll=2)

        @pl.when(step == steps - 1)
        def _():
            lower = lax.broadcasted_iota(jnp.int32, (depth, LANES), 1) < HALF

            def pack(f, carry):
                values = wide[pl.ds(f * pitch, depth), :]
                i_out[f] = values.astype(jnp.bfloat16).T[HALF:]
                if with_j:
                    turned = jnp.concatenate([-values[wins:], values[:wins]], axis=0)
                    j_out[f] = jnp.where(lower, values, pltpu.roll(turned, HALF, 1)).astype(jnp.bfloat16)
                return carry

            lax.fori_loop(0, bins, pack, 0, unroll=8)

    def in_spec(rows):
        return pl.BlockSpec((step_wins, rows.shape[1], samples), lambda g: (g, 0, 0))

    i_shape, j_shape = (bins, HALF, depth), (bins, depth, LANES)
    shapes = [i_shape, j_shape] if with_j else [i_shape]
    return kernel_call(
        kernel,
        "spectra",
        2 * samples * samples * wins * LANES,
        4 * wins * LANES * samples * 2,
        out_shape=[jax.ShapeDtypeStruct(shape, jnp.bfloat16) for shape in shapes],
        grid=(steps,),
        in_specs=[in_spec(rows) for rows in rows_j + rows_i] + [whole(table.shape)],
        out_specs=[whole(shape) for shape in shapes],
        scratch_shapes=[pltpu.VMEM(((bins + 1) * pitch, LANES), jnp.float32)],
    )(*rows_j, *rows_i, table)


def partial_correlations(lefts, rights, lag_rows, jobs):
    bins, depth, _ = rights[0].shape
    piece = HALF // BLOCKS
    pitch = bins + 1
    step_bins = 32
    steps = bins // step_bins
    flat = [(right, left, at) for right, pairs in enumerate(jobs) for left, at in pairs]
    dests = sorted({at for _, _, at in flat})
    places = {at: [entry for entry in flat if entry[2] == at] for at in dests}
    total = len(flat) * piece

    def kernel(*refs):
        left_refs, rest = refs[: len(lefts)], refs[len(lefts) :]
        right_refs, rest = rest[: len(rights)], rest[len(rights) :]
        lag_ref, out_refs, cross = rest[0], rest[1:-1], rest[-1]
        step = pl.program_id(0)

        def one_bin(f, carry):
            first = 0
            for right, pairs in enumerate(jobs):
                rows = [left_refs[left][f, at * piece : (at + 1) * piece] for left, at in pairs]
                lhs = jnp.concatenate(rows, axis=0) if len(rows) > 1 else rows[0]
                product = jnp.dot(lhs, right_refs[right][f], preferred_element_type=jnp.float32)
                here = first * pitch + step * step_bins + f
                cross[pl.ds(here, lhs.shape[0], stride=pitch), :] = product
                first += lhs.shape[0]
            return carry

        lax.fori_loop(0, step_bins, one_bin, 0, unroll=8)

        @pl.when(step == steps - 1)
        def _():
            lower = lax.broadcasted_iota(jnp.int32, (LAGS, LANES), 1) < HALF
            for index, entry in enumerate(flat):
                at = entry[2]
                out = out_refs[dests.index(at)]
                place = places[at].index(entry)

                def one_pair(pair, carry, index=index, at=at, out=out, place=place):
                    start = (index * piece + 2 * pair) * pitch
                    values = jnp.concatenate(
                        [cross[pl.ds(start, bins), :], cross[pl.ds(start + pitch, bins), :]], axis=1
                    ).astype(jnp.bfloat16)
                    both = jnp.dot(lag_ref[...], values, preferred_element_type=jnp.float32)
                    re, im = both[:LAGS], both[LAGS:]
                    lagged = jnp.where(lower, re[:, :LANES], pltpu.roll(re[:, LANES:], HALF, 1))
                    lagged += jnp.where(lower, pltpu.roll(im[:, :LANES], HALF, 1), im[:, LANES:])
                    turned = lagged.T.astype(out.dtype)
                    for half in range(2):
                        for there in range(BLOCKS):
                            if there != at:
                                after = (AHEAD[there] - AHEAD[at]) % BLOCKS - 1
                                row = half * HALF + there * piece
                                out[place, after, 2 * pair + half] = turned[row : row + piece]
                    return carry

                lax.fori_loop(0, piece // 2, one_pair, 0, unroll=2)

    shapes = [(len(places[at]), BLOCKS - 1, piece, piece, LAGS) for at in dests]
    types = [jnp.float32 if at == OWN_AT else jnp.bfloat16 for at in dests]
    return kernel_call(
        kernel,
        "partial_correlations",
        2 * total * bins * depth * LANES + 2 * total * bins * LANES * 2 * LAGS,
        2 * sum(array.size for array in lefts + rights),
        out_shape=[jax.ShapeDtypeStruct(shape, kind) for shape, kind in zip(shapes, types)],
        grid=(steps,),
        in_specs=[pl.BlockSpec((step_bins,) + array.shape[1:], lambda g: (g, 0, 0)) for array in lefts + rights]
        + [whole(lag_rows.shape)],
        out_specs=[whole(shape) for shape in shapes],
        scratch_shapes=[pltpu.VMEM(((total + 1) * pitch, LANES), jnp.float32)],
    )(*lefts, *rights, lag_rows)


def assembled(shares):
    arrays = []
    for array, _, _, _ in shares:
        if not any(array is known for known in arrays):
            arrays.append(array)
    index = [next(at for at, known in enumerate(arrays) if known is array) for array, _, _, _ in shares]
    _, rounds, piece, _, lags = arrays[0].shape
    width = 2 * piece

    def kernel(*refs):
        out = refs[-1]
        sub = lax.axis_index("sub")
        for i_other in range(2):
            for j_other in range(2):
                parts = [
                    refs[at][place, 0].astype(jnp.float32)
                    for at, (_, place, i_is, j_is) in zip(index, shares)
                    if (i_is, j_is) == (i_other, j_other)
                ]
                i_first = jnp.where(sub == 0, i_other, 1 - i_other) * piece
                j_first = pl.multiple_of(jnp.where(sub == 0, j_other, 1 - j_other) * piece, piece)
                out[0, 0, pl.ds(i_first, piece), pl.ds(j_first, piece), :] = functools.reduce(jnp.add, parts)

    return kernel_call(
        kernel,
        "assembled",
        0,
        sum(array.size for array in arrays) * 2,
        out_shape=jax.ShapeDtypeStruct((rounds, 1, width, width, lags), jnp.float32),
        grid=(rounds,),
        in_specs=[
            pl.BlockSpec((array.shape[0], 1, piece, piece, lags), lambda g: (0, g, 0, 0, 0)) for array in arrays
        ],
        out_specs=pl.BlockSpec((1, 1, width, width, lags), lambda g: (g, 0, 0, 0, 0)),
    )(*arrays)


def summed_in_place(traces, channel_slot):
    chan_count = lax.axis_size("chan")
    _, win_here, samples = traces.shape
    scale = (2.0 / (win_here * chan_count * (samples // 2))) ** 0.5
    dft_rows = dft_rows_table(samples)
    lag_rows = lag_rows_table(samples, scale)

    def over_sub(rows):
        return lax.ppermute(rows, "sub", [(0, 1), (1, 0)])

    def over_core(rows):
        return lax.ppermute(rows, ("sub", "rep"), [(0, 1), (3, 2)])

    def to_owner(share, at):
        by = AHEAD[at]
        return lax.ppermute(share, "chan", [(z, (z + by) % chan_count) for z in range(chan_count)])

    mine, mine_far, mine_near = order_rows(traces, channel_slot)
    far = over_sub(mine_far)
    near = over_sub(mine_near)
    shares = []

    def collect(at, share, kinds):
        arrived = share if at == OWN_AT else to_owner(share, at)
        shares.extend((arrived, place, i_other, j_other) for place, (i_other, j_other) in enumerate(kinds))

    own_i, own_j = spectra([mine], [over_core(mine)], dft_rows, True)
    parts = partial_correlations([own_i], [own_j], lag_rows, [[(0, at) for at in range(BLOCKS)]])
    for at in range(BLOCKS):
        collect(at, parts[at], [(0, 0)])

    far_core = over_core(far)
    (far_i,) = spectra([far], [far_core], dft_rows, False)
    parts = partial_correlations([far_i], [own_j], lag_rows, [[(0, at) for at in FAR]])
    for at, part in zip(FAR, parts):
        collect(at, part, [(1, 0)])

    other_i, other_j = spectra([far, near], [far_core, over_core(near)], dft_rows, True)
    parts = partial_correlations(
        [own_i, other_i], [other_j], lag_rows, [[(0, at) for at in FAR] + [(1, at) for at in FAR]]
    )
    for at, part in zip(FAR, parts):
        collect(at, part, [(0, 1), (1, 1)])
    parts = partial_correlations(
        [own_i, other_i],
        [other_j, own_j],
        lag_rows,
        [[(0, at) for at in NEAR] + [(1, at) for at in NEAR], [(1, at) for at in NEAR]],
    )
    for at, part in zip(NEAR, parts):
        collect(at, part, [(0, 1), (1, 1), (1, 0)])
    return assembled(shares)


def from_behind(shard, axis, by):
    count = lax.axis_size(axis)
    return lax.ppermute(shard, axis, [(i, (i + by) % count) for i in range(count)])


def dft_columns(samples, parts, sub_bins):
    shape = (samples, parts, 2, sub_bins)
    time_pos = lax.broadcasted_iota(jnp.int32, shape, 0)
    range_pos = lax.broadcasted_iota(jnp.int32, shape, 1)
    part_pos = lax.broadcasted_iota(jnp.int32, shape, 2)
    bin_pos = lax.broadcasted_iota(jnp.int32, shape, 3)
    frequency = range_pos * sub_bins + bin_pos
    angles = jnp.mod(time_pos * frequency, samples).astype(jnp.float32) * (2.0 * math.pi / samples)
    entries = jnp.where(part_pos == 0, jnp.cos(angles), -jnp.sin(angles))
    return entries.reshape(samples, parts * 2 * sub_bins).astype(jnp.bfloat16)


def lag_table(sub_bins, first_bin, lag_count, samples):
    frequency = first_bin + lax.broadcasted_iota(jnp.int32, (sub_bins, lag_count), 0)
    lag_offset = lax.broadcasted_iota(jnp.int32, (sub_bins, lag_count), 1) - lag_count // 2
    angles = jnp.mod(frequency * lag_offset, samples).astype(jnp.float32) * (2.0 * math.pi / samples)
    return jnp.stack([jnp.cos(angles), -jnp.sin(angles)], axis=1)


def moved_spectra(traces, channel_slot):
    chan_count = lax.axis_size("chan")
    sub_count = lax.axis_size("sub")
    group_rows, win_here, samples = traces.shape
    bin_count = samples // 2
    sub_bins = bin_count // sub_count
    bin_width = 2 * sub_bins
    piece_len = group_rows // chan_count
    picked = jnp.take(traces, channel_slot, axis=0)
    dft_rows = dft_columns(samples, sub_count, sub_bins)
    spectrum = jnp.dot(picked.reshape(-1, samples), dft_rows, preferred_element_type=jnp.float32)
    energy = jnp.sum(spectrum * spectrum, axis=1, keepdims=True) / bin_count
    whitened = (spectrum * lax.rsqrt(energy + 1e-05)).astype(jnp.bfloat16)
    whitened = whitened.reshape(chan_count, piece_len, win_here, sub_count, bin_width)
    regrouped = lax.all_to_all(whitened, "chan", split_axis=0, concat_axis=0, tiled=True)
    regrouped = lax.all_to_all(regrouped, "sub", split_axis=3, concat_axis=3, tiled=True)
    own_half = regrouped.transpose(3, 1, 0, 2, 4).reshape(sub_count * piece_len, chan_count * win_here, bin_width)
    own_block = lax.all_gather(own_half, "rep", axis=0, tiled=True)
    windows = own_block.shape[1]
    own_split = own_block.reshape(own_block.shape[0], windows, 2, sub_bins)
    lag_rows = lag_table(sub_bins, lax.axis_index("sub") * sub_bins, LAGS, samples)
    lag_scale = (2.0 / (windows * bin_count)) ** 0.5
    results = []
    for step in range(1, ROUNDS + 1):
        partner = from_behind(own_half, "chan", -step)
        partner_split = partner.reshape(partner.shape[0], windows, 2, sub_bins)
        turned = jnp.stack([-partner_split[:, :, 1], partner_split[:, :, 0]], axis=2)
        partner_pair = jnp.stack([partner_split, turned], axis=0)
        cross_spec = jnp.einsum("iwpf,qjwpf->fqij", own_split, partner_pair, preferred_element_type=jnp.float32)
        summed = jnp.einsum("fqij,fql->ijl", cross_spec, lag_rows, precision=lax.Precision.HIGHEST)
        results.append(lax.psum_scatter(lag_scale * summed, "sub", scatter_dimension=0, tiled=True))
    return jnp.stack(results)[:, None]


def solution(mesh):
    sizes = mesh.shape
    in_place = sizes["chan"] == BLOCKS == ROUNDS + 1 and sizes["sub"] == 2 and sizes["rep"] == 2
    return jax.shard_map(
        summed_in_place if in_place else moved_spectra,
        mesh=mesh,
        in_specs=(P(("groups", "sub", "rep"), "chan", None), P(("groups", "sub", "rep"))),
        out_specs=P(None, ("groups", "chan"), "sub", "rep", None),
        check_vma=False,
    )
```

```python
import functools
import math

import jax
import jax.numpy as jnp
import numpy as np
from jax import lax
from jax.experimental import pallas as pl
from jax.experimental.pallas import tpu as pltpu
from jax.sharding import PartitionSpec as P

LAGS = 128
ROUNDS = 3
LANES = 128
HALF = LANES // 2
VMEM_BYTES = 56 * 1024 * 1024
NT = (((1,), (1,)), ((), ()))
AHEAD = (2, 1, 3, 0)
BLOCKS = len(AHEAD)
FAR = (0, 1)
NEAR = (2, 3)
OWN_AT = 3


def kernel_call(kernel, name, flops, bytes_accessed, **more):
    return pl.pallas_call(
        kernel,
        name=name,
        compiler_params=pltpu.CompilerParams(vmem_limit_bytes=VMEM_BYTES),
        cost_estimate=pl.CostEstimate(flops=flops, bytes_accessed=bytes_accessed, transcendentals=0),
        **more,
    )


def whole(shape):
    return pl.BlockSpec(shape, lambda g: (0,) * len(shape))


def dft_rows_table(samples):
    bins = samples // 2
    turns = (np.arange(bins)[:, None] * np.arange(samples)[None, :]) % samples
    angles = turns.astype(np.float32) * np.float32(2.0 * math.pi / samples)
    table = np.concatenate([np.cos(angles), -np.sin(angles)], axis=0)
    return jnp.asarray(table.astype(np.float32)).astype(jnp.bfloat16)


def lag_columns_table(samples, scale):
    bins = samples // 2
    offsets = np.arange(LAGS) - LAGS // 2
    turns = (np.arange(bins)[:, None] * offsets[None, :]) % samples
    angles = turns.astype(np.float32) * np.float32(2.0 * math.pi / samples)
    table = np.concatenate([np.cos(angles), -np.sin(angles)], axis=0) * np.float32(scale)
    return jnp.asarray(table.astype(np.float32)).astype(jnp.bfloat16)


def order_rows(traces, slots):
    rows, wins, samples = traces.shape
    tiles = samples // LANES
    piece = rows // BLOCKS
    step_wins = 16
    pitch = rows + 1
    batch = 4

    def kernel(slot_ref, in_ref, all_ref, far_ref, near_ref, wide):
        z = lax.axis_index("chan")
        for at, ahead in enumerate(AHEAD):
            first = lax.rem(z + ahead, BLOCKS) * piece

            def move(group, carry, at=at, first=first):
                js = [group * batch + u for u in range(batch)]
                picked = [in_ref[slot_ref[first + j]].astype(jnp.float32) for j in js]
                for j, row in zip(js, picked):
                    for tile in range(tiles):
                        wide[tile, pl.ds(at * piece + j, step_wins, stride=pitch), :] = row[
                            :, tile * LANES : (tile + 1) * LANES
                        ]
                return carry

            lax.fori_loop(0, piece // batch, move, 0)

        def pack(w, carry):
            blocks = [wide[tile, pl.ds(w * pitch, rows), :].astype(jnp.bfloat16) for tile in range(tiles)]
            for tile, block in enumerate(blocks):
                here = slice(tile * LANES, (tile + 1) * LANES)
                all_ref[w, :, here] = block
                far_ref[w, :, here] = block[: rows // 2]
                near_ref[w, :, here] = block[rows // 2 :]
            return carry

        lax.fori_loop(0, step_wins, pack, 0, unroll=2)

    def out(count):
        return jax.ShapeDtypeStruct((wins, count, samples), jnp.bfloat16)

    def out_spec(count):
        return pl.BlockSpec((step_wins, count, samples), lambda g: (g, 0, 0))

    half = rows // 2
    return kernel_call(
        kernel,
        "order_rows",
        0,
        3 * traces.size * 2,
        out_shape=(out(rows), out(half), out(half)),
        grid=(wins // step_wins,),
        in_specs=[
            pl.BlockSpec(memory_space=pltpu.SMEM),
            pl.BlockSpec((rows, step_wins, samples), lambda g: (0, g, 0)),
        ],
        out_specs=(out_spec(rows), out_spec(half), out_spec(half)),
        scratch_shapes=[pltpu.VMEM((tiles, (step_wins + 1) * pitch, LANES), jnp.float32)],
    )(slots, traces)


def spectra(rows_j, rows_i, table, with_j):
    count = len(rows_j)
    wins, _, samples = rows_j[0].shape
    given = sum(rows.shape[1] for rows in rows_j)
    bins = samples // 2
    depth = 2 * wins
    pitch = depth + 1
    step_wins = 8
    steps = wins // step_wins
    batch = 4

    def kernel(*refs):
        j_refs, i_refs, table_ref = refs[:count], refs[count : 2 * count], refs[2 * count]
        i_out, j_out, wide = refs[2 * count + 1], refs[-2], refs[-1]
        same = lax.axis_index("sub") == lax.axis_index("rep")
        step = pl.program_id(0)
        blank = [jnp.zeros((HALF - given, samples), jnp.bfloat16)] if given < HALF else []

        def two_pairs(group, carry):
            spectra_here = []
            for pair in (2 * group, 2 * group + 1):
                stacked = []
                for half in range(2):
                    js = [ref[2 * pair + half] for ref in j_refs]
                    others = [ref[2 * pair + half] for ref in i_refs]
                    stacked += js + blank + [jnp.where(same, a, b) for a, b in zip(js, others)] + blank
                wave = jnp.concatenate(stacked, axis=0)
                spectra_here.append(lax.dot_general(table_ref[...], wave, NT, preferred_element_type=jnp.float32))
            for at, spectrum in enumerate(spectra_here):
                energy = jnp.sum(spectrum * spectrum, axis=0, keepdims=True) / bins
                white = spectrum * lax.rsqrt(energy + 1e-05)
                win = step * step_wins + 4 * group + 2 * at
                for half in range(2):
                    for part in range(2):
                        wide[pl.ds(part * wins + win + half, bins, stride=pitch), :] = white[
                            part * bins : (part + 1) * bins, half * LANES : (half + 1) * LANES
                        ]
            return carry

        lax.fori_loop(0, step_wins // 4, two_pairs, 0)

        @pl.when(step == steps - 1)
        def _():
            lower = lax.broadcasted_iota(jnp.int32, (depth, LANES), 1) < HALF

            def pack(group, carry):
                fs = [group * batch + u for u in range(batch)]
                loaded = [wide[pl.ds(f * pitch, depth), :] for f in fs]
                i_rows = [values.astype(jnp.bfloat16).T[HALF:] for values in loaded]
                if with_j:
                    turned = [jnp.concatenate([-values[wins:], values[:wins]], axis=0) for values in loaded]
                    j_rows = [
                        jnp.where(lower, values, pltpu.roll(other, HALF, 1)).astype(jnp.bfloat16)
                        for values, other in zip(loaded, turned)
                    ]
                    for f, rows in zip(fs, j_rows):
                        j_out[f] = rows
                for f, rows in zip(fs, i_rows):
                    i_out[f] = rows
                return carry

            lax.fori_loop(0, bins // batch, pack, 0)

    def in_spec(rows):
        return pl.BlockSpec((step_wins, rows.shape[1], samples), lambda g: (g, 0, 0))

    i_shape, j_shape = (bins, HALF, depth), (bins, depth, LANES)
    shapes = [i_shape, j_shape] if with_j else [i_shape]
    return kernel_call(
        kernel,
        "spectra",
        2 * samples * samples * wins * LANES,
        4 * wins * LANES * samples * 2,
        out_shape=[jax.ShapeDtypeStruct(shape, jnp.bfloat16) for shape in shapes],
        grid=(steps,),
        in_specs=[in_spec(rows) for rows in rows_j + rows_i] + [whole(table.shape)],
        out_specs=[whole(shape) for shape in shapes],
        scratch_shapes=[pltpu.VMEM(((bins + 1) * pitch, LANES), jnp.float32)],
    )(*rows_j, *rows_i, table)


def partial_correlations(lefts, rights, lag_columns, jobs):
    bins, depth, _ = rights[0].shape
    piece = HALF // BLOCKS
    pitch = bins + 1
    step_bins = 32
    steps = bins // step_bins
    flat = [(right, left, at) for right, pairs in enumerate(jobs) for left, at in pairs]
    dests = sorted({at for _, _, at in flat})
    places = {at: [entry for entry in flat if entry[2] == at] for at in dests}
    total = len(flat) * piece
    batch = 8 if total <= 2 * piece else 4
    together = 4

    def kernel(*refs):
        left_refs, rest = refs[: len(lefts)], refs[len(lefts) :]
        right_refs, rest = rest[: len(rights)], rest[len(rights) :]
        lag_ref, out_refs, cross = rest[0], rest[1:-1], rest[-1]
        step = pl.program_id(0)

        def some_bins(group, carry):
            found = []
            for f in [group * batch + u for u in range(batch)]:
                first = 0
                for right, pairs in enumerate(jobs):
                    rows = [left_refs[left][f, at * piece : (at + 1) * piece] for left, at in pairs]
                    lhs = jnp.concatenate(rows, axis=0) if len(rows) > 1 else rows[0]
                    product = jnp.dot(lhs, right_refs[right][f], preferred_element_type=jnp.float32)
                    found.append((first * pitch + step * step_bins + f, product))
                    first += lhs.shape[0]
            for here, product in found:
                cross[pl.ds(here, product.shape[0], stride=pitch), :] = product
            return carry

        lax.fori_loop(0, step_bins // batch, some_bins, 0)

        @pl.when(step == steps - 1)
        def _():
            for index, entry in enumerate(flat):
                at = entry[2]
                out = out_refs[dests.index(at)]
                place = places[at].index(entry)

                def some_channels(group, carry, index=index, at=at, out=out, place=place):
                    lines = []
                    for u in range(together):
                        start = (index * piece + together * group + u) * pitch
                        line = cross[pl.ds(start, bins), :].astype(jnp.bfloat16).T
                        lines.append(jnp.concatenate([line[:HALF], line[HALF:]], axis=1))
                    lagged = jnp.dot(
                        jnp.concatenate(lines, axis=0), lag_ref[...], preferred_element_type=jnp.float32
                    ).astype(out.dtype)
                    for u in range(together):
                        for there in range(BLOCKS):
                            if there != at:
                                after = (AHEAD[there] - AHEAD[at]) % BLOCKS - 1
                                row = u * HALF + there * piece
                                out[place, after, together * group + u] = lagged[row : row + piece]
                    return carry

                lax.fori_loop(0, piece // together, some_channels, 0)

    shapes = [(len(places[at]), BLOCKS - 1, piece, piece, LAGS) for at in dests]
    types = [jnp.float32 if at == OWN_AT else jnp.bfloat16 for at in dests]
    return kernel_call(
        kernel,
        "partial_correlations",
        2 * total * bins * depth * LANES + 2 * total * bins * LANES * 2 * LAGS,
        2 * sum(array.size for array in lefts + rights),
        out_shape=[jax.ShapeDtypeStruct(shape, kind) for shape, kind in zip(shapes, types)],
        grid=(steps,),
        in_specs=[pl.BlockSpec((step_bins,) + array.shape[1:], lambda g: (g, 0, 0)) for array in lefts + rights]
        + [whole(lag_columns.shape)],
        out_specs=[whole(shape) for shape in shapes],
        scratch_shapes=[pltpu.VMEM(((total + 1) * pitch, LANES), jnp.float32)],
    )(*lefts, *rights, lag_columns)


def assembled(shares):
    arrays = []
    for array, _, _, _ in shares:
        if not any(array is known for known in arrays):
            arrays.append(array)
    index = [next(at for at, known in enumerate(arrays) if known is array) for array, _, _, _ in shares]
    _, rounds, piece, _, lags = arrays[0].shape
    width = 2 * piece

    def kernel(*refs):
        out = refs[-1]
        sub = lax.axis_index("sub")
        for i_other in range(2):
            for j_other in range(2):
                parts = [
                    refs[at][place, 0].astype(jnp.float32)
                    for at, (_, place, i_is, j_is) in zip(index, shares)
                    if (i_is, j_is) == (i_other, j_other)
                ]
                i_first = jnp.where(sub == 0, i_other, 1 - i_other) * piece
                j_first = pl.multiple_of(jnp.where(sub == 0, j_other, 1 - j_other) * piece, piece)
                out[0, 0, pl.ds(i_first, piece), pl.ds(j_first, piece), :] = functools.reduce(jnp.add, parts)

    return kernel_call(
        kernel,
        "assembled",
        0,
        sum(array.size for array in arrays) * 2,
        out_shape=jax.ShapeDtypeStruct((rounds, 1, width, width, lags), jnp.float32),
        grid=(rounds,),
        in_specs=[
            pl.BlockSpec((array.shape[0], 1, piece, piece, lags), lambda g: (0, g, 0, 0, 0)) for array in arrays
        ],
        out_specs=pl.BlockSpec((1, 1, width, width, lags), lambda g: (g, 0, 0, 0, 0)),
    )(*arrays)


def summed_in_place(traces, channel_slot):
    chan_count = lax.axis_size("chan")
    _, win_here, samples = traces.shape
    scale = (2.0 / (win_here * chan_count * (samples // 2))) ** 0.5
    dft_rows = dft_rows_table(samples)
    lag_columns = lag_columns_table(samples, scale)

    def over_sub(rows):
        return lax.ppermute(rows, "sub", [(0, 1), (1, 0)])

    def over_core(rows):
        return lax.ppermute(rows, ("sub", "rep"), [(0, 1), (3, 2)])

    def to_owner(share, at):
        by = AHEAD[at]
        return lax.ppermute(share, "chan", [(z, (z + by) % chan_count) for z in range(chan_count)])

    def after(value, *others):
        return lax.optimization_barrier((value,) + others)[0]

    mine, mine_far, mine_near = order_rows(traces, channel_slot)
    far = over_sub(mine_far)
    near = over_sub(after(mine_near, mine_far))
    shares = []

    def collect(at, share, kinds):
        arrived = share if at == OWN_AT else to_owner(share, at)
        shares.extend((arrived, place, i_other, j_other) for place, (i_other, j_other) in enumerate(kinds))
        return arrived

    own_i, own_j = spectra([mine], [over_core(mine)], dft_rows, True)
    parts = partial_correlations([own_i], [own_j], lag_columns, [[(0, at) for at in range(BLOCKS)]])
    first_shares = [collect(at, parts[at], [(0, 0)]) for at in range(BLOCKS)]

    far = after(far, *parts)
    far_core = over_core(far)
    (far_i,) = spectra([far], [far_core], dft_rows, False)
    parts = partial_correlations([far_i], [own_j], lag_columns, [[(0, at) for at in FAR]])
    second_shares = [collect(at, part, [(1, 0)]) for at, part in zip(FAR, parts)]

    near = after(near, *parts, *first_shares)
    other_i, other_j = spectra([far, near], [far_core, over_core(near)], dft_rows, True)
    parts = partial_correlations(
        [own_i, other_i],
        [other_j, own_j],
        lag_columns,
        [[(0, at) for at in NEAR] + [(1, at) for at in NEAR], [(1, at) for at in NEAR]],
    )
    for at, part in zip(NEAR, parts):
        collect(at, part, [(0, 1), (1, 1), (1, 0)])
    other_j = after(other_j, *parts, *second_shares)
    parts = partial_correlations(
        [own_i, other_i], [other_j], lag_columns, [[(0, at) for at in FAR] + [(1, at) for at in FAR]]
    )
    for at, part in zip(FAR, parts):
        collect(at, part, [(0, 1), (1, 1)])
    return assembled(shares)


def from_behind(shard, axis, by):
    count = lax.axis_size(axis)
    return lax.ppermute(shard, axis, [(i, (i + by) % count) for i in range(count)])


def dft_columns(samples, parts, sub_bins):
    shape = (samples, parts, 2, sub_bins)
    time_pos = lax.broadcasted_iota(jnp.int32, shape, 0)
    range_pos = lax.broadcasted_iota(jnp.int32, shape, 1)
    part_pos = lax.broadcasted_iota(jnp.int32, shape, 2)
    bin_pos = lax.broadcasted_iota(jnp.int32, shape, 3)
    frequency = range_pos * sub_bins + bin_pos
    angles = jnp.mod(time_pos * frequency, samples).astype(jnp.float32) * (2.0 * math.pi / samples)
    entries = jnp.where(part_pos == 0, jnp.cos(angles), -jnp.sin(angles))
    return entries.reshape(samples, parts * 2 * sub_bins).astype(jnp.bfloat16)


def lag_table(sub_bins, first_bin, lag_count, samples):
    frequency = first_bin + lax.broadcasted_iota(jnp.int32, (sub_bins, lag_count), 0)
    lag_offset = lax.broadcasted_iota(jnp.int32, (sub_bins, lag_count), 1) - lag_count // 2
    angles = jnp.mod(frequency * lag_offset, samples).astype(jnp.float32) * (2.0 * math.pi / samples)
    return jnp.stack([jnp.cos(angles), -jnp.sin(angles)], axis=1)


def moved_spectra(traces, channel_slot):
    chan_count = lax.axis_size("chan")
    sub_count = lax.axis_size("sub")
    group_rows, win_here, samples = traces.shape
    bin_count = samples // 2
    sub_bins = bin_count // sub_count
    bin_width = 2 * sub_bins
    piece_len = group_rows // chan_count
    picked = jnp.take(traces, channel_slot, axis=0)
    dft_rows = dft_columns(samples, sub_count, sub_bins)
    spectrum = jnp.dot(picked.reshape(-1, samples), dft_rows, preferred_element_type=jnp.float32)
    energy = jnp.sum(spectrum * spectrum, axis=1, keepdims=True) / bin_count
    whitened = (spectrum * lax.rsqrt(energy + 1e-05)).astype(jnp.bfloat16)
    whitened = whitened.reshape(chan_count, piece_len, win_here, sub_count, bin_width)
    regrouped = lax.all_to_all(whitened, "chan", split_axis=0, concat_axis=0, tiled=True)
    regrouped = lax.all_to_all(regrouped, "sub", split_axis=3, concat_axis=3, tiled=True)
    own_half = regrouped.transpose(3, 1, 0, 2, 4).reshape(sub_count * piece_len, chan_count * win_here, bin_width)
    own_block = lax.all_gather(own_half, "rep", axis=0, tiled=True)
    windows = own_block.shape[1]
    own_split = own_block.reshape(own_block.shape[0], windows, 2, sub_bins)
    lag_columns = lag_table(sub_bins, lax.axis_index("sub") * sub_bins, LAGS, samples)
    lag_scale = (2.0 / (windows * bin_count)) ** 0.5
    results = []
    for step in range(1, ROUNDS + 1):
        partner = from_behind(own_half, "chan", -step)
        partner_split = partner.reshape(partner.shape[0], windows, 2, sub_bins)
        turned = jnp.stack([-partner_split[:, :, 1], partner_split[:, :, 0]], axis=2)
        partner_pair = jnp.stack([partner_split, turned], axis=0)
        cross_spec = jnp.einsum("iwpf,qjwpf->fqij", own_split, partner_pair, preferred_element_type=jnp.float32)
        summed = jnp.einsum("fqij,fql->ijl", cross_spec, lag_columns, precision=lax.Precision.HIGHEST)
        results.append(lax.psum_scatter(lag_scale * summed, "sub", scatter_dimension=0, tiled=True))
    return jnp.stack(results)[:, None]


def solution(mesh):
    sizes = mesh.shape
    in_place = sizes["chan"] == BLOCKS == ROUNDS + 1 and sizes["sub"] == 2 and sizes["rep"] == 2
    return jax.shard_map(
        summed_in_place if in_place else moved_spectra,
        mesh=mesh,
        in_specs=(P(("groups", "sub", "rep"), "chan", None), P(("groups", "sub", "rep"))),
        out_specs=P(None, ("groups", "chan"), "sub", "rep", None),
        check_vma=False,
    )
```

```python
import functools
import math

import jax
import jax.numpy as jnp
import numpy as np
from jax import lax
from jax.experimental import pallas as pl
from jax.experimental.pallas import tpu as pltpu
from jax.sharding import PartitionSpec as P

LAGS = 128
ROUNDS = 3
LANES = 128
HALF = LANES // 2
VMEM_BYTES = 56 * 1024 * 1024
NT = (((1,), (1,)), ((), ()))
AHEAD = (2, 1, 3, 0)
BLOCKS = len(AHEAD)
FAR = (0, 1)
NEAR = (2, 3)
OWN_AT = 3


def kernel_call(kernel, name, flops, bytes_accessed, **more):
    return pl.pallas_call(
        kernel,
        name=name,
        compiler_params=pltpu.CompilerParams(vmem_limit_bytes=VMEM_BYTES),
        cost_estimate=pl.CostEstimate(flops=flops, bytes_accessed=bytes_accessed, transcendentals=0),
        **more,
    )


def whole(shape):
    return pl.BlockSpec(shape, lambda g: (0,) * len(shape))


def dft_rows_table(samples):
    bins = samples // 2
    turns = (np.arange(bins)[:, None] * np.arange(samples)[None, :]) % samples
    angles = turns.astype(np.float32) * np.float32(2.0 * math.pi / samples)
    table = np.concatenate([np.cos(angles), -np.sin(angles)], axis=0)
    return jnp.asarray(table.astype(np.float32)).astype(jnp.bfloat16)


def lag_rows_table(samples, scale):
    bins = samples // 2
    offsets = np.arange(LAGS) - LAGS // 2
    turns = (offsets[:, None] * np.arange(bins)[None, :]) % samples
    angles = turns.astype(np.float32) * np.float32(2.0 * math.pi / samples)
    table = np.concatenate([np.cos(angles), -np.sin(angles)], axis=0) * np.float32(scale)
    return jnp.asarray(table.astype(np.float32)).astype(jnp.bfloat16)


def selection(rows, columns, ones):
    table = np.zeros((rows, columns), np.float32)
    for row, column in ones:
        table[row, column] = 1.0
    return jnp.asarray(table).astype(jnp.bfloat16)


def picks_i():
    return selection(HALF, LANES, [(i, HALF + i) for i in range(HALF)])


def picks_j():
    return selection(2 * LANES, LANES, [(j, j) for j in range(HALF)] + [(LANES + j, HALF + j) for j in range(HALF)])


def picks_lags():
    ones = []
    for half in range(2):
        for j in range(HALF):
            ones.append((half * HALF + j, half * LANES + j))
            ones.append((half * HALF + j, 2 * LANES + half * LANES + HALF + j))
    return selection(LANES, 4 * LANES, ones)


def order_rows(traces, slots):
    rows, wins, samples = traces.shape
    tiles = samples // LANES
    piece = rows // BLOCKS
    step_wins = 16
    pitch = rows + 1
    batch = 4

    def kernel(slot_ref, in_ref, all_ref, far_ref, near_ref, wide):
        z = lax.axis_index("chan")
        for at, ahead in enumerate(AHEAD):
            first = lax.rem(z + ahead, BLOCKS) * piece

            def move(group, carry, at=at, first=first):
                js = [group * batch + u for u in range(batch)]
                picked = [in_ref[slot_ref[first + j]].astype(jnp.float32) for j in js]
                for j, row in zip(js, picked):
                    for tile in range(tiles):
                        wide[tile, pl.ds(at * piece + j, step_wins, stride=pitch), :] = row[
                            :, tile * LANES : (tile + 1) * LANES
                        ]
                return carry

            lax.fori_loop(0, piece // batch, move, 0)

        def pack(w, carry):
            blocks = [wide[tile, pl.ds(w * pitch, rows), :].astype(jnp.bfloat16) for tile in range(tiles)]
            for tile, block in enumerate(blocks):
                here = slice(tile * LANES, (tile + 1) * LANES)
                all_ref[w, :, here] = block
                far_ref[w, :, here] = block[: rows // 2]
                near_ref[w, :, here] = block[rows // 2 :]
            return carry

        lax.fori_loop(0, step_wins, pack, 0, unroll=2)

    def out(count):
        return jax.ShapeDtypeStruct((wins, count, samples), jnp.bfloat16)

    def out_spec(count):
        return pl.BlockSpec((step_wins, count, samples), lambda g: (g, 0, 0))

    half = rows // 2
    return kernel_call(
        kernel,
        "order_rows",
        0,
        3 * traces.size * 2,
        out_shape=(out(rows), out(half), out(half)),
        grid=(wins // step_wins,),
        in_specs=[
            pl.BlockSpec(memory_space=pltpu.SMEM),
            pl.BlockSpec((rows, step_wins, samples), lambda g: (0, g, 0)),
        ],
        out_specs=(out_spec(rows), out_spec(half), out_spec(half)),
        scratch_shapes=[pltpu.VMEM((tiles, (step_wins + 1) * pitch, LANES), jnp.float32)],
    )(slots, traces)


def spectra(rows_j, rows_i, tables, with_j):
    count = len(rows_j)
    wins, _, samples = rows_j[0].shape
    given = sum(rows.shape[1] for rows in rows_j)
    bins = samples // 2
    depth = 2 * wins
    pitch = depth + 1
    step_wins = 8
    steps = wins // step_wins
    batch = 4

    def kernel(*refs):
        j_refs, i_refs = refs[:count], refs[count : 2 * count]
        table_ref, to_i_ref, to_j_ref, i_out = refs[2 * count : 2 * count + 4]
        j_out, wide = refs[-2:]
        same = lax.axis_index("sub") == lax.axis_index("rep")
        step = pl.program_id(0)
        blank = [jnp.zeros((HALF - given, samples), jnp.bfloat16)] if given < HALF else []

        def spectrum_of(pair):
            stacked = []
            for half in range(2):
                js = [ref[2 * pair + half] for ref in j_refs]
                others = [ref[2 * pair + half] for ref in i_refs]
                stacked += js + blank + [jnp.where(same, a, b) for a, b in zip(js, others)] + blank
            wave = jnp.concatenate(stacked, axis=0)
            return lax.dot_general(table_ref[...], wave, NT, preferred_element_type=jnp.float32)

        def keep(pair, spectrum):
            energy = jnp.sum(spectrum * spectrum, axis=0, keepdims=True) / bins
            white = spectrum * lax.rsqrt(energy + 1e-05)
            for half in range(2):
                for part in range(2):
                    row = part * wins + step * step_wins + 2 * pair + half
                    wide[pl.ds(row, bins, stride=pitch), :] = white[
                        part * bins : (part + 1) * bins, half * LANES : (half + 1) * LANES
                    ]

        last = spectrum_of(0)
        for pair in range(1, step_wins // 2):
            now = spectrum_of(pair)
            keep(pair - 1, last)
            last = now
        keep(step_wins // 2 - 1, last)

        @pl.when(step == steps - 1)
        def _():
            def moved(fs):
                loaded = [wide[pl.ds(f * pitch, depth), :].astype(jnp.bfloat16) for f in fs]
                i_rows = [
                    lax.dot_general(to_i_ref[...], values, NT, preferred_element_type=jnp.float32) for values in loaded
                ]
                if not with_j:
                    return fs, i_rows, None
                turned = [jnp.concatenate([-values[wins:], values[:wins]], axis=0) for values in loaded]
                both = jnp.concatenate(
                    [jnp.concatenate(loaded, axis=0), jnp.concatenate(turned, axis=0)], axis=1
                )
                return fs, i_rows, jnp.dot(both, to_j_ref[...], preferred_element_type=jnp.float32)

            def store(fs, i_rows, j_rows):
                for at, f in enumerate(fs):
                    i_out[f] = i_rows[at].astype(jnp.bfloat16)
                    if with_j:
                        j_out[f] = j_rows[at * depth : (at + 1) * depth].astype(jnp.bfloat16)

            def pack(group, carry):
                first = group * 4 * batch
                waiting = moved([first + u for u in range(batch)])
                for at in range(1, 4):
                    following = moved([first + at * batch + u for u in range(batch)])
                    store(*waiting)
                    waiting = following
                store(*waiting)
                return carry

            lax.fori_loop(0, bins // (4 * batch), pack, 0)

    def in_spec(rows):
        return pl.BlockSpec((step_wins, rows.shape[1], samples), lambda g: (g, 0, 0))

    i_shape, j_shape = (bins, HALF, depth), (bins, depth, LANES)
    shapes = [i_shape, j_shape] if with_j else [i_shape]
    return kernel_call(
        kernel,
        "spectra",
        2 * samples * samples * wins * LANES,
        4 * wins * LANES * samples * 2,
        out_shape=[jax.ShapeDtypeStruct(shape, jnp.bfloat16) for shape in shapes],
        grid=(steps,),
        in_specs=[in_spec(rows) for rows in rows_j + rows_i] + [whole(table.shape) for table in tables],
        out_specs=[whole(shape) for shape in shapes],
        scratch_shapes=[pltpu.VMEM(((bins + 1) * pitch, LANES), jnp.float32)],
    )(*rows_j, *rows_i, *tables)


def partial_correlations(lefts, rights, tables, jobs):
    bins, depth, _ = rights[0].shape
    piece = HALF // BLOCKS
    pitch = bins + 1
    step_bins = 32
    steps = bins // step_bins
    flat = [(right, left, at) for right, pairs in enumerate(jobs) for left, at in pairs]
    dests = sorted({at for _, _, at in flat})
    places = {at: [entry for entry in flat if entry[2] == at] for at in dests}
    total = len(flat) * piece
    batch = 8 if total <= 4 * piece else 4
    pairs_at_once = 4

    def kernel(*refs):
        left_refs, rest = refs[: len(lefts)], refs[len(lefts) :]
        right_refs, rest = rest[: len(rights)], rest[len(rights) :]
        lag_ref, pick_ref, out_refs, cross = rest[0], rest[1], rest[2:-1], rest[-1]
        step = pl.program_id(0)

        def products(fs):
            found = []
            for f in fs:
                first = 0
                for right, pairs in enumerate(jobs):
                    rows = [left_refs[left][f, at * piece : (at + 1) * piece] for left, at in pairs]
                    lhs = jnp.concatenate(rows, axis=0) if len(rows) > 1 else rows[0]
                    product = jnp.dot(lhs, right_refs[right][f], preferred_element_type=jnp.float32)
                    found.append((first * pitch + step * step_bins + f, product))
                    first += lhs.shape[0]
            return found

        def keep(found):
            for here, product in found:
                cross[pl.ds(here, product.shape[0], stride=pitch), :] = product

        waiting = products(range(batch))
        for first in range(batch, step_bins, batch):
            following = products(range(first, first + batch))
            keep(waiting)
            waiting = following
        keep(waiting)

        @pl.when(step == steps - 1)
        def _():
            for index, entry in enumerate(flat):
                at = entry[2]
                out = out_refs[dests.index(at)]
                place = places[at].index(entry)

                def summed(i, index=index):
                    start = (index * piece + i) * pitch
                    values = jnp.concatenate(
                        [cross[pl.ds(start, bins), :], cross[pl.ds(start + pitch, bins), :]], axis=1
                    ).astype(jnp.bfloat16)
                    return i, jnp.dot(lag_ref[...], values, preferred_element_type=jnp.float32)

                def gathered(i, both):
                    both = both.astype(jnp.bfloat16)
                    both = jnp.concatenate([both[:LAGS], both[LAGS:]], axis=1)
                    return i, lax.dot_general(pick_ref[...], both, NT, preferred_element_type=jnp.float32)

                def store(i, lagged, at=at, out=out, place=place):
                    lagged = lagged.astype(out.dtype)
                    for half in range(2):
                        for there in range(BLOCKS):
                            if there != at:
                                after = (AHEAD[there] - AHEAD[at]) % BLOCKS - 1
                                row = half * HALF + there * piece
                                out[place, after, i + half] = lagged[row : row + piece]

                def some_channels(group, carry, summed=summed, gathered=gathered, store=store):
                    first = 2 * pairs_at_once * group
                    sums, rows = summed(first), None
                    for pair in range(1, pairs_at_once):
                        more = summed(first + 2 * pair)
                        if rows is not None:
                            store(*rows)
                        rows = gathered(*sums)
                        sums = more
                    store(*rows)
                    store(*gathered(*sums))
                    return carry

                lax.fori_loop(0, piece // (2 * pairs_at_once), some_channels, 0)

    shapes = [(len(places[at]), BLOCKS - 1, piece, piece, LAGS) for at in dests]
    types = [jnp.float32 if at == OWN_AT else jnp.bfloat16 for at in dests]
    return kernel_call(
        kernel,
        "partial_correlations",
        2 * total * bins * depth * LANES + 2 * total * bins * LANES * 2 * LAGS,
        2 * sum(array.size for array in lefts + rights),
        out_shape=[jax.ShapeDtypeStruct(shape, kind) for shape, kind in zip(shapes, types)],
        grid=(steps,),
        in_specs=[pl.BlockSpec((step_bins,) + array.shape[1:], lambda g: (g, 0, 0)) for array in lefts + rights]
        + [whole(table.shape) for table in tables],
        out_specs=[whole(shape) for shape in shapes],
        scratch_shapes=[pltpu.VMEM(((total + 1) * pitch, LANES), jnp.float32)],
    )(*lefts, *rights, *tables)


def assembled(shares):
    arrays = []
    for array, _, _, _ in shares:
        if not any(array is known for known in arrays):
            arrays.append(array)
    index = [next(at for at, known in enumerate(arrays) if known is array) for array, _, _, _ in shares]
    _, rounds, piece, _, lags = arrays[0].shape
    width = 2 * piece

    def kernel(*refs):
        out = refs[-1]
        sub = lax.axis_index("sub")
        for i_other in range(2):
            for j_other in range(2):
                parts = [
                    refs[at][place, 0].astype(jnp.float32)
                    for at, (_, place, i_is, j_is) in zip(index, shares)
                    if (i_is, j_is) == (i_other, j_other)
                ]
                i_first = jnp.where(sub == 0, i_other, 1 - i_other) * piece
                j_first = pl.multiple_of(jnp.where(sub == 0, j_other, 1 - j_other) * piece, piece)
                out[0, 0, pl.ds(i_first, piece), pl.ds(j_first, piece), :] = functools.reduce(jnp.add, parts)

    return kernel_call(
        kernel,
        "assembled",
        0,
        sum(array.size for array in arrays) * 2,
        out_shape=jax.ShapeDtypeStruct((rounds, 1, width, width, lags), jnp.float32),
        grid=(rounds,),
        in_specs=[
            pl.BlockSpec((array.shape[0], 1, piece, piece, lags), lambda g: (0, g, 0, 0, 0)) for array in arrays
        ],
        out_specs=pl.BlockSpec((1, 1, width, width, lags), lambda g: (g, 0, 0, 0, 0)),
    )(*arrays)


def summed_in_place(traces, channel_slot):
    chan_count = lax.axis_size("chan")
    _, win_here, samples = traces.shape
    scale = (2.0 / (win_here * chan_count * (samples // 2))) ** 0.5
    dft_tables = [dft_rows_table(samples), picks_i(), picks_j()]
    lag_tables = [lag_rows_table(samples, scale), picks_lags()]

    def over_sub(rows):
        return lax.ppermute(rows, "sub", [(0, 1), (1, 0)])

    def over_core(rows):
        return lax.ppermute(rows, ("sub", "rep"), [(0, 1), (3, 2)])

    def to_owner(share, at):
        by = AHEAD[at]
        return lax.ppermute(share, "chan", [(z, (z + by) % chan_count) for z in range(chan_count)])

    def after(value, *others):
        return lax.optimization_barrier((value,) + others)[0]

    mine, mine_far, mine_near = order_rows(traces, channel_slot)
    far = over_sub(mine_far)
    near = over_sub(after(mine_near, mine_far))
    shares = []

    def collect(at, share, kinds):
        arrived = share if at == OWN_AT else to_owner(share, at)
        shares.extend((arrived, place, i_other, j_other) for place, (i_other, j_other) in enumerate(kinds))
        return arrived

    own_i, own_j = spectra([mine], [over_core(mine)], dft_tables, True)
    parts = partial_correlations([own_i], [own_j], lag_tables, [[(0, at) for at in range(BLOCKS)]])
    first_shares = [collect(at, parts[at], [(0, 0)]) for at in range(BLOCKS)]

    far = after(far, *parts)
    far_core = over_core(far)
    (far_i,) = spectra([far], [far_core], dft_tables, False)
    parts = partial_correlations([far_i], [own_j], lag_tables, [[(0, at) for at in FAR]])
    second_shares = [collect(at, part, [(1, 0)]) for at, part in zip(FAR, parts)]

    near = after(near, *parts, *first_shares)
    other_i, other_j = spectra([far, near], [far_core, over_core(near)], dft_tables, True)
    parts = partial_correlations(
        [own_i, other_i],
        [other_j, own_j],
        lag_tables,
        [[(0, at) for at in NEAR] + [(1, at) for at in NEAR], [(1, at) for at in NEAR]],
    )
    for at, part in zip(NEAR, parts):
        collect(at, part, [(0, 1), (1, 1), (1, 0)])
    other_j = after(other_j, *parts, *second_shares)
    parts = partial_correlations(
        [own_i, other_i], [other_j], lag_tables, [[(0, at) for at in FAR] + [(1, at) for at in FAR]]
    )
    for at, part in zip(FAR, parts):
        collect(at, part, [(0, 1), (1, 1)])
    return assembled(shares)


def from_behind(shard, axis, by):
    count = lax.axis_size(axis)
    return lax.ppermute(shard, axis, [(i, (i + by) % count) for i in range(count)])


def dft_columns(samples, parts, sub_bins):
    shape = (samples, parts, 2, sub_bins)
    time_pos = lax.broadcasted_iota(jnp.int32, shape, 0)
    range_pos = lax.broadcasted_iota(jnp.int32, shape, 1)
    part_pos = lax.broadcasted_iota(jnp.int32, shape, 2)
    bin_pos = lax.broadcasted_iota(jnp.int32, shape, 3)
    frequency = range_pos * sub_bins + bin_pos
    angles = jnp.mod(time_pos * frequency, samples).astype(jnp.float32) * (2.0 * math.pi / samples)
    entries = jnp.where(part_pos == 0, jnp.cos(angles), -jnp.sin(angles))
    return entries.reshape(samples, parts * 2 * sub_bins).astype(jnp.bfloat16)


def lag_table(sub_bins, first_bin, lag_count, samples):
    frequency = first_bin + lax.broadcasted_iota(jnp.int32, (sub_bins, lag_count), 0)
    lag_offset = lax.broadcasted_iota(jnp.int32, (sub_bins, lag_count), 1) - lag_count // 2
    angles = jnp.mod(frequency * lag_offset, samples).astype(jnp.float32) * (2.0 * math.pi / samples)
    return jnp.stack([jnp.cos(angles), -jnp.sin(angles)], axis=1)


def moved_spectra(traces, channel_slot):
    chan_count = lax.axis_size("chan")
    sub_count = lax.axis_size("sub")
    group_rows, win_here, samples = traces.shape
    bin_count = samples // 2
    sub_bins = bin_count // sub_count
    bin_width = 2 * sub_bins
    piece_len = group_rows // chan_count
    picked = jnp.take(traces, channel_slot, axis=0)
    dft_rows = dft_columns(samples, sub_count, sub_bins)
    spectrum = jnp.dot(picked.reshape(-1, samples), dft_rows, preferred_element_type=jnp.float32)
    energy = jnp.sum(spectrum * spectrum, axis=1, keepdims=True) / bin_count
    whitened = (spectrum * lax.rsqrt(energy + 1e-05)).astype(jnp.bfloat16)
    whitened = whitened.reshape(chan_count, piece_len, win_here, sub_count, bin_width)
    regrouped = lax.all_to_all(whitened, "chan", split_axis=0, concat_axis=0, tiled=True)
    regrouped = lax.all_to_all(regrouped, "sub", split_axis=3, concat_axis=3, tiled=True)
    own_half = regrouped.transpose(3, 1, 0, 2, 4).reshape(sub_count * piece_len, chan_count * win_here, bin_width)
    own_block = lax.all_gather(own_half, "rep", axis=0, tiled=True)
    windows = own_block.shape[1]
    own_split = own_block.reshape(own_block.shape[0], windows, 2, sub_bins)
    lag_rows = lag_table(sub_bins, lax.axis_index("sub") * sub_bins, LAGS, samples)
    lag_scale = (2.0 / (windows * bin_count)) ** 0.5
    results = []
    for step in range(1, ROUNDS + 1):
        partner = from_behind(own_half, "chan", -step)
        partner_split = partner.reshape(partner.shape[0], windows, 2, sub_bins)
        turned = jnp.stack([-partner_split[:, :, 1], partner_split[:, :, 0]], axis=2)
        partner_pair = jnp.stack([partner_split, turned], axis=0)
        cross_spec = jnp.einsum("iwpf,qjwpf->fqij", own_split, partner_pair, preferred_element_type=jnp.float32)
        summed = jnp.einsum("fqij,fql->ijl", cross_spec, lag_rows, precision=lax.Precision.HIGHEST)
        results.append(lax.psum_scatter(lag_scale * summed, "sub", scatter_dimension=0, tiled=True))
    return jnp.stack(results)[:, None]


def solution(mesh):
    sizes = mesh.shape
    in_place = sizes["chan"] == BLOCKS == ROUNDS + 1 and sizes["sub"] == 2 and sizes["rep"] == 2
    return jax.shard_map(
        summed_in_place if in_place else moved_spectra,
        mesh=mesh,
        in_specs=(P(("groups", "sub", "rep"), "chan", None), P(("groups", "sub", "rep"))),
        out_specs=P(None, ("groups", "chan"), "sub", "rep", None),
        check_vma=False,
    )
```

```python
import functools
import math

import jax
import jax.numpy as jnp
import numpy as np
from jax import lax
from jax.experimental import pallas as pl
from jax.experimental.pallas import tpu as pltpu
from jax.sharding import PartitionSpec as P

LAGS = 128
ROUNDS = 3
LANES = 128
HALF = LANES // 2
VMEM_BYTES = 32 * 1024 * 1024
NT = (((1,), (1,)), ((), ()))
AHEAD = (2, 1, 3, 0)
BLOCKS = len(AHEAD)
FAR = (0, 1)
NEAR = (2, 3)
OWN_AT = 3


def kernel_call(kernel, name, flops, bytes_accessed, **more):
    return pl.pallas_call(
        kernel,
        name=name,
        compiler_params=pltpu.CompilerParams(vmem_limit_bytes=VMEM_BYTES),
        cost_estimate=pl.CostEstimate(flops=flops, bytes_accessed=bytes_accessed, transcendentals=0),
        **more,
    )


def in_vmem():
    return pl.BlockSpec(memory_space=pltpu.VMEM)


def dft_rows_table(samples):
    bins = samples // 2
    turns = (np.arange(bins)[:, None] * np.arange(samples)[None, :]) % samples
    angles = turns.astype(np.float32) * np.float32(2.0 * math.pi / samples)
    table = np.concatenate([np.cos(angles), -np.sin(angles)], axis=0)
    return jnp.asarray(table.astype(np.float32)).astype(jnp.bfloat16)


def lag_rows_table(samples, scale):
    bins = samples // 2
    offsets = np.arange(LAGS) - LAGS // 2
    turns = (offsets[:, None] * np.arange(bins)[None, :]) % samples
    angles = turns.astype(np.float32) * np.float32(2.0 * math.pi / samples)
    table = np.concatenate([np.cos(angles), -np.sin(angles)], axis=0) * np.float32(scale)
    return jnp.asarray(table.astype(np.float32)).astype(jnp.bfloat16)


def selection(rows, columns, ones):
    table = np.zeros((rows, columns), np.float32)
    for row, column in ones:
        table[row, column] = 1.0
    return jnp.asarray(table).astype(jnp.bfloat16)


def picks_i():
    return selection(HALF, LANES, [(i, HALF + i) for i in range(HALF)])


def picks_j():
    return selection(2 * LANES, LANES, [(j, j) for j in range(HALF)] + [(LANES + j, HALF + j) for j in range(HALF)])


def picks_lags():
    ones = []
    for half in range(2):
        for j in range(HALF):
            ones.append((half * HALF + j, half * LANES + j))
            ones.append((half * HALF + j, 2 * LANES + half * LANES + HALF + j))
    return selection(LANES, 4 * LANES, ones)


def order_rows(traces, slots):
    rows, wins, samples = traces.shape
    tiles = samples // LANES
    piece = rows // BLOCKS
    step_wins = 16
    pitch = rows + 1
    batch = 4

    def kernel(slot_ref, in_ref, all_ref, far_ref, near_ref, wide):
        z = lax.axis_index("chan")
        for at, ahead in enumerate(AHEAD):
            first = lax.rem(z + ahead, BLOCKS) * piece

            def move(group, carry, at=at, first=first):
                js = [group * batch + u for u in range(batch)]
                picked = [in_ref[slot_ref[first + j]].astype(jnp.float32) for j in js]
                for j, row in zip(js, picked):
                    for tile in range(tiles):
                        wide[tile, pl.ds(at * piece + j, step_wins, stride=pitch), :] = row[
                            :, tile * LANES : (tile + 1) * LANES
                        ]
                return carry

            lax.fori_loop(0, piece // batch, move, 0)

        def pack(w, carry):
            blocks = [wide[tile, pl.ds(w * pitch, rows), :].astype(jnp.bfloat16) for tile in range(tiles)]
            for tile, block in enumerate(blocks):
                here = slice(tile * LANES, (tile + 1) * LANES)
                all_ref[w, :, here] = block
                far_ref[w, :, here] = block[: rows // 2]
                near_ref[w, :, here] = block[rows // 2 :]
            return carry

        lax.fori_loop(0, step_wins, pack, 0, unroll=2)

    def out(count):
        return jax.ShapeDtypeStruct((wins, count, samples), jnp.bfloat16)

    def out_spec(count):
        return pl.BlockSpec((step_wins, count, samples), lambda g: (g, 0, 0))

    half = rows // 2
    return kernel_call(
        kernel,
        "order_rows",
        0,
        3 * traces.size * 2,
        out_shape=(out(rows), out(half), out(half)),
        grid=(wins // step_wins,),
        in_specs=[
            pl.BlockSpec(memory_space=pltpu.SMEM),
            pl.BlockSpec((rows, step_wins, samples), lambda g: (0, g, 0)),
        ],
        out_specs=(out_spec(rows), out_spec(half), out_spec(half)),
        scratch_shapes=[pltpu.VMEM((tiles, (step_wins + 1) * pitch, LANES), jnp.float32)],
    )(slots, traces)


def spectra(rows_j, rows_i, tables, with_j):
    count = len(rows_j)
    wins, _, samples = rows_j[0].shape
    given = sum(rows.shape[1] for rows in rows_j)
    bins = samples // 2
    depth = 2 * wins
    pitch = depth + 1
    step_wins = 8
    batch = 4

    def kernel(*refs):
        j_refs, i_refs = refs[:count], refs[count : 2 * count]
        table_ref, to_i_ref, to_j_ref, i_out = refs[2 * count : 2 * count + 4]
        j_out, wide = refs[-2:]
        same = lax.axis_index("sub") == lax.axis_index("rep")
        blank = [jnp.zeros((HALF - given, samples), jnp.bfloat16)] if given < HALF else []

        def spectrum_of(pair):
            stacked = []
            for half in range(2):
                js = [ref[2 * pair + half] for ref in j_refs]
                others = [ref[2 * pair + half] for ref in i_refs]
                stacked += js + blank + [jnp.where(same, a, b) for a, b in zip(js, others)] + blank
            wave = jnp.concatenate(stacked, axis=0)
            return lax.dot_general(table_ref[...], wave, NT, preferred_element_type=jnp.float32)

        def keep(pair, spectrum):
            energy = jnp.sum(spectrum * spectrum, axis=0, keepdims=True) / bins
            white = spectrum * lax.rsqrt(energy + 1e-05)
            for half in range(2):
                for part in range(2):
                    row = part * wins + 2 * pair + half
                    wide[pl.ds(row, bins, stride=pitch), :] = white[
                        part * bins : (part + 1) * bins, half * LANES : (half + 1) * LANES
                    ]

        def some_windows(step, carry):
            first = step * (step_wins // 2)
            last = spectrum_of(first)
            for pair in range(1, step_wins // 2):
                now = spectrum_of(first + pair)
                keep(first + pair - 1, last)
                last = now
            keep(first + step_wins // 2 - 1, last)
            return carry

        lax.fori_loop(0, wins // step_wins, some_windows, 0)

        def moved(fs):
            loaded = [wide[pl.ds(f * pitch, depth), :].astype(jnp.bfloat16) for f in fs]
            i_rows = [
                lax.dot_general(to_i_ref[...], values, NT, preferred_element_type=jnp.float32) for values in loaded
            ]
            if not with_j:
                return fs, i_rows, None
            turned = [jnp.concatenate([-values[wins:], values[:wins]], axis=0) for values in loaded]
            both = jnp.concatenate(
                [jnp.concatenate(loaded, axis=0), jnp.concatenate(turned, axis=0)], axis=1
            )
            return fs, i_rows, jnp.dot(both, to_j_ref[...], preferred_element_type=jnp.float32)

        def store(fs, i_rows, j_rows):
            for at, f in enumerate(fs):
                i_out[f] = i_rows[at].astype(jnp.bfloat16)
                if with_j:
                    j_out[f] = j_rows[at * depth : (at + 1) * depth].astype(jnp.bfloat16)

        def pack(group, carry):
            first = group * 4 * batch
            waiting = moved([first + u for u in range(batch)])
            for at in range(1, 4):
                following = moved([first + at * batch + u for u in range(batch)])
                store(*waiting)
                waiting = following
            store(*waiting)
            return carry

        lax.fori_loop(0, bins // (4 * batch), pack, 0)

    i_shape, j_shape = (bins, HALF, depth), (bins, depth, LANES)
    shapes = [i_shape, j_shape] if with_j else [i_shape]
    return kernel_call(
        kernel,
        "spectra",
        2 * samples * samples * wins * LANES,
        4 * wins * LANES * samples * 2,
        out_shape=[jax.ShapeDtypeStruct(shape, jnp.bfloat16) for shape in shapes],
        in_specs=[in_vmem()] * (2 * count + len(tables)),
        out_specs=[in_vmem()] * len(shapes),
        scratch_shapes=[pltpu.VMEM(((bins + 1) * pitch, LANES), jnp.float32)],
    )(*rows_j, *rows_i, *tables)


def partial_correlations(lefts, rights, tables, jobs):
    bins, depth, _ = rights[0].shape
    piece = HALF // BLOCKS
    pitch = bins + 1
    step_bins = 32
    flat = [(right, left, at) for right, pairs in enumerate(jobs) for left, at in pairs]
    dests = sorted({at for _, _, at in flat})
    places = {at: [entry for entry in flat if entry[2] == at] for at in dests}
    total = len(flat) * piece
    batch = 8 if total <= 4 * piece else 4
    pairs_at_once = 4

    def kernel(*refs):
        left_refs, rest = refs[: len(lefts)], refs[len(lefts) :]
        right_refs, rest = rest[: len(rights)], rest[len(rights) :]
        lag_ref, pick_ref, out_refs, cross = rest[0], rest[1], rest[2:-1], rest[-1]

        def products(first_bin, count):
            found = []
            for f in [first_bin + u for u in range(count)]:
                first = 0
                for right, pairs in enumerate(jobs):
                    rows = [left_refs[left][f, at * piece : (at + 1) * piece] for left, at in pairs]
                    lhs = jnp.concatenate(rows, axis=0) if len(rows) > 1 else rows[0]
                    product = jnp.dot(lhs, right_refs[right][f], preferred_element_type=jnp.float32)
                    found.append((first * pitch + f, product))
                    first += lhs.shape[0]
            return found

        def keep(found):
            for here, product in found:
                cross[pl.ds(here, product.shape[0], stride=pitch), :] = product

        def some_bins(step, carry):
            first = step * step_bins
            waiting = products(first, batch)
            for at in range(batch, step_bins, batch):
                following = products(first + at, batch)
                keep(waiting)
                waiting = following
            keep(waiting)
            return carry

        lax.fori_loop(0, bins // step_bins, some_bins, 0)

        for index, entry in enumerate(flat):
            at = entry[2]
            out = out_refs[dests.index(at)]
            place = places[at].index(entry)

            def summed(i, index=index):
                start = (index * piece + i) * pitch
                values = jnp.concatenate(
                    [cross[pl.ds(start, bins), :], cross[pl.ds(start + pitch, bins), :]], axis=1
                ).astype(jnp.bfloat16)
                return i, jnp.dot(lag_ref[...], values, preferred_element_type=jnp.float32)

            def gathered(i, both):
                both = both.astype(jnp.bfloat16)
                both = jnp.concatenate([both[:LAGS], both[LAGS:]], axis=1)
                return i, lax.dot_general(pick_ref[...], both, NT, preferred_element_type=jnp.float32)

            def store(i, lagged, at=at, out=out, place=place):
                lagged = lagged.astype(out.dtype)
                for half in range(2):
                    for there in range(BLOCKS):
                        if there != at:
                            after = (AHEAD[there] - AHEAD[at]) % BLOCKS - 1
                            row = half * HALF + there * piece
                            out[place, after, i + half] = lagged[row : row + piece]

            def some_channels(group, carry, summed=summed, gathered=gathered, store=store):
                first = 2 * pairs_at_once * group
                sums, rows = summed(first), None
                for pair in range(1, pairs_at_once):
                    more = summed(first + 2 * pair)
                    if rows is not None:
                        store(*rows)
                    rows = gathered(*sums)
                    sums = more
                store(*rows)
                store(*gathered(*sums))
                return carry

            lax.fori_loop(0, piece // (2 * pairs_at_once), some_channels, 0)

    shapes = [(len(places[at]), BLOCKS - 1, piece, piece, LAGS) for at in dests]
    types = [jnp.float32 if at == OWN_AT else jnp.bfloat16 for at in dests]
    return kernel_call(
        kernel,
        "partial_correlations",
        2 * total * bins * depth * LANES + 2 * total * bins * LANES * 2 * LAGS,
        2 * sum(array.size for array in lefts + rights),
        out_shape=[jax.ShapeDtypeStruct(shape, kind) for shape, kind in zip(shapes, types)],
        in_specs=[in_vmem()] * (len(lefts) + len(rights) + len(tables)),
        out_specs=[in_vmem()] * len(shapes),
        scratch_shapes=[pltpu.VMEM(((total + 1) * pitch, LANES), jnp.float32)],
    )(*lefts, *rights, *tables)


def assembled(shares):
    arrays = []
    for array, _, _, _ in shares:
        if not any(array is known for known in arrays):
            arrays.append(array)
    index = [next(at for at, known in enumerate(arrays) if known is array) for array, _, _, _ in shares]
    _, rounds, piece, _, lags = arrays[0].shape
    width = 2 * piece

    def kernel(*refs):
        out = refs[-1]
        sub = lax.axis_index("sub")
        for i_other in range(2):
            for j_other in range(2):
                parts = [
                    refs[at][place, 0].astype(jnp.float32)
                    for at, (_, place, i_is, j_is) in zip(index, shares)
                    if (i_is, j_is) == (i_other, j_other)
                ]
                i_first = jnp.where(sub == 0, i_other, 1 - i_other) * piece
                j_first = pl.multiple_of(jnp.where(sub == 0, j_other, 1 - j_other) * piece, piece)
                out[0, 0, pl.ds(i_first, piece), pl.ds(j_first, piece), :] = functools.reduce(jnp.add, parts)

    return kernel_call(
        kernel,
        "assembled",
        0,
        sum(array.size for array in arrays) * 2,
        out_shape=jax.ShapeDtypeStruct((rounds, 1, width, width, lags), jnp.float32),
        grid=(rounds,),
        in_specs=[
            pl.BlockSpec((array.shape[0], 1, piece, piece, lags), lambda g: (0, g, 0, 0, 0)) for array in arrays
        ],
        out_specs=pl.BlockSpec((1, 1, width, width, lags), lambda g: (g, 0, 0, 0, 0)),
    )(*arrays)


def summed_in_place(traces, channel_slot):
    chan_count = lax.axis_size("chan")
    _, win_here, samples = traces.shape
    scale = (2.0 / (win_here * chan_count * (samples // 2))) ** 0.5
    dft_tables = [dft_rows_table(samples), picks_i(), picks_j()]
    lag_tables = [lag_rows_table(samples, scale), picks_lags()]

    def over_sub(rows):
        return lax.ppermute(rows, "sub", [(0, 1), (1, 0)])

    def over_core(rows):
        return lax.ppermute(rows, ("sub", "rep"), [(0, 1), (3, 2)])

    def to_owner(share, at):
        by = AHEAD[at]
        return lax.ppermute(share, "chan", [(z, (z + by) % chan_count) for z in range(chan_count)])

    def after(value, *others):
        return lax.optimization_barrier((value,) + others)[0]

    mine, mine_far, mine_near = order_rows(traces, channel_slot)
    far = over_sub(mine_far)
    near = over_sub(after(mine_near, mine_far))
    shares = []

    def collect(at, share, kinds):
        arrived = share if at == OWN_AT else to_owner(share, at)
        shares.extend((arrived, place, i_other, j_other) for place, (i_other, j_other) in enumerate(kinds))
        return arrived

    own_i, own_j = spectra([mine], [over_core(mine)], dft_tables, True)
    parts = partial_correlations([own_i], [own_j], lag_tables, [[(0, at) for at in range(BLOCKS)]])
    first_shares = [collect(at, parts[at], [(0, 0)]) for at in range(BLOCKS)]

    far = after(far, *parts)
    far_core = over_core(far)
    (far_i,) = spectra([far], [far_core], dft_tables, False)
    parts = partial_correlations([far_i], [own_j], lag_tables, [[(0, at) for at in FAR]])
    second_shares = [collect(at, part, [(1, 0)]) for at, part in zip(FAR, parts)]

    near = after(near, *parts, *first_shares)
    other_i, other_j = spectra([far, near], [far_core, over_core(near)], dft_tables, True)
    parts = partial_correlations(
        [own_i, other_i],
        [other_j, own_j],
        lag_tables,
        [[(0, at) for at in NEAR] + [(1, at) for at in NEAR], [(1, at) for at in NEAR]],
    )
    for at, part in zip(NEAR, parts):
        collect(at, part, [(0, 1), (1, 1), (1, 0)])
    other_j = after(other_j, *parts, *second_shares)
    parts = partial_correlations(
        [own_i, other_i], [other_j], lag_tables, [[(0, at) for at in FAR] + [(1, at) for at in FAR]]
    )
    for at, part in zip(FAR, parts):
        collect(at, part, [(0, 1), (1, 1)])
    return assembled(shares)


def from_behind(shard, axis, by):
    count = lax.axis_size(axis)
    return lax.ppermute(shard, axis, [(i, (i + by) % count) for i in range(count)])


def dft_columns(samples, parts, sub_bins):
    shape = (samples, parts, 2, sub_bins)
    time_pos = lax.broadcasted_iota(jnp.int32, shape, 0)
    range_pos = lax.broadcasted_iota(jnp.int32, shape, 1)
    part_pos = lax.broadcasted_iota(jnp.int32, shape, 2)
    bin_pos = lax.broadcasted_iota(jnp.int32, shape, 3)
    frequency = range_pos * sub_bins + bin_pos
    angles = jnp.mod(time_pos * frequency, samples).astype(jnp.float32) * (2.0 * math.pi / samples)
    entries = jnp.where(part_pos == 0, jnp.cos(angles), -jnp.sin(angles))
    return entries.reshape(samples, parts * 2 * sub_bins).astype(jnp.bfloat16)


def lag_table(sub_bins, first_bin, lag_count, samples):
    frequency = first_bin + lax.broadcasted_iota(jnp.int32, (sub_bins, lag_count), 0)
    lag_offset = lax.broadcasted_iota(jnp.int32, (sub_bins, lag_count), 1) - lag_count // 2
    angles = jnp.mod(frequency * lag_offset, samples).astype(jnp.float32) * (2.0 * math.pi / samples)
    return jnp.stack([jnp.cos(angles), -jnp.sin(angles)], axis=1)


def moved_spectra(traces, channel_slot):
    chan_count = lax.axis_size("chan")
    sub_count = lax.axis_size("sub")
    group_rows, win_here, samples = traces.shape
    bin_count = samples // 2
    sub_bins = bin_count // sub_count
    bin_width = 2 * sub_bins
    piece_len = group_rows // chan_count
    picked = jnp.take(traces, channel_slot, axis=0)
    dft_rows = dft_columns(samples, sub_count, sub_bins)
    spectrum = jnp.dot(picked.reshape(-1, samples), dft_rows, preferred_element_type=jnp.float32)
    energy = jnp.sum(spectrum * spectrum, axis=1, keepdims=True) / bin_count
    whitened = (spectrum * lax.rsqrt(energy + 1e-05)).astype(jnp.bfloat16)
    whitened = whitened.reshape(chan_count, piece_len, win_here, sub_count, bin_width)
    regrouped = lax.all_to_all(whitened, "chan", split_axis=0, concat_axis=0, tiled=True)
    regrouped = lax.all_to_all(regrouped, "sub", split_axis=3, concat_axis=3, tiled=True)
    own_half = regrouped.transpose(3, 1, 0, 2, 4).reshape(sub_count * piece_len, chan_count * win_here, bin_width)
    own_block = lax.all_gather(own_half, "rep", axis=0, tiled=True)
    windows = own_block.shape[1]
    own_split = own_block.reshape(own_block.shape[0], windows, 2, sub_bins)
    lag_rows = lag_table(sub_bins, lax.axis_index("sub") * sub_bins, LAGS, samples)
    lag_scale = (2.0 / (windows * bin_count)) ** 0.5
    results = []
    for step in range(1, ROUNDS + 1):
        partner = from_behind(own_half, "chan", -step)
        partner_split = partner.reshape(partner.shape[0], windows, 2, sub_bins)
        turned = jnp.stack([-partner_split[:, :, 1], partner_split[:, :, 0]], axis=2)
        partner_pair = jnp.stack([partner_split, turned], axis=0)
        cross_spec = jnp.einsum("iwpf,qjwpf->fqij", own_split, partner_pair, preferred_element_type=jnp.float32)
        summed = jnp.einsum("fqij,fql->ijl", cross_spec, lag_rows, precision=lax.Precision.HIGHEST)
        results.append(lax.psum_scatter(lag_scale * summed, "sub", scatter_dimension=0, tiled=True))
    return jnp.stack(results)[:, None]


def solution(mesh):
    sizes = mesh.shape
    in_place = sizes["chan"] == BLOCKS == ROUNDS + 1 and sizes["sub"] == 2 and sizes["rep"] == 2
    return jax.shard_map(
        summed_in_place if in_place else moved_spectra,
        mesh=mesh,
        in_specs=(P(("groups", "sub", "rep"), "chan", None), P(("groups", "sub", "rep"))),
        out_specs=P(None, ("groups", "chan"), "sub", "rep", None),
        check_vma=False,
    )
```

```python
import functools
import math

import jax
import jax.numpy as jnp
import numpy as np
from jax import lax
from jax.experimental import pallas as pl
from jax.experimental.pallas import tpu as pltpu
from jax.sharding import PartitionSpec as P

LAGS = 128
ROUNDS = 3
LANES = 128
HALF = LANES // 2
VMEM_BYTES = 32 * 1024 * 1024
NT = (((1,), (1,)), ((), ()))
AHEAD = (2, 1, 3, 0)
BLOCKS = len(AHEAD)
FAR = (0, 1)
NEAR = (2, 3)
OWN_AT = 3


def kernel_call(kernel, name, flops, bytes_accessed, **more):
    return pl.pallas_call(
        kernel,
        name=name,
        compiler_params=pltpu.CompilerParams(vmem_limit_bytes=VMEM_BYTES),
        cost_estimate=pl.CostEstimate(flops=flops, bytes_accessed=bytes_accessed, transcendentals=0),
        **more,
    )


def in_vmem():
    return pl.BlockSpec(memory_space=pltpu.VMEM)


def dft_rows_table(samples):
    bins = samples // 2
    turns = (np.arange(bins)[:, None] * np.arange(samples)[None, :]) % samples
    angles = turns.astype(np.float32) * np.float32(2.0 * math.pi / samples)
    table = np.concatenate([np.cos(angles), -np.sin(angles)], axis=0)
    return jnp.asarray(table.astype(np.float32)).astype(jnp.bfloat16)


def lag_rows_table(samples, scale):
    bins = samples // 2
    offsets = np.arange(LAGS) - LAGS // 2
    turns = (offsets[:, None] * np.arange(bins)[None, :]) % samples
    angles = turns.astype(np.float32) * np.float32(2.0 * math.pi / samples)
    table = np.concatenate([np.cos(angles), -np.sin(angles)], axis=0) * np.float32(scale)
    return jnp.asarray(table.astype(np.float32)).astype(jnp.bfloat16)


def selection(rows, columns, ones):
    table = np.zeros((rows, columns), np.float32)
    for row, column in ones:
        table[row, column] = 1.0
    return jnp.asarray(table).astype(jnp.bfloat16)


def own_picks():
    to_i = selection(HALF, LANES, [(i, HALF + i) for i in range(HALF)])
    to_j = selection(2 * LANES, LANES, [(j, j) for j in range(HALF)] + [(LANES + j, HALF + j) for j in range(HALF)])
    return to_i, to_j


def half_picks(place):
    count = HALF // 2
    to_i, to_j = [], []
    for odd in range(2):
        for n in range(count):
            lane = odd * HALF + n
            to_i.append((n, odd * LANES + lane + count))
            to_j.append((lane, odd * LANES + place * count + n))
            to_j.append((LANES + lane, odd * LANES + HALF + place * count + n))
    return selection(count, 2 * LANES, to_i), selection(2 * LANES, 2 * LANES, to_j)


def picks_lags():
    ones = []
    for half in range(2):
        for j in range(HALF):
            ones.append((half * HALF + j, half * LANES + j))
            ones.append((half * HALF + j, 2 * LANES + half * LANES + HALF + j))
    return selection(LANES, 4 * LANES, ones)


def order_rows(traces, slots, kinds):
    rows, wins, samples = traces.shape
    tiles = samples // LANES
    piece = rows // BLOCKS
    step_wins = 16
    batch = 4
    used = max(kinds, key=len)
    pitch = len(used) * piece + 1

    def kernel(slot_ref, in_ref, *refs):
        out_refs, wide = refs[:-1], refs[-1]
        z = lax.axis_index("chan")

        def some_windows(step, carry):
            first_win = pl.multiple_of(step * step_wins, step_wins)
            for at, position in enumerate(used):
                first = lax.rem(z + AHEAD[position], BLOCKS) * piece

                def move(group, carry, at=at, first=first):
                    js = [group * batch + u for u in range(batch)]
                    picked = [
                        in_ref[slot_ref[first + j], pl.ds(first_win, step_wins), :].astype(jnp.float32) for j in js
                    ]
                    for j, row in zip(js, picked):
                        for tile in range(tiles):
                            wide[tile, pl.ds(at * piece + j, step_wins, stride=pitch), :] = row[
                                :, tile * LANES : (tile + 1) * LANES
                            ]
                    return carry

                lax.fori_loop(0, piece // batch, move, 0)

            def pack(w, carry):
                blocks = [
                    wide[tile, pl.ds(w * pitch, len(used) * piece), :].astype(jnp.bfloat16) for tile in range(tiles)
                ]
                for out_ref, kind in zip(out_refs, kinds):
                    first = used.index(kind[0]) * piece
                    for tile, block in enumerate(blocks):
                        out_ref[first_win + w, :, tile * LANES : (tile + 1) * LANES] = block[
                            first : first + len(kind) * piece
                        ]
                return carry

            lax.fori_loop(0, step_wins, pack, 0, unroll=2)
            return carry

        lax.fori_loop(0, wins // step_wins, some_windows, 0)

    return kernel_call(
        kernel,
        "order_rows",
        0,
        3 * traces.size * 2,
        out_shape=[jax.ShapeDtypeStruct((wins, len(kind) * piece, samples), jnp.bfloat16) for kind in kinds],
        in_specs=[pl.BlockSpec(memory_space=pltpu.SMEM), in_vmem()],
        out_specs=[in_vmem()] * len(kinds),
        scratch_shapes=[pltpu.VMEM((tiles, (step_wins + 1) * pitch, LANES), jnp.float32)],
    )(slots, traces)


def spectra(rows_j, rows_i, tables):
    wins, given, samples = rows_j.shape
    bins = samples // 2
    pairs = wins // 2
    depth = 2 * wins
    folded = HALF // given
    line = depth // folded
    pitch = line + 1
    per_step = 2 * folded
    batch = 4

    def kernel(j_ref, i_ref, table_ref, to_i_ref, to_j_ref, i_out, j_out, wide):
        same = lax.axis_index("sub") == lax.axis_index("rep")

        def spectrum_of(group):
            stacked = []
            for win in [per_step * group + u for u in range(per_step)]:
                here = j_ref[win]
                stacked += [here, jnp.where(same, here, i_ref[win])]
            wave = jnp.concatenate(stacked, axis=0)
            return lax.dot_general(table_ref[...], wave, NT, preferred_element_type=jnp.float32)

        def keep(group, spectrum):
            energy = jnp.sum(spectrum * spectrum, axis=0, keepdims=True) / bins
            white = spectrum * lax.rsqrt(energy + 1e-05)
            for half in range(2):
                for part in range(2):
                    if folded == 1:
                        row = half * wins + part * pairs + group
                    else:
                        row = part * pairs + 2 * group + half
                    wide[pl.ds(row, bins, stride=pitch), :] = white[
                        part * bins : (part + 1) * bins, half * LANES : (half + 1) * LANES
                    ]

        groups = wins // per_step
        at_once = 4

        def some_windows(step, carry):
            first = step * at_once
            last = spectrum_of(first)
            for group in range(1, at_once):
                now = spectrum_of(first + group)
                keep(first + group - 1, last)
                last = now
            keep(first + at_once - 1, last)
            return carry

        lax.fori_loop(0, groups // at_once, some_windows, 0)

        def turn(values):
            swapped = []
            for first in range(0, line, wins):
                swapped += [-values[first + pairs : first + wins], values[first : first + pairs]]
            return jnp.concatenate(swapped, axis=0)

        def moved(fs):
            loaded = [wide[pl.ds(f * pitch, line), :].astype(jnp.bfloat16) for f in fs]
            i_rows = []
            for values in loaded:
                if folded == 2:
                    blank = jnp.zeros_like(values)
                    values = jnp.concatenate(
                        [jnp.concatenate([values, blank], axis=1), jnp.concatenate([blank, values], axis=1)], axis=0
                    )
                i_rows.append(lax.dot_general(to_i_ref[...], values, NT, preferred_element_type=jnp.float32))
            both = jnp.concatenate(
                [jnp.concatenate(loaded, axis=0), jnp.concatenate([turn(values) for values in loaded], axis=0)], axis=1
            )
            return fs, i_rows, jnp.dot(both, to_j_ref[...], preferred_element_type=jnp.float32)

        def store(fs, i_rows, j_rows):
            for at, f in enumerate(fs):
                i_out[f] = i_rows[at].astype(jnp.bfloat16)
                for odd in range(folded):
                    j_out[f, odd * line : (odd + 1) * line] = j_rows[
                        at * line : (at + 1) * line, odd * LANES : (odd + 1) * LANES
                    ].astype(jnp.bfloat16)

        def pack(group, carry):
            first = group * 4 * batch
            waiting = moved([first + u for u in range(batch)])
            for at in range(1, 4):
                following = moved([first + at * batch + u for u in range(batch)])
                store(*waiting)
                waiting = following
            store(*waiting)
            return carry

        lax.fori_loop(0, bins // (4 * batch), pack, 0)

    shapes = [(bins, given, depth), (bins, depth, LANES)]
    return kernel_call(
        kernel,
        "spectra",
        4 * samples * samples * wins * given,
        4 * wins * given * samples * 2,
        out_shape=[jax.ShapeDtypeStruct(shape, jnp.bfloat16) for shape in shapes],
        in_specs=[in_vmem()] * (2 + len(tables)),
        out_specs=[in_vmem()] * len(shapes),
        scratch_shapes=[pltpu.VMEM(((bins + 1) * pitch, LANES), jnp.float32)],
    )(rows_j, rows_i, *tables)


def partial_correlations(lefts, rights, tables, jobs):
    bins, depth, _ = rights[0].shape
    piece = HALF // BLOCKS
    pitch = bins + 1
    step_bins = 32
    flat = [(job, *segment) for job, (_, _, segments) in enumerate(jobs) for segment in segments]
    total = len(flat) * piece
    dests = sorted({entry[3] for entry in flat})
    slices = {at: [] for at in dests}
    for job, left, _, at in flat:
        for there in jobs[job][1]:
            if there != at:
                slices[at].append((left, jobs[job][0][0], (AHEAD[there] - AHEAD[at]) % BLOCKS, job, there))
    batch = 8 if total <= 4 * piece else 4
    pairs_at_once = 4

    def kernel(*refs):
        left_refs, rest = refs[: len(lefts)], refs[len(lefts) :]
        right_refs, rest = rest[: len(rights)], rest[len(rights) :]
        lag_ref, pick_ref, out_refs, cross = rest[0], rest[1], rest[2:-1], rest[-1]

        def products(first_bin, count):
            found = []
            for f in [first_bin + u for u in range(count)]:
                first = 0
                for added, _, segments in jobs:
                    rhs = functools.reduce(jnp.add, [right_refs[right][f] for right in added])
                    rows = [left_refs[left][f, row : row + piece] for left, row, _ in segments]
                    lhs = jnp.concatenate(rows, axis=0) if len(rows) > 1 else rows[0]
                    product = jnp.dot(lhs, rhs, preferred_element_type=jnp.float32)
                    found.append((first * pitch + f, product))
                    first += lhs.shape[0]
            return found

        def keep(found):
            for here, product in found:
                cross[pl.ds(here, product.shape[0], stride=pitch), :] = product

        def some_bins(step, carry):
            first = step * step_bins
            waiting = products(first, batch)
            for at in range(batch, step_bins, batch):
                following = products(first + at, batch)
                keep(waiting)
                waiting = following
            keep(waiting)
            return carry

        lax.fori_loop(0, bins // step_bins, some_bins, 0)

        for index, (job, left, _, at) in enumerate(flat):
            out = out_refs[dests.index(at)]
            places = [
                (place, entry[4]) for place, entry in enumerate(slices[at]) if entry[3] == job and entry[0] == left
            ]

            def summed(i, index=index):
                start = (index * piece + i) * pitch
                values = jnp.concatenate(
                    [cross[pl.ds(start, bins), :], cross[pl.ds(start + pitch, bins), :]], axis=1
                ).astype(jnp.bfloat16)
                return i, jnp.dot(lag_ref[...], values, preferred_element_type=jnp.float32)

            def gathered(i, both):
                both = both.astype(jnp.bfloat16)
                both = jnp.concatenate([both[:LAGS], both[LAGS:]], axis=1)
                return i, lax.dot_general(pick_ref[...], both, NT, preferred_element_type=jnp.float32)

            def store(i, lagged, out=out, places=places):
                lagged = lagged.astype(out.dtype)
                for half in range(2):
                    for place, there in places:
                        row = half * HALF + there * piece
                        out[place, i + half] = lagged[row : row + piece]

            def some_channels(group, carry, summed=summed, gathered=gathered, store=store):
                first = 2 * pairs_at_once * group
                sums, rows = summed(first), None
                for pair in range(1, pairs_at_once):
                    more = summed(first + 2 * pair)
                    if rows is not None:
                        store(*rows)
                    rows = gathered(*sums)
                    sums = more
                store(*rows)
                store(*gathered(*sums))
                return carry

            lax.fori_loop(0, piece // (2 * pairs_at_once), some_channels, 0)

    shapes = [(len(slices[at]), piece, piece, LAGS) for at in dests]
    types = [jnp.float32 if at == OWN_AT else jnp.bfloat16 for at in dests]
    results = kernel_call(
        kernel,
        "partial_correlations",
        2 * total * bins * depth * LANES + 2 * total * bins * LANES * 2 * LAGS,
        2 * sum(array.size for array in lefts + rights),
        out_shape=[jax.ShapeDtypeStruct(shape, kind) for shape, kind in zip(shapes, types)],
        in_specs=[in_vmem()] * (len(lefts) + len(rights) + len(tables)),
        out_specs=[in_vmem()] * len(shapes),
        scratch_shapes=[pltpu.VMEM(((total + 1) * pitch, LANES), jnp.float32)],
    )(*lefts, *rights, *tables)
    return {at: (result, [entry[:3] for entry in slices[at]]) for at, result in zip(dests, results)}


def assembled(shares):
    arrays = [array for array, _ in shares]
    _, piece, _, lags = arrays[0].shape
    width = 2 * piece

    def kernel(*refs):
        out, held, sems = refs[-3:]
        sub = lax.axis_index("sub")
        copies = []
        for after in range(1, ROUNDS + 1):
            for i_other in range(2):
                for j_other in range(2):
                    parts = [
                        refs[at][place].astype(jnp.float32)
                        for at, (_, kinds) in enumerate(shares)
                        for place, kind in enumerate(kinds)
                        if kind == (i_other, j_other, after)
                    ]
                    i_first = jnp.where(sub == 0, i_other, 1 - i_other) * piece
                    j_first = pl.multiple_of(jnp.where(sub == 0, j_other, 1 - j_other) * piece, piece)
                    held[after - 1, 0, pl.ds(i_first, piece), pl.ds(j_first, piece), :] = functools.reduce(
                        jnp.add, parts
                    )
            copies.append(pltpu.make_async_copy(held.at[after - 1], out.at[after - 1], sems.at[after - 1]))
            copies[-1].start()
        for copy in copies:
            copy.wait()

    shape = (ROUNDS, 1, width, width, lags)
    return kernel_call(
        kernel,
        "assembled",
        0,
        sum(array.size for array in arrays) * 2,
        out_shape=jax.ShapeDtypeStruct(shape, jnp.float32),
        in_specs=[in_vmem()] * len(arrays),
        out_specs=pl.BlockSpec(memory_space=pl.ANY),
        scratch_shapes=[pltpu.VMEM(shape, jnp.float32), pltpu.SemaphoreType.DMA((ROUNDS,))],
    )(*arrays)


def summed_in_place(traces, channel_slot):
    chan_count = lax.axis_size("chan")
    _, win_here, samples = traces.shape
    piece = HALF // BLOCKS
    scale = (2.0 / (win_here * chan_count * (samples // 2))) ** 0.5
    dft_rows = dft_rows_table(samples)
    lag_tables = [lag_rows_table(samples, scale), picks_lags()]
    everywhere = tuple(range(BLOCKS))

    def over_sub(rows):
        return lax.ppermute(rows, "sub", [(0, 1), (1, 0)])

    def over_core(rows):
        return lax.ppermute(rows, ("sub", "rep"), [(0, 1), (3, 2)])

    def after(value, *others):
        return lax.optimization_barrier((value,) + others)[0]

    def segments(left, positions, first):
        return [(left, (at - first) * piece, at) for at in positions]

    shares = []

    def send(parts, i_other, j_other):
        arrived = []
        for at, (part, kinds) in parts.items():
            if at != OWN_AT:
                by = AHEAD[at]
                part = lax.ppermute(part, "chan", [(z, (z + by) % chan_count) for z in range(chan_count)])
                arrived.append(part)
            shares.append((part, [(i_other[left], j_other[right], k) for left, right, k in kinds]))
        return arrived

    def arrays_of(parts):
        return [part for part, _ in parts.values()]

    mine, mine_far, mine_near = order_rows(traces, channel_slot, [everywhere, FAR, NEAR])
    far = over_sub(mine_far)
    near = over_sub(mine_near)

    own_i, own_j = spectra(mine, over_core(mine), (dft_rows, *own_picks()))
    parts = partial_correlations([own_i], [own_j], lag_tables, [((0,), everywhere, segments(0, everywhere, 0))])
    first_shares = send(parts, (0,), (0,))

    far = after(far, *arrays_of(parts))
    far_i, far_j = spectra(far, over_core(far), (dft_rows, *half_picks(0)))
    parts = partial_correlations(
        [own_i, far_i],
        [own_j, far_j],
        lag_tables,
        [
            ((0,), everywhere, segments(1, FAR, 0)),
            ((1,), FAR, segments(0, everywhere, 0) + segments(1, FAR, 0)),
        ],
    )
    second_shares = send(parts, (0, 1), (0, 1))

    near = after(near, *arrays_of(parts), *first_shares)
    near_i, near_j = spectra(near, over_core(near), (dft_rows, *half_picks(1)))
    parts = partial_correlations(
        [own_i, near_i],
        [own_j, far_j, near_j],
        lag_tables,
        [
            ((0,), everywhere, segments(1, NEAR, NEAR[0])),
            ((1, 2), everywhere, segments(1, NEAR, NEAR[0])),
            ((2,), NEAR, segments(0, NEAR, 0)),
        ],
    )
    send(parts, (0, 1), (0, 1, 1))
    near_j = after(near_j, *arrays_of(parts), *second_shares)
    parts = partial_correlations(
        [own_i, far_i], [near_j], lag_tables, [((0,), NEAR, segments(0, FAR, 0) + segments(1, FAR, 0))]
    )
    send(parts, (0, 1), (1,))
    return assembled(shares)


def from_behind(shard, axis, by):
    count = lax.axis_size(axis)
    return lax.ppermute(shard, axis, [(i, (i + by) % count) for i in range(count)])


def dft_columns(samples, parts, sub_bins):
    shape = (samples, parts, 2, sub_bins)
    time_pos = lax.broadcasted_iota(jnp.int32, shape, 0)
    range_pos = lax.broadcasted_iota(jnp.int32, shape, 1)
    part_pos = lax.broadcasted_iota(jnp.int32, shape, 2)
    bin_pos = lax.broadcasted_iota(jnp.int32, shape, 3)
    frequency = range_pos * sub_bins + bin_pos
    angles = jnp.mod(time_pos * frequency, samples).astype(jnp.float32) * (2.0 * math.pi / samples)
    entries = jnp.where(part_pos == 0, jnp.cos(angles), -jnp.sin(angles))
    return entries.reshape(samples, parts * 2 * sub_bins).astype(jnp.bfloat16)


def lag_table(sub_bins, first_bin, lag_count, samples):
    frequency = first_bin + lax.broadcasted_iota(jnp.int32, (sub_bins, lag_count), 0)
    lag_offset = lax.broadcasted_iota(jnp.int32, (sub_bins, lag_count), 1) - lag_count // 2
    angles = jnp.mod(frequency * lag_offset, samples).astype(jnp.float32) * (2.0 * math.pi / samples)
    return jnp.stack([jnp.cos(angles), -jnp.sin(angles)], axis=1)


def moved_spectra(traces, channel_slot):
    chan_count = lax.axis_size("chan")
    sub_count = lax.axis_size("sub")
    group_rows, win_here, samples = traces.shape
    bin_count = samples // 2
    sub_bins = bin_count // sub_count
    bin_width = 2 * sub_bins
    piece_len = group_rows // chan_count
    picked = jnp.take(traces, channel_slot, axis=0)
    dft_rows = dft_columns(samples, sub_count, sub_bins)
    spectrum = jnp.dot(picked.reshape(-1, samples), dft_rows, preferred_element_type=jnp.float32)
    energy = jnp.sum(spectrum * spectrum, axis=1, keepdims=True) / bin_count
    whitened = (spectrum * lax.rsqrt(energy + 1e-05)).astype(jnp.bfloat16)
    whitened = whitened.reshape(chan_count, piece_len, win_here, sub_count, bin_width)
    regrouped = lax.all_to_all(whitened, "chan", split_axis=0, concat_axis=0, tiled=True)
    regrouped = lax.all_to_all(regrouped, "sub", split_axis=3, concat_axis=3, tiled=True)
    own_half = regrouped.transpose(3, 1, 0, 2, 4).reshape(sub_count * piece_len, chan_count * win_here, bin_width)
    own_block = lax.all_gather(own_half, "rep", axis=0, tiled=True)
    windows = own_block.shape[1]
    own_split = own_block.reshape(own_block.shape[0], windows, 2, sub_bins)
    lag_rows = lag_table(sub_bins, lax.axis_index("sub") * sub_bins, LAGS, samples)
    lag_scale = (2.0 / (windows * bin_count)) ** 0.5
    results = []
    for step in range(1, ROUNDS + 1):
        partner = from_behind(own_half, "chan", -step)
        partner_split = partner.reshape(partner.shape[0], windows, 2, sub_bins)
        turned = jnp.stack([-partner_split[:, :, 1], partner_split[:, :, 0]], axis=2)
        partner_pair = jnp.stack([partner_split, turned], axis=0)
        cross_spec = jnp.einsum("iwpf,qjwpf->fqij", own_split, partner_pair, preferred_element_type=jnp.float32)
        summed = jnp.einsum("fqij,fql->ijl", cross_spec, lag_rows, precision=lax.Precision.HIGHEST)
        results.append(lax.psum_scatter(lag_scale * summed, "sub", scatter_dimension=0, tiled=True))
    return jnp.stack(results)[:, None]


def solution(mesh):
    sizes = mesh.shape
    in_place = sizes["chan"] == BLOCKS == ROUNDS + 1 and sizes["sub"] == 2 and sizes["rep"] == 2
    return jax.shard_map(
        summed_in_place if in_place else moved_spectra,
        mesh=mesh,
        in_specs=(P(("groups", "sub", "rep"), "chan", None), P(("groups", "sub", "rep"))),
        out_specs=P(None, ("groups", "chan"), "sub", "rep", None),
        check_vma=False,
    )
```

```python
import functools
import math

import jax
import jax.numpy as jnp
import numpy as np
from jax import lax
from jax.experimental import pallas as pl
from jax.experimental.pallas import tpu as pltpu
from jax.sharding import PartitionSpec as P

LAGS = 128
ROUNDS = 3
LANES = 128
HALF = LANES // 2
VMEM_BYTES = 32 * 1024 * 1024
NT = (((1,), (1,)), ((), ()))
BLOCKS = 4
FAR = (0, 1)
NEAR = (2, 3)
KEPT_AT, OWN_AT = 0, 2


def kernel_call(kernel, name, flops, bytes_accessed, **more):
    return pl.pallas_call(
        kernel,
        name=name,
        compiler_params=pltpu.CompilerParams(vmem_limit_bytes=VMEM_BYTES),
        cost_estimate=pl.CostEstimate(flops=flops, bytes_accessed=bytes_accessed, transcendentals=0),
        **more,
    )


def in_vmem():
    return pl.BlockSpec(memory_space=pltpu.VMEM)


def dft_rows_table(samples):
    bins = samples // 2
    turns = (np.arange(bins)[:, None] * np.arange(samples)[None, :]) % samples
    angles = turns.astype(np.float32) * np.float32(2.0 * math.pi / samples)
    table = np.concatenate([np.cos(angles), -np.sin(angles)], axis=0)
    return jnp.asarray(table.astype(np.float32)).astype(jnp.bfloat16)


def lag_rows_table(samples, scale):
    bins = samples // 2
    offsets = np.arange(LAGS) - LAGS // 2
    turns = (offsets[:, None] * np.arange(bins)[None, :]) % samples
    angles = turns.astype(np.float32) * np.float32(2.0 * math.pi / samples)
    table = np.concatenate([np.cos(angles), -np.sin(angles)], axis=1) * np.float32(scale)
    return jnp.asarray(table.astype(np.float32)).astype(jnp.bfloat16)


def selection(rows, columns, ones):
    table = np.zeros((rows, columns), np.float32)
    for row, column in ones:
        table[row, column] = 1.0
    return jnp.asarray(table).astype(jnp.bfloat16)


def own_picks():
    piece = HALF // BLOCKS
    to_i = []
    for at in range(BLOCKS):
        for n in range(piece):
            to_i.append((at // 2 * piece + n, at % 2 * LANES + HALF + at * piece + n))
    to_j = [(j, copy * HALF + j) for j in range(HALF) for copy in range(2)]
    return selection(2 * piece, 2 * LANES, to_i), selection(LANES, LANES, to_j)


def half_picks():
    piece, count = HALF // BLOCKS, HALF // 2
    to_i, to_j = [], []
    for odd in range(2):
        for at in range(2):
            for n in range(piece):
                to_i.append((n, (2 * at + odd) * LANES + odd * HALF + count + at * piece + n))
        for n in range(count):
            to_j += [(odd * HALF + n, odd * LANES + copy * count + n) for copy in range(4)]
    return selection(piece, 4 * LANES, to_i), selection(LANES, 2 * LANES, to_j)


def order_rows(traces, slots, kinds):
    rows, wins, samples = traces.shape
    tiles = samples // LANES
    piece = rows // BLOCKS
    step_wins = 16
    batch = 4
    used = max(kinds, key=len)
    pitch = len(used) * piece + 1

    def kernel(slot_ref, in_ref, *refs):
        out_refs, wide = refs[:-1], refs[-1]
        z = lax.axis_index("chan")
        odd = lax.rem(z, 2)
        pair = jnp.where(z < 2, 2, 0)

        def some_windows(step, carry):
            first_win = pl.multiple_of(step * step_wins, step_wins)
            for at, position in enumerate(used):
                block = pair + position + (odd if position % 2 == 0 else -odd)
                first = lax.rem(block, BLOCKS) * piece

                def move(group, carry, at=at, first=first):
                    js = [group * batch + u for u in range(batch)]
                    picked = [
                        in_ref[slot_ref[first + j], pl.ds(first_win, step_wins), :].astype(jnp.float32) for j in js
                    ]
                    for j, row in zip(js, picked):
                        for tile in range(tiles):
                            wide[tile, pl.ds(at * piece + j, step_wins, stride=pitch), :] = row[
                                :, tile * LANES : (tile + 1) * LANES
                            ]
                    return carry

                lax.fori_loop(0, piece // batch, move, 0)

            def pack(w, carry):
                blocks = [
                    wide[tile, pl.ds(w * pitch, len(used) * piece), :].astype(jnp.bfloat16) for tile in range(tiles)
                ]
                for out_ref, kind in zip(out_refs, kinds):
                    first = used.index(kind[0]) * piece
                    for tile, block in enumerate(blocks):
                        out_ref[first_win + w, :, tile * LANES : (tile + 1) * LANES] = block[
                            first : first + len(kind) * piece
                        ]
                return carry

            lax.fori_loop(0, step_wins, pack, 0, unroll=2)
            return carry

        lax.fori_loop(0, wins // step_wins, some_windows, 0)

    return kernel_call(
        kernel,
        "order_rows",
        0,
        3 * traces.size * 2,
        out_shape=[jax.ShapeDtypeStruct((wins, len(kind) * piece, samples), jnp.bfloat16) for kind in kinds],
        in_specs=[pl.BlockSpec(memory_space=pltpu.SMEM), in_vmem()],
        out_specs=[in_vmem()] * len(kinds),
        scratch_shapes=[pltpu.VMEM((tiles, (step_wins + 1) * pitch, LANES), jnp.float32)],
    )(slots, traces)


def diagonal(values, copies):
    blank = jnp.zeros_like(values)
    rows = [[values if at == copy else blank for at in range(copies)] for copy in range(copies)]
    return jnp.concatenate([jnp.concatenate(row, axis=1) for row in rows], axis=0)


def spectra(rows_j, rows_i, tables):
    wins, given, samples = rows_j.shape
    bins = samples // 2
    pairs = wins // 2
    depth = 2 * wins
    folded = HALF // given
    line = depth // folded
    pitch = line + 1
    per_step = 2 * folded
    batch = 8

    def kernel(j_ref, i_ref, table_ref, to_i_ref, to_j_ref, i_out, j_out, wide):
        same = lax.axis_index("sub") == lax.axis_index("rep")

        def spectrum_of(group):
            stacked = []
            for win in [per_step * group + u for u in range(per_step)]:
                here = j_ref[win]
                stacked += [here, jnp.where(same, here, i_ref[win])]
            wave = jnp.concatenate(stacked, axis=0)
            return lax.dot_general(table_ref[...], wave, NT, preferred_element_type=jnp.float32)

        def keep(group, spectrum):
            energy = jnp.sum(spectrum * spectrum, axis=0, keepdims=True) / bins
            white = spectrum * lax.rsqrt(energy + 1e-05)
            for half in range(2):
                for part in range(2):
                    if folded == 1:
                        row = half * wins + part * pairs + group
                    else:
                        row = part * pairs + 2 * group + half
                    wide[pl.ds(row, bins, stride=pitch), :] = white[
                        part * bins : (part + 1) * bins, half * LANES : (half + 1) * LANES
                    ]

        groups = wins // per_step
        at_once = 4

        def some_windows(step, carry):
            first = step * at_once
            last = spectrum_of(first)
            for group in range(1, at_once):
                now = spectrum_of(first + group)
                keep(first + group - 1, last)
                last = now
            keep(first + at_once - 1, last)
            return carry

        lax.fori_loop(0, groups // at_once, some_windows, 0)

        def moved(fs):
            loaded = [wide[pl.ds(f * pitch, line), :].astype(jnp.bfloat16) for f in fs]
            i_rows = [
                lax.dot_general(
                    to_i_ref[...], diagonal(values, 2 * folded), NT, preferred_element_type=jnp.float32
                )
                for values in loaded
            ]
            j_rows = jnp.dot(jnp.concatenate(loaded, axis=0), to_j_ref[...], preferred_element_type=jnp.float32)
            return fs, i_rows, j_rows

        def store(fs, i_rows, j_rows):
            for at, f in enumerate(fs):
                i_out[f] = i_rows[at].astype(jnp.bfloat16)
                for odd in range(folded):
                    j_out[f, odd * line : (odd + 1) * line] = j_rows[
                        at * line : (at + 1) * line, odd * LANES : (odd + 1) * LANES
                    ].astype(jnp.bfloat16)

        def pack(group, carry):
            first = group * 4 * batch
            waiting = moved([first + u for u in range(batch)])
            for at in range(1, 4):
                following = moved([first + at * batch + u for u in range(batch)])
                store(*waiting)
                waiting = following
            store(*waiting)
            return carry

        lax.fori_loop(0, bins // (4 * batch), pack, 0)

    shapes = [(bins, given // 2, LANES), (bins, depth, LANES)]
    return kernel_call(
        kernel,
        "spectra",
        4 * samples * samples * wins * given,
        4 * wins * given * samples * 2,
        out_shape=[jax.ShapeDtypeStruct(shape, jnp.bfloat16) for shape in shapes],
        in_specs=[in_vmem()] * (2 + len(tables)),
        out_specs=[in_vmem()] * len(shapes),
        scratch_shapes=[pltpu.VMEM(((bins + 1) * pitch, LANES), jnp.float32)],
    )(rows_j, rows_i, *tables)


def partial_correlations(lefts, rights, tables, jobs, outs):
    left_arrays = [array for array, _ in lefts]
    right_arrays = [array for array, _, _ in rights]
    bins, depth, _ = right_arrays[0].shape
    piece = HALF // BLOCKS
    pitch = bins + 1
    step_bins = 32
    groups = []
    slices = {}
    for job, (used, groups_here) in enumerate(jobs):
        js = [(rights[right][1], there) for right in used for there in rights[right][2]]
        span = len(js) * piece
        for sides in groups_here:
            found = []
            for side, (left, _, first) in enumerate(sides):
                for offset in range(2):
                    at = first + offset
                    for order, (j_other, there) in enumerate(js):
                        if there != at:
                            kind = (lefts[left][1], j_other, there ^ (at % 2))
                            found.append((at, kind, (2 * side + offset) * span + order * piece))
                            slices.setdefault(at, []).append(kind)
            groups.append((job, sides, found))
    for kinds in slices.values():
        kinds.sort()
    total = len(groups) * piece
    batch = 4
    at_once = 4

    def first_of(at):
        (out,) = [positions for positions in outs if at in positions]
        return outs.index(out), sum(len(slices[before]) for before in out[: out.index(at)])

    def kernel(*refs):
        left_refs, rest = refs[: len(lefts)], refs[len(lefts) :]
        right_refs, rest = rest[: len(rights)], rest[len(rights) :]
        lag_ref, same_ref, out_refs, cross = rest[0], rest[1], rest[2:-1], rest[-1]
        lanes = lax.broadcasted_iota(jnp.int32, (depth, LANES), 1)

        def mask(wanted):
            return wanted.astype(jnp.float32).astype(jnp.bfloat16)

        halves = [mask(lanes // HALF == at) for at in range(2)]
        quarters = [mask(lanes // (HALF // 2) == at) for at in range(4)]
        lower = mask(lanes % HALF < HALF // 2)
        upper = mask(lanes % HALF >= HALF // 2)

        def turn(values):
            swapped = []
            for first in range(0, depth, depth // 2):
                middle, last = first + depth // 4, first + depth // 2
                swapped += [-values[middle:last], values[first:middle]]
            return jnp.concatenate(swapped, axis=0)

        def right_hand(used, f, copies):
            values = right_refs[used[0]][f]
            if len(used) == 2:
                values = values * lower + right_refs[used[1]][f] * upper
            turned = turn(values)
            masks = quarters if len(rights[used[0]][2]) == 2 and len(used) == 1 else halves
            rows = [jnp.concatenate([values * here, turned * here], axis=1) for here in masks[:copies]]
            return jnp.concatenate(rows, axis=0)

        def left_hand(sides, f, width):
            parts = [left_refs[left][f, row : row + piece] for left, row, _ in sides]
            if len(parts) < width:
                parts += [jnp.zeros_like(parts[0])] * (width - len(parts))
            return jnp.concatenate(parts, axis=1) if width > 1 else parts[0]

        def products(first_bin, count):
            found = []
            for f in [first_bin + u for u in range(count)]:
                first = 0
                for used, groups_here in jobs:
                    width = max(len(sides) for sides in groups_here)
                    lhs = [left_hand(sides, f, width) for sides in groups_here]
                    lhs = jnp.concatenate(lhs, axis=0) if len(lhs) > 1 else lhs[0]
                    product = jnp.dot(lhs, right_hand(used, f, 2 * width), preferred_element_type=jnp.float32)
                    found.append((first * pitch + f, product))
                    first += lhs.shape[0]
            return found

        def keep(found):
            for here, product in found:
                for part in range(2):
                    cross[pl.ds(part * total * pitch + here, product.shape[0], stride=pitch), :] = product[
                        :, part * LANES : (part + 1) * LANES
                    ]

        def some_bins(step, carry):
            first = step * step_bins
            waiting = products(first, batch)
            for at in range(batch, step_bins, batch):
                following = products(first + at, batch)
                keep(waiting)
                waiting = following
            keep(waiting)
            return carry

        lax.fori_loop(0, bins // step_bins, some_bins, 0)

        for index, (_, _, found) in enumerate(groups):
            targets = []
            for at, kind, lane in found:
                out, first = first_of(at)
                targets.append((out_refs[out], first + slices[at].index(kind), lane))

            def summed(i, index=index):
                parts = []
                for part in range(2):
                    start = (part * total + index * piece + i) * pitch
                    parts.append(
                        jnp.concatenate([cross[pl.ds(start, bins), :], cross[pl.ds(start + pitch, bins), :]], axis=1)
                    )
                values = jnp.concatenate(parts, axis=0).astype(jnp.bfloat16)
                return i, jnp.dot(lag_ref[...], values, preferred_element_type=jnp.float32)

            def across(i, lagged):
                lagged = lagged.astype(jnp.bfloat16)
                return i, lax.dot_general(same_ref[...], lagged, NT, preferred_element_type=jnp.float32)

            def store(i, rows, targets=targets):
                for half in range(2):
                    for out, place, lane in targets:
                        row = half * LANES + lane
                        out[place, i + half] = rows[row : row + piece].astype(out.dtype)

            def some_channels(group, carry, summed=summed, across=across, store=store):
                first = 2 * at_once * group
                sums, rows = summed(first), None
                for pair in range(1, at_once):
                    more = summed(first + 2 * pair)
                    if rows is not None:
                        store(*rows)
                    rows = across(*sums)
                    sums = more
                store(*rows)
                store(*across(*sums))
                return carry

            lax.fori_loop(0, piece // (2 * at_once), some_channels, 0)

    shapes = [(sum(len(slices[at]) for at in positions), piece, piece, LAGS) for positions in outs]
    types = [jnp.float32 if positions == (OWN_AT,) else jnp.bfloat16 for positions in outs]
    results = kernel_call(
        kernel,
        "partial_correlations",
        4 * total * bins * depth * LANES + 4 * total * bins * LANES * LAGS,
        2 * sum(array.size for array in left_arrays + right_arrays),
        out_shape=[jax.ShapeDtypeStruct(shape, kind) for shape, kind in zip(shapes, types)],
        in_specs=[in_vmem()] * (len(lefts) + len(rights) + len(tables)),
        out_specs=[in_vmem()] * len(shapes),
        scratch_shapes=[pltpu.VMEM(((2 * total + 1) * pitch, LANES), jnp.float32)],
    )(*left_arrays, *right_arrays, *tables)
    return results, slices


def assembled(shares):
    arrays = [array for array, _ in shares]
    _, piece, _, lags = arrays[0].shape
    width = 2 * piece

    def kernel(*refs):
        out, held, sems = refs[-3:]
        sub = lax.axis_index("sub")
        odd = lax.rem(lax.axis_index("chan"), 2)
        copies = []
        for there, round_at in ((0, 1), (1, 2 - 2 * odd), (3, 2 * odd)):
            for i_other in range(2):
                for j_other in range(2):
                    parts = [
                        refs[at][place].astype(jnp.float32)
                        for at, (_, kinds) in enumerate(shares)
                        for place, kind in enumerate(kinds)
                        if kind == (i_other, j_other, there)
                    ]
                    i_first = jnp.where(sub == 0, i_other, 1 - i_other) * piece
                    j_first = pl.multiple_of(jnp.where(sub == 0, j_other, 1 - j_other) * piece, piece)
                    held[round_at, 0, pl.ds(i_first, piece), pl.ds(j_first, piece), :] = functools.reduce(
                        jnp.add, parts
                    )
            at = len(copies)
            copies.append(pltpu.make_async_copy(held.at[round_at], out.at[round_at], sems.at[at]))
            copies[-1].start()
        for copy in copies:
            copy.wait()

    shape = (ROUNDS, 1, width, width, lags)
    return kernel_call(
        kernel,
        "assembled",
        0,
        sum(array.size for array in arrays) * 2,
        out_shape=jax.ShapeDtypeStruct(shape, jnp.float32),
        in_specs=[in_vmem()] * len(arrays),
        out_specs=pl.BlockSpec(memory_space=pl.ANY),
        scratch_shapes=[pltpu.VMEM(shape, jnp.float32), pltpu.SemaphoreType.DMA((ROUNDS,))],
    )(*arrays)


def summed_in_place(traces, channel_slot):
    chan_count = lax.axis_size("chan")
    _, win_here, samples = traces.shape
    piece = HALF // BLOCKS
    scale = (2.0 / (win_here * chan_count * (samples // 2))) ** 0.5
    dft_rows = dft_rows_table(samples)
    same = selection(2 * LANES, 2 * LANES, [(n, n) for n in range(2 * LANES)])
    tables = [lag_rows_table(samples, scale), same]
    everywhere = tuple(range(BLOCKS))

    def over_sub(rows):
        return lax.ppermute(rows, "sub", [(0, 1), (1, 0)])

    def over_core(rows):
        return lax.ppermute(rows, ("sub", "rep"), [(0, 1), (3, 2)])

    def with_device(share, apart):
        return lax.ppermute(share, "chan", [(z, z ^ apart) for z in range(chan_count)])

    def after(value, *others):
        return lax.optimization_barrier((value,) + others)[0]

    def added(share, arrived):
        return (share.astype(jnp.float32) + arrived.astype(jnp.float32)).astype(jnp.bfloat16)

    def for_two_away(kinds):
        return [(i_other, j_other, there ^ 2) for i_other, j_other, there in kinds]

    mine, mine_far, mine_near = order_rows(traces, channel_slot, [everywhere, FAR, NEAR])
    far = over_sub(mine_far)
    near = over_sub(mine_near)

    own_i, own_j = spectra(mine, over_core(mine), (dft_rows, *own_picks()))
    own_left, own_right = (own_i, 0), (own_j, 0, everywhere)
    own_far, own_near = (0, 0, FAR[0]), (0, piece, NEAR[0])
    (kept_1, own_1, sent_1), kinds_1 = partial_correlations(
        [own_left], [own_right], tables, [((0,), [[own_far], [own_near]])], [(0,), (2,), (1, 3)]
    )
    arrived_1 = with_device(sent_1, 1)

    far = after(far, kept_1, own_1, sent_1)
    far_i, far_j = spectra(far, over_core(far), (dft_rows, *half_picks()))
    far_left, far_right = (far_i, 1), (far_j, 1, FAR)
    other_far = (1, 0, FAR[0])
    (kept_2, own_2, sent_2), kinds_2 = partial_correlations(
        [own_left, far_left],
        [own_right, far_right],
        tables,
        [((0,), [[other_far]]), ((1,), [[own_far, own_near], [other_far]])],
        [(0,), (2,), (1, 3)],
    )
    arrived_2 = with_device(sent_2, 1)

    near = after(near, kept_2, own_2, sent_2, arrived_1)
    near_i, near_j = spectra(near, over_core(near), (dft_rows, *half_picks()))
    near_left, near_right = (near_i, 1), (near_j, 1, NEAR)
    (kept_3, sent_3), kinds_3 = partial_correlations(
        [own_left, far_left], [near_right], tables, [((0,), [[own_far, other_far]])], [(0,), (1,)]
    )
    arrived_3 = with_device(sent_3, 1)
    far_count_1, far_count_2 = kept_1.shape[0], kept_2.shape[0]
    pair_12 = jnp.concatenate([added(kept_1, arrived_1[:far_count_1]), added(kept_2, arrived_2[:far_count_2])])
    far_12 = with_device(pair_12, 2)
    near_j = after(near_j, kept_3, sent_3, pair_12)
    near_right = (near_j, 1, NEAR)
    (own_4, sent_4), kinds_4 = partial_correlations(
        [own_left, near_left],
        [own_right, far_right, near_right],
        tables,
        [((0,), [[(1, 0, NEAR[0])]]), ((1, 2), [[(1, 0, NEAR[0])]]), ((2,), [[own_near]])],
        [(2,), (3,)],
    )
    far_3 = with_device(added(kept_3, arrived_3), 2)
    arrived_4 = with_device(sent_4, 1)
    shares = [
        (own_1, kinds_1[2]),
        (own_2, kinds_2[2]),
        (own_4, kinds_4[2]),
        (arrived_1, [None] * far_count_1 + kinds_1[3]),
        (arrived_2, [None] * far_count_2 + kinds_2[3]),
        (arrived_4, kinds_4[3]),
        (far_12, for_two_away(kinds_1[0] + kinds_2[0])),
        (far_3, for_two_away(kinds_3[0])),
    ]
    return assembled(shares)


def from_behind(shard, axis, by):
    count = lax.axis_size(axis)
    return lax.ppermute(shard, axis, [(i, (i + by) % count) for i in range(count)])


def dft_columns(samples, parts, sub_bins):
    shape = (samples, parts, 2, sub_bins)
    time_pos = lax.broadcasted_iota(jnp.int32, shape, 0)
    range_pos = lax.broadcasted_iota(jnp.int32, shape, 1)
    part_pos = lax.broadcasted_iota(jnp.int32, shape, 2)
    bin_pos = lax.broadcasted_iota(jnp.int32, shape, 3)
    frequency = range_pos * sub_bins + bin_pos
    angles = jnp.mod(time_pos * frequency, samples).astype(jnp.float32) * (2.0 * math.pi / samples)
    entries = jnp.where(part_pos == 0, jnp.cos(angles), -jnp.sin(angles))
    return entries.reshape(samples, parts * 2 * sub_bins).astype(jnp.bfloat16)


def lag_table(sub_bins, first_bin, lag_count, samples):
    frequency = first_bin + lax.broadcasted_iota(jnp.int32, (sub_bins, lag_count), 0)
    lag_offset = lax.broadcasted_iota(jnp.int32, (sub_bins, lag_count), 1) - lag_count // 2
    angles = jnp.mod(frequency * lag_offset, samples).astype(jnp.float32) * (2.0 * math.pi / samples)
    return jnp.stack([jnp.cos(angles), -jnp.sin(angles)], axis=1)


def moved_spectra(traces, channel_slot):
    chan_count = lax.axis_size("chan")
    sub_count = lax.axis_size("sub")
    group_rows, win_here, samples = traces.shape
    bin_count = samples // 2
    sub_bins = bin_count // sub_count
    bin_width = 2 * sub_bins
    piece_len = group_rows // chan_count
    picked = jnp.take(traces, channel_slot, axis=0)
    dft_rows = dft_columns(samples, sub_count, sub_bins)
    spectrum = jnp.dot(picked.reshape(-1, samples), dft_rows, preferred_element_type=jnp.float32)
    energy = jnp.sum(spectrum * spectrum, axis=1, keepdims=True) / bin_count
    whitened = (spectrum * lax.rsqrt(energy + 1e-05)).astype(jnp.bfloat16)
    whitened = whitened.reshape(chan_count, piece_len, win_here, sub_count, bin_width)
    regrouped = lax.all_to_all(whitened, "chan", split_axis=0, concat_axis=0, tiled=True)
    regrouped = lax.all_to_all(regrouped, "sub", split_axis=3, concat_axis=3, tiled=True)
    own_half = regrouped.transpose(3, 1, 0, 2, 4).reshape(sub_count * piece_len, chan_count * win_here, bin_width)
    own_block = lax.all_gather(own_half, "rep", axis=0, tiled=True)
    windows = own_block.shape[1]
    own_split = own_block.reshape(own_block.shape[0], windows, 2, sub_bins)
    lag_rows = lag_table(sub_bins, lax.axis_index("sub") * sub_bins, LAGS, samples)
    lag_scale = (2.0 / (windows * bin_count)) ** 0.5
    results = []
    for step in range(1, ROUNDS + 1):
        partner = from_behind(own_half, "chan", -step)
        partner_split = partner.reshape(partner.shape[0], windows, 2, sub_bins)
        turned = jnp.stack([-partner_split[:, :, 1], partner_split[:, :, 0]], axis=2)
        partner_pair = jnp.stack([partner_split, turned], axis=0)
        cross_spec = jnp.einsum("iwpf,qjwpf->fqij", own_split, partner_pair, preferred_element_type=jnp.float32)
        summed = jnp.einsum("fqij,fql->ijl", cross_spec, lag_rows, precision=lax.Precision.HIGHEST)
        results.append(lax.psum_scatter(lag_scale * summed, "sub", scatter_dimension=0, tiled=True))
    return jnp.stack(results)[:, None]


def solution(mesh):
    sizes = mesh.shape
    in_place = sizes["chan"] == BLOCKS == ROUNDS + 1 and sizes["sub"] == 2 and sizes["rep"] == 2
    return jax.shard_map(
        summed_in_place if in_place else moved_spectra,
        mesh=mesh,
        in_specs=(P(("groups", "sub", "rep"), "chan", None), P(("groups", "sub", "rep"))),
        out_specs=P(None, ("groups", "chan"), "sub", "rep", None),
        check_vma=False,
    )
```

```python
import functools
import math

import jax
import jax.numpy as jnp
import numpy as np
from jax import lax
from jax.experimental import pallas as pl
from jax.experimental.pallas import tpu as pltpu
from jax.sharding import PartitionSpec as P

LAGS = 128
ROUNDS = 3
LANES = 128
HALF = LANES // 2
VMEM_BYTES = 32 * 1024 * 1024
NT = (((1,), (1,)), ((), ()))
BLOCKS = 4
FAR = (0, 1)
NEAR = (2, 3)
KEPT_AT, OWN_AT = 0, 2


def kernel_call(kernel, name, flops, bytes_accessed, **more):
    return pl.pallas_call(
        kernel,
        name=name,
        compiler_params=pltpu.CompilerParams(vmem_limit_bytes=VMEM_BYTES),
        cost_estimate=pl.CostEstimate(flops=flops, bytes_accessed=bytes_accessed, transcendentals=0),
        **more,
    )


def in_vmem():
    return pl.BlockSpec(memory_space=pltpu.VMEM)


def dft_rows_table(samples):
    bins = samples // 2
    turns = (np.arange(bins)[:, None] * np.arange(samples)[None, :]) % samples
    angles = turns.astype(np.float32) * np.float32(2.0 * math.pi / samples)
    table = np.concatenate([np.cos(angles), -np.sin(angles)], axis=0)
    return jnp.asarray(table.astype(np.float32)).astype(jnp.bfloat16)


def lag_rows_table(samples, scale):
    bins = samples // 2
    offsets = np.arange(LAGS) - LAGS // 2
    turns = (offsets[:, None] * np.arange(bins)[None, :]) % samples
    angles = turns.astype(np.float32) * np.float32(2.0 * math.pi / samples)
    table = np.concatenate([np.cos(angles), -np.sin(angles)], axis=1) * np.float32(scale)
    return jnp.asarray(table.astype(np.float32)).astype(jnp.bfloat16)


def selection(rows, columns, ones):
    table = np.zeros((rows, columns), np.float32)
    for row, column in ones:
        table[row, column] = 1.0
    return jnp.asarray(table).astype(jnp.bfloat16)


def own_picks():
    piece = HALF // BLOCKS
    to_i = []
    for at in range(BLOCKS):
        for n in range(piece):
            to_i.append((at // 2 * piece + n, at % 2 * LANES + HALF + at * piece + n))
    to_j = [(j, copy * HALF + j) for j in range(HALF) for copy in range(2)]
    return selection(2 * piece, 2 * LANES, to_i), selection(LANES, LANES, to_j)


def half_picks():
    count = HALF // 2
    to_i, to_j = [], []
    for odd in range(2):
        for n in range(count):
            to_i.append((n, odd * LANES + odd * HALF + count + n))
            to_j += [(odd * HALF + n, odd * LANES + copy * count + n) for copy in range(4)]
    return selection(count, 2 * LANES, to_i), selection(LANES, 2 * LANES, to_j)


def order_rows(traces, slots, kinds):
    rows, wins, samples = traces.shape
    tiles = samples // LANES
    piece = rows // BLOCKS
    step_wins = 16
    batch = 4
    used = max(kinds, key=len)
    pitch = len(used) * piece + 1

    def kernel(slot_ref, in_ref, *refs):
        out_refs, wide = refs[:-1], refs[-1]
        z = lax.axis_index("chan")
        odd = lax.rem(z, 2)
        pair = jnp.where(z < 2, 2, 0)

        def some_windows(step, carry):
            first_win = pl.multiple_of(step * step_wins, step_wins)
            for at, position in enumerate(used):
                block = pair + position + (odd if position % 2 == 0 else -odd)
                first = lax.rem(block, BLOCKS) * piece

                def move(group, carry, at=at, first=first):
                    js = [group * batch + u for u in range(batch)]
                    picked = [
                        in_ref[slot_ref[first + j], pl.ds(first_win, step_wins), :].astype(jnp.float32) for j in js
                    ]
                    for j, row in zip(js, picked):
                        for tile in range(tiles):
                            wide[tile, pl.ds(at * piece + j, step_wins, stride=pitch), :] = row[
                                :, tile * LANES : (tile + 1) * LANES
                            ]
                    return carry

                lax.fori_loop(0, piece // batch, move, 0)

            def pack(w, carry):
                blocks = [
                    wide[tile, pl.ds(w * pitch, len(used) * piece), :].astype(jnp.bfloat16) for tile in range(tiles)
                ]
                for out_ref, kind in zip(out_refs, kinds):
                    first = used.index(kind[0]) * piece
                    for tile, block in enumerate(blocks):
                        out_ref[first_win + w, :, tile * LANES : (tile + 1) * LANES] = block[
                            first : first + len(kind) * piece
                        ]
                return carry

            lax.fori_loop(0, step_wins, pack, 0, unroll=2)
            return carry

        lax.fori_loop(0, wins // step_wins, some_windows, 0)

    return kernel_call(
        kernel,
        "order_rows",
        0,
        3 * traces.size * 2,
        out_shape=[jax.ShapeDtypeStruct((wins, len(kind) * piece, samples), jnp.bfloat16) for kind in kinds],
        in_specs=[pl.BlockSpec(memory_space=pltpu.SMEM), in_vmem()],
        out_specs=[in_vmem()] * len(kinds),
        scratch_shapes=[pltpu.VMEM((tiles, (step_wins + 1) * pitch, LANES), jnp.float32)],
    )(slots, traces)


def diagonal(values, copies):
    blank = jnp.zeros_like(values)
    rows = [[values if at == copy else blank for at in range(copies)] for copy in range(copies)]
    return jnp.concatenate([jnp.concatenate(row, axis=1) for row in rows], axis=0)


def spectra(rows_j, rows_i, tables):
    wins, given, samples = rows_j.shape
    bins = samples // 2
    pairs = wins // 2
    depth = 2 * wins
    folded = HALF // given
    line = depth // folded
    pitch = line + 1
    per_step = 2 * folded
    batch = 8

    def kernel(j_ref, i_ref, table_ref, to_i_ref, to_j_ref, i_out, j_out, wide):
        same = lax.axis_index("sub") == lax.axis_index("rep")

        def spectrum_of(group):
            stacked = []
            for win in [per_step * group + u for u in range(per_step)]:
                here = j_ref[win]
                stacked += [here, jnp.where(same, here, i_ref[win])]
            wave = jnp.concatenate(stacked, axis=0)
            return lax.dot_general(table_ref[...], wave, NT, preferred_element_type=jnp.float32)

        def keep(group, spectrum):
            energy = jnp.sum(spectrum * spectrum, axis=0, keepdims=True) / bins
            white = spectrum * lax.rsqrt(energy + 1e-05)
            for half in range(2):
                for part in range(2):
                    if folded == 1:
                        row = half * wins + part * pairs + group
                    else:
                        row = part * pairs + 2 * group + half
                    wide[pl.ds(row, bins, stride=pitch), :] = white[
                        part * bins : (part + 1) * bins, half * LANES : (half + 1) * LANES
                    ]

        groups = wins // per_step
        at_once = 4

        def some_windows(step, carry):
            first = step * at_once
            last = spectrum_of(first)
            for group in range(1, at_once):
                now = spectrum_of(first + group)
                keep(first + group - 1, last)
                last = now
            keep(first + at_once - 1, last)
            return carry

        lax.fori_loop(0, groups // at_once, some_windows, 0)

        def moved(fs):
            loaded = [wide[pl.ds(f * pitch, line), :].astype(jnp.bfloat16) for f in fs]
            i_rows = [
                lax.dot_general(to_i_ref[...], diagonal(values, 2), NT, preferred_element_type=jnp.float32)
                for values in loaded
            ]
            if folded == 2:
                i_rows = [jnp.concatenate([rows[: given // 2], rows[given // 2 :]], axis=1) for rows in i_rows]
            j_rows = jnp.dot(jnp.concatenate(loaded, axis=0), to_j_ref[...], preferred_element_type=jnp.float32)
            return fs, i_rows, j_rows

        def store(fs, i_rows, j_rows):
            for at, f in enumerate(fs):
                i_out[f] = i_rows[at].astype(jnp.bfloat16)
                for odd in range(folded):
                    j_out[f, odd * line : (odd + 1) * line] = j_rows[
                        at * line : (at + 1) * line, odd * LANES : (odd + 1) * LANES
                    ].astype(jnp.bfloat16)

        def pack(group, carry):
            first = group * 4 * batch
            waiting = moved([first + u for u in range(batch)])
            for at in range(1, 4):
                following = moved([first + at * batch + u for u in range(batch)])
                store(*waiting)
                waiting = following
            store(*waiting)
            return carry

        lax.fori_loop(0, bins // (4 * batch), pack, 0)

    shapes = [(bins, given // 2, LANES), (bins, depth, LANES)]
    return kernel_call(
        kernel,
        "spectra",
        4 * samples * samples * wins * given,
        4 * wins * given * samples * 2,
        out_shape=[jax.ShapeDtypeStruct(shape, jnp.bfloat16) for shape in shapes],
        in_specs=[in_vmem()] * (2 + len(tables)),
        out_specs=[in_vmem()] * len(shapes),
        scratch_shapes=[pltpu.VMEM(((bins + 1) * pitch, LANES), jnp.float32)],
    )(rows_j, rows_i, *tables)


def partial_correlations(lefts, rights, tables, jobs, outs):
    left_arrays = [array for array, _ in lefts]
    right_arrays = [array for array, _, _ in rights]
    bins, depth, _ = right_arrays[0].shape
    piece = HALF // BLOCKS
    pitch = bins + 1
    step_bins = 32
    groups = []
    slices = {}
    for used, groups_here in jobs:
        js = [(rights[right][1], there) for right in used for there in rights[right][2]]
        for left, _, first in groups_here:
            found = []
            for offset in range(2):
                at = first + offset
                for order, (j_other, there) in enumerate(js):
                    if there != at:
                        kind = (lefts[left][1], j_other, there ^ (at % 2))
                        found.append((at, kind, offset * HALF + order * piece))
                        slices.setdefault(at, []).append(kind)
            groups.append(found)
    for kinds in slices.values():
        kinds.sort()
    total = len(groups) * piece
    batch = 4

    def first_of(at):
        (out,) = [positions for positions in outs if at in positions]
        return outs.index(out), sum(len(slices[before]) for before in out[: out.index(at)])

    def kernel(*refs):
        left_refs, rest = refs[: len(lefts)], refs[len(lefts) :]
        right_refs, rest = rest[: len(rights)], rest[len(rights) :]
        lag_ref, same_ref, out_refs, cross = rest[0], rest[1], rest[2:-1], rest[-1]
        lanes = lax.broadcasted_iota(jnp.int32, (depth, LANES), 1)

        def mask(wanted):
            return wanted.astype(jnp.float32).astype(jnp.bfloat16)

        halves = [mask(lanes // HALF == at) for at in range(2)]
        lower = mask(lanes % HALF < HALF // 2)
        upper = mask(lanes % HALF >= HALF // 2)

        def turn(values):
            swapped = []
            for first in range(0, depth, depth // 2):
                middle, last = first + depth // 4, first + depth // 2
                swapped += [-values[middle:last], values[first:middle]]
            return jnp.concatenate(swapped, axis=0)

        def right_hand(used, f):
            values = right_refs[used[0]][f]
            if len(used) == 2:
                values = values * lower + right_refs[used[1]][f] * upper
            turned = turn(values)
            return jnp.concatenate(
                [jnp.concatenate([values * here, turned * here], axis=1) for here in halves], axis=0
            )

        def products(first_bin, count):
            found = []
            for f in [first_bin + u for u in range(count)]:
                first = 0
                for used, groups_here in jobs:
                    lhs = [left_refs[left][f, row : row + piece] for left, row, _ in groups_here]
                    lhs = jnp.concatenate(lhs, axis=0) if len(lhs) > 1 else lhs[0]
                    product = jnp.dot(lhs, right_hand(used, f), preferred_element_type=jnp.float32)
                    found.append((first * pitch + f, product))
                    first += lhs.shape[0]
            return found

        def keep(found):
            for here, product in found:
                for part in range(2):
                    cross[pl.ds(part * total * pitch + here, product.shape[0], stride=pitch), :] = product[
                        :, part * LANES : (part + 1) * LANES
                    ]

        def some_bins(step, carry):
            first = step * step_bins
            waiting = products(first, batch)
            for at in range(batch, step_bins, batch):
                following = products(first + at, batch)
                keep(waiting)
                waiting = following
            keep(waiting)
            return carry

        lax.fori_loop(0, bins // step_bins, some_bins, 0)

        for index, found in enumerate(groups):
            targets = []
            for at, kind, lane in found:
                out, first = first_of(at)
                targets.append((out_refs[out], first + slices[at].index(kind), lane))

            def summed(i):
                parts = []
                for part in range(2):
                    start = (part * total + index * piece + i) * pitch
                    parts.append(
                        jnp.concatenate([cross[pl.ds(start, bins), :], cross[pl.ds(start + pitch, bins), :]], axis=1)
                    )
                values = jnp.concatenate(parts, axis=0).astype(jnp.bfloat16)
                return i, jnp.dot(lag_ref[...], values, preferred_element_type=jnp.float32)

            def across(i, lagged):
                lagged = lagged.astype(jnp.bfloat16)
                return i, lax.dot_general(same_ref[...], lagged, NT, preferred_element_type=jnp.float32)

            def store(i, rows):
                for half in range(2):
                    for out, place, lane in targets:
                        row = half * LANES + lane
                        out[place, i + half] = rows[row : row + piece].astype(out.dtype)

            sums, rows = summed(0), None
            for i in range(2, piece, 2):
                more = summed(i)
                if rows is not None:
                    store(*rows)
                rows = across(*sums)
                sums = more
            store(*rows)
            store(*across(*sums))

    shapes = [(sum(len(slices[at]) for at in positions), piece, piece, LAGS) for positions in outs]
    types = [jnp.float32 if positions == (OWN_AT,) else jnp.bfloat16 for positions in outs]
    results = kernel_call(
        kernel,
        "partial_correlations",
        4 * total * bins * depth * LANES + 4 * total * bins * LANES * LAGS,
        2 * sum(array.size for array in left_arrays + right_arrays),
        out_shape=[jax.ShapeDtypeStruct(shape, kind) for shape, kind in zip(shapes, types)],
        in_specs=[in_vmem()] * (len(lefts) + len(rights) + len(tables)),
        out_specs=[in_vmem()] * len(shapes),
        scratch_shapes=[pltpu.VMEM(((2 * total + 1) * pitch, LANES), jnp.float32)],
    )(*left_arrays, *right_arrays, *tables)
    return results, slices


def assembled(shares):
    arrays = [array for array, _ in shares]
    _, piece, _, lags = arrays[0].shape
    width = 2 * piece

    def kernel(*refs):
        out, held, sems = refs[-3:]
        sub = lax.axis_index("sub")
        odd = lax.rem(lax.axis_index("chan"), 2)
        copies = []
        for there, round_at in ((0, 1), (1, 2 - 2 * odd), (3, 2 * odd)):
            for i_other in range(2):
                for j_other in range(2):
                    parts = [
                        refs[at][place].astype(jnp.float32)
                        for at, (_, kinds) in enumerate(shares)
                        for place, kind in enumerate(kinds)
                        if kind == (i_other, j_other, there)
                    ]
                    i_first = jnp.where(sub == 0, i_other, 1 - i_other) * piece
                    j_first = pl.multiple_of(jnp.where(sub == 0, j_other, 1 - j_other) * piece, piece)
                    held[round_at, 0, pl.ds(i_first, piece), pl.ds(j_first, piece), :] = functools.reduce(
                        jnp.add, parts
                    )
            at = len(copies)
            copies.append(pltpu.make_async_copy(held.at[round_at], out.at[round_at], sems.at[at]))
            copies[-1].start()
        for copy in copies:
            copy.wait()

    shape = (ROUNDS, 1, width, width, lags)
    return kernel_call(
        kernel,
        "assembled",
        0,
        sum(array.size for array in arrays) * 2,
        out_shape=jax.ShapeDtypeStruct(shape, jnp.float32),
        in_specs=[in_vmem()] * len(arrays),
        out_specs=pl.BlockSpec(memory_space=pl.ANY),
        scratch_shapes=[pltpu.VMEM(shape, jnp.float32), pltpu.SemaphoreType.DMA((ROUNDS,))],
    )(*arrays)


def summed_in_place(traces, channel_slot):
    chan_count = lax.axis_size("chan")
    _, win_here, samples = traces.shape
    piece = HALF // BLOCKS
    scale = (2.0 / (win_here * chan_count * (samples // 2))) ** 0.5
    dft_rows = dft_rows_table(samples)
    same = selection(2 * LANES, 2 * LANES, [(n, n) for n in range(2 * LANES)])
    tables = [lag_rows_table(samples, scale), same]
    everywhere = tuple(range(BLOCKS))

    def over_sub(rows):
        return lax.ppermute(rows, "sub", [(0, 1), (1, 0)])

    def over_core(rows):
        return lax.ppermute(rows, ("sub", "rep"), [(0, 1), (3, 2)])

    def with_device(share, apart):
        return lax.ppermute(share, "chan", [(z, z ^ apart) for z in range(chan_count)])

    def after(value, *others):
        return lax.optimization_barrier((value,) + others)[0]

    def added(share, arrived):
        return (share.astype(jnp.float32) + arrived.astype(jnp.float32)).astype(jnp.bfloat16)

    def for_two_away(kinds):
        return [(i_other, j_other, there ^ 2) for i_other, j_other, there in kinds]

    mine, mine_far, mine_near = order_rows(traces, channel_slot, [everywhere, FAR, NEAR])
    far = over_sub(mine_far)
    near = over_sub(mine_near)

    own_i, own_j = spectra(mine, over_core(mine), (dft_rows, *own_picks()))
    own_left, own_right = (own_i, 0), (own_j, 0, everywhere)
    own_far, own_near = (0, 0, FAR[0]), (0, piece, NEAR[0])
    (kept_1, own_1, sent_1), kinds_1 = partial_correlations(
        [own_left], [own_right], tables, [((0,), [own_far, own_near])], [(0,), (2,), (1, 3)]
    )
    arrived_1 = with_device(sent_1, 1)

    far = after(far, kept_1, own_1, sent_1)
    far_i, far_j = spectra(far, over_core(far), (dft_rows, *half_picks()))
    far_count_1 = kept_1.shape[0]
    summed_1 = added(after(kept_1, far_i), arrived_1[:far_count_1])
    far_1 = with_device(summed_1, 2)
    far_left, far_right = (after(far_i, summed_1), 1), (far_j, 1, FAR)
    other_far = (1, 0, FAR[0])
    (kept_2, own_2, sent_2), kinds_2 = partial_correlations(
        [own_left, far_left],
        [own_right, far_right],
        tables,
        [((0,), [other_far]), ((1,), [own_far, own_near, other_far])],
        [(0,), (2,), (1, 3)],
    )
    arrived_2 = with_device(sent_2, 1)
    far_count_2 = kept_2.shape[0]

    near = after(near, kept_2, own_2, sent_2, far_1)
    near_i, near_j = spectra(near, over_core(near), (dft_rows, *half_picks()))
    near_left, near_right = (near_i, 1), (near_j, 1, NEAR)
    other_near = (1, 0, NEAR[0])
    (kept_3, sent_3), kinds_3 = partial_correlations(
        [own_left, far_left], [near_right], tables, [((0,), [own_far, other_far])], [(0,), (1,)]
    )
    arrived_3 = with_device(sent_3, 1)
    summed_2 = added(kept_2, arrived_2[:far_count_2])
    far_2 = with_device(summed_2, 2)
    near_j = after(near_j, kept_3, sent_3, summed_2)
    near_right = (near_j, 1, NEAR)
    (own_4, sent_4), kinds_4 = partial_correlations(
        [own_left, near_left],
        [own_right, far_right, near_right],
        tables,
        [((0,), [other_near]), ((1, 2), [other_near]), ((2,), [own_near])],
        [(2,), (3,)],
    )
    far_3 = with_device(added(kept_3, arrived_3), 2)
    arrived_4 = with_device(sent_4, 1)
    shares = [
        (own_1, kinds_1[2]),
        (own_2, kinds_2[2]),
        (own_4, kinds_4[2]),
        (arrived_1, [None] * far_count_1 + kinds_1[3]),
        (arrived_2, [None] * far_count_2 + kinds_2[3]),
        (arrived_4, kinds_4[3]),
        (far_1, for_two_away(kinds_1[0])),
        (far_2, for_two_away(kinds_2[0])),
        (far_3, for_two_away(kinds_3[0])),
    ]
    return assembled(shares)


def from_behind(shard, axis, by):
    count = lax.axis_size(axis)
    return lax.ppermute(shard, axis, [(i, (i + by) % count) for i in range(count)])


def dft_columns(samples, parts, sub_bins):
    shape = (samples, parts, 2, sub_bins)
    time_pos = lax.broadcasted_iota(jnp.int32, shape, 0)
    range_pos = lax.broadcasted_iota(jnp.int32, shape, 1)
    part_pos = lax.broadcasted_iota(jnp.int32, shape, 2)
    bin_pos = lax.broadcasted_iota(jnp.int32, shape, 3)
    frequency = range_pos * sub_bins + bin_pos
    angles = jnp.mod(time_pos * frequency, samples).astype(jnp.float32) * (2.0 * math.pi / samples)
    entries = jnp.where(part_pos == 0, jnp.cos(angles), -jnp.sin(angles))
    return entries.reshape(samples, parts * 2 * sub_bins).astype(jnp.bfloat16)


def lag_table(sub_bins, first_bin, lag_count, samples):
    frequency = first_bin + lax.broadcasted_iota(jnp.int32, (sub_bins, lag_count), 0)
    lag_offset = lax.broadcasted_iota(jnp.int32, (sub_bins, lag_count), 1) - lag_count // 2
    angles = jnp.mod(frequency * lag_offset, samples).astype(jnp.float32) * (2.0 * math.pi / samples)
    return jnp.stack([jnp.cos(angles), -jnp.sin(angles)], axis=1)


def moved_spectra(traces, channel_slot):
    chan_count = lax.axis_size("chan")
    sub_count = lax.axis_size("sub")
    group_rows, win_here, samples = traces.shape
    bin_count = samples // 2
    sub_bins = bin_count // sub_count
    bin_width = 2 * sub_bins
    piece_len = group_rows // chan_count
    picked = jnp.take(traces, channel_slot, axis=0)
    dft_rows = dft_columns(samples, sub_count, sub_bins)
    spectrum = jnp.dot(picked.reshape(-1, samples), dft_rows, preferred_element_type=jnp.float32)
    energy = jnp.sum(spectrum * spectrum, axis=1, keepdims=True) / bin_count
    whitened = (spectrum * lax.rsqrt(energy + 1e-05)).astype(jnp.bfloat16)
    whitened = whitened.reshape(chan_count, piece_len, win_here, sub_count, bin_width)
    regrouped = lax.all_to_all(whitened, "chan", split_axis=0, concat_axis=0, tiled=True)
    regrouped = lax.all_to_all(regrouped, "sub", split_axis=3, concat_axis=3, tiled=True)
    own_half = regrouped.transpose(3, 1, 0, 2, 4).reshape(sub_count * piece_len, chan_count * win_here, bin_width)
    own_block = lax.all_gather(own_half, "rep", axis=0, tiled=True)
    windows = own_block.shape[1]
    own_split = own_block.reshape(own_block.shape[0], windows, 2, sub_bins)
    lag_rows = lag_table(sub_bins, lax.axis_index("sub") * sub_bins, LAGS, samples)
    lag_scale = (2.0 / (windows * bin_count)) ** 0.5
    results = []
    for step in range(1, ROUNDS + 1):
        partner = from_behind(own_half, "chan", -step)
        partner_split = partner.reshape(partner.shape[0], windows, 2, sub_bins)
        turned = jnp.stack([-partner_split[:, :, 1], partner_split[:, :, 0]], axis=2)
        partner_pair = jnp.stack([partner_split, turned], axis=0)
        cross_spec = jnp.einsum("iwpf,qjwpf->fqij", own_split, partner_pair, preferred_element_type=jnp.float32)
        summed = jnp.einsum("fqij,fql->ijl", cross_spec, lag_rows, precision=lax.Precision.HIGHEST)
        results.append(lax.psum_scatter(lag_scale * summed, "sub", scatter_dimension=0, tiled=True))
    return jnp.stack(results)[:, None]


def solution(mesh):
    sizes = mesh.shape
    in_place = sizes["chan"] == BLOCKS == ROUNDS + 1 and sizes["sub"] == 2 and sizes["rep"] == 2
    return jax.shard_map(
        summed_in_place if in_place else moved_spectra,
        mesh=mesh,
        in_specs=(P(("groups", "sub", "rep"), "chan", None), P(("groups", "sub", "rep"))),
        out_specs=P(None, ("groups", "chan"), "sub", "rep", None),
        check_vma=False,
    )
```

```python
import functools
import math

import jax
import jax.numpy as jnp
import numpy as np
from jax import lax
from jax.experimental import pallas as pl
from jax.experimental.pallas import tpu as pltpu
from jax.sharding import PartitionSpec as P

LAGS = 128
ROUNDS = 3
LANES = 128
HALF = LANES // 2
VMEM_BYTES = 32 * 1024 * 1024
NT = (((1,), (1,)), ((), ()))
BLOCKS = 4
FAR = (0, 1)
NEAR = (2, 3)
KEPT_AT, OWN_AT = 0, 2


def kernel_call(kernel, name, flops, bytes_accessed, **more):
    return pl.pallas_call(
        kernel,
        name=name,
        compiler_params=pltpu.CompilerParams(vmem_limit_bytes=VMEM_BYTES),
        cost_estimate=pl.CostEstimate(flops=flops, bytes_accessed=bytes_accessed, transcendentals=0),
        **more,
    )


def in_vmem():
    return pl.BlockSpec(memory_space=pltpu.VMEM)


def dft_rows_table(samples):
    bins = samples // 2
    turns = (np.arange(bins)[:, None] * np.arange(samples)[None, :]) % samples
    angles = turns.astype(np.float32) * np.float32(2.0 * math.pi / samples)
    table = np.concatenate([np.cos(angles), -np.sin(angles)], axis=0)
    return jnp.asarray(table.astype(np.float32)).astype(jnp.bfloat16)


def lag_rows_table(samples, scale):
    bins = samples // 2
    offsets = np.arange(LAGS) - LAGS // 2
    turns = (offsets[:, None] * np.arange(bins)[None, :]) % samples
    angles = turns.astype(np.float32) * np.float32(2.0 * math.pi / samples)
    table = np.concatenate([np.cos(angles), -np.sin(angles)], axis=1) * np.float32(scale)
    return jnp.asarray(table.astype(np.float32)).astype(jnp.bfloat16)


def selection(rows, columns, ones):
    table = np.zeros((rows, columns), np.float32)
    for row, column in ones:
        table[row, column] = 1.0
    return jnp.asarray(table).astype(jnp.bfloat16)


def own_picks():
    piece = HALF // BLOCKS
    to_i = []
    for at in range(BLOCKS):
        for n in range(piece):
            to_i.append((at // 2 * piece + n, at % 2 * LANES + HALF + at * piece + n))
    to_j = [(j, copy * HALF + j) for j in range(HALF) for copy in range(2)]
    return selection(2 * piece, 2 * LANES, to_i), selection(LANES, LANES, to_j)


def half_picks():
    count = HALF // 2
    to_i, to_j = [], []
    for odd in range(2):
        for n in range(count):
            to_i.append((n, odd * LANES + odd * HALF + count + n))
            to_j += [(odd * HALF + n, odd * LANES + copy * count + n) for copy in range(4)]
    return selection(count, 2 * LANES, to_i), selection(LANES, 2 * LANES, to_j)


def order_rows(traces, slots, kinds):
    rows, wins, samples = traces.shape
    tiles = samples // LANES
    piece = rows // BLOCKS
    step_wins = 16
    batch = 4
    used = max(kinds, key=len)
    pitch = len(used) * piece + 1

    def kernel(slot_ref, in_ref, *refs):
        out_refs, wide = refs[:-1], refs[-1]
        z = lax.axis_index("chan")
        odd = lax.rem(z, 2)
        pair = jnp.where(z < 2, 2, 0)

        def some_windows(step, carry):
            first_win = pl.multiple_of(step * step_wins, step_wins)
            for at, position in enumerate(used):
                block = pair + position + (odd if position % 2 == 0 else -odd)
                first = lax.rem(block, BLOCKS) * piece

                def move(group, carry, at=at, first=first):
                    js = [group * batch + u for u in range(batch)]
                    picked = [
                        in_ref[slot_ref[first + j], pl.ds(first_win, step_wins), :].astype(jnp.float32) for j in js
                    ]
                    for j, row in zip(js, picked):
                        for tile in range(tiles):
                            wide[tile, pl.ds(at * piece + j, step_wins, stride=pitch), :] = row[
                                :, tile * LANES : (tile + 1) * LANES
                            ]
                    return carry

                lax.fori_loop(0, piece // batch, move, 0)

            def pack(w, carry):
                blocks = [
                    wide[tile, pl.ds(w * pitch, len(used) * piece), :].astype(jnp.bfloat16) for tile in range(tiles)
                ]
                for out_ref, kind in zip(out_refs, kinds):
                    first = used.index(kind[0]) * piece
                    for tile, block in enumerate(blocks):
                        out_ref[first_win + w, :, tile * LANES : (tile + 1) * LANES] = block[
                            first : first + len(kind) * piece
                        ]
                return carry

            lax.fori_loop(0, step_wins, pack, 0, unroll=2)
            return carry

        lax.fori_loop(0, wins // step_wins, some_windows, 0)

    return kernel_call(
        kernel,
        "order_rows",
        0,
        3 * traces.size * 2,
        out_shape=[jax.ShapeDtypeStruct((wins, len(kind) * piece, samples), jnp.bfloat16) for kind in kinds],
        in_specs=[pl.BlockSpec(memory_space=pltpu.SMEM), in_vmem()],
        out_specs=[in_vmem()] * len(kinds),
        scratch_shapes=[pltpu.VMEM((tiles, (step_wins + 1) * pitch, LANES), jnp.float32)],
    )(slots, traces)


def diagonal(values, copies):
    blank = jnp.zeros_like(values)
    rows = [[values if at == copy else blank for at in range(copies)] for copy in range(copies)]
    return jnp.concatenate([jnp.concatenate(row, axis=1) for row in rows], axis=0)


def spectra(rows_j, rows_i, tables):
    wins, given, samples = rows_j.shape
    bins = samples // 2
    pairs = wins // 2
    depth = 2 * wins
    folded = HALF // given
    line = depth // folded
    pitch = line + 1
    per_step = 2 * folded
    batch = 8

    def kernel(j_ref, i_ref, table_ref, to_i_ref, to_j_ref, i_out, j_out, wide):
        same = lax.axis_index("sub") == lax.axis_index("rep")

        def spectrum_of(group):
            stacked = []
            for win in [per_step * group + u for u in range(per_step)]:
                here = j_ref[win]
                stacked += [here, jnp.where(same, here, i_ref[win])]
            wave = jnp.concatenate(stacked, axis=0)
            return lax.dot_general(table_ref[...], wave, NT, preferred_element_type=jnp.float32)

        def keep(group, spectrum):
            energy = jnp.sum(spectrum * spectrum, axis=0, keepdims=True) / bins
            white = spectrum * lax.rsqrt(energy + 1e-05)
            for half in range(2):
                for part in range(2):
                    if folded == 1:
                        row = half * wins + part * pairs + group
                    else:
                        row = part * pairs + 2 * group + half
                    wide[pl.ds(row, bins, stride=pitch), :] = white[
                        part * bins : (part + 1) * bins, half * LANES : (half + 1) * LANES
                    ]

        groups = wins // per_step
        at_once = 4

        def some_windows(step, carry):
            first = step * at_once
            last = spectrum_of(first)
            for group in range(1, at_once):
                now = spectrum_of(first + group)
                keep(first + group - 1, last)
                last = now
            keep(first + at_once - 1, last)
            return carry

        lax.fori_loop(0, groups // at_once, some_windows, 0)

        def moved(fs):
            loaded = [wide[pl.ds(f * pitch, line), :].astype(jnp.bfloat16) for f in fs]
            i_rows = [
                lax.dot_general(to_i_ref[...], diagonal(values, 2), NT, preferred_element_type=jnp.float32)
                for values in loaded
            ]
            if folded == 2:
                i_rows = [jnp.concatenate([rows[: given // 2], rows[given // 2 :]], axis=1) for rows in i_rows]
            j_rows = jnp.dot(jnp.concatenate(loaded, axis=0), to_j_ref[...], preferred_element_type=jnp.float32)
            return fs, i_rows, j_rows

        def store(fs, i_rows, j_rows):
            for at, f in enumerate(fs):
                i_out[f] = i_rows[at].astype(jnp.bfloat16)
                for odd in range(folded):
                    j_out[f, odd * line : (odd + 1) * line] = j_rows[
                        at * line : (at + 1) * line, odd * LANES : (odd + 1) * LANES
                    ].astype(jnp.bfloat16)

        def pack(group, carry):
            first = group * 4 * batch
            waiting = moved([first + u for u in range(batch)])
            for at in range(1, 4):
                following = moved([first + at * batch + u for u in range(batch)])
                store(*waiting)
                waiting = following
            store(*waiting)
            return carry

        lax.fori_loop(0, bins // (4 * batch), pack, 0)

    shapes = [(bins, given // 2, LANES), (bins, depth, LANES)]
    return kernel_call(
        kernel,
        "spectra",
        4 * samples * samples * wins * given,
        4 * wins * given * samples * 2,
        out_shape=[jax.ShapeDtypeStruct(shape, jnp.bfloat16) for shape in shapes],
        in_specs=[in_vmem()] * (2 + len(tables)),
        out_specs=[in_vmem()] * len(shapes),
        scratch_shapes=[pltpu.VMEM(((bins + 1) * pitch, LANES), jnp.float32)],
    )(rows_j, rows_i, *tables)


def partial_correlations(lefts, rights, tables, jobs, outs):
    left_arrays = [array for array, _ in lefts]
    right_arrays = [array for array, _, _ in rights]
    bins, depth, _ = right_arrays[0].shape
    piece = HALF // BLOCKS
    pitch = bins + 1
    step_bins = 32
    groups = []
    slices = {}
    for used, groups_here in jobs:
        js = [(rights[right][1], there) for right in used for there in rights[right][2]]
        for left, _, first in groups_here:
            found = []
            for offset in range(2):
                at = first + offset
                for order, (j_other, there) in enumerate(js):
                    if there != at:
                        kind = (lefts[left][1], j_other, there ^ (at % 2))
                        found.append((at, kind, offset * HALF + order * piece))
                        slices.setdefault(at, []).append(kind)
            groups.append(found)
    for kinds in slices.values():
        kinds.sort()
    total = len(groups) * piece
    batch = 4

    def first_of(at):
        (out,) = [positions for positions in outs if at in positions]
        return outs.index(out), sum(len(slices[before]) for before in out[: out.index(at)])

    def kernel(*refs):
        left_refs, rest = refs[: len(lefts)], refs[len(lefts) :]
        right_refs, rest = rest[: len(rights)], rest[len(rights) :]
        lag_ref, same_ref, out_refs, cross = rest[0], rest[1], rest[2:-1], rest[-1]
        lanes = lax.broadcasted_iota(jnp.int32, (depth, LANES), 1)

        def mask(wanted):
            return wanted.astype(jnp.float32).astype(jnp.bfloat16)

        halves = [mask(lanes // HALF == at) for at in range(2)]
        lower = mask(lanes % HALF < HALF // 2)
        upper = mask(lanes % HALF >= HALF // 2)

        def turn(values):
            swapped = []
            for first in range(0, depth, depth // 2):
                middle, last = first + depth // 4, first + depth // 2
                swapped += [-values[middle:last], values[first:middle]]
            return jnp.concatenate(swapped, axis=0)

        def right_hand(used, f):
            values = right_refs[used[0]][f]
            if len(used) == 2:
                values = values * lower + right_refs[used[1]][f] * upper
            turned = turn(values)
            return jnp.concatenate(
                [jnp.concatenate([values * here, turned * here], axis=1) for here in halves], axis=0
            )

        def products(first_bin, count):
            found = []
            for f in [first_bin + u for u in range(count)]:
                first = 0
                for used, groups_here in jobs:
                    lhs = [left_refs[left][f, row : row + piece] for left, row, _ in groups_here]
                    lhs = jnp.concatenate(lhs, axis=0) if len(lhs) > 1 else lhs[0]
                    product = jnp.dot(lhs, right_hand(used, f), preferred_element_type=jnp.float32)
                    found.append((first * pitch + f, product))
                    first += lhs.shape[0]
            return found

        def keep(found):
            for here, product in found:
                for part in range(2):
                    cross[pl.ds(part * total * pitch + here, product.shape[0], stride=pitch), :] = product[
                        :, part * LANES : (part + 1) * LANES
                    ]

        def some_bins(step, carry):
            first = step * step_bins
            waiting = products(first, batch)
            for at in range(batch, step_bins, batch):
                following = products(first + at, batch)
                keep(waiting)
                waiting = following
            keep(waiting)
            return carry

        lax.fori_loop(0, bins // step_bins, some_bins, 0)

        for index, found in enumerate(groups):
            targets = []
            for at, kind, lane in found:
                out, first = first_of(at)
                targets.append((out_refs[out], first + slices[at].index(kind), lane))

            def summed(i):
                parts = []
                for part in range(2):
                    start = (part * total + index * piece + i) * pitch
                    parts.append(
                        jnp.concatenate([cross[pl.ds(start, bins), :], cross[pl.ds(start + pitch, bins), :]], axis=1)
                    )
                values = jnp.concatenate(parts, axis=0).astype(jnp.bfloat16)
                return i, jnp.dot(lag_ref[...], values, preferred_element_type=jnp.float32)

            def across(i, lagged):
                lagged = lagged.astype(jnp.bfloat16)
                return i, lax.dot_general(same_ref[...], lagged, NT, preferred_element_type=jnp.float32)

            def store(i, rows):
                for half in range(2):
                    for out, place, lane in targets:
                        row = half * LANES + lane
                        out[place, i + half] = rows[row : row + piece].astype(out.dtype)

            sums, rows = summed(0), None
            for i in range(2, piece, 2):
                more = summed(i)
                if rows is not None:
                    store(*rows)
                rows = across(*sums)
                sums = more
            store(*rows)
            store(*across(*sums))

    shapes = [(sum(len(slices[at]) for at in positions), piece, piece, LAGS) for positions in outs]
    types = [jnp.float32 if positions == (OWN_AT,) else jnp.bfloat16 for positions in outs]
    results = kernel_call(
        kernel,
        "partial_correlations",
        4 * total * bins * depth * LANES + 4 * total * bins * LANES * LAGS,
        2 * sum(array.size for array in left_arrays + right_arrays),
        out_shape=[jax.ShapeDtypeStruct(shape, kind) for shape, kind in zip(shapes, types)],
        in_specs=[in_vmem()] * (len(lefts) + len(rights) + len(tables)),
        out_specs=[in_vmem()] * len(shapes),
        scratch_shapes=[pltpu.VMEM(((2 * total + 1) * pitch, LANES), jnp.float32)],
    )(*left_arrays, *right_arrays, *tables)
    return results, slices


def assembled(shares):
    arrays = [array for array, _ in shares]
    _, piece, _, lags = arrays[0].shape
    width = 2 * piece

    def kernel(*refs):
        out, held, sems = refs[-3:]
        sub = lax.axis_index("sub")
        odd = lax.rem(lax.axis_index("chan"), 2)
        copies = []
        for there, round_at in ((0, 1), (1, 2 - 2 * odd), (3, 2 * odd)):
            for i_other in range(2):
                for j_other in range(2):
                    parts = [
                        refs[at][place].astype(jnp.float32)
                        for at, (_, kinds) in enumerate(shares)
                        for place, kind in enumerate(kinds)
                        if kind == (i_other, j_other, there)
                    ]
                    i_first = jnp.where(sub == 0, i_other, 1 - i_other) * piece
                    j_first = pl.multiple_of(jnp.where(sub == 0, j_other, 1 - j_other) * piece, piece)
                    held[round_at, 0, pl.ds(i_first, piece), pl.ds(j_first, piece), :] = functools.reduce(
                        jnp.add, parts
                    )
            at = len(copies)
            copies.append(pltpu.make_async_copy(held.at[round_at], out.at[round_at], sems.at[at]))
            copies[-1].start()
        for copy in copies:
            copy.wait()

    shape = (ROUNDS, 1, width, width, lags)
    return kernel_call(
        kernel,
        "assembled",
        0,
        sum(array.size for array in arrays) * 2,
        out_shape=jax.ShapeDtypeStruct(shape, jnp.float32),
        in_specs=[in_vmem()] * len(arrays),
        out_specs=pl.BlockSpec(memory_space=pl.ANY),
        scratch_shapes=[pltpu.VMEM(shape, jnp.float32), pltpu.SemaphoreType.DMA((ROUNDS,))],
    )(*arrays)


def summed_in_place(traces, channel_slot):
    chan_count = lax.axis_size("chan")
    _, win_here, samples = traces.shape
    piece = HALF // BLOCKS
    scale = (2.0 / (win_here * chan_count * (samples // 2))) ** 0.5
    dft_rows = dft_rows_table(samples)
    same = selection(2 * LANES, 2 * LANES, [(n, n) for n in range(2 * LANES)])
    tables = [lag_rows_table(samples, scale), same]
    everywhere = tuple(range(BLOCKS))

    def over_sub(rows):
        return lax.ppermute(rows, "sub", [(0, 1), (1, 0)])

    def over_core(rows):
        return lax.ppermute(rows, ("sub", "rep"), [(0, 1), (3, 2)])

    def with_device(share, apart):
        return lax.ppermute(share, "chan", [(z, z ^ apart) for z in range(chan_count)])

    def after(value, *others):
        return lax.optimization_barrier((value,) + others)[0]

    def added(share, arrived):
        return (share.astype(jnp.float32) + arrived.astype(jnp.float32)).astype(jnp.bfloat16)

    def for_two_away(kinds):
        return [(i_other, j_other, there ^ 2) for i_other, j_other, there in kinds]

    mine, mine_far, mine_near = order_rows(traces, channel_slot, [everywhere, FAR, NEAR])
    far = over_sub(mine_far)
    near = over_sub(mine_near)

    own_i, own_j = spectra(mine, over_core(mine), (dft_rows, *own_picks()))
    own_left, own_right = (own_i, 0), (own_j, 0, everywhere)
    own_far, own_near = (0, 0, FAR[0]), (0, piece, NEAR[0])
    (kept_1, sent_far_1, own_1, sent_near_1), kinds_1 = partial_correlations(
        [own_left], [own_right], tables, [((0,), [own_far, own_near])], [(0,), (1,), (2,), (3,)]
    )
    arrived_far_1 = with_device(sent_far_1, 1)

    far = after(far, kept_1, sent_far_1, own_1, sent_near_1)
    far_i, far_j = spectra(far, over_core(far), (dft_rows, *half_picks()))
    far_i, arrived_far_1 = lax.optimization_barrier((far_i, arrived_far_1))
    far_left, far_right = (far_i, 1), (far_j, 1, FAR)
    other_far = (1, 0, FAR[0])
    (kept_2, sent_far_2, own_2, sent_near_2), kinds_2 = partial_correlations(
        [own_left, far_left],
        [own_right, far_right],
        tables,
        [((0,), [other_far]), ((1,), [own_far, own_near, other_far])],
        [(0,), (1,), (2,), (3,)],
    )
    arrived_far_2 = with_device(sent_far_2, 1)

    near, arrived_far_2 = lax.optimization_barrier((near, arrived_far_2))
    near_i, near_j = spectra(near, over_core(near), (dft_rows, *half_picks()))
    summed_2 = added(kept_2, arrived_far_2)
    far_2 = with_device(summed_2, 2)
    summed_1 = added(after(kept_1, near_j), arrived_far_1)
    far_1 = with_device(summed_1, 2)
    near_j = after(near_j, summed_2)
    near_left, near_right = (near_i, 1), (near_j, 1, NEAR)
    other_near = (1, 0, NEAR[0])
    (kept_3, sent_3), kinds_3 = partial_correlations(
        [own_left, far_left], [near_right], tables, [((0,), [own_far, other_far])], [(0,), (1,)]
    )
    arrived_3 = with_device(sent_3, 1)
    arrived_near = with_device(jnp.concatenate([sent_near_1, sent_near_2]), 1)
    near_right = (after(near_j, kept_3, sent_3, far_2, summed_1), 1, NEAR)
    (own_4, sent_4), kinds_4 = partial_correlations(
        [own_left, near_left],
        [far_right, near_right],
        tables,
        [((0, 1), [other_near]), ((1,), [own_near])],
        [(2,), (3,)],
    )
    arrived_4 = with_device(sent_4, 1)
    summed_3 = added(after(kept_3, own_4), arrived_3)
    far_3 = with_device(summed_3, 2)
    near_left = (after(near_i, own_4, sent_4, summed_3, arrived_near, far_1), 1)
    (own_5, sent_5), kinds_5 = partial_correlations(
        [near_left], [own_right], tables, [((0,), [(0, 0, NEAR[0])])], [(2,), (3,)]
    )
    arrived_5 = with_device(sent_5, 1)
    shares = [
        (own_1, kinds_1[2]),
        (own_2, kinds_2[2]),
        (own_4, kinds_4[2]),
        (own_5, kinds_5[2]),
        (arrived_near, kinds_1[3] + kinds_2[3]),
        (arrived_4, kinds_4[3]),
        (arrived_5, kinds_5[3]),
        (far_1, for_two_away(kinds_1[0])),
        (far_2, for_two_away(kinds_2[0])),
        (far_3, for_two_away(kinds_3[0])),
    ]
    return assembled(shares)


def from_behind(shard, axis, by):
    count = lax.axis_size(axis)
    return lax.ppermute(shard, axis, [(i, (i + by) % count) for i in range(count)])


def dft_columns(samples, parts, sub_bins):
    shape = (samples, parts, 2, sub_bins)
    time_pos = lax.broadcasted_iota(jnp.int32, shape, 0)
    range_pos = lax.broadcasted_iota(jnp.int32, shape, 1)
    part_pos = lax.broadcasted_iota(jnp.int32, shape, 2)
    bin_pos = lax.broadcasted_iota(jnp.int32, shape, 3)
    frequency = range_pos * sub_bins + bin_pos
    angles = jnp.mod(time_pos * frequency, samples).astype(jnp.float32) * (2.0 * math.pi / samples)
    entries = jnp.where(part_pos == 0, jnp.cos(angles), -jnp.sin(angles))
    return entries.reshape(samples, parts * 2 * sub_bins).astype(jnp.bfloat16)


def lag_table(sub_bins, first_bin, lag_count, samples):
    frequency = first_bin + lax.broadcasted_iota(jnp.int32, (sub_bins, lag_count), 0)
    lag_offset = lax.broadcasted_iota(jnp.int32, (sub_bins, lag_count), 1) - lag_count // 2
    angles = jnp.mod(frequency * lag_offset, samples).astype(jnp.float32) * (2.0 * math.pi / samples)
    return jnp.stack([jnp.cos(angles), -jnp.sin(angles)], axis=1)


def moved_spectra(traces, channel_slot):
    chan_count = lax.axis_size("chan")
    sub_count = lax.axis_size("sub")
    group_rows, win_here, samples = traces.shape
    bin_count = samples // 2
    sub_bins = bin_count // sub_count
    bin_width = 2 * sub_bins
    piece_len = group_rows // chan_count
    picked = jnp.take(traces, channel_slot, axis=0)
    dft_rows = dft_columns(samples, sub_count, sub_bins)
    spectrum = jnp.dot(picked.reshape(-1, samples), dft_rows, preferred_element_type=jnp.float32)
    energy = jnp.sum(spectrum * spectrum, axis=1, keepdims=True) / bin_count
    whitened = (spectrum * lax.rsqrt(energy + 1e-05)).astype(jnp.bfloat16)
    whitened = whitened.reshape(chan_count, piece_len, win_here, sub_count, bin_width)
    regrouped = lax.all_to_all(whitened, "chan", split_axis=0, concat_axis=0, tiled=True)
    regrouped = lax.all_to_all(regrouped, "sub", split_axis=3, concat_axis=3, tiled=True)
    own_half = regrouped.transpose(3, 1, 0, 2, 4).reshape(sub_count * piece_len, chan_count * win_here, bin_width)
    own_block = lax.all_gather(own_half, "rep", axis=0, tiled=True)
    windows = own_block.shape[1]
    own_split = own_block.reshape(own_block.shape[0], windows, 2, sub_bins)
    lag_rows = lag_table(sub_bins, lax.axis_index("sub") * sub_bins, LAGS, samples)
    lag_scale = (2.0 / (windows * bin_count)) ** 0.5
    results = []
    for step in range(1, ROUNDS + 1):
        partner = from_behind(own_half, "chan", -step)
        partner_split = partner.reshape(partner.shape[0], windows, 2, sub_bins)
        turned = jnp.stack([-partner_split[:, :, 1], partner_split[:, :, 0]], axis=2)
        partner_pair = jnp.stack([partner_split, turned], axis=0)
        cross_spec = jnp.einsum("iwpf,qjwpf->fqij", own_split, partner_pair, preferred_element_type=jnp.float32)
        summed = jnp.einsum("fqij,fql->ijl", cross_spec, lag_rows, precision=lax.Precision.HIGHEST)
        results.append(lax.psum_scatter(lag_scale * summed, "sub", scatter_dimension=0, tiled=True))
    return jnp.stack(results)[:, None]


def solution(mesh):
    sizes = mesh.shape
    in_place = sizes["chan"] == BLOCKS == ROUNDS + 1 and sizes["sub"] == 2 and sizes["rep"] == 2
    return jax.shard_map(
        summed_in_place if in_place else moved_spectra,
        mesh=mesh,
        in_specs=(P(("groups", "sub", "rep"), "chan", None), P(("groups", "sub", "rep"))),
        out_specs=P(None, ("groups", "chan"), "sub", "rep", None),
        check_vma=False,
    )
```

```python
import functools
import math

import jax
import jax.numpy as jnp
import numpy as np
from jax import lax
from jax.experimental import pallas as pl
from jax.experimental.pallas import tpu as pltpu
from jax.sharding import PartitionSpec as P

LAGS = 128
ROUNDS = 3
LANES = 128
HALF = LANES // 2
VMEM_BYTES = 32 * 1024 * 1024
NT = (((1,), (1,)), ((), ()))
BLOCKS = 4
FAR = (0, 1)
NEAR = (2, 3)
KEPT_AT, OWN_AT = 0, 2


def kernel_call(kernel, name, flops, bytes_accessed, **more):
    return pl.pallas_call(
        kernel,
        name=name,
        compiler_params=pltpu.CompilerParams(vmem_limit_bytes=VMEM_BYTES),
        cost_estimate=pl.CostEstimate(flops=flops, bytes_accessed=bytes_accessed, transcendentals=0),
        **more,
    )


def in_vmem():
    return pl.BlockSpec(memory_space=pltpu.VMEM)


def dft_rows_table(samples):
    bins = samples // 2
    turns = (np.arange(bins)[:, None] * np.arange(samples)[None, :]) % samples
    angles = turns.astype(np.float32) * np.float32(2.0 * math.pi / samples)
    table = np.concatenate([np.cos(angles), -np.sin(angles)], axis=0)
    return jnp.asarray(table.astype(np.float32)).astype(jnp.bfloat16)


def lag_rows_table(samples, scale):
    bins = samples // 2
    offsets = np.arange(LAGS) - LAGS // 2
    turns = (offsets[:, None] * np.arange(bins)[None, :]) % samples
    angles = turns.astype(np.float32) * np.float32(2.0 * math.pi / samples)
    table = np.concatenate([np.cos(angles), -np.sin(angles)], axis=1) * np.float32(scale)
    return jnp.asarray(table.astype(np.float32)).astype(jnp.bfloat16)


def selection(rows, columns, ones):
    table = np.zeros((rows, columns), np.float32)
    for row, column in ones:
        table[row, column] = 1.0
    return jnp.asarray(table).astype(jnp.bfloat16)


def own_picks():
    piece = HALF // BLOCKS
    to_i = []
    for at in range(BLOCKS):
        for n in range(piece):
            to_i.append((at // 2 * piece + n, at % 2 * LANES + HALF + at * piece + n))
    to_j = [(j, copy * HALF + j) for j in range(HALF) for copy in range(2)]
    return selection(2 * piece, 2 * LANES, to_i), selection(LANES, LANES, to_j)


def half_picks():
    count = HALF // 2
    to_i, to_j = [], []
    for odd in range(2):
        for n in range(count):
            to_i.append((n, odd * LANES + odd * HALF + count + n))
            to_j += [(odd * HALF + n, odd * LANES + copy * count + n) for copy in range(4)]
    return selection(count, 2 * LANES, to_i), selection(LANES, 2 * LANES, to_j)


def order_rows(traces, slots, kinds):
    rows, wins, samples = traces.shape
    tiles = samples // LANES
    piece = rows // BLOCKS
    step_wins = 16
    batch = 4
    used = max(kinds, key=len)
    pitch = len(used) * piece + 1

    def kernel(slot_ref, in_ref, *refs):
        out_refs, wide = refs[:-1], refs[-1]
        z = lax.axis_index("chan")
        odd = lax.rem(z, 2)
        pair = jnp.where(z < 2, 2, 0)

        def some_windows(step, carry):
            first_win = pl.multiple_of(step * step_wins, step_wins)
            for at, position in enumerate(used):
                block = pair + position + (odd if position % 2 == 0 else -odd)
                first = lax.rem(block, BLOCKS) * piece

                def move(group, carry, at=at, first=first):
                    js = [group * batch + u for u in range(batch)]
                    picked = [
                        in_ref[slot_ref[first + j], pl.ds(first_win, step_wins), :].astype(jnp.float32) for j in js
                    ]
                    for j, row in zip(js, picked):
                        for tile in range(tiles):
                            wide[tile, pl.ds(at * piece + j, step_wins, stride=pitch), :] = row[
                                :, tile * LANES : (tile + 1) * LANES
                            ]
                    return carry

                lax.fori_loop(0, piece // batch, move, 0)

            def pack(w, carry):
                blocks = [
                    wide[tile, pl.ds(w * pitch, len(used) * piece), :].astype(jnp.bfloat16) for tile in range(tiles)
                ]
                for out_ref, kind in zip(out_refs, kinds):
                    first = used.index(kind[0]) * piece
                    for tile, block in enumerate(blocks):
                        out_ref[first_win + w, :, tile * LANES : (tile + 1) * LANES] = block[
                            first : first + len(kind) * piece
                        ]
                return carry

            lax.fori_loop(0, step_wins, pack, 0, unroll=2)
            return carry

        lax.fori_loop(0, wins // step_wins, some_windows, 0)

    return kernel_call(
        kernel,
        "order_rows",
        0,
        3 * traces.size * 2,
        out_shape=[jax.ShapeDtypeStruct((wins, len(kind) * piece, samples), jnp.bfloat16) for kind in kinds],
        in_specs=[pl.BlockSpec(memory_space=pltpu.SMEM), in_vmem()],
        out_specs=[in_vmem()] * len(kinds),
        scratch_shapes=[pltpu.VMEM((tiles, (step_wins + 1) * pitch, LANES), jnp.float32)],
    )(slots, traces)


def diagonal(values, copies):
    blank = jnp.zeros_like(values)
    rows = [[values if at == copy else blank for at in range(copies)] for copy in range(copies)]
    return jnp.concatenate([jnp.concatenate(row, axis=1) for row in rows], axis=0)


def spectra(rows_j, rows_i, tables):
    wins, given, samples = rows_j.shape
    bins = samples // 2
    pairs = wins // 2
    depth = 2 * wins
    folded = HALF // given
    line = depth // folded
    pitch = line + 1
    per_step = 2 * folded
    batch = 8

    def kernel(j_ref, i_ref, table_ref, to_i_ref, to_j_ref, i_out, j_out, wide):
        same = lax.axis_index("sub") == lax.axis_index("rep")

        def spectrum_of(group):
            stacked = []
            for win in [per_step * group + u for u in range(per_step)]:
                here = j_ref[win]
                stacked += [here, jnp.where(same, here, i_ref[win])]
            wave = jnp.concatenate(stacked, axis=0)
            return lax.dot_general(table_ref[...], wave, NT, preferred_element_type=jnp.float32)

        def keep(group, spectrum):
            energy = jnp.sum(spectrum * spectrum, axis=0, keepdims=True) / bins
            white = spectrum * lax.rsqrt(energy + 1e-05)
            for half in range(2):
                for part in range(2):
                    if folded == 1:
                        row = half * wins + part * pairs + group
                    else:
                        row = part * pairs + 2 * group + half
                    wide[pl.ds(row, bins, stride=pitch), :] = white[
                        part * bins : (part + 1) * bins, half * LANES : (half + 1) * LANES
                    ]

        groups = wins // per_step
        at_once = 4

        def some_windows(step, carry):
            first = step * at_once
            last = spectrum_of(first)
            for group in range(1, at_once):
                now = spectrum_of(first + group)
                keep(first + group - 1, last)
                last = now
            keep(first + at_once - 1, last)
            return carry

        lax.fori_loop(0, groups // at_once, some_windows, 0)

        def moved(fs):
            loaded = [wide[pl.ds(f * pitch, line), :].astype(jnp.bfloat16) for f in fs]
            i_rows = [
                lax.dot_general(to_i_ref[...], diagonal(values, 2), NT, preferred_element_type=jnp.float32)
                for values in loaded
            ]
            if folded == 2:
                i_rows = [jnp.concatenate([rows[: given // 2], rows[given // 2 :]], axis=1) for rows in i_rows]
            j_rows = jnp.dot(jnp.concatenate(loaded, axis=0), to_j_ref[...], preferred_element_type=jnp.float32)
            return fs, i_rows, j_rows

        def store(fs, i_rows, j_rows):
            for at, f in enumerate(fs):
                i_out[f] = i_rows[at].astype(jnp.bfloat16)
                for odd in range(folded):
                    j_out[f, odd * line : (odd + 1) * line] = j_rows[
                        at * line : (at + 1) * line, odd * LANES : (odd + 1) * LANES
                    ].astype(jnp.bfloat16)

        def pack(group, carry):
            first = group * 4 * batch
            waiting = moved([first + u for u in range(batch)])
            for at in range(1, 4):
                following = moved([first + at * batch + u for u in range(batch)])
                store(*waiting)
                waiting = following
            store(*waiting)
            return carry

        lax.fori_loop(0, bins // (4 * batch), pack, 0)

    shapes = [(bins, given // 2, LANES), (bins, depth, LANES)]
    return kernel_call(
        kernel,
        "spectra",
        4 * samples * samples * wins * given,
        4 * wins * given * samples * 2,
        out_shape=[jax.ShapeDtypeStruct(shape, jnp.bfloat16) for shape in shapes],
        in_specs=[in_vmem()] * (2 + len(tables)),
        out_specs=[in_vmem()] * len(shapes),
        scratch_shapes=[pltpu.VMEM(((bins + 1) * pitch, LANES), jnp.float32)],
    )(rows_j, rows_i, *tables)


def partial_correlations(lefts, rights, tables, jobs, outs):
    left_arrays = [array for array, _ in lefts]
    right_arrays = [array for array, _, _ in rights]
    bins, depth, _ = right_arrays[0].shape
    piece = HALF // BLOCKS
    pitch = bins + 1
    step_bins = 32
    groups = []
    slices = {}
    for used, groups_here in jobs:
        js = [(rights[right][1], there) for right in used for there in rights[right][2]]
        for left, _, first in groups_here:
            found = []
            for offset in range(2):
                at = first + offset
                for order, (j_other, there) in enumerate(js):
                    if there != at:
                        kind = (lefts[left][1], j_other, there ^ (at % 2))
                        found.append((at, kind, offset * HALF + order * piece))
                        slices.setdefault(at, []).append(kind)
            groups.append(found)
    for kinds in slices.values():
        kinds.sort()
    total = len(groups) * piece
    batch = 4

    def first_of(at):
        (out,) = [positions for positions in outs if at in positions]
        return outs.index(out), sum(len(slices[before]) for before in out[: out.index(at)])

    def kernel(*refs):
        left_refs, rest = refs[: len(lefts)], refs[len(lefts) :]
        right_refs, rest = rest[: len(rights)], rest[len(rights) :]
        lag_ref, same_ref, out_refs, cross = rest[0], rest[1], rest[2:-1], rest[-1]
        lanes = lax.broadcasted_iota(jnp.int32, (depth, LANES), 1)

        first_half = lanes < HALF
        lower = lanes % HALF < HALF // 2
        blank = jnp.zeros((depth, LANES), jnp.bfloat16)

        def turn(values):
            swapped = []
            for first in range(0, depth, depth // 2):
                middle, last = first + depth // 4, first + depth // 2
                swapped += [-values[middle:last], values[first:middle]]
            return jnp.concatenate(swapped, axis=0)

        def right_hand(used, f):
            values = right_refs[used[0]][f]
            if len(used) == 2:
                values = jnp.where(lower, values, right_refs[used[1]][f])
            turned = turn(values)
            return jnp.concatenate(
                [
                    jnp.concatenate([jnp.where(first_half, part, blank) for part in (values, turned)], axis=1),
                    jnp.concatenate([jnp.where(first_half, blank, part) for part in (values, turned)], axis=1),
                ],
                axis=0,
            )

        def products(first_bin, count):
            found = []
            for f in [first_bin + u for u in range(count)]:
                first = 0
                for used, groups_here in jobs:
                    lhs = [left_refs[left][f, row : row + piece] for left, row, _ in groups_here]
                    lhs = jnp.concatenate(lhs, axis=0) if len(lhs) > 1 else lhs[0]
                    product = jnp.dot(lhs, right_hand(used, f), preferred_element_type=jnp.float32)
                    found.append((first * pitch + f, product))
                    first += lhs.shape[0]
            return found

        def keep(found):
            for here, product in found:
                for part in range(2):
                    cross[pl.ds(part * total * pitch + here, product.shape[0], stride=pitch), :] = product[
                        :, part * LANES : (part + 1) * LANES
                    ]

        def some_bins(step, carry):
            first = step * step_bins
            waiting = products(first, batch)
            for at in range(batch, step_bins, batch):
                following = products(first + at, batch)
                keep(waiting)
                waiting = following
            keep(waiting)
            return carry

        lax.fori_loop(0, bins // step_bins, some_bins, 0)

        for index, found in enumerate(groups):
            targets = []
            for at, kind, lane in found:
                out, first = first_of(at)
                targets.append((out_refs[out], first + slices[at].index(kind), lane))

            def summed(i):
                parts = []
                for part in range(2):
                    start = (part * total + index * piece + i) * pitch
                    parts.append(
                        jnp.concatenate([cross[pl.ds(start, bins), :], cross[pl.ds(start + pitch, bins), :]], axis=1)
                    )
                values = jnp.concatenate(parts, axis=0).astype(jnp.bfloat16)
                return i, jnp.dot(lag_ref[...], values, preferred_element_type=jnp.float32)

            def across(i, lagged):
                lagged = lagged.astype(jnp.bfloat16)
                return i, lax.dot_general(same_ref[...], lagged, NT, preferred_element_type=jnp.float32)

            def store(i, rows):
                for half in range(2):
                    for out, place, lane in targets:
                        row = half * LANES + lane
                        out[place, i + half] = rows[row : row + piece].astype(out.dtype)

            sums, rows = summed(0), None
            for i in range(2, piece, 2):
                more = summed(i)
                if rows is not None:
                    store(*rows)
                rows = across(*sums)
                sums = more
            store(*rows)
            store(*across(*sums))

    shapes = [(sum(len(slices[at]) for at in positions), piece, piece, LAGS) for positions in outs]
    types = [jnp.float32 if positions == (OWN_AT,) else jnp.bfloat16 for positions in outs]
    results = kernel_call(
        kernel,
        "partial_correlations",
        4 * total * bins * depth * LANES + 4 * total * bins * LANES * LAGS,
        2 * sum(array.size for array in left_arrays + right_arrays),
        out_shape=[jax.ShapeDtypeStruct(shape, kind) for shape, kind in zip(shapes, types)],
        in_specs=[in_vmem()] * (len(lefts) + len(rights) + len(tables)),
        out_specs=[in_vmem()] * len(shapes),
        scratch_shapes=[pltpu.VMEM(((2 * total + 1) * pitch, LANES), jnp.float32)],
    )(*left_arrays, *right_arrays, *tables)
    return results, slices


def assembled(shares):
    arrays = [array for array, _ in shares]
    _, piece, _, lags = arrays[0].shape
    width = 2 * piece

    def kernel(*refs):
        out, held, sems = refs[-3:]
        sub = lax.axis_index("sub")
        odd = lax.rem(lax.axis_index("chan"), 2)
        copies = []
        for there, round_at in ((0, 1), (1, 2 - 2 * odd), (3, 2 * odd)):
            for i_other in range(2):
                for j_other in range(2):
                    parts = [
                        refs[at][place].astype(jnp.float32)
                        for at, (_, kinds) in enumerate(shares)
                        for place, kind in enumerate(kinds)
                        if kind == (i_other, j_other, there)
                    ]
                    i_first = jnp.where(sub == 0, i_other, 1 - i_other) * piece
                    j_first = pl.multiple_of(jnp.where(sub == 0, j_other, 1 - j_other) * piece, piece)
                    held[round_at, 0, pl.ds(i_first, piece), pl.ds(j_first, piece), :] = functools.reduce(
                        jnp.add, parts
                    )
            at = len(copies)
            copies.append(pltpu.make_async_copy(held.at[round_at], out.at[round_at], sems.at[at]))
            copies[-1].start()
        for copy in copies:
            copy.wait()

    shape = (ROUNDS, 1, width, width, lags)
    return kernel_call(
        kernel,
        "assembled",
        0,
        sum(array.size for array in arrays) * 2,
        out_shape=jax.ShapeDtypeStruct(shape, jnp.float32),
        in_specs=[in_vmem()] * len(arrays),
        out_specs=pl.BlockSpec(memory_space=pl.ANY),
        scratch_shapes=[pltpu.VMEM(shape, jnp.float32), pltpu.SemaphoreType.DMA((ROUNDS,))],
    )(*arrays)


def summed_in_place(traces, channel_slot):
    chan_count = lax.axis_size("chan")
    _, win_here, samples = traces.shape
    piece = HALF // BLOCKS
    scale = (2.0 / (win_here * chan_count * (samples // 2))) ** 0.5
    dft_rows = dft_rows_table(samples)
    same = selection(2 * LANES, 2 * LANES, [(n, n) for n in range(2 * LANES)])
    tables = [lag_rows_table(samples, scale), same]
    everywhere = tuple(range(BLOCKS))

    def over_sub(rows):
        return lax.ppermute(rows, "sub", [(0, 1), (1, 0)])

    def over_core(rows):
        return lax.ppermute(rows, ("sub", "rep"), [(0, 1), (3, 2)])

    def with_device(share, apart):
        return lax.ppermute(share, "chan", [(z, z ^ apart) for z in range(chan_count)])

    def after(value, *others):
        return lax.optimization_barrier((value,) + others)[0]

    def added(share, arrived):
        return (share.astype(jnp.float32) + arrived.astype(jnp.float32)).astype(jnp.bfloat16)

    def for_two_away(kinds):
        return [(i_other, j_other, there ^ 2) for i_other, j_other, there in kinds]

    mine, mine_far, mine_near = order_rows(traces, channel_slot, [everywhere, FAR, NEAR])
    far = over_sub(mine_far)
    near = over_sub(mine_near)

    own_i, own_j = spectra(mine, over_core(mine), (dft_rows, *own_picks()))
    own_left, own_right = (own_i, 0), (own_j, 0, everywhere)
    own_far, own_near = (0, 0, FAR[0]), (0, piece, NEAR[0])
    (kept_1, sent_far_1, own_1, sent_near_1), kinds_1 = partial_correlations(
        [own_left], [own_right], tables, [((0,), [own_far, own_near])], [(0,), (1,), (2,), (3,)]
    )
    arrived_far_1 = with_device(sent_far_1, 1)

    far = after(far, kept_1, sent_far_1, own_1, sent_near_1)
    far_i, far_j = spectra(far, over_core(far), (dft_rows, *half_picks()))
    far_i, arrived_far_1 = lax.optimization_barrier((far_i, arrived_far_1))
    far_left, far_right = (far_i, 1), (far_j, 1, FAR)
    other_far = (1, 0, FAR[0])
    (kept_2, sent_far_2, own_2, sent_near_2), kinds_2 = partial_correlations(
        [own_left, far_left],
        [own_right, far_right],
        tables,
        [((0,), [other_far]), ((1,), [own_far, own_near, other_far])],
        [(0,), (1,), (2,), (3,)],
    )
    arrived_far_2 = with_device(sent_far_2, 1)

    near, arrived_far_2 = lax.optimization_barrier((near, arrived_far_2))
    near_i, near_j = spectra(near, over_core(near), (dft_rows, *half_picks()))
    summed_2 = added(kept_2, arrived_far_2)
    far_2 = with_device(summed_2, 2)
    summed_1 = added(after(kept_1, near_j), arrived_far_1)
    far_1 = with_device(summed_1, 2)
    near_j = after(near_j, summed_2)
    near_left, near_right = (near_i, 1), (near_j, 1, NEAR)
    other_near = (1, 0, NEAR[0])
    (kept_3, sent_3), kinds_3 = partial_correlations(
        [own_left, far_left], [near_right], tables, [((0,), [own_far, other_far])], [(0,), (1,)]
    )
    arrived_3 = with_device(sent_3, 1)
    arrived_near = with_device(jnp.concatenate([sent_near_1, sent_near_2]), 1)
    near_right = (after(near_j, kept_3, sent_3, far_2, summed_1), 1, NEAR)
    (own_4, sent_4), kinds_4 = partial_correlations(
        [own_left, near_left],
        [far_right, near_right],
        tables,
        [((0, 1), [other_near]), ((1,), [own_near])],
        [(2,), (3,)],
    )
    arrived_4 = with_device(sent_4, 1)
    summed_3 = added(after(kept_3, own_4), arrived_3)
    far_3 = with_device(summed_3, 2)
    near_left = (after(near_i, own_4, sent_4, summed_3, arrived_near, far_1), 1)
    (own_5, sent_5), kinds_5 = partial_correlations(
        [near_left], [own_right], tables, [((0,), [(0, 0, NEAR[0])])], [(2,), (3,)]
    )
    arrived_5 = with_device(sent_5, 1)
    shares = [
        (own_1, kinds_1[2]),
        (own_2, kinds_2[2]),
        (own_4, kinds_4[2]),
        (own_5, kinds_5[2]),
        (arrived_near, kinds_1[3] + kinds_2[3]),
        (arrived_4, kinds_4[3]),
        (arrived_5, kinds_5[3]),
        (far_1, for_two_away(kinds_1[0])),
        (far_2, for_two_away(kinds_2[0])),
        (far_3, for_two_away(kinds_3[0])),
    ]
    return assembled(shares)


def from_behind(shard, axis, by):
    count = lax.axis_size(axis)
    return lax.ppermute(shard, axis, [(i, (i + by) % count) for i in range(count)])


def dft_columns(samples, parts, sub_bins):
    shape = (samples, parts, 2, sub_bins)
    time_pos = lax.broadcasted_iota(jnp.int32, shape, 0)
    range_pos = lax.broadcasted_iota(jnp.int32, shape, 1)
    part_pos = lax.broadcasted_iota(jnp.int32, shape, 2)
    bin_pos = lax.broadcasted_iota(jnp.int32, shape, 3)
    frequency = range_pos * sub_bins + bin_pos
    angles = jnp.mod(time_pos * frequency, samples).astype(jnp.float32) * (2.0 * math.pi / samples)
    entries = jnp.where(part_pos == 0, jnp.cos(angles), -jnp.sin(angles))
    return entries.reshape(samples, parts * 2 * sub_bins).astype(jnp.bfloat16)


def lag_table(sub_bins, first_bin, lag_count, samples):
    frequency = first_bin + lax.broadcasted_iota(jnp.int32, (sub_bins, lag_count), 0)
    lag_offset = lax.broadcasted_iota(jnp.int32, (sub_bins, lag_count), 1) - lag_count // 2
    angles = jnp.mod(frequency * lag_offset, samples).astype(jnp.float32) * (2.0 * math.pi / samples)
    return jnp.stack([jnp.cos(angles), -jnp.sin(angles)], axis=1)


def moved_spectra(traces, channel_slot):
    chan_count = lax.axis_size("chan")
    sub_count = lax.axis_size("sub")
    group_rows, win_here, samples = traces.shape
    bin_count = samples // 2
    sub_bins = bin_count // sub_count
    bin_width = 2 * sub_bins
    piece_len = group_rows // chan_count
    picked = jnp.take(traces, channel_slot, axis=0)
    dft_rows = dft_columns(samples, sub_count, sub_bins)
    spectrum = jnp.dot(picked.reshape(-1, samples), dft_rows, preferred_element_type=jnp.float32)
    energy = jnp.sum(spectrum * spectrum, axis=1, keepdims=True) / bin_count
    whitened = (spectrum * lax.rsqrt(energy + 1e-05)).astype(jnp.bfloat16)
    whitened = whitened.reshape(chan_count, piece_len, win_here, sub_count, bin_width)
    regrouped = lax.all_to_all(whitened, "chan", split_axis=0, concat_axis=0, tiled=True)
    regrouped = lax.all_to_all(regrouped, "sub", split_axis=3, concat_axis=3, tiled=True)
    own_half = regrouped.transpose(3, 1, 0, 2, 4).reshape(sub_count * piece_len, chan_count * win_here, bin_width)
    own_block = lax.all_gather(own_half, "rep", axis=0, tiled=True)
    windows = own_block.shape[1]
    own_split = own_block.reshape(own_block.shape[0], windows, 2, sub_bins)
    lag_rows = lag_table(sub_bins, lax.axis_index("sub") * sub_bins, LAGS, samples)
    lag_scale = (2.0 / (windows * bin_count)) ** 0.5
    results = []
    for step in range(1, ROUNDS + 1):
        partner = from_behind(own_half, "chan", -step)
        partner_split = partner.reshape(partner.shape[0], windows, 2, sub_bins)
        turned = jnp.stack([-partner_split[:, :, 1], partner_split[:, :, 0]], axis=2)
        partner_pair = jnp.stack([partner_split, turned], axis=0)
        cross_spec = jnp.einsum("iwpf,qjwpf->fqij", own_split, partner_pair, preferred_element_type=jnp.float32)
        summed = jnp.einsum("fqij,fql->ijl", cross_spec, lag_rows, precision=lax.Precision.HIGHEST)
        results.append(lax.psum_scatter(lag_scale * summed, "sub", scatter_dimension=0, tiled=True))
    return jnp.stack(results)[:, None]


def solution(mesh):
    sizes = mesh.shape
    in_place = sizes["chan"] == BLOCKS == ROUNDS + 1 and sizes["sub"] == 2 and sizes["rep"] == 2
    return jax.shard_map(
        summed_in_place if in_place else moved_spectra,
        mesh=mesh,
        in_specs=(P(("groups", "sub", "rep"), "chan", None), P(("groups", "sub", "rep"))),
        out_specs=P(None, ("groups", "chan"), "sub", "rep", None),
        check_vma=False,
    )
```

```python
import functools
import math

import jax
import jax.numpy as jnp
import numpy as np
from jax import lax
from jax.experimental import pallas as pl
from jax.experimental.pallas import tpu as pltpu
from jax.sharding import PartitionSpec as P

LAGS = 128
ROUNDS = 3
LANES = 128
HALF = LANES // 2
VMEM_BYTES = 32 * 1024 * 1024
ORDER_VMEM_BYTES = 48 * 1024 * 1024
NT = (((1,), (1,)), ((), ()))
BLOCKS = 4
FAR = (0, 1)
NEAR = (2, 3)
KEPT_AT, OWN_AT = 0, 2


def kernel_call(kernel, name, flops, bytes_accessed, vmem_bytes=VMEM_BYTES, **more):
    return pl.pallas_call(
        kernel,
        name=name,
        compiler_params=pltpu.CompilerParams(vmem_limit_bytes=vmem_bytes),
        cost_estimate=pl.CostEstimate(flops=flops, bytes_accessed=bytes_accessed, transcendentals=0),
        **more,
    )


def in_vmem():
    return pl.BlockSpec(memory_space=pltpu.VMEM)


def dft_rows_table(samples):
    bins = samples // 2
    turns = (np.arange(bins)[:, None] * np.arange(samples)[None, :]) % samples
    angles = turns.astype(np.float32) * np.float32(2.0 * math.pi / samples)
    table = np.concatenate([np.cos(angles), -np.sin(angles)], axis=0)
    return jnp.asarray(table.astype(np.float32)).astype(jnp.bfloat16)


def lag_rows_table(samples, scale):
    bins = samples // 2
    offsets = np.arange(LAGS) - LAGS // 2
    turns = (offsets[:, None] * np.arange(bins)[None, :]) % samples
    angles = turns.astype(np.float32) * np.float32(2.0 * math.pi / samples)
    table = np.concatenate([np.cos(angles), -np.sin(angles)], axis=1) * np.float32(scale)
    return jnp.asarray(table.astype(np.float32)).astype(jnp.bfloat16)


def selection(rows, columns, ones):
    table = np.zeros((rows, columns), np.float32)
    for row, column in ones:
        table[row, column] = 1.0
    return jnp.asarray(table).astype(jnp.bfloat16)


def own_picks():
    piece = HALF // BLOCKS
    to_i = []
    for at in range(BLOCKS):
        for n in range(piece):
            to_i.append((at // 2 * piece + n, at % 2 * LANES + HALF + at * piece + n))
    to_j = [(j, copy * HALF + j) for j in range(HALF) for copy in range(2)]
    return selection(2 * piece, 2 * LANES, to_i), selection(LANES, LANES, to_j)


def half_picks():
    count = HALF // 2
    to_i, to_j = [], []
    for odd in range(2):
        for n in range(count):
            to_i.append((n, odd * LANES + odd * HALF + count + n))
            to_j += [(odd * HALF + n, odd * LANES + copy * count + n) for copy in range(4)]
    return selection(count, 2 * LANES, to_i), selection(LANES, 2 * LANES, to_j)


def order_rows(traces, slots, kinds):
    rows, wins, samples = traces.shape
    tiles = samples // LANES
    piece = rows // BLOCKS
    step_wins = 16
    steps = wins // step_wins
    batch = 4
    used = max(kinds, key=len)
    pitch = len(used) * piece + 1

    def kernel(slots_ref, traces_ref, *refs):
        out_refs, (wide, in_ref, slot_ref, sems) = refs[:-4], refs[-4:]
        slot_copy = pltpu.make_async_copy(slots_ref, slot_ref, sems.at[steps])
        slot_copy.start()
        copies = []
        for step in range(steps):
            here = pl.ds(step * step_wins, step_wins)
            copies.append(
                pltpu.make_async_copy(traces_ref.at[:, here, :], in_ref.at[:, here, :], sems.at[step])
            )
            copies[-1].start()
        slot_copy.wait()
        z = lax.axis_index("chan")
        odd = lax.rem(z, 2)
        pair = jnp.where(z < 2, 2, 0)

        def some_windows(step):
            first_win = step * step_wins
            for at, position in enumerate(used):
                block = pair + position + (odd if position % 2 == 0 else -odd)
                first = lax.rem(block, BLOCKS) * piece

                def move(group, carry, at=at, first=first):
                    js = [group * batch + u for u in range(batch)]
                    picked = [
                        in_ref[slot_ref[first + j], pl.ds(first_win, step_wins), :].astype(jnp.float32) for j in js
                    ]
                    for j, row in zip(js, picked):
                        for tile in range(tiles):
                            wide[tile, pl.ds(at * piece + j, step_wins, stride=pitch), :] = row[
                                :, tile * LANES : (tile + 1) * LANES
                            ]
                    return carry

                lax.fori_loop(0, piece // batch, move, 0)

            def pack(w, carry):
                blocks = [
                    wide[tile, pl.ds(w * pitch, len(used) * piece), :].astype(jnp.bfloat16) for tile in range(tiles)
                ]
                for out_ref, kind in zip(out_refs, kinds):
                    first = used.index(kind[0]) * piece
                    for tile, block in enumerate(blocks):
                        out_ref[first_win + w, :, tile * LANES : (tile + 1) * LANES] = block[
                            first : first + len(kind) * piece
                        ]
                return carry

            lax.fori_loop(0, step_wins, pack, 0, unroll=2)

        for step in range(steps):
            copies[step].wait()
            some_windows(step)

    return kernel_call(
        kernel,
        "order_rows",
        0,
        3 * traces.size * 2,
        vmem_bytes=ORDER_VMEM_BYTES,
        out_shape=[jax.ShapeDtypeStruct((wins, len(kind) * piece, samples), jnp.bfloat16) for kind in kinds],
        in_specs=[pl.BlockSpec(memory_space=pltpu.HBM)] * 2,
        out_specs=[in_vmem()] * len(kinds),
        scratch_shapes=[
            pltpu.VMEM((tiles, (step_wins + 1) * pitch, LANES), jnp.float32),
            pltpu.VMEM(traces.shape, traces.dtype),
            pltpu.SMEM(slots.shape, slots.dtype),
            pltpu.SemaphoreType.DMA((steps + 1,)),
        ],
    )(slots, traces)


def diagonal(values, copies):
    blank = jnp.zeros_like(values)
    rows = [[values if at == copy else blank for at in range(copies)] for copy in range(copies)]
    return jnp.concatenate([jnp.concatenate(row, axis=1) for row in rows], axis=0)


def spectra(rows_j, rows_i, tables):
    wins, given, samples = rows_j.shape
    bins = samples // 2
    pairs = wins // 2
    depth = 2 * wins
    folded = HALF // given
    line = depth // folded
    pitch = line + 1
    per_step = 2 * folded
    batch = 8

    def kernel(j_ref, i_ref, table_ref, to_i_ref, to_j_ref, i_out, j_out, wide):
        same = lax.axis_index("sub") == lax.axis_index("rep")

        def spectrum_of(group):
            stacked = []
            for win in [per_step * group + u for u in range(per_step)]:
                here = j_ref[win]
                stacked += [here, jnp.where(same, here, i_ref[win])]
            wave = jnp.concatenate(stacked, axis=0)
            return lax.dot_general(table_ref[...], wave, NT, preferred_element_type=jnp.float32)

        def keep(group, spectrum):
            energy = jnp.sum(spectrum * spectrum, axis=0, keepdims=True) / bins
            white = spectrum * lax.rsqrt(energy + 1e-05)
            for half in range(2):
                for part in range(2):
                    if folded == 1:
                        row = half * wins + part * pairs + group
                    else:
                        row = part * pairs + 2 * group + half
                    wide[pl.ds(row, bins, stride=pitch), :] = white[
                        part * bins : (part + 1) * bins, half * LANES : (half + 1) * LANES
                    ]

        groups = wins // per_step
        at_once = 4

        def some_windows(step, carry):
            first = step * at_once
            last = spectrum_of(first)
            for group in range(1, at_once):
                now = spectrum_of(first + group)
                keep(first + group - 1, last)
                last = now
            keep(first + at_once - 1, last)
            return carry

        lax.fori_loop(0, groups // at_once, some_windows, 0)

        def moved(fs):
            loaded = [wide[pl.ds(f * pitch, line), :].astype(jnp.bfloat16) for f in fs]
            i_rows = [
                lax.dot_general(to_i_ref[...], diagonal(values, 2), NT, preferred_element_type=jnp.float32)
                for values in loaded
            ]
            if folded == 2:
                i_rows = [jnp.concatenate([rows[: given // 2], rows[given // 2 :]], axis=1) for rows in i_rows]
            j_rows = jnp.dot(jnp.concatenate(loaded, axis=0), to_j_ref[...], preferred_element_type=jnp.float32)
            return fs, i_rows, j_rows

        def store(fs, i_rows, j_rows):
            for at, f in enumerate(fs):
                i_out[f] = i_rows[at].astype(jnp.bfloat16)
                for odd in range(folded):
                    j_out[f, odd * line : (odd + 1) * line] = j_rows[
                        at * line : (at + 1) * line, odd * LANES : (odd + 1) * LANES
                    ].astype(jnp.bfloat16)

        def pack(group, carry):
            first = group * 4 * batch
            waiting = moved([first + u for u in range(batch)])
            for at in range(1, 4):
                following = moved([first + at * batch + u for u in range(batch)])
                store(*waiting)
                waiting = following
            store(*waiting)
            return carry

        lax.fori_loop(0, bins // (4 * batch), pack, 0)

    shapes = [(bins, given // 2, LANES), (bins, depth, LANES)]
    return kernel_call(
        kernel,
        "spectra",
        4 * samples * samples * wins * given,
        4 * wins * given * samples * 2,
        out_shape=[jax.ShapeDtypeStruct(shape, jnp.bfloat16) for shape in shapes],
        in_specs=[in_vmem()] * (2 + len(tables)),
        out_specs=[in_vmem()] * len(shapes),
        scratch_shapes=[pltpu.VMEM(((bins + 1) * pitch, LANES), jnp.float32)],
    )(rows_j, rows_i, *tables)


def partial_correlations(lefts, rights, tables, jobs, outs):
    left_arrays = [array for array, _ in lefts]
    right_arrays = [array for array, _, _ in rights]
    bins, depth, _ = right_arrays[0].shape
    piece = HALF // BLOCKS
    pitch = bins + 1
    step_bins = 32
    groups = []
    slices = {}
    for used, groups_here in jobs:
        js = [(rights[right][1], there) for right in used for there in rights[right][2]]
        for left, _, first in groups_here:
            found = []
            for offset in range(2):
                at = first + offset
                for order, (j_other, there) in enumerate(js):
                    if there != at:
                        kind = (lefts[left][1], j_other, there ^ (at % 2))
                        found.append((at, kind, offset * HALF + order * piece))
                        slices.setdefault(at, []).append(kind)
            groups.append(found)
    for kinds in slices.values():
        kinds.sort()
    total = len(groups) * piece
    batch = 4

    def first_of(at):
        (out,) = [positions for positions in outs if at in positions]
        return outs.index(out), sum(len(slices[before]) for before in out[: out.index(at)])

    def kernel(*refs):
        left_refs, rest = refs[: len(lefts)], refs[len(lefts) :]
        right_refs, rest = rest[: len(rights)], rest[len(rights) :]
        lag_ref, same_ref, out_refs, cross = rest[0], rest[1], rest[2:-1], rest[-1]
        lanes = lax.broadcasted_iota(jnp.int32, (depth, LANES), 1)

        first_half = lanes < HALF
        lower = lanes % HALF < HALF // 2
        blank = jnp.zeros((depth, LANES), jnp.bfloat16)

        def turn(values):
            swapped = []
            for first in range(0, depth, depth // 2):
                middle, last = first + depth // 4, first + depth // 2
                swapped += [-values[middle:last], values[first:middle]]
            return jnp.concatenate(swapped, axis=0)

        def right_hand(used, f):
            values = right_refs[used[0]][f]
            if len(used) == 2:
                values = jnp.where(lower, values, right_refs[used[1]][f])
            turned = turn(values)
            return jnp.concatenate(
                [
                    jnp.concatenate([jnp.where(first_half, part, blank) for part in (values, turned)], axis=1),
                    jnp.concatenate([jnp.where(first_half, blank, part) for part in (values, turned)], axis=1),
                ],
                axis=0,
            )

        def products(first_bin, count):
            found = []
            for f in [first_bin + u for u in range(count)]:
                first = 0
                for used, groups_here in jobs:
                    lhs = [left_refs[left][f, row : row + piece] for left, row, _ in groups_here]
                    lhs = jnp.concatenate(lhs, axis=0) if len(lhs) > 1 else lhs[0]
                    product = jnp.dot(lhs, right_hand(used, f), preferred_element_type=jnp.float32)
                    found.append((first * pitch + f, product))
                    first += lhs.shape[0]
            return found

        def keep(found):
            for here, product in found:
                for part in range(2):
                    cross[pl.ds(part * total * pitch + here, product.shape[0], stride=pitch), :] = product[
                        :, part * LANES : (part + 1) * LANES
                    ]

        def some_bins(step, carry):
            first = step * step_bins
            waiting = products(first, batch)
            for at in range(batch, step_bins, batch):
                following = products(first + at, batch)
                keep(waiting)
                waiting = following
            keep(waiting)
            return carry

        lax.fori_loop(0, bins // step_bins, some_bins, 0)

        for index, found in enumerate(groups):
            targets = []
            for at, kind, lane in found:
                out, first = first_of(at)
                targets.append((out_refs[out], first + slices[at].index(kind), lane))

            def summed(i):
                parts = []
                for part in range(2):
                    start = (part * total + index * piece + i) * pitch
                    parts.append(
                        jnp.concatenate([cross[pl.ds(start, bins), :], cross[pl.ds(start + pitch, bins), :]], axis=1)
                    )
                values = jnp.concatenate(parts, axis=0).astype(jnp.bfloat16)
                return i, jnp.dot(lag_ref[...], values, preferred_element_type=jnp.float32)

            def across(i, lagged):
                lagged = lagged.astype(jnp.bfloat16)
                return i, lax.dot_general(same_ref[...], lagged, NT, preferred_element_type=jnp.float32)

            def store(i, rows):
                for half in range(2):
                    for out, place, lane in targets:
                        row = half * LANES + lane
                        out[place, i + half] = rows[row : row + piece].astype(out.dtype)

            sums, rows = summed(0), None
            for i in range(2, piece, 2):
                more = summed(i)
                if rows is not None:
                    store(*rows)
                rows = across(*sums)
                sums = more
            store(*rows)
            store(*across(*sums))

    shapes = [(sum(len(slices[at]) for at in positions), piece, piece, LAGS) for positions in outs]
    types = [jnp.float32 if positions == (OWN_AT,) else jnp.bfloat16 for positions in outs]
    results = kernel_call(
        kernel,
        "partial_correlations",
        4 * total * bins * depth * LANES + 4 * total * bins * LANES * LAGS,
        2 * sum(array.size for array in left_arrays + right_arrays),
        out_shape=[jax.ShapeDtypeStruct(shape, kind) for shape, kind in zip(shapes, types)],
        in_specs=[in_vmem()] * (len(lefts) + len(rights) + len(tables)),
        out_specs=[in_vmem()] * len(shapes),
        scratch_shapes=[pltpu.VMEM(((2 * total + 1) * pitch, LANES), jnp.float32)],
    )(*left_arrays, *right_arrays, *tables)
    return results, slices


def assembled(shares):
    arrays = [array for array, _ in shares]
    _, piece, _, lags = arrays[0].shape
    width = 2 * piece

    def kernel(*refs):
        out, held, sems = refs[-3:]
        sub = lax.axis_index("sub")
        odd = lax.rem(lax.axis_index("chan"), 2)
        copies = []
        for there, round_at in ((0, 1), (1, 2 - 2 * odd), (3, 2 * odd)):
            for i_other in range(2):
                for j_other in range(2):
                    parts = [
                        refs[at][place].astype(jnp.float32)
                        for at, (_, kinds) in enumerate(shares)
                        for place, kind in enumerate(kinds)
                        if kind == (i_other, j_other, there)
                    ]
                    i_first = jnp.where(sub == 0, i_other, 1 - i_other) * piece
                    j_first = pl.multiple_of(jnp.where(sub == 0, j_other, 1 - j_other) * piece, piece)
                    held[round_at, 0, pl.ds(i_first, piece), pl.ds(j_first, piece), :] = functools.reduce(
                        jnp.add, parts
                    )
            at = len(copies)
            copies.append(pltpu.make_async_copy(held.at[round_at], out.at[round_at], sems.at[at]))
            copies[-1].start()
        for copy in copies:
            copy.wait()

    shape = (ROUNDS, 1, width, width, lags)
    return kernel_call(
        kernel,
        "assembled",
        0,
        sum(array.size for array in arrays) * 2,
        out_shape=jax.ShapeDtypeStruct(shape, jnp.float32),
        in_specs=[in_vmem()] * len(arrays),
        out_specs=pl.BlockSpec(memory_space=pl.ANY),
        scratch_shapes=[pltpu.VMEM(shape, jnp.float32), pltpu.SemaphoreType.DMA((ROUNDS,))],
    )(*arrays)


def summed_in_place(traces, channel_slot):
    chan_count = lax.axis_size("chan")
    _, win_here, samples = traces.shape
    piece = HALF // BLOCKS
    scale = (2.0 / (win_here * chan_count * (samples // 2))) ** 0.5
    dft_rows = dft_rows_table(samples)
    same = selection(2 * LANES, 2 * LANES, [(n, n) for n in range(2 * LANES)])
    tables = [lag_rows_table(samples, scale), same]
    everywhere = tuple(range(BLOCKS))

    def over_sub(rows):
        return lax.ppermute(rows, "sub", [(0, 1), (1, 0)])

    def over_core(rows):
        return lax.ppermute(rows, "rep", [(0, 1), (1, 0)])

    def with_device(share, apart):
        return lax.ppermute(share, "chan", [(z, z ^ apart) for z in range(chan_count)])

    def after(value, *others):
        return lax.optimization_barrier((value,) + others)[0]

    def added(share, arrived):
        return (share.astype(jnp.float32) + arrived.astype(jnp.float32)).astype(jnp.bfloat16)

    def for_two_away(kinds):
        return [(i_other, j_other, there ^ 2) for i_other, j_other, there in kinds]

    mine, mine_far, mine_near = order_rows(traces, channel_slot, [everywhere, FAR, NEAR])
    far = over_sub(mine_far)
    near = over_sub(mine_near)

    own_i, own_j = spectra(mine, over_core(mine), (dft_rows, *own_picks()))
    own_left, own_right = (own_i, 0), (own_j, 0, everywhere)
    own_far, own_near = (0, 0, FAR[0]), (0, piece, NEAR[0])
    (kept_1, sent_far_1, own_1, sent_near_1), kinds_1 = partial_correlations(
        [own_left], [own_right], tables, [((0,), [own_far, own_near])], [(0,), (1,), (2,), (3,)]
    )
    arrived_far_1 = with_device(sent_far_1, 1)

    far = after(far, kept_1, sent_far_1, own_1, sent_near_1)
    far_i, far_j = spectra(far, over_core(far), (dft_rows, *half_picks()))
    far_i, arrived_far_1 = lax.optimization_barrier((far_i, arrived_far_1))
    far_left, far_right = (far_i, 1), (far_j, 1, FAR)
    other_far = (1, 0, FAR[0])
    (kept_2, sent_far_2, own_2, sent_near_2), kinds_2 = partial_correlations(
        [own_left, far_left],
        [own_right, far_right],
        tables,
        [((0,), [other_far]), ((1,), [own_far, own_near, other_far])],
        [(0,), (1,), (2,), (3,)],
    )
    arrived_far_2 = with_device(sent_far_2, 1)

    near, arrived_far_2 = lax.optimization_barrier((near, arrived_far_2))
    near_i, near_j = spectra(near, over_core(near), (dft_rows, *half_picks()))
    summed_2 = added(kept_2, arrived_far_2)
    far_2 = with_device(summed_2, 2)
    summed_1 = added(after(kept_1, near_j), arrived_far_1)
    far_1 = with_device(summed_1, 2)
    near_j = after(near_j, summed_2)
    near_left, near_right = (near_i, 1), (near_j, 1, NEAR)
    other_near = (1, 0, NEAR[0])
    (kept_3, sent_3), kinds_3 = partial_correlations(
        [own_left, far_left], [near_right], tables, [((0,), [own_far, other_far])], [(0,), (1,)]
    )
    arrived_3 = with_device(sent_3, 1)
    arrived_near = with_device(jnp.concatenate([sent_near_1, sent_near_2]), 1)
    near_right = (after(near_j, kept_3, sent_3, far_2, summed_1), 1, NEAR)
    (own_4, sent_4), kinds_4 = partial_correlations(
        [own_left, near_left],
        [far_right, near_right],
        tables,
        [((0, 1), [other_near]), ((1,), [own_near])],
        [(2,), (3,)],
    )
    arrived_4 = with_device(sent_4, 1)
    summed_3 = added(after(kept_3, own_4), arrived_3)
    far_3 = with_device(summed_3, 2)
    near_left = (after(near_i, own_4, sent_4, summed_3, arrived_near, far_1), 1)
    (own_5, sent_5), kinds_5 = partial_correlations(
        [near_left], [own_right], tables, [((0,), [(0, 0, NEAR[0])])], [(2,), (3,)]
    )
    arrived_5 = with_device(sent_5, 1)
    shares = [
        (own_1, kinds_1[2]),
        (own_2, kinds_2[2]),
        (own_4, kinds_4[2]),
        (own_5, kinds_5[2]),
        (arrived_near, kinds_1[3] + kinds_2[3]),
        (arrived_4, kinds_4[3]),
        (arrived_5, kinds_5[3]),
        (far_1, for_two_away(kinds_1[0])),
        (far_2, for_two_away(kinds_2[0])),
        (far_3, for_two_away(kinds_3[0])),
    ]
    return assembled(shares)


def from_behind(shard, axis, by):
    count = lax.axis_size(axis)
    return lax.ppermute(shard, axis, [(i, (i + by) % count) for i in range(count)])


def dft_columns(samples, parts, sub_bins):
    shape = (samples, parts, 2, sub_bins)
    time_pos = lax.broadcasted_iota(jnp.int32, shape, 0)
    range_pos = lax.broadcasted_iota(jnp.int32, shape, 1)
    part_pos = lax.broadcasted_iota(jnp.int32, shape, 2)
    bin_pos = lax.broadcasted_iota(jnp.int32, shape, 3)
    frequency = range_pos * sub_bins + bin_pos
    angles = jnp.mod(time_pos * frequency, samples).astype(jnp.float32) * (2.0 * math.pi / samples)
    entries = jnp.where(part_pos == 0, jnp.cos(angles), -jnp.sin(angles))
    return entries.reshape(samples, parts * 2 * sub_bins).astype(jnp.bfloat16)


def lag_table(sub_bins, first_bin, lag_count, samples):
    frequency = first_bin + lax.broadcasted_iota(jnp.int32, (sub_bins, lag_count), 0)
    lag_offset = lax.broadcasted_iota(jnp.int32, (sub_bins, lag_count), 1) - lag_count // 2
    angles = jnp.mod(frequency * lag_offset, samples).astype(jnp.float32) * (2.0 * math.pi / samples)
    return jnp.stack([jnp.cos(angles), -jnp.sin(angles)], axis=1)


def moved_spectra(traces, channel_slot):
    chan_count = lax.axis_size("chan")
    sub_count = lax.axis_size("sub")
    group_rows, win_here, samples = traces.shape
    bin_count = samples // 2
    sub_bins = bin_count // sub_count
    bin_width = 2 * sub_bins
    piece_len = group_rows // chan_count
    picked = jnp.take(traces, channel_slot, axis=0)
    dft_rows = dft_columns(samples, sub_count, sub_bins)
    spectrum = jnp.dot(picked.reshape(-1, samples), dft_rows, preferred_element_type=jnp.float32)
    energy = jnp.sum(spectrum * spectrum, axis=1, keepdims=True) / bin_count
    whitened = (spectrum * lax.rsqrt(energy + 1e-05)).astype(jnp.bfloat16)
    whitened = whitened.reshape(chan_count, piece_len, win_here, sub_count, bin_width)
    regrouped = lax.all_to_all(whitened, "chan", split_axis=0, concat_axis=0, tiled=True)
    regrouped = lax.all_to_all(regrouped, "sub", split_axis=3, concat_axis=3, tiled=True)
    own_half = regrouped.transpose(3, 1, 0, 2, 4).reshape(sub_count * piece_len, chan_count * win_here, bin_width)
    own_block = lax.all_gather(own_half, "rep", axis=0, tiled=True)
    windows = own_block.shape[1]
    own_split = own_block.reshape(own_block.shape[0], windows, 2, sub_bins)
    lag_rows = lag_table(sub_bins, lax.axis_index("sub") * sub_bins, LAGS, samples)
    lag_scale = (2.0 / (windows * bin_count)) ** 0.5
    results = []
    for step in range(1, ROUNDS + 1):
        partner = from_behind(own_half, "chan", -step)
        partner_split = partner.reshape(partner.shape[0], windows, 2, sub_bins)
        turned = jnp.stack([-partner_split[:, :, 1], partner_split[:, :, 0]], axis=2)
        partner_pair = jnp.stack([partner_split, turned], axis=0)
        cross_spec = jnp.einsum("iwpf,qjwpf->fqij", own_split, partner_pair, preferred_element_type=jnp.float32)
        summed = jnp.einsum("fqij,fql->ijl", cross_spec, lag_rows, precision=lax.Precision.HIGHEST)
        results.append(lax.psum_scatter(lag_scale * summed, "sub", scatter_dimension=0, tiled=True))
    return jnp.stack(results)[:, None]


def solution(mesh):
    sizes = mesh.shape
    in_place = sizes["chan"] == BLOCKS == ROUNDS + 1 and sizes["sub"] == 2 and sizes["rep"] == 2
    return jax.shard_map(
        summed_in_place if in_place else moved_spectra,
        mesh=mesh,
        in_specs=(P(("groups", "sub", "rep"), "chan", None), P(("groups", "sub", "rep"))),
        out_specs=P(None, ("groups", "chan"), "sub", "rep", None),
        check_vma=False,
    )
```

```python
import functools
import math

import jax
import jax.numpy as jnp
import numpy as np
from jax import lax
from jax.experimental import pallas as pl
from jax.experimental.pallas import tpu as pltpu
from jax.sharding import PartitionSpec as P

LAGS = 128
ROUNDS = 3
LANES = 128
HALF = LANES // 2
VMEM_BYTES = 32 * 1024 * 1024
ORDER_VMEM_BYTES = 48 * 1024 * 1024
NT = (((1,), (1,)), ((), ()))
BLOCKS = 4
FAR = (0, 1)
NEAR = (2, 3)
KEPT_AT, OWN_AT = 0, 2


def kernel_call(kernel, name, flops, bytes_accessed, vmem_bytes=VMEM_BYTES, **more):
    return pl.pallas_call(
        kernel,
        name=name,
        compiler_params=pltpu.CompilerParams(vmem_limit_bytes=vmem_bytes),
        cost_estimate=pl.CostEstimate(flops=flops, bytes_accessed=bytes_accessed, transcendentals=0),
        **more,
    )


def in_vmem():
    return pl.BlockSpec(memory_space=pltpu.VMEM)


def dft_rows_table(samples):
    bins = samples // 2
    turns = (np.arange(bins)[:, None] * np.arange(samples)[None, :]) % samples
    angles = turns.astype(np.float32) * np.float32(2.0 * math.pi / samples)
    table = np.concatenate([np.cos(angles), -np.sin(angles)], axis=0)
    return jnp.asarray(table.astype(np.float32)).astype(jnp.bfloat16)


def lag_rows_table(samples, scale):
    bins = samples // 2
    offsets = np.arange(LAGS) - LAGS // 2
    turns = (offsets[:, None] * np.arange(bins)[None, :]) % samples
    angles = turns.astype(np.float32) * np.float32(2.0 * math.pi / samples)
    table = np.concatenate([np.cos(angles), -np.sin(angles)], axis=1) * np.float32(scale)
    return jnp.asarray(table.astype(np.float32)).astype(jnp.bfloat16)


def selection(rows, columns, ones):
    table = np.zeros((rows, columns), np.float32)
    for row, column in ones:
        table[row, column] = 1.0
    return jnp.asarray(table).astype(jnp.bfloat16)


def own_picks():
    piece = HALF // BLOCKS
    to_i = []
    for at in range(BLOCKS):
        for n in range(piece):
            to_i.append((at // 2 * piece + n, at % 2 * LANES + HALF + at * piece + n))
    to_j = [(j, copy * HALF + j) for j in range(HALF) for copy in range(2)]
    return selection(2 * piece, 2 * LANES, to_i), selection(LANES, LANES, to_j)


def half_picks():
    count = HALF // 2
    to_i, to_j = [], []
    for odd in range(2):
        for n in range(count):
            to_i.append((n, odd * LANES + odd * HALF + count + n))
            to_j += [(odd * HALF + n, odd * LANES + copy * count + n) for copy in range(4)]
    return selection(count, 2 * LANES, to_i), selection(LANES, 2 * LANES, to_j)


def order_rows(traces, slots, kinds):
    rows, wins, samples = traces.shape
    tiles = samples // LANES
    piece = rows // BLOCKS
    step_wins = 16
    steps = wins // step_wins
    batch = 4
    used = max(kinds, key=len)
    pitch = len(used) * piece + 1

    def kernel(slots_ref, traces_ref, *refs):
        out_refs, (wide, in_ref, slot_ref, sems) = refs[:-4], refs[-4:]
        slot_copy = pltpu.make_async_copy(slots_ref, slot_ref, sems.at[steps])
        slot_copy.start()
        copies = []
        for step in range(steps):
            here = pl.ds(step * step_wins, step_wins)
            copies.append(
                pltpu.make_async_copy(traces_ref.at[:, here, :], in_ref.at[:, here, :], sems.at[step])
            )
            copies[-1].start()
        slot_copy.wait()
        z = lax.axis_index("chan")
        odd = lax.rem(z, 2)
        pair = jnp.where(z < 2, 2, 0)

        def some_windows(step):
            first_win = step * step_wins
            for at, position in enumerate(used):
                block = pair + position + (odd if position % 2 == 0 else -odd)
                first = lax.rem(block, BLOCKS) * piece

                def move(group, carry, at=at, first=first):
                    js = [group * batch + u for u in range(batch)]
                    picked = [
                        in_ref[slot_ref[first + j], pl.ds(first_win, step_wins), :].astype(jnp.float32) for j in js
                    ]
                    for j, row in zip(js, picked):
                        for tile in range(tiles):
                            wide[tile, pl.ds(at * piece + j, step_wins, stride=pitch), :] = row[
                                :, tile * LANES : (tile + 1) * LANES
                            ]
                    return carry

                lax.fori_loop(0, piece // batch, move, 0)

            def pack(w, carry):
                blocks = [
                    wide[tile, pl.ds(w * pitch, len(used) * piece), :].astype(jnp.bfloat16) for tile in range(tiles)
                ]
                for out_ref, kind in zip(out_refs, kinds):
                    first = used.index(kind[0]) * piece
                    for tile, block in enumerate(blocks):
                        out_ref[first_win + w, :, tile * LANES : (tile + 1) * LANES] = block[
                            first : first + len(kind) * piece
                        ]
                return carry

            lax.fori_loop(0, step_wins, pack, 0, unroll=2)

        for step in range(steps):
            copies[step].wait()
            some_windows(step)

    return kernel_call(
        kernel,
        "order_rows",
        0,
        3 * traces.size * 2,
        vmem_bytes=ORDER_VMEM_BYTES,
        out_shape=[jax.ShapeDtypeStruct((wins, len(kind) * piece, samples), jnp.bfloat16) for kind in kinds],
        in_specs=[pl.BlockSpec(memory_space=pltpu.HBM)] * 2,
        out_specs=[in_vmem()] * len(kinds),
        scratch_shapes=[
            pltpu.VMEM((tiles, (step_wins + 1) * pitch, LANES), jnp.float32),
            pltpu.VMEM(traces.shape, traces.dtype),
            pltpu.SMEM(slots.shape, slots.dtype),
            pltpu.SemaphoreType.DMA((steps + 1,)),
        ],
    )(slots, traces)


def diagonal(values, copies):
    blank = jnp.zeros_like(values)
    rows = [[values if at == copy else blank for at in range(copies)] for copy in range(copies)]
    return jnp.concatenate([jnp.concatenate(row, axis=1) for row in rows], axis=0)


def spectra(rows_j, rows_i, tables):
    wins, given, samples = rows_j.shape
    bins = samples // 2
    pairs = wins // 2
    depth = 2 * wins
    folded = HALF // given
    line = depth // folded
    pitch = line + 1
    per_step = 2 * folded
    batch = 8

    def kernel(j_ref, i_ref, table_ref, to_i_ref, to_j_ref, i_out, j_out, wide):
        same = lax.axis_index("sub") == lax.axis_index("rep")

        def spectrum_of(group):
            stacked = []
            for win in [per_step * group + u for u in range(per_step)]:
                here = j_ref[win]
                stacked += [here, jnp.where(same, here, i_ref[win])]
            wave = jnp.concatenate(stacked, axis=0)
            return lax.dot_general(table_ref[...], wave, NT, preferred_element_type=jnp.float32)

        def keep(group, spectrum):
            energy = jnp.sum(spectrum * spectrum, axis=0, keepdims=True) / bins
            white = spectrum * lax.rsqrt(energy + 1e-05)
            for half in range(2):
                for part in range(2):
                    if folded == 1:
                        row = half * wins + part * pairs + group
                    else:
                        row = part * pairs + 2 * group + half
                    wide[pl.ds(row, bins, stride=pitch), :] = white[
                        part * bins : (part + 1) * bins, half * LANES : (half + 1) * LANES
                    ]

        groups = wins // per_step
        at_once = 4

        def some_windows(step, carry):
            first = step * at_once
            last = spectrum_of(first)
            for group in range(1, at_once):
                now = spectrum_of(first + group)
                keep(first + group - 1, last)
                last = now
            keep(first + at_once - 1, last)
            return carry

        lax.fori_loop(0, groups // at_once, some_windows, 0)

        def moved(fs):
            loaded = [wide[pl.ds(f * pitch, line), :].astype(jnp.bfloat16) for f in fs]
            i_rows = [
                lax.dot_general(to_i_ref[...], diagonal(values, 2), NT, preferred_element_type=jnp.float32)
                for values in loaded
            ]
            if folded == 2:
                i_rows = [jnp.concatenate([rows[: given // 2], rows[given // 2 :]], axis=1) for rows in i_rows]
            j_rows = jnp.dot(jnp.concatenate(loaded, axis=0), to_j_ref[...], preferred_element_type=jnp.float32)
            return fs, i_rows, j_rows

        def store(fs, i_rows, j_rows):
            for at, f in enumerate(fs):
                i_out[f] = i_rows[at].astype(jnp.bfloat16)
                for odd in range(folded):
                    j_out[f, odd * line : (odd + 1) * line] = j_rows[
                        at * line : (at + 1) * line, odd * LANES : (odd + 1) * LANES
                    ].astype(jnp.bfloat16)

        def pack(group, carry):
            first = group * 4 * batch
            waiting = moved([first + u for u in range(batch)])
            for at in range(1, 4):
                following = moved([first + at * batch + u for u in range(batch)])
                store(*waiting)
                waiting = following
            store(*waiting)
            return carry

        lax.fori_loop(0, bins // (4 * batch), pack, 0)

    shapes = [(bins, given // 2, LANES), (bins, depth, LANES)]
    return kernel_call(
        kernel,
        "spectra",
        4 * samples * samples * wins * given,
        4 * wins * given * samples * 2,
        out_shape=[jax.ShapeDtypeStruct(shape, jnp.bfloat16) for shape in shapes],
        in_specs=[in_vmem()] * (2 + len(tables)),
        out_specs=[in_vmem()] * len(shapes),
        scratch_shapes=[pltpu.VMEM(((bins + 1) * pitch, LANES), jnp.float32)],
    )(rows_j, rows_i, *tables)


def partial_correlations(lefts, rights, tables, jobs, outs):
    left_arrays = [array for array, _ in lefts]
    right_arrays = [array for array, _, _ in rights]
    bins, depth, _ = right_arrays[0].shape
    piece = HALF // BLOCKS
    pitch = bins + 1
    step_bins = 32
    groups = []
    slices = {}
    for used, groups_here in jobs:
        js = [(rights[right][1], there) for right in used for there in rights[right][2]]
        for left, _, first in groups_here:
            found = []
            for offset in range(2):
                at = first + offset
                for order, (j_other, there) in enumerate(js):
                    if there != at:
                        kind = (lefts[left][1], j_other, there ^ (at % 2))
                        found.append((at, kind, offset * HALF + order * piece))
                        slices.setdefault(at, []).append(kind)
            groups.append(found)
    for kinds in slices.values():
        kinds.sort()
    total = len(groups) * piece
    batch = 4

    def first_of(at):
        (out,) = [positions for positions in outs if at in positions]
        return outs.index(out), sum(len(slices[before]) for before in out[: out.index(at)])

    def kernel(*refs):
        left_refs, rest = refs[: len(lefts)], refs[len(lefts) :]
        right_refs, rest = rest[: len(rights)], rest[len(rights) :]
        lag_ref, same_ref, out_refs, cross = rest[0], rest[1], rest[2:-1], rest[-1]
        lanes = lax.broadcasted_iota(jnp.int32, (depth, LANES), 1)

        first_half = lanes < HALF
        lower = lanes % HALF < HALF // 2
        blank = jnp.zeros((depth, LANES), jnp.bfloat16)

        def turn(values):
            swapped = []
            for first in range(0, depth, depth // 2):
                middle, last = first + depth // 4, first + depth // 2
                swapped += [-values[middle:last], values[first:middle]]
            return jnp.concatenate(swapped, axis=0)

        def right_hand(used, f):
            values = right_refs[used[0]][f]
            if len(used) == 2:
                values = jnp.where(lower, values, right_refs[used[1]][f])
            turned = turn(values)
            return jnp.concatenate(
                [
                    jnp.concatenate([jnp.where(first_half, part, blank) for part in (values, turned)], axis=1),
                    jnp.concatenate([jnp.where(first_half, blank, part) for part in (values, turned)], axis=1),
                ],
                axis=0,
            )

        def products(first_bin, count):
            found = []
            for f in [first_bin + u for u in range(count)]:
                first = 0
                for used, groups_here in jobs:
                    lhs = [left_refs[left][f, row : row + piece] for left, row, _ in groups_here]
                    lhs = jnp.concatenate(lhs, axis=0) if len(lhs) > 1 else lhs[0]
                    product = jnp.dot(lhs, right_hand(used, f), preferred_element_type=jnp.float32)
                    found.append((first * pitch + f, product))
                    first += lhs.shape[0]
            return found

        def keep(found):
            for here, product in found:
                for part in range(2):
                    cross[pl.ds(part * total * pitch + here, product.shape[0], stride=pitch), :] = product[
                        :, part * LANES : (part + 1) * LANES
                    ]

        def some_bins(step, carry):
            first = step * step_bins
            waiting = products(first, batch)
            for at in range(batch, step_bins, batch):
                following = products(first + at, batch)
                keep(waiting)
                waiting = following
            keep(waiting)
            return carry

        lax.fori_loop(0, bins // step_bins, some_bins, 0)

        for index, found in enumerate(groups):
            targets = []
            for at, kind, lane in found:
                out, first = first_of(at)
                targets.append((out_refs[out], first + slices[at].index(kind), lane))

            def summed(i):
                parts = []
                for part in range(2):
                    start = (part * total + index * piece + i) * pitch
                    parts.append(
                        jnp.concatenate([cross[pl.ds(start, bins), :], cross[pl.ds(start + pitch, bins), :]], axis=1)
                    )
                values = jnp.concatenate(parts, axis=0).astype(jnp.bfloat16)
                return i, jnp.dot(lag_ref[...], values, preferred_element_type=jnp.float32)

            def across(i, lagged):
                lagged = lagged.astype(jnp.bfloat16)
                return i, lax.dot_general(same_ref[...], lagged, NT, preferred_element_type=jnp.float32)

            def store(i, rows):
                for half in range(2):
                    for out, place, lane in targets:
                        row = half * LANES + lane
                        out[place, i + half] = rows[row : row + piece].astype(out.dtype)

            sums, rows = summed(0), None
            for i in range(2, piece, 2):
                more = summed(i)
                if rows is not None:
                    store(*rows)
                rows = across(*sums)
                sums = more
            store(*rows)
            store(*across(*sums))

    shapes = [(sum(len(slices[at]) for at in positions), piece, piece, LAGS) for positions in outs]
    types = [jnp.float32 if positions == (OWN_AT,) else jnp.bfloat16 for positions in outs]
    results = kernel_call(
        kernel,
        "partial_correlations",
        4 * total * bins * depth * LANES + 4 * total * bins * LANES * LAGS,
        2 * sum(array.size for array in left_arrays + right_arrays),
        out_shape=[jax.ShapeDtypeStruct(shape, kind) for shape, kind in zip(shapes, types)],
        in_specs=[in_vmem()] * (len(lefts) + len(rights) + len(tables)),
        out_specs=[in_vmem()] * len(shapes),
        scratch_shapes=[pltpu.VMEM(((2 * total + 1) * pitch, LANES), jnp.float32)],
    )(*left_arrays, *right_arrays, *tables)
    return results, slices


def assembled(shares):
    arrays = [array for array, _ in shares]
    _, piece, _, lags = arrays[0].shape
    width = 2 * piece

    def kernel(*refs):
        out, held, sems = refs[-3:]
        sub = lax.axis_index("sub")
        odd = lax.rem(lax.axis_index("chan"), 2)
        copies = []
        for there, round_at in ((0, 1), (1, 2 - 2 * odd), (3, 2 * odd)):
            for i_other in range(2):
                for j_other in range(2):
                    parts = [
                        refs[at][place].astype(jnp.float32)
                        for at, (_, kinds) in enumerate(shares)
                        for place, kind in enumerate(kinds)
                        if kind == (i_other, j_other, there)
                    ]
                    i_first = jnp.where(sub == 0, i_other, 1 - i_other) * piece
                    j_first = pl.multiple_of(jnp.where(sub == 0, j_other, 1 - j_other) * piece, piece)
                    held[round_at, 0, pl.ds(i_first, piece), pl.ds(j_first, piece), :] = functools.reduce(
                        jnp.add, parts
                    )
            at = len(copies)
            copies.append(pltpu.make_async_copy(held.at[round_at], out.at[round_at], sems.at[at]))
            copies[-1].start()
        for copy in copies:
            copy.wait()

    shape = (ROUNDS, 1, width, width, lags)
    return kernel_call(
        kernel,
        "assembled",
        0,
        sum(array.size for array in arrays) * 2,
        out_shape=jax.ShapeDtypeStruct(shape, jnp.float32),
        in_specs=[in_vmem()] * len(arrays),
        out_specs=pl.BlockSpec(memory_space=pl.ANY),
        scratch_shapes=[pltpu.VMEM(shape, jnp.float32), pltpu.SemaphoreType.DMA((ROUNDS,))],
    )(*arrays)


def summed_in_place(traces, channel_slot):
    chan_count = lax.axis_size("chan")
    _, win_here, samples = traces.shape
    piece = HALF // BLOCKS
    scale = (2.0 / (win_here * chan_count * (samples // 2))) ** 0.5
    dft_rows = dft_rows_table(samples)
    same = selection(2 * LANES, 2 * LANES, [(n, n) for n in range(2 * LANES)])
    tables = [lag_rows_table(samples, scale), same]
    everywhere = tuple(range(BLOCKS))

    def over_sub(rows):
        return lax.ppermute(rows, "sub", [(0, 1), (1, 0)])

    def over_core(rows):
        return lax.ppermute(rows, "rep", [(0, 1), (1, 0)])

    def with_device(share, apart):
        return lax.ppermute(share, "chan", [(z, z ^ apart) for z in range(chan_count)])

    def after(value, *others):
        return lax.optimization_barrier((value,) + others)[0]

    def added(share, arrived):
        return (share.astype(jnp.float32) + arrived.astype(jnp.float32)).astype(jnp.bfloat16)

    def for_two_away(kinds):
        return [(i_other, j_other, there ^ 2) for i_other, j_other, there in kinds]

    mine, mine_far, mine_near = order_rows(traces, channel_slot, [everywhere, FAR, NEAR])
    far = over_sub(mine_far)
    near = over_sub(mine_near)

    own_i, own_j = spectra(mine, over_core(mine), (dft_rows, *own_picks()))
    own_left, own_right = (own_i, 0), (own_j, 0, everywhere)
    own_far, own_near = (0, 0, FAR[0]), (0, piece, NEAR[0])
    (kept_1, sent_far_1, own_1, sent_near_1), kinds_1 = partial_correlations(
        [own_left], [own_right], tables, [((0,), [own_far, own_near])], [(0,), (1,), (2,), (3,)]
    )
    arrived_far_1 = with_device(sent_far_1, 1)

    far = after(far, kept_1, sent_far_1, own_1, sent_near_1)
    far_i, far_j = spectra(far, over_core(far), (dft_rows, *half_picks()))
    far_i, arrived_far_1 = lax.optimization_barrier((far_i, arrived_far_1))
    far_left, far_right = (far_i, 1), (far_j, 1, FAR)
    other_far = (1, 0, FAR[0])
    (kept_2, sent_far_2, own_2, sent_near_2), kinds_2 = partial_correlations(
        [own_left, far_left],
        [own_right, far_right],
        tables,
        [((0,), [other_far]), ((1,), [own_far, own_near, other_far])],
        [(0,), (1,), (2,), (3,)],
    )
    arrived_far_2 = with_device(sent_far_2, 1)

    near, arrived_far_2 = lax.optimization_barrier((near, arrived_far_2))
    near_i, near_j = spectra(near, over_core(near), (dft_rows, *half_picks()))
    summed_2 = added(kept_2, arrived_far_2)
    far_2 = with_device(summed_2, 2)
    summed_1 = added(after(kept_1, near_j), arrived_far_1)
    far_1 = with_device(summed_1, 2)
    near_j = after(near_j, summed_2)
    near_left, near_right = (near_i, 1), (near_j, 1, NEAR)
    (kept_3, sent_far_3, own_3, sent_near_3), kinds_3 = partial_correlations(
        [own_left, far_left],
        [near_right],
        tables,
        [((0,), [own_far, other_far, own_near])],
        [(0,), (1,), (2,), (3,)],
    )
    arrived_far_3 = with_device(sent_far_3, 1)
    arrived_near = with_device(jnp.concatenate([sent_near_1, sent_near_2]), 1)
    near_right = (after(near_j, kept_3, sent_far_3, far_2, summed_1), 1, NEAR)
    (own_4, sent_4), kinds_4 = partial_correlations(
        [near_left], [far_right, near_right], tables, [((0, 1), [(0, 0, NEAR[0])])], [(2,), (3,)]
    )
    arrived_4 = with_device(jnp.concatenate([sent_near_3, sent_4]), 1)
    summed_3 = added(after(kept_3, own_4), arrived_far_3)
    far_3 = with_device(summed_3, 2)
    near_left = (after(near_i, own_4, sent_4, summed_3, arrived_near, far_1), 1)
    (own_5, sent_5), kinds_5 = partial_correlations(
        [near_left], [own_right], tables, [((0,), [(0, 0, NEAR[0])])], [(2,), (3,)]
    )
    arrived_5 = with_device(sent_5, 1)
    shares = [
        (own_1, kinds_1[2]),
        (own_2, kinds_2[2]),
        (own_3, kinds_3[2]),
        (own_4, kinds_4[2]),
        (own_5, kinds_5[2]),
        (arrived_near, kinds_1[3] + kinds_2[3]),
        (arrived_4, kinds_3[3] + kinds_4[3]),
        (arrived_5, kinds_5[3]),
        (far_1, for_two_away(kinds_1[0])),
        (far_2, for_two_away(kinds_2[0])),
        (far_3, for_two_away(kinds_3[0])),
    ]
    return assembled(shares)


def from_behind(shard, axis, by):
    count = lax.axis_size(axis)
    return lax.ppermute(shard, axis, [(i, (i + by) % count) for i in range(count)])


def dft_columns(samples, parts, sub_bins):
    shape = (samples, parts, 2, sub_bins)
    time_pos = lax.broadcasted_iota(jnp.int32, shape, 0)
    range_pos = lax.broadcasted_iota(jnp.int32, shape, 1)
    part_pos = lax.broadcasted_iota(jnp.int32, shape, 2)
    bin_pos = lax.broadcasted_iota(jnp.int32, shape, 3)
    frequency = range_pos * sub_bins + bin_pos
    angles = jnp.mod(time_pos * frequency, samples).astype(jnp.float32) * (2.0 * math.pi / samples)
    entries = jnp.where(part_pos == 0, jnp.cos(angles), -jnp.sin(angles))
    return entries.reshape(samples, parts * 2 * sub_bins).astype(jnp.bfloat16)


def lag_table(sub_bins, first_bin, lag_count, samples):
    frequency = first_bin + lax.broadcasted_iota(jnp.int32, (sub_bins, lag_count), 0)
    lag_offset = lax.broadcasted_iota(jnp.int32, (sub_bins, lag_count), 1) - lag_count // 2
    angles = jnp.mod(frequency * lag_offset, samples).astype(jnp.float32) * (2.0 * math.pi / samples)
    return jnp.stack([jnp.cos(angles), -jnp.sin(angles)], axis=1)


def moved_spectra(traces, channel_slot):
    chan_count = lax.axis_size("chan")
    sub_count = lax.axis_size("sub")
    group_rows, win_here, samples = traces.shape
    bin_count = samples // 2
    sub_bins = bin_count // sub_count
    bin_width = 2 * sub_bins
    piece_len = group_rows // chan_count
    picked = jnp.take(traces, channel_slot, axis=0)
    dft_rows = dft_columns(samples, sub_count, sub_bins)
    spectrum = jnp.dot(picked.reshape(-1, samples), dft_rows, preferred_element_type=jnp.float32)
    energy = jnp.sum(spectrum * spectrum, axis=1, keepdims=True) / bin_count
    whitened = (spectrum * lax.rsqrt(energy + 1e-05)).astype(jnp.bfloat16)
    whitened = whitened.reshape(chan_count, piece_len, win_here, sub_count, bin_width)
    regrouped = lax.all_to_all(whitened, "chan", split_axis=0, concat_axis=0, tiled=True)
    regrouped = lax.all_to_all(regrouped, "sub", split_axis=3, concat_axis=3, tiled=True)
    own_half = regrouped.transpose(3, 1, 0, 2, 4).reshape(sub_count * piece_len, chan_count * win_here, bin_width)
    own_block = lax.all_gather(own_half, "rep", axis=0, tiled=True)
    windows = own_block.shape[1]
    own_split = own_block.reshape(own_block.shape[0], windows, 2, sub_bins)
    lag_rows = lag_table(sub_bins, lax.axis_index("sub") * sub_bins, LAGS, samples)
    lag_scale = (2.0 / (windows * bin_count)) ** 0.5
    results = []
    for step in range(1, ROUNDS + 1):
        partner = from_behind(own_half, "chan", -step)
        partner_split = partner.reshape(partner.shape[0], windows, 2, sub_bins)
        turned = jnp.stack([-partner_split[:, :, 1], partner_split[:, :, 0]], axis=2)
        partner_pair = jnp.stack([partner_split, turned], axis=0)
        cross_spec = jnp.einsum("iwpf,qjwpf->fqij", own_split, partner_pair, preferred_element_type=jnp.float32)
        summed = jnp.einsum("fqij,fql->ijl", cross_spec, lag_rows, precision=lax.Precision.HIGHEST)
        results.append(lax.psum_scatter(lag_scale * summed, "sub", scatter_dimension=0, tiled=True))
    return jnp.stack(results)[:, None]


def solution(mesh):
    sizes = mesh.shape
    in_place = sizes["chan"] == BLOCKS == ROUNDS + 1 and sizes["sub"] == 2 and sizes["rep"] == 2
    return jax.shard_map(
        summed_in_place if in_place else moved_spectra,
        mesh=mesh,
        in_specs=(P(("groups", "sub", "rep"), "chan", None), P(("groups", "sub", "rep"))),
        out_specs=P(None, ("groups", "chan"), "sub", "rep", None),
        check_vma=False,
    )
```

```python
import functools
import math

import jax
import jax.numpy as jnp
import numpy as np
from jax import lax
from jax.experimental import pallas as pl
from jax.experimental.pallas import tpu as pltpu
from jax.sharding import PartitionSpec as P

LAGS = 128
ROUNDS = 3
LANES = 128
HALF = LANES // 2
VMEM_BYTES = 32 * 1024 * 1024
ORDER_VMEM_BYTES = 48 * 1024 * 1024
NT = (((1,), (1,)), ((), ()))
BLOCKS = 4
FAR = (0, 1)
NEAR = (2, 3)
KEPT_AT, OWN_AT = 0, 2


def kernel_call(kernel, name, flops, bytes_accessed, vmem_bytes=VMEM_BYTES, **more):
    return pl.pallas_call(
        kernel,
        name=name,
        compiler_params=pltpu.CompilerParams(vmem_limit_bytes=vmem_bytes),
        cost_estimate=pl.CostEstimate(flops=flops, bytes_accessed=bytes_accessed, transcendentals=0),
        **more,
    )


def in_vmem():
    return pl.BlockSpec(memory_space=pltpu.VMEM)


def dft_rows_table(samples):
    bins = samples // 2
    turns = (np.arange(bins)[:, None] * np.arange(samples)[None, :]) % samples
    angles = turns.astype(np.float32) * np.float32(2.0 * math.pi / samples)
    table = np.concatenate([np.cos(angles), -np.sin(angles)], axis=0)
    return jnp.asarray(table.astype(np.float32)).astype(jnp.bfloat16)


def lag_rows_table(samples, scale):
    bins = samples // 2
    offsets = np.arange(LAGS) - LAGS // 2
    turns = (offsets[:, None] * np.arange(bins)[None, :]) % samples
    angles = turns.astype(np.float32) * np.float32(2.0 * math.pi / samples)
    table = np.concatenate([np.cos(angles), -np.sin(angles)], axis=1) * np.float32(scale)
    return jnp.asarray(table.astype(np.float32)).astype(jnp.bfloat16)


def selection(rows, columns, ones):
    table = np.zeros((rows, columns), np.float32)
    for row, column in ones:
        table[row, column] = 1.0
    return jnp.asarray(table).astype(jnp.bfloat16)


def own_picks():
    piece = HALF // BLOCKS
    to_i = []
    for at in range(BLOCKS):
        for n in range(piece):
            to_i.append((at // 2 * piece + n, at % 2 * LANES + HALF + at * piece + n))
    to_j = [(j, copy * HALF + j) for j in range(HALF) for copy in range(2)]
    return selection(2 * piece, 2 * LANES, to_i), selection(LANES, LANES, to_j)


def half_picks():
    count = HALF // 2
    to_i, to_j = [], []
    for odd in range(2):
        for n in range(count):
            to_i.append((n, odd * LANES + odd * HALF + count + n))
            to_j += [(odd * HALF + n, odd * LANES + copy * count + n) for copy in range(4)]
    return selection(count, 2 * LANES, to_i), selection(LANES, 2 * LANES, to_j)


def order_rows(traces, slots, kinds):
    rows, wins, samples = traces.shape
    tiles = samples // LANES
    piece = rows // BLOCKS
    step_wins = 16
    steps = wins // step_wins
    batch = 4
    used = max(kinds, key=len)
    pitch = len(used) * piece + 1

    def kernel(slots_ref, traces_ref, *refs):
        out_refs, (wide, in_ref, slot_ref, sems) = refs[:-4], refs[-4:]
        slot_copy = pltpu.make_async_copy(slots_ref, slot_ref, sems.at[steps])
        slot_copy.start()
        copies = []
        for step in range(steps):
            here = pl.ds(step * step_wins, step_wins)
            copies.append(
                pltpu.make_async_copy(traces_ref.at[:, here, :], in_ref.at[:, here, :], sems.at[step])
            )
            copies[-1].start()
        slot_copy.wait()
        z = lax.axis_index("chan")
        odd = lax.rem(z, 2)
        pair = jnp.where(z < 2, 2, 0)

        def some_windows(step):
            first_win = step * step_wins
            for at, position in enumerate(used):
                block = pair + position + (odd if position % 2 == 0 else -odd)
                first = lax.rem(block, BLOCKS) * piece

                def move(group, carry, at=at, first=first):
                    js = [group * batch + u for u in range(batch)]
                    picked = [
                        in_ref[slot_ref[first + j], pl.ds(first_win, step_wins), :].astype(jnp.float32) for j in js
                    ]
                    for j, row in zip(js, picked):
                        for tile in range(tiles):
                            wide[tile, pl.ds(at * piece + j, step_wins, stride=pitch), :] = row[
                                :, tile * LANES : (tile + 1) * LANES
                            ]
                    return carry

                lax.fori_loop(0, piece // batch, move, 0)

            def pack(w, carry):
                blocks = [
                    wide[tile, pl.ds(w * pitch, len(used) * piece), :].astype(jnp.bfloat16) for tile in range(tiles)
                ]
                for out_ref, kind in zip(out_refs, kinds):
                    first = used.index(kind[0]) * piece
                    for tile, block in enumerate(blocks):
                        out_ref[first_win + w, :, tile * LANES : (tile + 1) * LANES] = block[
                            first : first + len(kind) * piece
                        ]
                return carry

            lax.fori_loop(0, step_wins, pack, 0, unroll=2)

        for step in range(steps):
            copies[step].wait()
            some_windows(step)

    return kernel_call(
        kernel,
        "order_rows",
        0,
        3 * traces.size * 2,
        vmem_bytes=ORDER_VMEM_BYTES,
        out_shape=[jax.ShapeDtypeStruct((wins, len(kind) * piece, samples), jnp.bfloat16) for kind in kinds],
        in_specs=[pl.BlockSpec(memory_space=pltpu.HBM)] * 2,
        out_specs=[in_vmem()] * len(kinds),
        scratch_shapes=[
            pltpu.VMEM((tiles, (step_wins + 1) * pitch, LANES), jnp.float32),
            pltpu.VMEM(traces.shape, traces.dtype),
            pltpu.SMEM(slots.shape, slots.dtype),
            pltpu.SemaphoreType.DMA((steps + 1,)),
        ],
    )(slots, traces)


def diagonal(values, copies):
    blank = jnp.zeros_like(values)
    rows = [[values if at == copy else blank for at in range(copies)] for copy in range(copies)]
    return jnp.concatenate([jnp.concatenate(row, axis=1) for row in rows], axis=0)


def spectra(rows_j, rows_i, tables):
    wins, given, samples = rows_j.shape
    bins = samples // 2
    pairs = wins // 2
    depth = 2 * wins
    folded = HALF // given
    line = depth // folded
    pitch = line + 1
    per_step = 2 * folded
    batch = 8

    def kernel(j_ref, i_ref, table_ref, to_i_ref, to_j_ref, i_out, j_out, wide):
        same = lax.axis_index("sub") == lax.axis_index("rep")

        def spectrum_of(group):
            stacked = []
            for win in [per_step * group + u for u in range(per_step)]:
                here = j_ref[win]
                stacked += [here, jnp.where(same, here, i_ref[win])]
            wave = jnp.concatenate(stacked, axis=0)
            return lax.dot_general(table_ref[...], wave, NT, preferred_element_type=jnp.float32)

        def keep(group, spectrum):
            energy = jnp.sum(spectrum * spectrum, axis=0, keepdims=True) / bins
            white = spectrum * lax.rsqrt(energy + 1e-05)
            for half in range(2):
                for part in range(2):
                    if folded == 1:
                        row = half * wins + part * pairs + group
                    else:
                        row = part * pairs + 2 * group + half
                    wide[pl.ds(row, bins, stride=pitch), :] = white[
                        part * bins : (part + 1) * bins, half * LANES : (half + 1) * LANES
                    ]

        groups = wins // per_step
        at_once = 4

        def some_windows(step, carry):
            first = step * at_once
            last = spectrum_of(first)
            for group in range(1, at_once):
                now = spectrum_of(first + group)
                keep(first + group - 1, last)
                last = now
            keep(first + at_once - 1, last)
            return carry

        lax.fori_loop(0, groups // at_once, some_windows, 0)

        def moved(fs):
            loaded = [wide[pl.ds(f * pitch, line), :].astype(jnp.bfloat16) for f in fs]
            i_rows = [
                lax.dot_general(to_i_ref[...], diagonal(values, 2), NT, preferred_element_type=jnp.float32)
                for values in loaded
            ]
            if folded == 2:
                i_rows = [jnp.concatenate([rows[: given // 2], rows[given // 2 :]], axis=1) for rows in i_rows]
            j_rows = jnp.dot(jnp.concatenate(loaded, axis=0), to_j_ref[...], preferred_element_type=jnp.float32)
            return fs, i_rows, j_rows

        def store(fs, i_rows, j_rows):
            for at, f in enumerate(fs):
                i_out[f] = i_rows[at].astype(jnp.bfloat16)
                for odd in range(folded):
                    j_out[f, odd * line : (odd + 1) * line] = j_rows[
                        at * line : (at + 1) * line, odd * LANES : (odd + 1) * LANES
                    ].astype(jnp.bfloat16)

        def pack(group, carry):
            first = group * 4 * batch
            waiting = moved([first + u for u in range(batch)])
            for at in range(1, 4):
                following = moved([first + at * batch + u for u in range(batch)])
                store(*waiting)
                waiting = following
            store(*waiting)
            return carry

        lax.fori_loop(0, bins // (4 * batch), pack, 0)

    shapes = [(bins, given // 2, LANES), (bins, depth, LANES)]
    return kernel_call(
        kernel,
        "spectra",
        4 * samples * samples * wins * given,
        4 * wins * given * samples * 2,
        out_shape=[jax.ShapeDtypeStruct(shape, jnp.bfloat16) for shape in shapes],
        in_specs=[in_vmem()] * (2 + len(tables)),
        out_specs=[in_vmem()] * len(shapes),
        scratch_shapes=[pltpu.VMEM(((bins + 1) * pitch, LANES), jnp.float32)],
    )(rows_j, rows_i, *tables)


def partial_correlations(lefts, rights, tables, jobs, outs):
    left_arrays = [array for array, _ in lefts]
    right_arrays = [array for array, _, _ in rights]
    bins, depth, _ = right_arrays[0].shape
    piece = HALF // BLOCKS
    pitch = bins + 1
    step_bins = 32
    groups = []
    slices = {}
    for used, groups_here in jobs:
        js = [(rights[right][1], there) for right in used for there in rights[right][2]]
        for left, _, first in groups_here:
            found = []
            for offset in range(2):
                at = first + offset
                for order, (j_other, there) in enumerate(js):
                    if there != at:
                        kind = (lefts[left][1], j_other, there ^ (at % 2))
                        found.append((at, kind, offset * HALF + order * piece))
                        slices.setdefault(at, []).append(kind)
            groups.append(found)
    for kinds in slices.values():
        kinds.sort()
    total = len(groups) * piece
    batch = 4

    def first_of(at):
        (out,) = [positions for positions in outs if at in positions]
        return outs.index(out), sum(len(slices[before]) for before in out[: out.index(at)])

    def kernel(*refs):
        left_refs, rest = refs[: len(lefts)], refs[len(lefts) :]
        right_refs, rest = rest[: len(rights)], rest[len(rights) :]
        lag_ref, same_ref, out_refs, cross = rest[0], rest[1], rest[2:-1], rest[-1]
        lanes = lax.broadcasted_iota(jnp.int32, (depth, LANES), 1)

        first_half = lanes < HALF
        lower = lanes % HALF < HALF // 2
        blank = jnp.zeros((depth, LANES), jnp.bfloat16)

        def turn(values):
            swapped = []
            for first in range(0, depth, depth // 2):
                middle, last = first + depth // 4, first + depth // 2
                swapped += [-values[middle:last], values[first:middle]]
            return jnp.concatenate(swapped, axis=0)

        def right_hand(used, f):
            values = right_refs[used[0]][f]
            if len(used) == 2:
                values = jnp.where(lower, values, right_refs[used[1]][f])
            turned = turn(values)
            return jnp.concatenate(
                [
                    jnp.concatenate([jnp.where(first_half, part, blank) for part in (values, turned)], axis=1),
                    jnp.concatenate([jnp.where(first_half, blank, part) for part in (values, turned)], axis=1),
                ],
                axis=0,
            )

        def products(first_bin, count):
            found = []
            for f in [first_bin + u for u in range(count)]:
                first = 0
                for used, groups_here in jobs:
                    lhs = [left_refs[left][f, row : row + piece] for left, row, _ in groups_here]
                    lhs = jnp.concatenate(lhs, axis=0) if len(lhs) > 1 else lhs[0]
                    product = jnp.dot(lhs, right_hand(used, f), preferred_element_type=jnp.float32)
                    found.append((first * pitch + f, product))
                    first += lhs.shape[0]
            return found

        def keep(found):
            for here, product in found:
                for part in range(2):
                    cross[pl.ds(part * total * pitch + here, product.shape[0], stride=pitch), :] = product[
                        :, part * LANES : (part + 1) * LANES
                    ]

        def some_bins(step, carry):
            first = step * step_bins
            waiting = products(first, batch)
            for at in range(batch, step_bins, batch):
                following = products(first + at, batch)
                keep(waiting)
                waiting = following
            keep(waiting)
            return carry

        lax.fori_loop(0, bins // step_bins, some_bins, 0)

        for index, found in enumerate(groups):
            targets = []
            for at, kind, lane in found:
                out, first = first_of(at)
                targets.append((out_refs[out], first + slices[at].index(kind), lane))

            def summed(i):
                parts = []
                for part in range(2):
                    start = (part * total + index * piece + i) * pitch
                    parts.append(
                        jnp.concatenate([cross[pl.ds(start, bins), :], cross[pl.ds(start + pitch, bins), :]], axis=1)
                    )
                values = jnp.concatenate(parts, axis=0).astype(jnp.bfloat16)
                return i, jnp.dot(lag_ref[...], values, preferred_element_type=jnp.float32)

            def across(i, lagged):
                lagged = lagged.astype(jnp.bfloat16)
                return i, lax.dot_general(same_ref[...], lagged, NT, preferred_element_type=jnp.float32)

            def store(i, rows):
                for half in range(2):
                    for out, place, lane in targets:
                        row = half * LANES + lane
                        out[place, i + half] = rows[row : row + piece].astype(out.dtype)

            sums, rows = summed(0), None
            for i in range(2, piece, 2):
                more = summed(i)
                if rows is not None:
                    store(*rows)
                rows = across(*sums)
                sums = more
            store(*rows)
            store(*across(*sums))

    shapes = [(sum(len(slices[at]) for at in positions), piece, piece, LAGS) for positions in outs]
    types = [jnp.float32 if positions == (OWN_AT,) else jnp.bfloat16 for positions in outs]
    results = kernel_call(
        kernel,
        "partial_correlations",
        4 * total * bins * depth * LANES + 4 * total * bins * LANES * LAGS,
        2 * sum(array.size for array in left_arrays + right_arrays),
        out_shape=[jax.ShapeDtypeStruct(shape, kind) for shape, kind in zip(shapes, types)],
        in_specs=[in_vmem()] * (len(lefts) + len(rights) + len(tables)),
        out_specs=[in_vmem()] * len(shapes),
        scratch_shapes=[pltpu.VMEM(((2 * total + 1) * pitch, LANES), jnp.float32)],
    )(*left_arrays, *right_arrays, *tables)
    return results, slices


def assembled(shares):
    arrays = [array for array, _ in shares]
    _, piece, _, lags = arrays[0].shape
    width = 2 * piece

    def kernel(*refs):
        out, held, sems = refs[-3:]
        sub = lax.axis_index("sub")
        odd = lax.rem(lax.axis_index("chan"), 2)
        copies = []
        for there, round_at in ((0, 1), (1, 2 - 2 * odd), (3, 2 * odd)):
            for i_other in range(2):
                for j_other in range(2):
                    parts = [
                        refs[at][place].astype(jnp.float32)
                        for at, (_, kinds) in enumerate(shares)
                        for place, kind in enumerate(kinds)
                        if kind == (i_other, j_other, there)
                    ]
                    i_first = jnp.where(sub == 0, i_other, 1 - i_other) * piece
                    j_first = pl.multiple_of(jnp.where(sub == 0, j_other, 1 - j_other) * piece, piece)
                    held[round_at, 0, pl.ds(i_first, piece), pl.ds(j_first, piece), :] = functools.reduce(
                        jnp.add, parts
                    )
            at = len(copies)
            copies.append(pltpu.make_async_copy(held.at[round_at], out.at[round_at], sems.at[at]))
            copies[-1].start()
        for copy in copies:
            copy.wait()

    shape = (ROUNDS, 1, width, width, lags)
    return kernel_call(
        kernel,
        "assembled",
        0,
        sum(array.size for array in arrays) * 2,
        out_shape=jax.ShapeDtypeStruct(shape, jnp.float32),
        in_specs=[in_vmem()] * len(arrays),
        out_specs=pl.BlockSpec(memory_space=pl.ANY),
        scratch_shapes=[pltpu.VMEM(shape, jnp.float32), pltpu.SemaphoreType.DMA((ROUNDS,))],
    )(*arrays)


def summed_in_place(traces, channel_slot):
    chan_count = lax.axis_size("chan")
    _, win_here, samples = traces.shape
    piece = HALF // BLOCKS
    scale = (2.0 / (win_here * chan_count * (samples // 2))) ** 0.5
    dft_rows = dft_rows_table(samples)
    same = selection(2 * LANES, 2 * LANES, [(n, n) for n in range(2 * LANES)])
    tables = [lag_rows_table(samples, scale), same]
    everywhere = tuple(range(BLOCKS))

    def over_sub(rows):
        return lax.ppermute(rows, "sub", [(0, 1), (1, 0)])

    def over_core(rows):
        return lax.ppermute(rows, "rep", [(0, 1), (1, 0)])

    def with_device(share, apart):
        return lax.ppermute(share, "chan", [(z, z ^ apart) for z in range(chan_count)])

    def after(value, *others):
        return lax.optimization_barrier((value,) + others)[0]

    def added(share, arrived):
        return (share.astype(jnp.float32) + arrived.astype(jnp.float32)).astype(jnp.bfloat16)

    def for_two_away(kinds):
        return [(i_other, j_other, there ^ 2) for i_other, j_other, there in kinds]

    mine, mine_far, mine_near = order_rows(traces, channel_slot, [everywhere, FAR, NEAR])
    far = over_sub(mine_far)
    near = over_sub(mine_near)

    own_i, own_j = spectra(mine, over_core(mine), (dft_rows, *own_picks()))
    own_left, own_right = (own_i, 0), (own_j, 0, everywhere)
    own_far, own_near = (0, 0, FAR[0]), (0, piece, NEAR[0])
    (kept_1, own_1, sent_1), kinds_1 = partial_correlations(
        [own_left], [own_right], tables, [((0,), [own_far, own_near])], [(0,), (2,), (1, 3)]
    )
    arrived_1 = with_device(sent_1, 1)

    far = after(far, kept_1, own_1, sent_1)
    far_i, far_j = spectra(far, over_core(far), (dft_rows, *half_picks()))
    far_left, far_right = (far_i, 1), (far_j, 1, FAR)
    other_far = (1, 0, FAR[0])
    (kept_2, sent_far_2, own_2, sent_near_2), kinds_2 = partial_correlations(
        [own_left, far_left],
        [own_right, far_right],
        tables,
        [((0,), [other_far]), ((1,), [own_far, own_near, other_far])],
        [(0,), (1,), (2,), (3,)],
    )
    arrived_far_2 = with_device(sent_far_2, 1)

    near, arrived_far_2, arrived_1 = lax.optimization_barrier((near, arrived_far_2, arrived_1))
    near_i, near_j = spectra(near, over_core(near), (dft_rows, *half_picks()))
    summed_2 = added(kept_2, arrived_far_2)
    far_2 = with_device(summed_2, 2)
    far_count_1 = kept_1.shape[0]
    summed_1 = added(after(kept_1, near_j), arrived_1[:far_count_1])
    far_1 = with_device(summed_1, 2)
    near_j = after(near_j, summed_2)
    near_left, near_right = (near_i, 1), (near_j, 1, NEAR)
    (kept_3, sent_far_3, own_3, sent_near_3), kinds_3 = partial_correlations(
        [own_left, far_left],
        [near_right],
        tables,
        [((0,), [own_far, other_far, own_near])],
        [(0,), (1,), (2,), (3,)],
    )
    arrived_far_3 = with_device(sent_far_3, 1)
    arrived_near_2 = with_device(sent_near_2, 1)
    near_right = (after(near_j, kept_3, sent_far_3, far_2, summed_1, arrived_near_2), 1, NEAR)
    (own_4, sent_4), kinds_4 = partial_correlations(
        [near_left], [far_right, near_right], tables, [((0, 1), [(0, 0, NEAR[0])])], [(2,), (3,)]
    )
    arrived_4 = with_device(jnp.concatenate([sent_near_3, sent_4]), 1)
    summed_3 = added(after(kept_3, own_4), arrived_far_3)
    far_3 = with_device(summed_3, 2)
    near_left = (after(near_i, own_4, sent_4, summed_3, far_1), 1)
    (own_5, sent_5), kinds_5 = partial_correlations(
        [near_left], [own_right], tables, [((0,), [(0, 0, NEAR[0])])], [(2,), (3,)]
    )
    arrived_5 = with_device(sent_5, 1)
    shares = [
        (own_1, kinds_1[2]),
        (own_2, kinds_2[2]),
        (own_3, kinds_3[2]),
        (own_4, kinds_4[2]),
        (own_5, kinds_5[2]),
        (arrived_1, [None] * far_count_1 + kinds_1[3]),
        (arrived_near_2, kinds_2[3]),
        (arrived_4, kinds_3[3] + kinds_4[3]),
        (arrived_5, kinds_5[3]),
        (far_1, for_two_away(kinds_1[0])),
        (far_2, for_two_away(kinds_2[0])),
        (far_3, for_two_away(kinds_3[0])),
    ]
    return assembled(shares)


def from_behind(shard, axis, by):
    count = lax.axis_size(axis)
    return lax.ppermute(shard, axis, [(i, (i + by) % count) for i in range(count)])


def dft_columns(samples, parts, sub_bins):
    shape = (samples, parts, 2, sub_bins)
    time_pos = lax.broadcasted_iota(jnp.int32, shape, 0)
    range_pos = lax.broadcasted_iota(jnp.int32, shape, 1)
    part_pos = lax.broadcasted_iota(jnp.int32, shape, 2)
    bin_pos = lax.broadcasted_iota(jnp.int32, shape, 3)
    frequency = range_pos * sub_bins + bin_pos
    angles = jnp.mod(time_pos * frequency, samples).astype(jnp.float32) * (2.0 * math.pi / samples)
    entries = jnp.where(part_pos == 0, jnp.cos(angles), -jnp.sin(angles))
    return entries.reshape(samples, parts * 2 * sub_bins).astype(jnp.bfloat16)


def lag_table(sub_bins, first_bin, lag_count, samples):
    frequency = first_bin + lax.broadcasted_iota(jnp.int32, (sub_bins, lag_count), 0)
    lag_offset = lax.broadcasted_iota(jnp.int32, (sub_bins, lag_count), 1) - lag_count // 2
    angles = jnp.mod(frequency * lag_offset, samples).astype(jnp.float32) * (2.0 * math.pi / samples)
    return jnp.stack([jnp.cos(angles), -jnp.sin(angles)], axis=1)


def moved_spectra(traces, channel_slot):
    chan_count = lax.axis_size("chan")
    sub_count = lax.axis_size("sub")
    group_rows, win_here, samples = traces.shape
    bin_count = samples // 2
    sub_bins = bin_count // sub_count
    bin_width = 2 * sub_bins
    piece_len = group_rows // chan_count
    picked = jnp.take(traces, channel_slot, axis=0)
    dft_rows = dft_columns(samples, sub_count, sub_bins)
    spectrum = jnp.dot(picked.reshape(-1, samples), dft_rows, preferred_element_type=jnp.float32)
    energy = jnp.sum(spectrum * spectrum, axis=1, keepdims=True) / bin_count
    whitened = (spectrum * lax.rsqrt(energy + 1e-05)).astype(jnp.bfloat16)
    whitened = whitened.reshape(chan_count, piece_len, win_here, sub_count, bin_width)
    regrouped = lax.all_to_all(whitened, "chan", split_axis=0, concat_axis=0, tiled=True)
    regrouped = lax.all_to_all(regrouped, "sub", split_axis=3, concat_axis=3, tiled=True)
    own_half = regrouped.transpose(3, 1, 0, 2, 4).reshape(sub_count * piece_len, chan_count * win_here, bin_width)
    own_block = lax.all_gather(own_half, "rep", axis=0, tiled=True)
    windows = own_block.shape[1]
    own_split = own_block.reshape(own_block.shape[0], windows, 2, sub_bins)
    lag_rows = lag_table(sub_bins, lax.axis_index("sub") * sub_bins, LAGS, samples)
    lag_scale = (2.0 / (windows * bin_count)) ** 0.5
    results = []
    for step in range(1, ROUNDS + 1):
        partner = from_behind(own_half, "chan", -step)
        partner_split = partner.reshape(partner.shape[0], windows, 2, sub_bins)
        turned = jnp.stack([-partner_split[:, :, 1], partner_split[:, :, 0]], axis=2)
        partner_pair = jnp.stack([partner_split, turned], axis=0)
        cross_spec = jnp.einsum("iwpf,qjwpf->fqij", own_split, partner_pair, preferred_element_type=jnp.float32)
        summed = jnp.einsum("fqij,fql->ijl", cross_spec, lag_rows, precision=lax.Precision.HIGHEST)
        results.append(lax.psum_scatter(lag_scale * summed, "sub", scatter_dimension=0, tiled=True))
    return jnp.stack(results)[:, None]


def solution(mesh):
    sizes = mesh.shape
    in_place = sizes["chan"] == BLOCKS == ROUNDS + 1 and sizes["sub"] == 2 and sizes["rep"] == 2
    return jax.shard_map(
        summed_in_place if in_place else moved_spectra,
        mesh=mesh,
        in_specs=(P(("groups", "sub", "rep"), "chan", None), P(("groups", "sub", "rep"))),
        out_specs=P(None, ("groups", "chan"), "sub", "rep", None),
        check_vma=False,
    )
```

```python
import functools
import math

import jax
import jax.numpy as jnp
import numpy as np
from jax import lax
from jax.experimental import pallas as pl
from jax.experimental.pallas import tpu as pltpu
from jax.sharding import PartitionSpec as P

LAGS = 128
ROUNDS = 3
LANES = 128
HALF = LANES // 2
VMEM_BYTES = 32 * 1024 * 1024
ORDER_VMEM_BYTES = 48 * 1024 * 1024
NT = (((1,), (1,)), ((), ()))
BLOCKS = 4
FAR = (0, 1)
NEAR = (2, 3)
KEPT_AT, OWN_AT = 0, 2


def kernel_call(kernel, name, flops, bytes_accessed, vmem_bytes=VMEM_BYTES, **more):
    return pl.pallas_call(
        kernel,
        name=name,
        compiler_params=pltpu.CompilerParams(vmem_limit_bytes=vmem_bytes),
        cost_estimate=pl.CostEstimate(flops=flops, bytes_accessed=bytes_accessed, transcendentals=0),
        **more,
    )


def in_vmem():
    return pl.BlockSpec(memory_space=pltpu.VMEM)


def dft_rows_table(samples):
    bins = samples // 2
    turns = (np.arange(bins)[:, None] * np.arange(samples)[None, :]) % samples
    angles = turns.astype(np.float32) * np.float32(2.0 * math.pi / samples)
    table = np.concatenate([np.cos(angles), -np.sin(angles)], axis=0)
    return jnp.asarray(table.astype(np.float32)).astype(jnp.bfloat16)


def lag_rows_table(samples, scale):
    bins = samples // 2
    offsets = np.arange(LAGS) - LAGS // 2
    turns = (offsets[:, None] * np.arange(bins)[None, :]) % samples
    angles = turns.astype(np.float32) * np.float32(2.0 * math.pi / samples)
    table = np.concatenate([np.cos(angles), -np.sin(angles)], axis=1) * np.float32(scale)
    return jnp.asarray(table.astype(np.float32)).astype(jnp.bfloat16)


def selection(rows, columns, ones):
    table = np.zeros((rows, columns), np.float32)
    for row, column in ones:
        table[row, column] = 1.0
    return jnp.asarray(table).astype(jnp.bfloat16)


def own_picks():
    piece = HALF // BLOCKS
    to_i = []
    for at in range(BLOCKS):
        for n in range(piece):
            to_i.append((at // 2 * piece + n, at % 2 * LANES + HALF + at * piece + n))
    to_j = [(j, copy * HALF + j) for j in range(HALF) for copy in range(2)]
    return selection(2 * piece, 2 * LANES, to_i), selection(LANES, LANES, to_j)


def half_picks():
    count = HALF // 2
    to_i, to_j = [], []
    for odd in range(2):
        for n in range(count):
            to_i.append((n, odd * LANES + odd * HALF + count + n))
            to_j += [(odd * HALF + n, odd * LANES + copy * count + n) for copy in range(4)]
    return selection(count, 2 * LANES, to_i), selection(LANES, 2 * LANES, to_j)


def order_rows(traces, slots, kinds):
    rows, wins, samples = traces.shape
    tiles = samples // LANES
    piece = rows // BLOCKS
    step_wins = 16
    steps = wins // step_wins
    batch = 4
    used = max(kinds, key=len)
    pitch = len(used) * piece + 1

    def kernel(slots_ref, traces_ref, *refs):
        out_refs, (wide, in_ref, slot_ref, sems) = refs[:-4], refs[-4:]
        slot_copy = pltpu.make_async_copy(slots_ref, slot_ref, sems.at[steps])
        slot_copy.start()
        copies = []
        for step in range(steps):
            here = pl.ds(step * step_wins, step_wins)
            copies.append(
                pltpu.make_async_copy(traces_ref.at[:, here, :], in_ref.at[:, here, :], sems.at[step])
            )
            copies[-1].start()
        slot_copy.wait()
        z = lax.axis_index("chan")
        odd = lax.rem(z, 2)
        pair = jnp.where(z < 2, 2, 0)

        def some_windows(step):
            first_win = step * step_wins
            for at, position in enumerate(used):
                block = pair + position + (odd if position % 2 == 0 else -odd)
                first = lax.rem(block, BLOCKS) * piece

                def move(group, carry, at=at, first=first):
                    js = [group * batch + u for u in range(batch)]
                    picked = [
                        in_ref[slot_ref[first + j], pl.ds(first_win, step_wins), :].astype(jnp.float32) for j in js
                    ]
                    for j, row in zip(js, picked):
                        for tile in range(tiles):
                            wide[tile, pl.ds(at * piece + j, step_wins, stride=pitch), :] = row[
                                :, tile * LANES : (tile + 1) * LANES
                            ]
                    return carry

                lax.fori_loop(0, piece // batch, move, 0)

            def pack(w, carry):
                blocks = [
                    wide[tile, pl.ds(w * pitch, len(used) * piece), :].astype(jnp.bfloat16) for tile in range(tiles)
                ]
                for out_ref, kind in zip(out_refs, kinds):
                    first = used.index(kind[0]) * piece
                    for tile, block in enumerate(blocks):
                        out_ref[first_win + w, :, tile * LANES : (tile + 1) * LANES] = block[
                            first : first + len(kind) * piece
                        ]
                return carry

            lax.fori_loop(0, step_wins, pack, 0, unroll=2)

        for step in range(steps):
            copies[step].wait()
            some_windows(step)

    return kernel_call(
        kernel,
        "order_rows",
        0,
        3 * traces.size * 2,
        vmem_bytes=ORDER_VMEM_BYTES,
        out_shape=[jax.ShapeDtypeStruct((wins, len(kind) * piece, samples), jnp.bfloat16) for kind in kinds],
        in_specs=[pl.BlockSpec(memory_space=pltpu.HBM)] * 2,
        out_specs=[in_vmem()] * len(kinds),
        scratch_shapes=[
            pltpu.VMEM((tiles, (step_wins + 1) * pitch, LANES), jnp.float32),
            pltpu.VMEM(traces.shape, traces.dtype),
            pltpu.SMEM(slots.shape, slots.dtype),
            pltpu.SemaphoreType.DMA((steps + 1,)),
        ],
    )(slots, traces)


def diagonal(values, copies):
    blank = jnp.zeros_like(values)
    rows = [[values if at == copy else blank for at in range(copies)] for copy in range(copies)]
    return jnp.concatenate([jnp.concatenate(row, axis=1) for row in rows], axis=0)


def spectra(rows_j, rows_i, tables):
    wins, given, samples = rows_j.shape
    bins = samples // 2
    pairs = wins // 2
    depth = 2 * wins
    folded = HALF // given
    line = depth // folded
    pitch = line + 1
    per_step = 2 * folded
    batch = 8

    def kernel(j_ref, i_ref, table_ref, to_i_ref, to_j_ref, i_out, j_out, wide):
        same = lax.axis_index("sub") == lax.axis_index("rep")

        def spectrum_of(group):
            stacked = []
            for win in [per_step * group + u for u in range(per_step)]:
                here = j_ref[win]
                stacked += [here, jnp.where(same, here, i_ref[win])]
            wave = jnp.concatenate(stacked, axis=0)
            return lax.dot_general(table_ref[...], wave, NT, preferred_element_type=jnp.float32)

        def keep(group, spectrum):
            energy = jnp.sum(spectrum * spectrum, axis=0, keepdims=True) / bins
            white = spectrum * lax.rsqrt(energy + 1e-05)
            for half in range(2):
                for part in range(2):
                    if folded == 1:
                        row = half * wins + part * pairs + group
                    else:
                        row = part * pairs + 2 * group + half
                    wide[pl.ds(row, bins, stride=pitch), :] = white[
                        part * bins : (part + 1) * bins, half * LANES : (half + 1) * LANES
                    ]

        groups = wins // per_step
        at_once = 4

        def some_windows(step, carry):
            first = step * at_once
            last = spectrum_of(first)
            for group in range(1, at_once):
                now = spectrum_of(first + group)
                keep(first + group - 1, last)
                last = now
            keep(first + at_once - 1, last)
            return carry

        lax.fori_loop(0, groups // at_once, some_windows, 0)

        def moved(fs):
            loaded = [wide[pl.ds(f * pitch, line), :].astype(jnp.bfloat16) for f in fs]
            i_rows = [
                lax.dot_general(to_i_ref[...], diagonal(values, 2), NT, preferred_element_type=jnp.float32)
                for values in loaded
            ]
            if folded == 2:
                i_rows = [jnp.concatenate([rows[: given // 2], rows[given // 2 :]], axis=1) for rows in i_rows]
            j_rows = jnp.dot(jnp.concatenate(loaded, axis=0), to_j_ref[...], preferred_element_type=jnp.float32)
            return fs, i_rows, j_rows

        def store(fs, i_rows, j_rows):
            for at, f in enumerate(fs):
                i_out[f] = i_rows[at].astype(jnp.bfloat16)
                for odd in range(folded):
                    j_out[f, odd * line : (odd + 1) * line] = j_rows[
                        at * line : (at + 1) * line, odd * LANES : (odd + 1) * LANES
                    ].astype(jnp.bfloat16)

        def pack(group, carry):
            first = group * 4 * batch
            waiting = moved([first + u for u in range(batch)])
            for at in range(1, 4):
                following = moved([first + at * batch + u for u in range(batch)])
                store(*waiting)
                waiting = following
            store(*waiting)
            return carry

        lax.fori_loop(0, bins // (4 * batch), pack, 0)

    shapes = [(bins, given // 2, LANES), (bins, depth, LANES)]
    return kernel_call(
        kernel,
        "spectra",
        4 * samples * samples * wins * given,
        4 * wins * given * samples * 2,
        out_shape=[jax.ShapeDtypeStruct(shape, jnp.bfloat16) for shape in shapes],
        in_specs=[in_vmem()] * (2 + len(tables)),
        out_specs=[in_vmem()] * len(shapes),
        scratch_shapes=[pltpu.VMEM(((bins + 1) * pitch, LANES), jnp.float32)],
    )(rows_j, rows_i, *tables)


def partial_correlations(lefts, rights, tables, jobs, outs):
    left_arrays = [array for array, _ in lefts]
    right_arrays = [array for array, _, _ in rights]
    bins, depth, _ = right_arrays[0].shape
    piece = HALF // BLOCKS
    pitch = bins + 1
    step_bins = 32
    groups = []
    slices = {}
    for used, groups_here in jobs:
        js = [(rights[right][1], there) for right in used for there in rights[right][2]]
        for left, _, first in groups_here:
            found = []
            for offset in range(2):
                at = first + offset
                for order, (j_other, there) in enumerate(js):
                    if there != at:
                        kind = (lefts[left][1], j_other, there ^ (at % 2))
                        found.append((at, kind, offset * HALF + order * piece))
                        slices.setdefault(at, []).append(kind)
            groups.append(found)
    for kinds in slices.values():
        kinds.sort()
    total = len(groups) * piece
    batch = 4

    def first_of(at):
        (out,) = [positions for positions in outs if at in positions]
        return outs.index(out), sum(len(slices[before]) for before in out[: out.index(at)])

    def kernel(*refs):
        left_refs, rest = refs[: len(lefts)], refs[len(lefts) :]
        right_refs, rest = rest[: len(rights)], rest[len(rights) :]
        lag_ref, same_ref, out_refs, cross = rest[0], rest[1], rest[2:-1], rest[-1]
        lanes = lax.broadcasted_iota(jnp.int32, (depth, LANES), 1)

        first_half = lanes < HALF
        lower = lanes % HALF < HALF // 2
        blank = jnp.zeros((depth, LANES), jnp.bfloat16)

        def turn(values):
            swapped = []
            for first in range(0, depth, depth // 2):
                middle, last = first + depth // 4, first + depth // 2
                swapped += [-values[middle:last], values[first:middle]]
            return jnp.concatenate(swapped, axis=0)

        def right_hand(used, f):
            values = right_refs[used[0]][f]
            if len(used) == 2:
                values = jnp.where(lower, values, right_refs[used[1]][f])
            turned = turn(values)
            return jnp.concatenate(
                [
                    jnp.concatenate([jnp.where(first_half, part, blank) for part in (values, turned)], axis=1),
                    jnp.concatenate([jnp.where(first_half, blank, part) for part in (values, turned)], axis=1),
                ],
                axis=0,
            )

        def products(first_bin, count):
            found = []
            for f in [first_bin + u for u in range(count)]:
                first = 0
                for used, groups_here in jobs:
                    lhs = [left_refs[left][f, row : row + piece] for left, row, _ in groups_here]
                    lhs = jnp.concatenate(lhs, axis=0) if len(lhs) > 1 else lhs[0]
                    product = jnp.dot(lhs, right_hand(used, f), preferred_element_type=jnp.float32)
                    found.append((first * pitch + f, product))
                    first += lhs.shape[0]
            return found

        def keep(found):
            for here, product in found:
                for part in range(2):
                    cross[pl.ds(part * total * pitch + here, product.shape[0], stride=pitch), :] = product[
                        :, part * LANES : (part + 1) * LANES
                    ]

        def some_bins(step, carry):
            first = step * step_bins
            waiting = products(first, batch)
            for at in range(batch, step_bins, batch):
                following = products(first + at, batch)
                keep(waiting)
                waiting = following
            keep(waiting)
            return carry

        lax.fori_loop(0, bins // step_bins, some_bins, 0)

        for index, found in enumerate(groups):
            targets = []
            for at, kind, lane in found:
                out, first = first_of(at)
                targets.append((out_refs[out], first + slices[at].index(kind), lane))

            def summed(i):
                parts = []
                for part in range(2):
                    start = (part * total + index * piece + i) * pitch
                    parts.append(
                        jnp.concatenate([cross[pl.ds(start, bins), :], cross[pl.ds(start + pitch, bins), :]], axis=1)
                    )
                values = jnp.concatenate(parts, axis=0).astype(jnp.bfloat16)
                return i, jnp.dot(lag_ref[...], values, preferred_element_type=jnp.float32)

            def across(i, lagged):
                lagged = lagged.astype(jnp.bfloat16)
                return i, lax.dot_general(same_ref[...], lagged, NT, preferred_element_type=jnp.float32)

            def store(i, rows):
                for half in range(2):
                    for out, place, lane in targets:
                        row = half * LANES + lane
                        out[place, i + half] = rows[row : row + piece].astype(out.dtype)

            sums, rows = summed(0), None
            for i in range(2, piece, 2):
                more = summed(i)
                if rows is not None:
                    store(*rows)
                rows = across(*sums)
                sums = more
            store(*rows)
            store(*across(*sums))

    shapes = [(sum(len(slices[at]) for at in positions), piece, piece, LAGS) for positions in outs]
    types = [jnp.float32 if positions == (OWN_AT,) else jnp.bfloat16 for positions in outs]
    results = kernel_call(
        kernel,
        "partial_correlations",
        4 * total * bins * depth * LANES + 4 * total * bins * LANES * LAGS,
        2 * sum(array.size for array in left_arrays + right_arrays),
        out_shape=[jax.ShapeDtypeStruct(shape, kind) for shape, kind in zip(shapes, types)],
        in_specs=[in_vmem()] * (len(lefts) + len(rights) + len(tables)),
        out_specs=[in_vmem()] * len(shapes),
        scratch_shapes=[pltpu.VMEM(((2 * total + 1) * pitch, LANES), jnp.float32)],
    )(*left_arrays, *right_arrays, *tables)
    return results, slices


def assembled(shares):
    arrays = [array for array, _ in shares]
    _, piece, _, lags = arrays[0].shape
    width = 2 * piece

    def kernel(*refs):
        out, held, sems = refs[-3:]
        sub = lax.axis_index("sub")
        odd = lax.rem(lax.axis_index("chan"), 2)
        copies = []
        for there, round_at in ((0, 1), (1, 2 - 2 * odd), (3, 2 * odd)):
            for i_other in range(2):
                for j_other in range(2):
                    parts = [
                        refs[at][place].astype(jnp.float32)
                        for at, (_, kinds) in enumerate(shares)
                        for place, kind in enumerate(kinds)
                        if kind == (i_other, j_other, there)
                    ]
                    i_first = jnp.where(sub == 0, i_other, 1 - i_other) * piece
                    j_first = pl.multiple_of(jnp.where(sub == 0, j_other, 1 - j_other) * piece, piece)
                    held[round_at, 0, pl.ds(i_first, piece), pl.ds(j_first, piece), :] = functools.reduce(
                        jnp.add, parts
                    )
            at = len(copies)
            copies.append(pltpu.make_async_copy(held.at[round_at], out.at[round_at], sems.at[at]))
            copies[-1].start()
        for copy in copies:
            copy.wait()

    shape = (ROUNDS, 1, width, width, lags)
    return kernel_call(
        kernel,
        "assembled",
        0,
        sum(array.size for array in arrays) * 2,
        out_shape=jax.ShapeDtypeStruct(shape, jnp.float32),
        in_specs=[in_vmem()] * len(arrays),
        out_specs=pl.BlockSpec(memory_space=pl.ANY),
        scratch_shapes=[pltpu.VMEM(shape, jnp.float32), pltpu.SemaphoreType.DMA((ROUNDS,))],
    )(*arrays)


def summed_in_place(traces, channel_slot):
    chan_count = lax.axis_size("chan")
    _, win_here, samples = traces.shape
    piece = HALF // BLOCKS
    scale = (2.0 / (win_here * chan_count * (samples // 2))) ** 0.5
    dft_rows = dft_rows_table(samples)
    same = selection(2 * LANES, 2 * LANES, [(n, n) for n in range(2 * LANES)])
    tables = [lag_rows_table(samples, scale), same]
    everywhere = tuple(range(BLOCKS))

    def over_sub(rows):
        return lax.ppermute(rows, "sub", [(0, 1), (1, 0)])

    def over_core(rows):
        return lax.ppermute(rows, "rep", [(0, 1), (1, 0)])

    def with_device(share, apart):
        return lax.ppermute(share, "chan", [(z, z ^ apart) for z in range(chan_count)])

    def after(value, *others):
        return lax.optimization_barrier((value,) + others)[0]

    def added(share, arrived):
        return (share.astype(jnp.float32) + arrived.astype(jnp.float32)).astype(jnp.bfloat16)

    def for_two_away(kinds):
        return [(i_other, j_other, there ^ 2) for i_other, j_other, there in kinds]

    mine, mine_far, mine_near = order_rows(traces, channel_slot, [everywhere, FAR, NEAR])
    far = over_sub(mine_far)
    near = over_sub(mine_near)

    own_i, own_j = spectra(mine, over_core(mine), (dft_rows, *own_picks()))
    own_left, own_right = (own_i, 0), (own_j, 0, everywhere)
    own_far, own_near = (0, 0, FAR[0]), (0, piece, NEAR[0])
    (kept_1, sent_far_1, own_1, sent_near_1), kinds_1 = partial_correlations(
        [own_left], [own_right], tables, [((0,), [own_far, own_near])], [(0,), (1,), (2,), (3,)]
    )
    arrived_far_1 = with_device(sent_far_1, 1)

    far, arrived_far_1 = lax.optimization_barrier((far, arrived_far_1))
    far_1 = with_device(added(kept_1, arrived_far_1), 2)
    far_i, far_j = spectra(far, over_core(far), (dft_rows, *half_picks()))
    far_i, far_1 = lax.optimization_barrier((far_i, far_1))
    far_left, far_right = (far_i, 1), (far_j, 1, FAR)
    other_far = (1, 0, FAR[0])
    (kept_2, sent_far_2, own_2, sent_near_2), kinds_2 = partial_correlations(
        [own_left, far_left],
        [own_right, far_right],
        tables,
        [((0,), [other_far]), ((1,), [own_far, own_near, other_far])],
        [(0,), (1,), (2,), (3,)],
    )
    arrived_far_2 = with_device(sent_far_2, 1)

    near, arrived_far_2 = lax.optimization_barrier((near, arrived_far_2))
    near_i, near_j = spectra(near, over_core(near), (dft_rows, *half_picks()))
    summed_2 = added(kept_2, arrived_far_2)
    far_2 = with_device(summed_2, 2)
    near_j = after(near_j, summed_2)
    near_left, near_right = (near_i, 1), (near_j, 1, NEAR)
    (kept_3, sent_far_3, own_3, sent_near_3), kinds_3 = partial_correlations(
        [own_left, far_left],
        [near_right],
        tables,
        [((0,), [own_far, other_far, own_near])],
        [(0,), (1,), (2,), (3,)],
    )
    arrived_far_3 = with_device(sent_far_3, 1)
    arrived_near = with_device(jnp.concatenate([sent_near_1, sent_near_2]), 1)
    near_right = (after(near_j, kept_3, sent_far_3, far_2, arrived_near), 1, NEAR)
    (own_4, sent_4), kinds_4 = partial_correlations(
        [near_left], [far_right, near_right], tables, [((0, 1), [(0, 0, NEAR[0])])], [(2,), (3,)]
    )
    arrived_4 = with_device(jnp.concatenate([sent_near_3, sent_4]), 1)
    summed_3 = added(after(kept_3, own_4), arrived_far_3)
    far_3 = with_device(summed_3, 2)
    near_left = (after(near_i, own_4, sent_4, summed_3), 1)
    (own_5, sent_5), kinds_5 = partial_correlations(
        [near_left], [own_right], tables, [((0,), [(0, 0, NEAR[0])])], [(2,), (3,)]
    )
    arrived_5 = with_device(sent_5, 1)
    shares = [
        (own_1, kinds_1[2]),
        (own_2, kinds_2[2]),
        (own_3, kinds_3[2]),
        (own_4, kinds_4[2]),
        (own_5, kinds_5[2]),
        (arrived_near, kinds_1[3] + kinds_2[3]),
        (arrived_4, kinds_3[3] + kinds_4[3]),
        (arrived_5, kinds_5[3]),
        (far_1, for_two_away(kinds_1[0])),
        (far_2, for_two_away(kinds_2[0])),
        (far_3, for_two_away(kinds_3[0])),
    ]
    return assembled(shares)


def from_behind(shard, axis, by):
    count = lax.axis_size(axis)
    return lax.ppermute(shard, axis, [(i, (i + by) % count) for i in range(count)])


def dft_columns(samples, parts, sub_bins):
    shape = (samples, parts, 2, sub_bins)
    time_pos = lax.broadcasted_iota(jnp.int32, shape, 0)
    range_pos = lax.broadcasted_iota(jnp.int32, shape, 1)
    part_pos = lax.broadcasted_iota(jnp.int32, shape, 2)
    bin_pos = lax.broadcasted_iota(jnp.int32, shape, 3)
    frequency = range_pos * sub_bins + bin_pos
    angles = jnp.mod(time_pos * frequency, samples).astype(jnp.float32) * (2.0 * math.pi / samples)
    entries = jnp.where(part_pos == 0, jnp.cos(angles), -jnp.sin(angles))
    return entries.reshape(samples, parts * 2 * sub_bins).astype(jnp.bfloat16)


def lag_table(sub_bins, first_bin, lag_count, samples):
    frequency = first_bin + lax.broadcasted_iota(jnp.int32, (sub_bins, lag_count), 0)
    lag_offset = lax.broadcasted_iota(jnp.int32, (sub_bins, lag_count), 1) - lag_count // 2
    angles = jnp.mod(frequency * lag_offset, samples).astype(jnp.float32) * (2.0 * math.pi / samples)
    return jnp.stack([jnp.cos(angles), -jnp.sin(angles)], axis=1)


def moved_spectra(traces, channel_slot):
    chan_count = lax.axis_size("chan")
    sub_count = lax.axis_size("sub")
    group_rows, win_here, samples = traces.shape
    bin_count = samples // 2
    sub_bins = bin_count // sub_count
    bin_width = 2 * sub_bins
    piece_len = group_rows // chan_count
    picked = jnp.take(traces, channel_slot, axis=0)
    dft_rows = dft_columns(samples, sub_count, sub_bins)
    spectrum = jnp.dot(picked.reshape(-1, samples), dft_rows, preferred_element_type=jnp.float32)
    energy = jnp.sum(spectrum * spectrum, axis=1, keepdims=True) / bin_count
    whitened = (spectrum * lax.rsqrt(energy + 1e-05)).astype(jnp.bfloat16)
    whitened = whitened.reshape(chan_count, piece_len, win_here, sub_count, bin_width)
    regrouped = lax.all_to_all(whitened, "chan", split_axis=0, concat_axis=0, tiled=True)
    regrouped = lax.all_to_all(regrouped, "sub", split_axis=3, concat_axis=3, tiled=True)
    own_half = regrouped.transpose(3, 1, 0, 2, 4).reshape(sub_count * piece_len, chan_count * win_here, bin_width)
    own_block = lax.all_gather(own_half, "rep", axis=0, tiled=True)
    windows = own_block.shape[1]
    own_split = own_block.reshape(own_block.shape[0], windows, 2, sub_bins)
    lag_rows = lag_table(sub_bins, lax.axis_index("sub") * sub_bins, LAGS, samples)
    lag_scale = (2.0 / (windows * bin_count)) ** 0.5
    results = []
    for step in range(1, ROUNDS + 1):
        partner = from_behind(own_half, "chan", -step)
        partner_split = partner.reshape(partner.shape[0], windows, 2, sub_bins)
        turned = jnp.stack([-partner_split[:, :, 1], partner_split[:, :, 0]], axis=2)
        partner_pair = jnp.stack([partner_split, turned], axis=0)
        cross_spec = jnp.einsum("iwpf,qjwpf->fqij", own_split, partner_pair, preferred_element_type=jnp.float32)
        summed = jnp.einsum("fqij,fql->ijl", cross_spec, lag_rows, precision=lax.Precision.HIGHEST)
        results.append(lax.psum_scatter(lag_scale * summed, "sub", scatter_dimension=0, tiled=True))
    return jnp.stack(results)[:, None]


def solution(mesh):
    sizes = mesh.shape
    in_place = sizes["chan"] == BLOCKS == ROUNDS + 1 and sizes["sub"] == 2 and sizes["rep"] == 2
    return jax.shard_map(
        summed_in_place if in_place else moved_spectra,
        mesh=mesh,
        in_specs=(P(("groups", "sub", "rep"), "chan", None), P(("groups", "sub", "rep"))),
        out_specs=P(None, ("groups", "chan"), "sub", "rep", None),
        check_vma=False,
    )
```

```python
import functools
import math

import jax
import jax.numpy as jnp
import numpy as np
from jax import lax
from jax.experimental import pallas as pl
from jax.experimental.pallas import tpu as pltpu
from jax.sharding import PartitionSpec as P

LAGS = 128
ROUNDS = 3
LANES = 128
HALF = LANES // 2
VMEM_BYTES = 32 * 1024 * 1024
ORDER_VMEM_BYTES = 48 * 1024 * 1024
NT = (((1,), (1,)), ((), ()))
BLOCKS = 4
FAR = (0, 1)
NEAR = (2, 3)
KEPT_AT, OWN_AT = 0, 2


def kernel_call(kernel, name, flops, bytes_accessed, vmem_bytes=VMEM_BYTES, **more):
    return pl.pallas_call(
        kernel,
        name=name,
        compiler_params=pltpu.CompilerParams(vmem_limit_bytes=vmem_bytes),
        cost_estimate=pl.CostEstimate(flops=flops, bytes_accessed=bytes_accessed, transcendentals=0),
        **more,
    )


def in_vmem():
    return pl.BlockSpec(memory_space=pltpu.VMEM)


def dft_rows_table(samples):
    bins = samples // 2
    turns = (np.arange(bins)[:, None] * np.arange(samples)[None, :]) % samples
    angles = turns.astype(np.float32) * np.float32(2.0 * math.pi / samples)
    table = np.concatenate([np.cos(angles), -np.sin(angles)], axis=0)
    return jnp.asarray(table.astype(np.float32)).astype(jnp.bfloat16)


def lag_rows_table(samples, scale):
    bins = samples // 2
    offsets = np.arange(LAGS) - LAGS // 2
    turns = (offsets[:, None] * np.arange(bins)[None, :]) % samples
    angles = turns.astype(np.float32) * np.float32(2.0 * math.pi / samples)
    table = np.concatenate([np.cos(angles), -np.sin(angles)], axis=1) * np.float32(scale)
    return jnp.asarray(table.astype(np.float32)).astype(jnp.bfloat16)


def selection(rows, columns, ones):
    table = np.zeros((rows, columns), np.float32)
    for row, column in ones:
        table[row, column] = 1.0
    return jnp.asarray(table).astype(jnp.bfloat16)


def own_picks():
    piece = HALF // BLOCKS
    to_i = []
    for at in range(BLOCKS):
        for n in range(piece):
            to_i.append((at // 2 * piece + n, at % 2 * LANES + HALF + at * piece + n))
    to_j = [(j, copy * HALF + j) for j in range(HALF) for copy in range(2)]
    return selection(2 * piece, 2 * LANES, to_i), selection(LANES, LANES, to_j)


def half_picks():
    count = HALF // 2
    to_i, to_j = [], []
    for odd in range(2):
        for n in range(count):
            to_i.append((n, odd * LANES + odd * HALF + count + n))
            to_j += [(odd * HALF + n, odd * LANES + copy * count + n) for copy in range(4)]
    return selection(count, 2 * LANES, to_i), selection(LANES, 2 * LANES, to_j)


def order_rows(traces, slots, kinds):
    rows, wins, samples = traces.shape
    tiles = samples // LANES
    piece = rows // BLOCKS
    step_wins = 16
    steps = wins // step_wins
    batch = 4
    used = max(kinds, key=len)
    pitch = len(used) * piece + 1

    def kernel(slots_ref, traces_ref, *refs):
        out_refs, (wide, in_ref, slot_ref, sems) = refs[:-4], refs[-4:]
        slot_copy = pltpu.make_async_copy(slots_ref, slot_ref, sems.at[steps])
        slot_copy.start()
        copies = []
        for step in range(steps):
            here = pl.ds(step * step_wins, step_wins)
            copies.append(
                pltpu.make_async_copy(traces_ref.at[:, here, :], in_ref.at[:, here, :], sems.at[step])
            )
            copies[-1].start()
        slot_copy.wait()
        z = lax.axis_index("chan")
        odd = lax.rem(z, 2)
        pair = jnp.where(z < 2, 2, 0)

        def some_windows(step):
            first_win = step * step_wins
            for at, position in enumerate(used):
                block = pair + position + (odd if position % 2 == 0 else -odd)
                first = lax.rem(block, BLOCKS) * piece

                def move(group, carry, at=at, first=first):
                    js = [group * batch + u for u in range(batch)]
                    picked = [
                        in_ref[slot_ref[first + j], pl.ds(first_win, step_wins), :].astype(jnp.float32) for j in js
                    ]
                    for j, row in zip(js, picked):
                        for tile in range(tiles):
                            wide[tile, pl.ds(at * piece + j, step_wins, stride=pitch), :] = row[
                                :, tile * LANES : (tile + 1) * LANES
                            ]
                    return carry

                lax.fori_loop(0, piece // batch, move, 0)

            def pack(w, carry):
                blocks = [
                    wide[tile, pl.ds(w * pitch, len(used) * piece), :].astype(jnp.bfloat16) for tile in range(tiles)
                ]
                for out_ref, kind in zip(out_refs, kinds):
                    first = used.index(kind[0]) * piece
                    for tile, block in enumerate(blocks):
                        out_ref[first_win + w, :, tile * LANES : (tile + 1) * LANES] = block[
                            first : first + len(kind) * piece
                        ]
                return carry

            lax.fori_loop(0, step_wins, pack, 0, unroll=2)

        for step in range(steps):
            copies[step].wait()
            some_windows(step)

    return kernel_call(
        kernel,
        "order_rows",
        0,
        3 * traces.size * 2,
        vmem_bytes=ORDER_VMEM_BYTES,
        out_shape=[jax.ShapeDtypeStruct((wins, len(kind) * piece, samples), jnp.bfloat16) for kind in kinds],
        in_specs=[pl.BlockSpec(memory_space=pltpu.HBM)] * 2,
        out_specs=[in_vmem()] * len(kinds),
        scratch_shapes=[
            pltpu.VMEM((tiles, (step_wins + 1) * pitch, LANES), jnp.float32),
            pltpu.VMEM(traces.shape, traces.dtype),
            pltpu.SMEM(slots.shape, slots.dtype),
            pltpu.SemaphoreType.DMA((steps + 1,)),
        ],
    )(slots, traces)


def diagonal(values, copies):
    blank = jnp.zeros_like(values)
    rows = [[values if at == copy else blank for at in range(copies)] for copy in range(copies)]
    return jnp.concatenate([jnp.concatenate(row, axis=1) for row in rows], axis=0)


def spectra_steps(rows_j):
    wins, given, samples = rows_j.shape
    bins = samples // 2
    pairs = wins // 2
    depth = 2 * wins
    folded = HALF // given
    line = depth // folded
    pitch = line + 1
    per_step = 2 * folded
    batch = 8

    def run(j_ref, i_ref, table_ref, to_i_ref, to_j_ref, i_out, j_out, wide):
        same = lax.axis_index("sub") == lax.axis_index("rep")

        def spectrum_of(group):
            stacked = []
            for win in [per_step * group + u for u in range(per_step)]:
                here = j_ref[win]
                stacked += [here, jnp.where(same, here, i_ref[win])]
            wave = jnp.concatenate(stacked, axis=0)
            return lax.dot_general(table_ref[...], wave, NT, preferred_element_type=jnp.float32)

        def keep(group, spectrum):
            energy = jnp.sum(spectrum * spectrum, axis=0, keepdims=True) / bins
            white = spectrum * lax.rsqrt(energy + 1e-05)
            for half in range(2):
                for part in range(2):
                    if folded == 1:
                        row = half * wins + part * pairs + group
                    else:
                        row = part * pairs + 2 * group + half
                    wide[pl.ds(row, bins, stride=pitch), :] = white[
                        part * bins : (part + 1) * bins, half * LANES : (half + 1) * LANES
                    ]

        groups = wins // per_step
        at_once = 4

        def some_windows(step, carry):
            first = step * at_once
            last = spectrum_of(first)
            for group in range(1, at_once):
                now = spectrum_of(first + group)
                keep(first + group - 1, last)
                last = now
            keep(first + at_once - 1, last)
            return carry

        lax.fori_loop(0, groups // at_once, some_windows, 0)

        def moved(fs):
            loaded = [wide[pl.ds(f * pitch, line), :].astype(jnp.bfloat16) for f in fs]
            i_rows = [
                lax.dot_general(to_i_ref[...], diagonal(values, 2), NT, preferred_element_type=jnp.float32)
                for values in loaded
            ]
            if folded == 2:
                i_rows = [jnp.concatenate([rows[: given // 2], rows[given // 2 :]], axis=1) for rows in i_rows]
            j_rows = jnp.dot(jnp.concatenate(loaded, axis=0), to_j_ref[...], preferred_element_type=jnp.float32)
            return fs, i_rows, j_rows

        def store(fs, i_rows, j_rows):
            for at, f in enumerate(fs):
                i_out[f] = i_rows[at].astype(jnp.bfloat16)
                for odd in range(folded):
                    j_out[f, odd * line : (odd + 1) * line] = j_rows[
                        at * line : (at + 1) * line, odd * LANES : (odd + 1) * LANES
                    ].astype(jnp.bfloat16)

        def pack(group, carry):
            first = group * 4 * batch
            waiting = moved([first + u for u in range(batch)])
            for at in range(1, 4):
                following = moved([first + at * batch + u for u in range(batch)])
                store(*waiting)
                waiting = following
            store(*waiting)
            return carry

        lax.fori_loop(0, bins // (4 * batch), pack, 0)

    shapes = [(bins, given // 2, LANES), (bins, depth, LANES)]
    outs = [jax.ShapeDtypeStruct(shape, jnp.bfloat16) for shape in shapes]
    scratch = [pltpu.VMEM(((bins + 1) * pitch, LANES), jnp.float32)]
    return run, outs, scratch, 4 * samples * samples * wins * given


def spectra(rows_j, rows_i, tables):
    run, outs, scratch, flops = spectra_steps(rows_j)
    return kernel_call(
        run,
        "spectra",
        flops,
        8 * rows_j.size,
        out_shape=outs,
        in_specs=[in_vmem()] * (2 + len(tables)),
        out_specs=[in_vmem()] * len(outs),
        scratch_shapes=scratch,
    )(rows_j, rows_i, *tables)


def correlation_steps(lefts, rights, jobs, outs):
    bins, depth, _ = rights[0][0].shape
    piece = HALF // BLOCKS
    pitch = bins + 1
    step_bins = 32
    groups = []
    slices = {}
    for used, groups_here in jobs:
        js = [(rights[right][1], there) for right in used for there in rights[right][2]]
        for left, _, first in groups_here:
            found = []
            for offset in range(2):
                at = first + offset
                for order, (j_other, there) in enumerate(js):
                    if there != at:
                        kind = (lefts[left][1], j_other, there ^ (at % 2))
                        found.append((at, kind, offset * HALF + order * piece))
                        slices.setdefault(at, []).append(kind)
            groups.append(found)
    for kinds in slices.values():
        kinds.sort()
    total = len(groups) * piece
    batch = 4

    def first_of(at):
        (out,) = [positions for positions in outs if at in positions]
        return outs.index(out), sum(len(slices[before]) for before in out[: out.index(at)])

    def run(left_refs, right_refs, lag_ref, same_ref, out_refs, cross):
        lanes = lax.broadcasted_iota(jnp.int32, (depth, LANES), 1)

        first_half = lanes < HALF
        lower = lanes % HALF < HALF // 2
        blank = jnp.zeros((depth, LANES), jnp.bfloat16)

        def turn(values):
            swapped = []
            for first in range(0, depth, depth // 2):
                middle, last = first + depth // 4, first + depth // 2
                swapped += [-values[middle:last], values[first:middle]]
            return jnp.concatenate(swapped, axis=0)

        def right_hand(used, f):
            values = right_refs[used[0]][f]
            if len(used) == 2:
                values = jnp.where(lower, values, right_refs[used[1]][f])
            turned = turn(values)
            return jnp.concatenate(
                [
                    jnp.concatenate([jnp.where(first_half, part, blank) for part in (values, turned)], axis=1),
                    jnp.concatenate([jnp.where(first_half, blank, part) for part in (values, turned)], axis=1),
                ],
                axis=0,
            )

        def products(first_bin, count):
            found = []
            for f in [first_bin + u for u in range(count)]:
                first = 0
                for used, groups_here in jobs:
                    lhs = [left_refs[left][f, row : row + piece] for left, row, _ in groups_here]
                    lhs = jnp.concatenate(lhs, axis=0) if len(lhs) > 1 else lhs[0]
                    product = jnp.dot(lhs, right_hand(used, f), preferred_element_type=jnp.float32)
                    found.append((first * pitch + f, product))
                    first += lhs.shape[0]
            return found

        def keep(found):
            for here, product in found:
                for part in range(2):
                    cross[pl.ds(part * total * pitch + here, product.shape[0], stride=pitch), :] = product[
                        :, part * LANES : (part + 1) * LANES
                    ]

        def some_bins(step, carry):
            first = step * step_bins
            waiting = products(first, batch)
            for at in range(batch, step_bins, batch):
                following = products(first + at, batch)
                keep(waiting)
                waiting = following
            keep(waiting)
            return carry

        lax.fori_loop(0, bins // step_bins, some_bins, 0)

        for index, found in enumerate(groups):
            targets = []
            for at, kind, lane in found:
                out, first = first_of(at)
                targets.append((out_refs[out], first + slices[at].index(kind), lane))

            def summed(i):
                parts = []
                for part in range(2):
                    start = (part * total + index * piece + i) * pitch
                    parts.append(
                        jnp.concatenate([cross[pl.ds(start, bins), :], cross[pl.ds(start + pitch, bins), :]], axis=1)
                    )
                values = jnp.concatenate(parts, axis=0).astype(jnp.bfloat16)
                return i, jnp.dot(lag_ref[...], values, preferred_element_type=jnp.float32)

            def across(i, lagged):
                lagged = lagged.astype(jnp.bfloat16)
                return i, lax.dot_general(same_ref[...], lagged, NT, preferred_element_type=jnp.float32)

            def store(i, rows):
                for half in range(2):
                    for out, place, lane in targets:
                        row = half * LANES + lane
                        out[place, i + half] = rows[row : row + piece].astype(out.dtype)

            sums, rows = summed(0), None
            for i in range(2, piece, 2):
                more = summed(i)
                if rows is not None:
                    store(*rows)
                rows = across(*sums)
                sums = more
            store(*rows)
            store(*across(*sums))

    shapes = [(sum(len(slices[at]) for at in positions), piece, piece, LAGS) for positions in outs]
    types = [jnp.float32 if positions == (OWN_AT,) else jnp.bfloat16 for positions in outs]
    out_shapes = [jax.ShapeDtypeStruct(shape, kind) for shape, kind in zip(shapes, types)]
    scratch = [pltpu.VMEM(((2 * total + 1) * pitch, LANES), jnp.float32)]
    return run, out_shapes, scratch, 4 * total * bins * (depth + LAGS) * LANES, slices


def partial_correlations(lefts, rights, tables, jobs, outs):
    run, out_shapes, scratch, flops, slices = correlation_steps(lefts, rights, jobs, outs)
    arrays = [left[0] for left in lefts] + [right[0] for right in rights]

    def kernel(*refs):
        left_refs, rest = refs[: len(lefts)], refs[len(lefts) :]
        right_refs, rest = rest[: len(rights)], rest[len(rights) :]
        run(left_refs, right_refs, rest[0], rest[1], rest[2:-1], rest[-1])

    results = kernel_call(
        kernel,
        "partial_correlations",
        flops,
        2 * sum(array.size for array in arrays),
        out_shape=out_shapes,
        in_specs=[in_vmem()] * (len(arrays) + len(tables)),
        out_specs=[in_vmem()] * len(out_shapes),
        scratch_shapes=scratch,
    )(*arrays, *tables)
    return results, slices


def spectra_and_correlations(rows_j, rows_i, spectra_tables, js, lefts, rights, tables, jobs, outs):
    run_spectra, spectra_outs, spectra_scratch, spectra_flops = spectra_steps(rows_j)
    run, out_shapes, scratch, flops, slices = correlation_steps(
        lefts + [(spectra_outs[0], 1)], rights + [(spectra_outs[1], 1, js)], jobs, outs
    )
    given = [rows_j, rows_i, *spectra_tables]
    arrays = [left[0] for left in lefts] + [right[0] for right in rights]
    last_right = len(given) + len(arrays)

    def kernel(*refs):
        left_refs = refs[len(given) : len(given) + len(lefts)]
        right_refs = refs[len(given) + len(lefts) : last_right]
        lag_ref, same_ref, i_out, j_out = refs[last_right : last_right + 4]
        out_refs, (wide, cross) = refs[last_right + 4 : -2], refs[-2:]
        run_spectra(*refs[: len(given)], i_out, j_out, wide)
        run([*left_refs, i_out], [*right_refs, j_out], lag_ref, same_ref, out_refs, cross)

    results = kernel_call(
        kernel,
        "spectra_and_correlations",
        spectra_flops + flops,
        8 * rows_j.size,
        out_shape=spectra_outs + out_shapes,
        in_specs=[in_vmem()] * (last_right + len(tables)),
        out_specs=[in_vmem()] * (2 + len(out_shapes)),
        scratch_shapes=spectra_scratch + scratch,
    )(*given, *arrays, *tables)
    return results[0], results[1], results[2:], slices


def assembled(shares):
    arrays = [array for array, _ in shares]
    _, piece, _, lags = arrays[0].shape
    width = 2 * piece

    def kernel(*refs):
        out, held, sems = refs[-3:]
        sub = lax.axis_index("sub")
        odd = lax.rem(lax.axis_index("chan"), 2)
        copies = []
        for there, round_at in ((0, 1), (1, 2 - 2 * odd), (3, 2 * odd)):
            for i_other in range(2):
                for j_other in range(2):
                    parts = [
                        refs[at][place].astype(jnp.float32)
                        for at, (_, kinds) in enumerate(shares)
                        for place, kind in enumerate(kinds)
                        if kind == (i_other, j_other, there)
                    ]
                    i_first = jnp.where(sub == 0, i_other, 1 - i_other) * piece
                    j_first = pl.multiple_of(jnp.where(sub == 0, j_other, 1 - j_other) * piece, piece)
                    held[round_at, 0, pl.ds(i_first, piece), pl.ds(j_first, piece), :] = functools.reduce(
                        jnp.add, parts
                    )
            at = len(copies)
            copies.append(pltpu.make_async_copy(held.at[round_at], out.at[round_at], sems.at[at]))
            copies[-1].start()
        for copy in copies:
            copy.wait()

    shape = (ROUNDS, 1, width, width, lags)
    return kernel_call(
        kernel,
        "assembled",
        0,
        sum(array.size for array in arrays) * 2,
        out_shape=jax.ShapeDtypeStruct(shape, jnp.float32),
        in_specs=[in_vmem()] * len(arrays),
        out_specs=pl.BlockSpec(memory_space=pl.ANY),
        scratch_shapes=[pltpu.VMEM(shape, jnp.float32), pltpu.SemaphoreType.DMA((ROUNDS,))],
    )(*arrays)


def summed_in_place(traces, channel_slot):
    chan_count = lax.axis_size("chan")
    _, win_here, samples = traces.shape
    piece = HALF // BLOCKS
    scale = (2.0 / (win_here * chan_count * (samples // 2))) ** 0.5
    dft_rows = dft_rows_table(samples)
    same = selection(2 * LANES, 2 * LANES, [(n, n) for n in range(2 * LANES)])
    tables = [lag_rows_table(samples, scale), same]
    everywhere = tuple(range(BLOCKS))

    def over_sub(rows):
        return lax.ppermute(rows, "sub", [(0, 1), (1, 0)])

    def over_core(rows):
        return lax.ppermute(rows, "rep", [(0, 1), (1, 0)])

    def with_device(share, apart):
        return lax.ppermute(share, "chan", [(z, z ^ apart) for z in range(chan_count)])

    def after(value, *others):
        return lax.optimization_barrier((value,) + others)[0]

    def added(share, arrived):
        return (share.astype(jnp.float32) + arrived.astype(jnp.float32)).astype(jnp.bfloat16)

    def for_two_away(kinds):
        return [(i_other, j_other, there ^ 2) for i_other, j_other, there in kinds]

    mine, mine_far, mine_near = order_rows(traces, channel_slot, [everywhere, FAR, NEAR])
    far = over_sub(mine_far)
    near = over_sub(mine_near)

    own_i, own_j = spectra(mine, over_core(mine), (dft_rows, *own_picks()))
    own_left, own_right = (own_i, 0), (own_j, 0, everywhere)
    own_far, own_near = (0, 0, FAR[0]), (0, piece, NEAR[0])
    (kept_1, own_1, sent_1), kinds_1 = partial_correlations(
        [own_left], [own_right], tables, [((0,), [own_far, own_near])], [(0,), (2,), (1, 3)]
    )
    arrived_1 = with_device(sent_1, 1)

    far = after(far, kept_1, own_1, sent_1)
    far_i, far_j, (kept_2, sent_far_2, own_2, sent_near_2), kinds_2 = spectra_and_correlations(
        far,
        over_core(far),
        (dft_rows, *half_picks()),
        FAR,
        [own_left],
        [own_right],
        tables,
        [((0,), [(1, 0, FAR[0])]), ((1,), [own_far, own_near, (1, 0, FAR[0])])],
        [(0,), (1,), (2,), (3,)],
    )
    far_left, far_right = (far_i, 1), (far_j, 1, FAR)
    arrived_far_2 = with_device(sent_far_2, 1)

    near, arrived_far_2, arrived_1 = lax.optimization_barrier((near, arrived_far_2, arrived_1))
    near_core = over_core(near)
    summed_2 = added(kept_2, arrived_far_2)
    far_2 = with_device(summed_2, 2)
    near_i, near_j, (kept_3, sent_far_3, own_3, sent_near_3), kinds_3 = spectra_and_correlations(
        after(near, summed_2),
        near_core,
        (dft_rows, *half_picks()),
        NEAR,
        [own_left, far_left],
        [],
        tables,
        [((0,), [own_far, (1, 0, FAR[0]), own_near])],
        [(0,), (1,), (2,), (3,)],
    )
    near_left, near_right = (near_i, 1), (near_j, 1, NEAR)
    far_count_1 = kept_1.shape[0]
    summed_1 = added(after(kept_1, kept_3), arrived_1[:far_count_1])
    far_1 = with_device(summed_1, 2)
    arrived_far_3 = with_device(sent_far_3, 1)
    arrived_near_2 = with_device(sent_near_2, 1)
    near_right = (after(near_j, kept_3, sent_far_3, far_2, summed_1, arrived_near_2), 1, NEAR)
    (own_4, sent_4), kinds_4 = partial_correlations(
        [near_left], [far_right, near_right], tables, [((0, 1), [(0, 0, NEAR[0])])], [(2,), (3,)]
    )
    arrived_4 = with_device(jnp.concatenate([sent_near_3, sent_4]), 1)
    summed_3 = added(after(kept_3, own_4), arrived_far_3)
    far_3 = with_device(summed_3, 2)
    near_left = (after(near_i, own_4, sent_4, summed_3, far_1), 1)
    (own_5, sent_5), kinds_5 = partial_correlations(
        [near_left], [own_right], tables, [((0,), [(0, 0, NEAR[0])])], [(2,), (3,)]
    )
    arrived_5 = with_device(sent_5, 1)
    shares = [
        (own_1, kinds_1[2]),
        (own_2, kinds_2[2]),
        (own_3, kinds_3[2]),
        (own_4, kinds_4[2]),
        (own_5, kinds_5[2]),
        (arrived_1, [None] * far_count_1 + kinds_1[3]),
        (arrived_near_2, kinds_2[3]),
        (arrived_4, kinds_3[3] + kinds_4[3]),
        (arrived_5, kinds_5[3]),
        (far_1, for_two_away(kinds_1[0])),
        (far_2, for_two_away(kinds_2[0])),
        (far_3, for_two_away(kinds_3[0])),
    ]
    return assembled(shares)


def from_behind(shard, axis, by):
    count = lax.axis_size(axis)
    return lax.ppermute(shard, axis, [(i, (i + by) % count) for i in range(count)])


def dft_columns(samples, parts, sub_bins):
    shape = (samples, parts, 2, sub_bins)
    time_pos = lax.broadcasted_iota(jnp.int32, shape, 0)
    range_pos = lax.broadcasted_iota(jnp.int32, shape, 1)
    part_pos = lax.broadcasted_iota(jnp.int32, shape, 2)
    bin_pos = lax.broadcasted_iota(jnp.int32, shape, 3)
    frequency = range_pos * sub_bins + bin_pos
    angles = jnp.mod(time_pos * frequency, samples).astype(jnp.float32) * (2.0 * math.pi / samples)
    entries = jnp.where(part_pos == 0, jnp.cos(angles), -jnp.sin(angles))
    return entries.reshape(samples, parts * 2 * sub_bins).astype(jnp.bfloat16)


def lag_table(sub_bins, first_bin, lag_count, samples):
    frequency = first_bin + lax.broadcasted_iota(jnp.int32, (sub_bins, lag_count), 0)
    lag_offset = lax.broadcasted_iota(jnp.int32, (sub_bins, lag_count), 1) - lag_count // 2
    angles = jnp.mod(frequency * lag_offset, samples).astype(jnp.float32) * (2.0 * math.pi / samples)
    return jnp.stack([jnp.cos(angles), -jnp.sin(angles)], axis=1)


def moved_spectra(traces, channel_slot):
    chan_count = lax.axis_size("chan")
    sub_count = lax.axis_size("sub")
    group_rows, win_here, samples = traces.shape
    bin_count = samples // 2
    sub_bins = bin_count // sub_count
    bin_width = 2 * sub_bins
    piece_len = group_rows // chan_count
    picked = jnp.take(traces, channel_slot, axis=0)
    dft_rows = dft_columns(samples, sub_count, sub_bins)
    spectrum = jnp.dot(picked.reshape(-1, samples), dft_rows, preferred_element_type=jnp.float32)
    energy = jnp.sum(spectrum * spectrum, axis=1, keepdims=True) / bin_count
    whitened = (spectrum * lax.rsqrt(energy + 1e-05)).astype(jnp.bfloat16)
    whitened = whitened.reshape(chan_count, piece_len, win_here, sub_count, bin_width)
    regrouped = lax.all_to_all(whitened, "chan", split_axis=0, concat_axis=0, tiled=True)
    regrouped = lax.all_to_all(regrouped, "sub", split_axis=3, concat_axis=3, tiled=True)
    own_half = regrouped.transpose(3, 1, 0, 2, 4).reshape(sub_count * piece_len, chan_count * win_here, bin_width)
    own_block = lax.all_gather(own_half, "rep", axis=0, tiled=True)
    windows = own_block.shape[1]
    own_split = own_block.reshape(own_block.shape[0], windows, 2, sub_bins)
    lag_rows = lag_table(sub_bins, lax.axis_index("sub") * sub_bins, LAGS, samples)
    lag_scale = (2.0 / (windows * bin_count)) ** 0.5
    results = []
    for step in range(1, ROUNDS + 1):
        partner = from_behind(own_half, "chan", -step)
        partner_split = partner.reshape(partner.shape[0], windows, 2, sub_bins)
        turned = jnp.stack([-partner_split[:, :, 1], partner_split[:, :, 0]], axis=2)
        partner_pair = jnp.stack([partner_split, turned], axis=0)
        cross_spec = jnp.einsum("iwpf,qjwpf->fqij", own_split, partner_pair, preferred_element_type=jnp.float32)
        summed = jnp.einsum("fqij,fql->ijl", cross_spec, lag_rows, precision=lax.Precision.HIGHEST)
        results.append(lax.psum_scatter(lag_scale * summed, "sub", scatter_dimension=0, tiled=True))
    return jnp.stack(results)[:, None]


def solution(mesh):
    sizes = mesh.shape
    in_place = sizes["chan"] == BLOCKS == ROUNDS + 1 and sizes["sub"] == 2 and sizes["rep"] == 2
    return jax.shard_map(
        summed_in_place if in_place else moved_spectra,
        mesh=mesh,
        in_specs=(P(("groups", "sub", "rep"), "chan", None), P(("groups", "sub", "rep"))),
        out_specs=P(None, ("groups", "chan"), "sub", "rep", None),
        check_vma=False,
    )
```

```python
import functools
import math

import jax
import jax.numpy as jnp
import numpy as np
from jax import lax
from jax.experimental import pallas as pl
from jax.experimental.pallas import tpu as pltpu
from jax.sharding import PartitionSpec as P

LAGS = 128
ROUNDS = 3
LANES = 128
HALF = LANES // 2
VMEM_BYTES = 32 * 1024 * 1024
ORDER_VMEM_BYTES = 48 * 1024 * 1024
NT = (((1,), (1,)), ((), ()))
BLOCKS = 4
FAR = (0, 1)
NEAR = (2, 3)
KEPT_AT, OWN_AT = 0, 2


def kernel_call(kernel, name, flops, bytes_accessed, vmem_bytes=VMEM_BYTES, **more):
    return pl.pallas_call(
        kernel,
        name=name,
        compiler_params=pltpu.CompilerParams(vmem_limit_bytes=vmem_bytes),
        cost_estimate=pl.CostEstimate(flops=flops, bytes_accessed=bytes_accessed, transcendentals=0),
        **more,
    )


def in_vmem():
    return pl.BlockSpec(memory_space=pltpu.VMEM)


def dft_rows_table(samples):
    bins = samples // 2
    turns = (np.arange(bins)[:, None] * np.arange(samples)[None, :]) % samples
    angles = turns.astype(np.float32) * np.float32(2.0 * math.pi / samples)
    table = np.concatenate([np.cos(angles), -np.sin(angles)], axis=0)
    return jnp.asarray(table.astype(np.float32)).astype(jnp.bfloat16)


def lag_rows_table(samples, scale):
    bins = samples // 2
    offsets = np.arange(LAGS) - LAGS // 2
    turns = (offsets[:, None] * np.arange(bins)[None, :]) % samples
    angles = turns.astype(np.float32) * np.float32(2.0 * math.pi / samples)
    table = np.concatenate([np.cos(angles), -np.sin(angles)], axis=1) * np.float32(scale)
    return jnp.asarray(table.astype(np.float32)).astype(jnp.bfloat16)


def selection(rows, columns, ones):
    table = np.zeros((rows, columns), np.float32)
    for row, column in ones:
        table[row, column] = 1.0
    return jnp.asarray(table).astype(jnp.bfloat16)


def own_picks():
    piece = HALF // BLOCKS
    to_i = []
    for at in range(BLOCKS):
        for n in range(piece):
            to_i.append((at // 2 * piece + n, at % 2 * LANES + HALF + at * piece + n))
    to_j = [(j, copy * HALF + j) for j in range(HALF) for copy in range(2)]
    return selection(2 * piece, 2 * LANES, to_i), selection(LANES, LANES, to_j)


def half_picks():
    count = HALF // 2
    to_i, to_j = [], []
    for odd in range(2):
        for n in range(count):
            to_i.append((n, odd * LANES + odd * HALF + count + n))
            to_j += [(odd * HALF + n, odd * LANES + copy * count + n) for copy in range(4)]
    return selection(count, 2 * LANES, to_i), selection(LANES, 2 * LANES, to_j)


def order_rows(traces, slots, kinds):
    rows, wins, samples = traces.shape
    tiles = samples // LANES
    piece = rows // BLOCKS
    step_wins = 16
    steps = wins // step_wins
    batch = 4
    used = max(kinds, key=len)
    pitch = len(used) * piece + 1

    def kernel(slots_ref, traces_ref, *refs):
        out_refs, (wide, in_ref, slot_ref, sems) = refs[:-4], refs[-4:]
        slot_copy = pltpu.make_async_copy(slots_ref, slot_ref, sems.at[steps])
        slot_copy.start()
        copies = []
        for step in range(steps):
            here = pl.ds(step * step_wins, step_wins)
            copies.append(
                pltpu.make_async_copy(traces_ref.at[:, here, :], in_ref.at[:, here, :], sems.at[step])
            )
            copies[-1].start()
        slot_copy.wait()
        z = lax.axis_index("chan")
        odd = lax.rem(z, 2)
        pair = jnp.where(z < 2, 2, 0)

        def some_windows(step):
            first_win = step * step_wins
            for at, position in enumerate(used):
                block = pair + position + (odd if position % 2 == 0 else -odd)
                first = lax.rem(block, BLOCKS) * piece

                def move(group, carry, at=at, first=first):
                    js = [group * batch + u for u in range(batch)]
                    picked = [
                        in_ref[slot_ref[first + j], pl.ds(first_win, step_wins), :].astype(jnp.float32) for j in js
                    ]
                    for j, row in zip(js, picked):
                        for tile in range(tiles):
                            wide[tile, pl.ds(at * piece + j, step_wins, stride=pitch), :] = row[
                                :, tile * LANES : (tile + 1) * LANES
                            ]
                    return carry

                lax.fori_loop(0, piece // batch, move, 0)

            def pack(w, carry):
                blocks = [
                    wide[tile, pl.ds(w * pitch, len(used) * piece), :].astype(jnp.bfloat16) for tile in range(tiles)
                ]
                for out_ref, kind in zip(out_refs, kinds):
                    first = used.index(kind[0]) * piece
                    for tile, block in enumerate(blocks):
                        out_ref[first_win + w, :, tile * LANES : (tile + 1) * LANES] = block[
                            first : first + len(kind) * piece
                        ]
                return carry

            lax.fori_loop(0, step_wins, pack, 0, unroll=2)

        for step in range(steps):
            copies[step].wait()
            some_windows(step)

    return kernel_call(
        kernel,
        "order_rows",
        0,
        3 * traces.size * 2,
        vmem_bytes=ORDER_VMEM_BYTES,
        out_shape=[jax.ShapeDtypeStruct((wins, len(kind) * piece, samples), jnp.bfloat16) for kind in kinds],
        in_specs=[pl.BlockSpec(memory_space=pltpu.HBM)] * 2,
        out_specs=[in_vmem()] * len(kinds),
        scratch_shapes=[
            pltpu.VMEM((tiles, (step_wins + 1) * pitch, LANES), jnp.float32),
            pltpu.VMEM(traces.shape, traces.dtype),
            pltpu.SMEM(slots.shape, slots.dtype),
            pltpu.SemaphoreType.DMA((steps + 1,)),
        ],
    )(slots, traces)


def diagonal(values, copies):
    blank = jnp.zeros_like(values)
    rows = [[values if at == copy else blank for at in range(copies)] for copy in range(copies)]
    return jnp.concatenate([jnp.concatenate(row, axis=1) for row in rows], axis=0)


def spectra(rows_j, rows_i, tables):
    wins, given, samples = rows_j.shape
    bins = samples // 2
    pairs = wins // 2
    depth = 2 * wins
    folded = HALF // given
    line = depth // folded
    pitch = line + 1
    per_step = 2 * folded
    batch = 8

    def kernel(j_ref, i_ref, table_ref, to_i_ref, to_j_ref, i_out, j_out, wide):
        same = lax.axis_index("sub") == lax.axis_index("rep")

        def spectrum_of(group):
            stacked = []
            for win in [per_step * group + u for u in range(per_step)]:
                here = j_ref[win]
                stacked += [here, jnp.where(same, here, i_ref[win])]
            wave = jnp.concatenate(stacked, axis=0)
            return lax.dot_general(table_ref[...], wave, NT, preferred_element_type=jnp.float32)

        def keep(group, spectrum):
            energy = jnp.sum(spectrum * spectrum, axis=0, keepdims=True) / bins
            white = spectrum * lax.rsqrt(energy + 1e-05)
            for half in range(2):
                for part in range(2):
                    if folded == 1:
                        row = half * wins + part * pairs + group
                    else:
                        row = part * pairs + 2 * group + half
                    wide[pl.ds(row, bins, stride=pitch), :] = white[
                        part * bins : (part + 1) * bins, half * LANES : (half + 1) * LANES
                    ]

        groups = wins // per_step
        at_once = 4

        def some_windows(step, carry):
            first = step * at_once
            last = spectrum_of(first)
            for group in range(1, at_once):
                now = spectrum_of(first + group)
                keep(first + group - 1, last)
                last = now
            keep(first + at_once - 1, last)
            return carry

        lax.fori_loop(0, groups // at_once, some_windows, 0)

        def moved(fs):
            loaded = [wide[pl.ds(f * pitch, line), :].astype(jnp.bfloat16) for f in fs]
            i_rows = [
                lax.dot_general(to_i_ref[...], diagonal(values, 2), NT, preferred_element_type=jnp.float32)
                for values in loaded
            ]
            if folded == 2:
                i_rows = [jnp.concatenate([rows[: given // 2], rows[given // 2 :]], axis=1) for rows in i_rows]
            j_rows = jnp.dot(jnp.concatenate(loaded, axis=0), to_j_ref[...], preferred_element_type=jnp.float32)
            return fs, i_rows, j_rows

        def store(fs, i_rows, j_rows):
            for at, f in enumerate(fs):
                i_out[f] = i_rows[at].astype(jnp.bfloat16)
                for odd in range(folded):
                    j_out[f, odd * line : (odd + 1) * line] = j_rows[
                        at * line : (at + 1) * line, odd * LANES : (odd + 1) * LANES
                    ].astype(jnp.bfloat16)

        def pack(group, carry):
            first = group * 4 * batch
            waiting = moved([first + u for u in range(batch)])
            for at in range(1, 4):
                following = moved([first + at * batch + u for u in range(batch)])
                store(*waiting)
                waiting = following
            store(*waiting)
            return carry

        lax.fori_loop(0, bins // (4 * batch), pack, 0)

    shapes = [(bins, given // 2, LANES), (bins, depth, LANES)]
    return kernel_call(
        kernel,
        "spectra",
        4 * samples * samples * wins * given,
        4 * wins * given * samples * 2,
        out_shape=[jax.ShapeDtypeStruct(shape, jnp.bfloat16) for shape in shapes],
        in_specs=[in_vmem()] * (2 + len(tables)),
        out_specs=[in_vmem()] * len(shapes),
        scratch_shapes=[pltpu.VMEM(((bins + 1) * pitch, LANES), jnp.float32)],
    )(rows_j, rows_i, *tables)


def partial_correlations(lefts, rights, tables, jobs, outs):
    left_arrays = [array for array, _ in lefts]
    right_arrays = [array for array, _, _ in rights]
    bins, depth, _ = right_arrays[0].shape
    piece = HALF // BLOCKS
    pitch = bins + 1
    step_bins = 32
    groups = []
    slices = {}
    for used, groups_here in jobs:
        js = [(rights[right][1], there) for right in used for there in rights[right][2]]
        for left, _, first in groups_here:
            found = []
            for offset in range(2):
                at = first + offset
                for order, (j_other, there) in enumerate(js):
                    if there != at:
                        kind = (lefts[left][1], j_other, there ^ (at % 2))
                        found.append((at, kind, offset * HALF + order * piece))
                        slices.setdefault(at, []).append(kind)
            groups.append(found)
    for kinds in slices.values():
        kinds.sort()
    total = len(groups) * piece
    batch = 4

    def first_of(at):
        (out,) = [positions for positions in outs if at in positions]
        return outs.index(out), sum(len(slices[before]) for before in out[: out.index(at)])

    def kernel(*refs):
        left_refs, rest = refs[: len(lefts)], refs[len(lefts) :]
        right_refs, rest = rest[: len(rights)], rest[len(rights) :]
        lag_ref, same_ref, out_refs, cross = rest[0], rest[1], rest[2:-1], rest[-1]
        lanes = lax.broadcasted_iota(jnp.int32, (depth, LANES), 1)

        first_half = lanes < HALF
        lower = lanes % HALF < HALF // 2
        blank = jnp.zeros((depth, LANES), jnp.bfloat16)

        def turn(values):
            swapped = []
            for first in range(0, depth, depth // 2):
                middle, last = first + depth // 4, first + depth // 2
                swapped += [-values[middle:last], values[first:middle]]
            return jnp.concatenate(swapped, axis=0)

        def right_hand(used, f):
            values = right_refs[used[0]][f]
            if len(used) == 2:
                values = jnp.where(lower, values, right_refs[used[1]][f])
            turned = turn(values)
            return jnp.concatenate(
                [
                    jnp.concatenate([jnp.where(first_half, part, blank) for part in (values, turned)], axis=1),
                    jnp.concatenate([jnp.where(first_half, blank, part) for part in (values, turned)], axis=1),
                ],
                axis=0,
            )

        def products(first_bin, count):
            found = []
            for f in [first_bin + u for u in range(count)]:
                first = 0
                for used, groups_here in jobs:
                    lhs = [left_refs[left][f, row : row + piece] for left, row, _ in groups_here]
                    lhs = jnp.concatenate(lhs, axis=0) if len(lhs) > 1 else lhs[0]
                    product = jnp.dot(lhs, right_hand(used, f), preferred_element_type=jnp.float32)
                    found.append((first * pitch + f, product))
                    first += lhs.shape[0]
            return found

        def keep(found):
            for here, product in found:
                for part in range(2):
                    cross[pl.ds(part * total * pitch + here, product.shape[0], stride=pitch), :] = product[
                        :, part * LANES : (part + 1) * LANES
                    ]

        def some_bins(step, carry):
            first = step * step_bins
            waiting = products(first, batch)
            for at in range(batch, step_bins, batch):
                following = products(first + at, batch)
                keep(waiting)
                waiting = following
            keep(waiting)
            return carry

        lax.fori_loop(0, bins // step_bins, some_bins, 0)

        for index, found in enumerate(groups):
            targets = []
            for at, kind, lane in found:
                out, first = first_of(at)
                targets.append((out_refs[out], first + slices[at].index(kind), lane))

            def summed(i):
                parts = []
                for part in range(2):
                    start = (part * total + index * piece + i) * pitch
                    parts.append(
                        jnp.concatenate([cross[pl.ds(start, bins), :], cross[pl.ds(start + pitch, bins), :]], axis=1)
                    )
                values = jnp.concatenate(parts, axis=0).astype(jnp.bfloat16)
                return i, jnp.dot(lag_ref[...], values, preferred_element_type=jnp.float32)

            def across(i, lagged):
                lagged = lagged.astype(jnp.bfloat16)
                return i, lax.dot_general(same_ref[...], lagged, NT, preferred_element_type=jnp.float32)

            def store(i, rows):
                for half in range(2):
                    for out, place, lane in targets:
                        row = half * LANES + lane
                        out[place, i + half] = rows[row : row + piece].astype(out.dtype)

            sums, rows = summed(0), None
            for i in range(2, piece, 2):
                more = summed(i)
                if rows is not None:
                    store(*rows)
                rows = across(*sums)
                sums = more
            store(*rows)
            store(*across(*sums))

    shapes = [(sum(len(slices[at]) for at in positions), piece, piece, LAGS) for positions in outs]
    types = [jnp.float32 if positions == (OWN_AT,) else jnp.bfloat16 for positions in outs]
    results = kernel_call(
        kernel,
        "partial_correlations",
        4 * total * bins * depth * LANES + 4 * total * bins * LANES * LAGS,
        2 * sum(array.size for array in left_arrays + right_arrays),
        out_shape=[jax.ShapeDtypeStruct(shape, kind) for shape, kind in zip(shapes, types)],
        in_specs=[in_vmem()] * (len(lefts) + len(rights) + len(tables)),
        out_specs=[in_vmem()] * len(shapes),
        scratch_shapes=[pltpu.VMEM(((2 * total + 1) * pitch, LANES), jnp.float32)],
    )(*left_arrays, *right_arrays, *tables)
    return results, slices


def assembled(shares):
    arrays = [array for array, _ in shares]
    _, piece, _, lags = arrays[0].shape
    width = 2 * piece

    def kernel(*refs):
        out, held, sems = refs[-3:]
        sub = lax.axis_index("sub")
        odd = lax.rem(lax.axis_index("chan"), 2)
        copies = []
        for there, round_at in ((0, 1), (1, 2 - 2 * odd), (3, 2 * odd)):
            for i_other in range(2):
                for j_other in range(2):
                    parts = [
                        refs[at][place].astype(jnp.float32)
                        for at, (_, kinds) in enumerate(shares)
                        for place, kind in enumerate(kinds)
                        if kind == (i_other, j_other, there)
                    ]
                    i_first = jnp.where(sub == 0, i_other, 1 - i_other) * piece
                    j_first = pl.multiple_of(jnp.where(sub == 0, j_other, 1 - j_other) * piece, piece)
                    held[round_at, 0, pl.ds(i_first, piece), pl.ds(j_first, piece), :] = functools.reduce(
                        jnp.add, parts
                    )
            at = len(copies)
            copies.append(pltpu.make_async_copy(held.at[round_at], out.at[round_at], sems.at[at]))
            copies[-1].start()
        for copy in copies:
            copy.wait()

    shape = (ROUNDS, 1, width, width, lags)
    return kernel_call(
        kernel,
        "assembled",
        0,
        sum(array.size for array in arrays) * 2,
        out_shape=jax.ShapeDtypeStruct(shape, jnp.float32),
        in_specs=[in_vmem()] * len(arrays),
        out_specs=pl.BlockSpec(memory_space=pl.ANY),
        scratch_shapes=[pltpu.VMEM(shape, jnp.float32), pltpu.SemaphoreType.DMA((ROUNDS,))],
    )(*arrays)


def summed_in_place(traces, channel_slot):
    chan_count = lax.axis_size("chan")
    _, win_here, samples = traces.shape
    piece = HALF // BLOCKS
    scale = (2.0 / (win_here * chan_count * (samples // 2))) ** 0.5
    dft_rows = dft_rows_table(samples)
    same = selection(2 * LANES, 2 * LANES, [(n, n) for n in range(2 * LANES)])
    tables = [lag_rows_table(samples, scale), same]
    everywhere = tuple(range(BLOCKS))

    def over_sub(rows):
        return lax.ppermute(rows, "sub", [(0, 1), (1, 0)])

    def over_core(rows):
        return lax.ppermute(rows, "rep", [(0, 1), (1, 0)])

    def with_device(share, apart):
        return lax.ppermute(share, "chan", [(z, z ^ apart) for z in range(chan_count)])

    def after(value, *others):
        return lax.optimization_barrier((value,) + others)[0]

    def added(share, arrived):
        return (share.astype(jnp.float32) + arrived.astype(jnp.float32)).astype(jnp.bfloat16)

    def for_two_away(kinds):
        return [(i_other, j_other, there ^ 2) for i_other, j_other, there in kinds]

    mine, mine_far, mine_near = order_rows(traces, channel_slot, [everywhere, FAR, NEAR])
    far = over_sub(mine_far)
    near = over_sub(mine_near)

    own_i, own_j = spectra(mine, over_core(mine), (dft_rows, *own_picks()))
    own_left, own_right = (own_i, 0), (own_j, 0, everywhere)
    own_far, own_near = (0, 0, FAR[0]), (0, piece, NEAR[0])
    (kept_1, sent_far_1, own_1, sent_near_1), kinds_1 = partial_correlations(
        [own_left], [own_right], tables, [((0,), [own_far, own_near])], [(0,), (1,), (2,), (3,)]
    )
    arrived_far_1 = with_device(sent_far_1, 1)

    far, arrived_far_1 = lax.optimization_barrier((far, arrived_far_1))
    far_1 = with_device(added(kept_1, arrived_far_1), 2)
    far_i, far_j = spectra(far, over_core(far), (dft_rows, *half_picks()))
    far_left, far_right = (far_i, 1), (far_j, 1, FAR)
    other_far = (1, 0, FAR[0])
    (kept_2, sent_far_2, own_2, sent_near_2), kinds_2 = partial_correlations(
        [own_left, far_left],
        [own_right, far_right],
        tables,
        [((0,), [other_far]), ((1,), [own_far, own_near, other_far])],
        [(0,), (1,), (2,), (3,)],
    )
    sent_far_2, far_1 = lax.optimization_barrier((sent_far_2, far_1))
    arrived_far_2 = with_device(sent_far_2, 1)

    near, arrived_far_2 = lax.optimization_barrier((near, arrived_far_2))
    near_i, near_j = spectra(near, over_core(near), (dft_rows, *half_picks()))
    summed_2 = added(kept_2, arrived_far_2)
    far_2 = with_device(summed_2, 2)
    near_j = after(near_j, summed_2)
    near_left, near_right = (near_i, 1), (near_j, 1, NEAR)
    (kept_3, sent_far_3, own_3, sent_near_3), kinds_3 = partial_correlations(
        [own_left, far_left],
        [near_right],
        tables,
        [((0,), [own_far, other_far, own_near])],
        [(0,), (1,), (2,), (3,)],
    )
    arrived_far_3 = with_device(sent_far_3, 1)
    arrived_near = with_device(jnp.concatenate([sent_near_1, sent_near_2]), 1)
    near_right = (after(near_j, kept_3, sent_far_3, far_2, arrived_near), 1, NEAR)
    (own_4, sent_4), kinds_4 = partial_correlations(
        [near_left], [far_right, near_right], tables, [((0, 1), [(0, 0, NEAR[0])])], [(2,), (3,)]
    )
    arrived_4 = with_device(jnp.concatenate([sent_near_3, sent_4]), 1)
    summed_3 = added(after(kept_3, own_4), arrived_far_3)
    far_3 = with_device(summed_3, 2)
    near_left = (after(near_i, own_4, sent_4, summed_3), 1)
    (own_5, sent_5), kinds_5 = partial_correlations(
        [near_left], [own_right], tables, [((0,), [(0, 0, NEAR[0])])], [(2,), (3,)]
    )
    arrived_5 = with_device(sent_5, 1)
    shares = [
        (own_1, kinds_1[2]),
        (own_2, kinds_2[2]),
        (own_3, kinds_3[2]),
        (own_4, kinds_4[2]),
        (own_5, kinds_5[2]),
        (arrived_near, kinds_1[3] + kinds_2[3]),
        (arrived_4, kinds_3[3] + kinds_4[3]),
        (arrived_5, kinds_5[3]),
        (far_1, for_two_away(kinds_1[0])),
        (far_2, for_two_away(kinds_2[0])),
        (far_3, for_two_away(kinds_3[0])),
    ]
    return assembled(shares)


def from_behind(shard, axis, by):
    count = lax.axis_size(axis)
    return lax.ppermute(shard, axis, [(i, (i + by) % count) for i in range(count)])


def dft_columns(samples, parts, sub_bins):
    shape = (samples, parts, 2, sub_bins)
    time_pos = lax.broadcasted_iota(jnp.int32, shape, 0)
    range_pos = lax.broadcasted_iota(jnp.int32, shape, 1)
    part_pos = lax.broadcasted_iota(jnp.int32, shape, 2)
    bin_pos = lax.broadcasted_iota(jnp.int32, shape, 3)
    frequency = range_pos * sub_bins + bin_pos
    angles = jnp.mod(time_pos * frequency, samples).astype(jnp.float32) * (2.0 * math.pi / samples)
    entries = jnp.where(part_pos == 0, jnp.cos(angles), -jnp.sin(angles))
    return entries.reshape(samples, parts * 2 * sub_bins).astype(jnp.bfloat16)


def lag_table(sub_bins, first_bin, lag_count, samples):
    frequency = first_bin + lax.broadcasted_iota(jnp.int32, (sub_bins, lag_count), 0)
    lag_offset = lax.broadcasted_iota(jnp.int32, (sub_bins, lag_count), 1) - lag_count // 2
    angles = jnp.mod(frequency * lag_offset, samples).astype(jnp.float32) * (2.0 * math.pi / samples)
    return jnp.stack([jnp.cos(angles), -jnp.sin(angles)], axis=1)


def moved_spectra(traces, channel_slot):
    chan_count = lax.axis_size("chan")
    sub_count = lax.axis_size("sub")
    group_rows, win_here, samples = traces.shape
    bin_count = samples // 2
    sub_bins = bin_count // sub_count
    bin_width = 2 * sub_bins
    piece_len = group_rows // chan_count
    picked = jnp.take(traces, channel_slot, axis=0)
    dft_rows = dft_columns(samples, sub_count, sub_bins)
    spectrum = jnp.dot(picked.reshape(-1, samples), dft_rows, preferred_element_type=jnp.float32)
    energy = jnp.sum(spectrum * spectrum, axis=1, keepdims=True) / bin_count
    whitened = (spectrum * lax.rsqrt(energy + 1e-05)).astype(jnp.bfloat16)
    whitened = whitened.reshape(chan_count, piece_len, win_here, sub_count, bin_width)
    regrouped = lax.all_to_all(whitened, "chan", split_axis=0, concat_axis=0, tiled=True)
    regrouped = lax.all_to_all(regrouped, "sub", split_axis=3, concat_axis=3, tiled=True)
    own_half = regrouped.transpose(3, 1, 0, 2, 4).reshape(sub_count * piece_len, chan_count * win_here, bin_width)
    own_block = lax.all_gather(own_half, "rep", axis=0, tiled=True)
    windows = own_block.shape[1]
    own_split = own_block.reshape(own_block.shape[0], windows, 2, sub_bins)
    lag_rows = lag_table(sub_bins, lax.axis_index("sub") * sub_bins, LAGS, samples)
    lag_scale = (2.0 / (windows * bin_count)) ** 0.5
    results = []
    for step in range(1, ROUNDS + 1):
        partner = from_behind(own_half, "chan", -step)
        partner_split = partner.reshape(partner.shape[0], windows, 2, sub_bins)
        turned = jnp.stack([-partner_split[:, :, 1], partner_split[:, :, 0]], axis=2)
        partner_pair = jnp.stack([partner_split, turned], axis=0)
        cross_spec = jnp.einsum("iwpf,qjwpf->fqij", own_split, partner_pair, preferred_element_type=jnp.float32)
        summed = jnp.einsum("fqij,fql->ijl", cross_spec, lag_rows, precision=lax.Precision.HIGHEST)
        results.append(lax.psum_scatter(lag_scale * summed, "sub", scatter_dimension=0, tiled=True))
    return jnp.stack(results)[:, None]


def solution(mesh):
    sizes = mesh.shape
    in_place = sizes["chan"] == BLOCKS == ROUNDS + 1 and sizes["sub"] == 2 and sizes["rep"] == 2
    return jax.shard_map(
        summed_in_place if in_place else moved_spectra,
        mesh=mesh,
        in_specs=(P(("groups", "sub", "rep"), "chan", None), P(("groups", "sub", "rep"))),
        out_specs=P(None, ("groups", "chan"), "sub", "rep", None),
        check_vma=False,
    )
```

```python
import functools
import math

import jax
import jax.numpy as jnp
import numpy as np
from jax import lax
from jax.experimental import pallas as pl
from jax.experimental.pallas import tpu as pltpu
from jax.sharding import PartitionSpec as P

LAGS = 128
ROUNDS = 3
LANES = 128
HALF = LANES // 2
VMEM_BYTES = 32 * 1024 * 1024
ORDER_VMEM_BYTES = 48 * 1024 * 1024
NT = (((1,), (1,)), ((), ()))
BLOCKS = 4
FAR = (0, 1)
NEAR = (2, 3)
KEPT_AT, OWN_AT = 0, 2


def kernel_call(kernel, name, flops, bytes_accessed, vmem_bytes=VMEM_BYTES, **more):
    return pl.pallas_call(
        kernel,
        name=name,
        compiler_params=pltpu.CompilerParams(vmem_limit_bytes=vmem_bytes),
        cost_estimate=pl.CostEstimate(flops=flops, bytes_accessed=bytes_accessed, transcendentals=0),
        **more,
    )


def in_vmem():
    return pl.BlockSpec(memory_space=pltpu.VMEM)


def dft_rows_table(samples):
    bins = samples // 2
    turns = (np.arange(bins)[:, None] * np.arange(samples)[None, :]) % samples
    angles = turns.astype(np.float32) * np.float32(2.0 * math.pi / samples)
    table = np.concatenate([np.cos(angles), -np.sin(angles)], axis=0)
    return jnp.asarray(table.astype(np.float32)).astype(jnp.bfloat16)


def lag_rows_table(samples, scale):
    bins = samples // 2
    offsets = np.arange(LAGS) - LAGS // 2
    turns = (offsets[:, None] * np.arange(bins)[None, :]) % samples
    angles = turns.astype(np.float32) * np.float32(2.0 * math.pi / samples)
    table = np.concatenate([np.cos(angles), -np.sin(angles)], axis=1) * np.float32(scale)
    return jnp.asarray(table.astype(np.float32)).astype(jnp.bfloat16)


def selection(rows, columns, ones):
    table = np.zeros((rows, columns), np.float32)
    for row, column in ones:
        table[row, column] = 1.0
    return jnp.asarray(table).astype(jnp.bfloat16)


def own_picks():
    piece = HALF // BLOCKS
    to_i = []
    for at in range(BLOCKS):
        for n in range(piece):
            to_i.append((at // 2 * piece + n, at % 2 * LANES + HALF + at * piece + n))
    to_j = [(j, copy * HALF + j) for j in range(HALF) for copy in range(2)]
    return selection(2 * piece, 2 * LANES, to_i), selection(LANES, LANES, to_j)


def half_picks():
    count = HALF // 2
    to_i, to_j = [], []
    for odd in range(2):
        for n in range(count):
            to_i.append((n, odd * LANES + odd * HALF + count + n))
            to_j += [(odd * HALF + n, odd * LANES + copy * count + n) for copy in range(4)]
    return selection(count, 2 * LANES, to_i), selection(LANES, 2 * LANES, to_j)


def order_rows(traces, slots, kinds):
    rows, wins, samples = traces.shape
    tiles = samples // LANES
    piece = rows // BLOCKS
    step_wins = 16
    steps = wins // step_wins
    batch = 4
    used = max(kinds, key=len)
    pitch = len(used) * piece + 1

    def kernel(slots_ref, traces_ref, *refs):
        out_refs, (wide, in_ref, slot_ref, sems) = refs[:-4], refs[-4:]
        slot_copy = pltpu.make_async_copy(slots_ref, slot_ref, sems.at[steps])
        slot_copy.start()
        copies = []
        for step in range(steps):
            here = pl.ds(step * step_wins, step_wins)
            copies.append(
                pltpu.make_async_copy(traces_ref.at[:, here, :], in_ref.at[:, here, :], sems.at[step])
            )
            copies[-1].start()
        slot_copy.wait()
        z = lax.axis_index("chan")
        odd = lax.rem(z, 2)
        pair = jnp.where(z < 2, 2, 0)

        def some_windows(step):
            first_win = step * step_wins
            for at, position in enumerate(used):
                block = pair + position + (odd if position % 2 == 0 else -odd)
                first = lax.rem(block, BLOCKS) * piece

                def move(group, carry, at=at, first=first):
                    js = [group * batch + u for u in range(batch)]
                    picked = [
                        in_ref[slot_ref[first + j], pl.ds(first_win, step_wins), :].astype(jnp.float32) for j in js
                    ]
                    for j, row in zip(js, picked):
                        for tile in range(tiles):
                            wide[tile, pl.ds(at * piece + j, step_wins, stride=pitch), :] = row[
                                :, tile * LANES : (tile + 1) * LANES
                            ]
                    return carry

                lax.fori_loop(0, piece // batch, move, 0)

            def pack(w, carry):
                blocks = [
                    wide[tile, pl.ds(w * pitch, len(used) * piece), :].astype(jnp.bfloat16) for tile in range(tiles)
                ]
                for out_ref, kind in zip(out_refs, kinds):
                    first = used.index(kind[0]) * piece
                    for tile, block in enumerate(blocks):
                        out_ref[first_win + w, :, tile * LANES : (tile + 1) * LANES] = block[
                            first : first + len(kind) * piece
                        ]
                return carry

            lax.fori_loop(0, step_wins, pack, 0, unroll=2)

        for step in range(steps):
            copies[step].wait()
            some_windows(step)

    return kernel_call(
        kernel,
        "order_rows",
        0,
        3 * traces.size * 2,
        vmem_bytes=ORDER_VMEM_BYTES,
        out_shape=[jax.ShapeDtypeStruct((wins, len(kind) * piece, samples), jnp.bfloat16) for kind in kinds],
        in_specs=[pl.BlockSpec(memory_space=pltpu.HBM)] * 2,
        out_specs=[in_vmem()] * len(kinds),
        scratch_shapes=[
            pltpu.VMEM((tiles, (step_wins + 1) * pitch, LANES), jnp.float32),
            pltpu.VMEM(traces.shape, traces.dtype),
            pltpu.SMEM(slots.shape, slots.dtype),
            pltpu.SemaphoreType.DMA((steps + 1,)),
        ],
    )(slots, traces)


def diagonal(values, copies):
    blank = jnp.zeros_like(values)
    rows = [[values if at == copy else blank for at in range(copies)] for copy in range(copies)]
    return jnp.concatenate([jnp.concatenate(row, axis=1) for row in rows], axis=0)


def spectra(rows_j, rows_i, tables):
    wins, given, samples = rows_j.shape
    bins = samples // 2
    pairs = wins // 2
    depth = 2 * wins
    folded = HALF // given
    line = depth // folded
    pitch = line + 1
    per_step = 2 * folded
    batch = 8

    def kernel(j_ref, i_ref, table_ref, to_i_ref, to_j_ref, i_out, j_out, wide):
        same = lax.axis_index("sub") == lax.axis_index("rep")

        def spectrum_of(group):
            stacked = []
            for win in [per_step * group + u for u in range(per_step)]:
                here = j_ref[win]
                stacked += [here, jnp.where(same, here, i_ref[win])]
            wave = jnp.concatenate(stacked, axis=0)
            return lax.dot_general(table_ref[...], wave, NT, preferred_element_type=jnp.float32)

        def keep(group, spectrum):
            energy = jnp.sum(spectrum * spectrum, axis=0, keepdims=True) / bins
            white = spectrum * lax.rsqrt(energy + 1e-05)
            for half in range(2):
                for part in range(2):
                    if folded == 1:
                        row = half * wins + part * pairs + group
                    else:
                        row = part * pairs + 2 * group + half
                    wide[pl.ds(row, bins, stride=pitch), :] = white[
                        part * bins : (part + 1) * bins, half * LANES : (half + 1) * LANES
                    ]

        groups = wins // per_step
        at_once = 4

        def some_windows(step, carry):
            first = step * at_once
            last = spectrum_of(first)
            for group in range(1, at_once):
                now = spectrum_of(first + group)
                keep(first + group - 1, last)
                last = now
            keep(first + at_once - 1, last)
            return carry

        lax.fori_loop(0, groups // at_once, some_windows, 0)

        def moved(fs):
            loaded = [wide[pl.ds(f * pitch, line), :].astype(jnp.bfloat16) for f in fs]
            i_rows = [
                lax.dot_general(to_i_ref[...], diagonal(values, 2), NT, preferred_element_type=jnp.float32)
                for values in loaded
            ]
            if folded == 2:
                i_rows = [jnp.concatenate([rows[: given // 2], rows[given // 2 :]], axis=1) for rows in i_rows]
            j_rows = jnp.dot(jnp.concatenate(loaded, axis=0), to_j_ref[...], preferred_element_type=jnp.float32)
            return fs, i_rows, j_rows

        def store(fs, i_rows, j_rows):
            for at, f in enumerate(fs):
                i_out[f] = i_rows[at].astype(jnp.bfloat16)
                for odd in range(folded):
                    j_out[f, odd * line : (odd + 1) * line] = j_rows[
                        at * line : (at + 1) * line, odd * LANES : (odd + 1) * LANES
                    ].astype(jnp.bfloat16)

        def pack(group, carry):
            first = group * 4 * batch
            waiting = moved([first + u for u in range(batch)])
            for at in range(1, 4):
                following = moved([first + at * batch + u for u in range(batch)])
                store(*waiting)
                waiting = following
            store(*waiting)
            return carry

        lax.fori_loop(0, bins // (4 * batch), pack, 0)

    shapes = [(bins, given // 2, LANES), (bins, depth, LANES)]
    return kernel_call(
        kernel,
        "spectra",
        4 * samples * samples * wins * given,
        4 * wins * given * samples * 2,
        out_shape=[jax.ShapeDtypeStruct(shape, jnp.bfloat16) for shape in shapes],
        in_specs=[in_vmem()] * (2 + len(tables)),
        out_specs=[in_vmem()] * len(shapes),
        scratch_shapes=[pltpu.VMEM(((bins + 1) * pitch, LANES), jnp.float32)],
    )(rows_j, rows_i, *tables)


def partial_correlations(lefts, rights, tables, jobs, outs):
    left_arrays = [array for array, _ in lefts]
    right_arrays = [array for array, _, _ in rights]
    bins, depth, _ = right_arrays[0].shape
    piece = HALF // BLOCKS
    pitch = bins + 1
    step_bins = 32
    groups = []
    slices = {}
    for used, groups_here in jobs:
        js = [(rights[right][1], there) for right in used for there in rights[right][2]]
        for left, _, first in groups_here:
            found = []
            for offset in range(2):
                at = first + offset
                for order, (j_other, there) in enumerate(js):
                    if there != at:
                        kind = (lefts[left][1], j_other, there ^ (at % 2))
                        found.append((at, kind, offset * HALF + order * piece))
                        slices.setdefault(at, []).append(kind)
            groups.append(found)
    for kinds in slices.values():
        kinds.sort()
    total = len(groups) * piece
    batch = 4

    def first_of(at):
        (out,) = [positions for positions in outs if at in positions]
        return outs.index(out), sum(len(slices[before]) for before in out[: out.index(at)])

    def kernel(*refs):
        left_refs, rest = refs[: len(lefts)], refs[len(lefts) :]
        right_refs, rest = rest[: len(rights)], rest[len(rights) :]
        lag_ref, same_ref, out_refs, cross = rest[0], rest[1], rest[2:-1], rest[-1]
        lanes = lax.broadcasted_iota(jnp.int32, (depth, LANES), 1)

        first_half = lanes < HALF
        lower = lanes % HALF < HALF // 2
        blank = jnp.zeros((depth, LANES), jnp.bfloat16)

        def turn(values):
            swapped = []
            for first in range(0, depth, depth // 2):
                middle, last = first + depth // 4, first + depth // 2
                swapped += [-values[middle:last], values[first:middle]]
            return jnp.concatenate(swapped, axis=0)

        def right_hand(used, f):
            values = right_refs[used[0]][f]
            if len(used) == 2:
                values = jnp.where(lower, values, right_refs[used[1]][f])
            turned = turn(values)
            return jnp.concatenate(
                [
                    jnp.concatenate([jnp.where(first_half, part, blank) for part in (values, turned)], axis=1),
                    jnp.concatenate([jnp.where(first_half, blank, part) for part in (values, turned)], axis=1),
                ],
                axis=0,
            )

        def products(first_bin, count):
            found = []
            for f in [first_bin + u for u in range(count)]:
                first = 0
                for used, groups_here in jobs:
                    lhs = [left_refs[left][f, row : row + piece] for left, row, _ in groups_here]
                    lhs = jnp.concatenate(lhs, axis=0) if len(lhs) > 1 else lhs[0]
                    product = jnp.dot(lhs, right_hand(used, f), preferred_element_type=jnp.float32)
                    found.append((first * pitch + f, product))
                    first += lhs.shape[0]
            return found

        def keep(found):
            for here, product in found:
                for part in range(2):
                    cross[pl.ds(part * total * pitch + here, product.shape[0], stride=pitch), :] = product[
                        :, part * LANES : (part + 1) * LANES
                    ]

        def some_bins(step, carry):
            first = step * step_bins
            waiting = products(first, batch)
            for at in range(batch, step_bins, batch):
                following = products(first + at, batch)
                keep(waiting)
                waiting = following
            keep(waiting)
            return carry

        lax.fori_loop(0, bins // step_bins, some_bins, 0)

        for index, found in enumerate(groups):
            targets = []
            for at, kind, lane in found:
                out, first = first_of(at)
                targets.append((out_refs[out], first + slices[at].index(kind), lane))

            def summed(i):
                parts = []
                for part in range(2):
                    start = (part * total + index * piece + i) * pitch
                    parts.append(
                        jnp.concatenate([cross[pl.ds(start, bins), :], cross[pl.ds(start + pitch, bins), :]], axis=1)
                    )
                values = jnp.concatenate(parts, axis=0).astype(jnp.bfloat16)
                return i, jnp.dot(lag_ref[...], values, preferred_element_type=jnp.float32)

            def across(i, lagged):
                lagged = lagged.astype(jnp.bfloat16)
                return i, lax.dot_general(same_ref[...], lagged, NT, preferred_element_type=jnp.float32)

            def store(i, rows):
                for half in range(2):
                    for out, place, lane in targets:
                        row = half * LANES + lane
                        out[place, i + half] = rows[row : row + piece].astype(out.dtype)

            sums, rows = summed(0), None
            for i in range(2, piece, 2):
                more = summed(i)
                if rows is not None:
                    store(*rows)
                rows = across(*sums)
                sums = more
            store(*rows)
            store(*across(*sums))

    shapes = [(sum(len(slices[at]) for at in positions), piece, piece, LAGS) for positions in outs]
    types = [jnp.float32 if positions == (OWN_AT,) else jnp.bfloat16 for positions in outs]
    results = kernel_call(
        kernel,
        "partial_correlations",
        4 * total * bins * depth * LANES + 4 * total * bins * LANES * LAGS,
        2 * sum(array.size for array in left_arrays + right_arrays),
        out_shape=[jax.ShapeDtypeStruct(shape, kind) for shape, kind in zip(shapes, types)],
        in_specs=[in_vmem()] * (len(lefts) + len(rights) + len(tables)),
        out_specs=[in_vmem()] * len(shapes),
        scratch_shapes=[pltpu.VMEM(((2 * total + 1) * pitch, LANES), jnp.float32)],
    )(*left_arrays, *right_arrays, *tables)
    return results, slices


def assembled(shares):
    arrays = [array for array, _ in shares]
    _, piece, _, lags = arrays[0].shape
    width = 2 * piece

    def kernel(*refs):
        out, held, sems = refs[-3:]
        sub = lax.axis_index("sub")
        odd = lax.rem(lax.axis_index("chan"), 2)
        copies = []
        for there, round_at in ((0, 1), (1, 2 - 2 * odd), (3, 2 * odd)):
            for i_other in range(2):
                for j_other in range(2):
                    parts = [
                        refs[at][place].astype(jnp.float32)
                        for at, (_, kinds) in enumerate(shares)
                        for place, kind in enumerate(kinds)
                        if kind == (i_other, j_other, there)
                    ]
                    i_first = jnp.where(sub == 0, i_other, 1 - i_other) * piece
                    j_first = pl.multiple_of(jnp.where(sub == 0, j_other, 1 - j_other) * piece, piece)
                    held[round_at, 0, pl.ds(i_first, piece), pl.ds(j_first, piece), :] = functools.reduce(
                        jnp.add, parts
                    )
            at = len(copies)
            copies.append(pltpu.make_async_copy(held.at[round_at], out.at[round_at], sems.at[at]))
            copies[-1].start()
        for copy in copies:
            copy.wait()

    shape = (ROUNDS, 1, width, width, lags)
    return kernel_call(
        kernel,
        "assembled",
        0,
        sum(array.size for array in arrays) * 2,
        out_shape=jax.ShapeDtypeStruct(shape, jnp.float32),
        in_specs=[in_vmem()] * len(arrays),
        out_specs=pl.BlockSpec(memory_space=pl.ANY),
        scratch_shapes=[pltpu.VMEM(shape, jnp.float32), pltpu.SemaphoreType.DMA((ROUNDS,))],
    )(*arrays)


def summed_in_place(traces, channel_slot):
    chan_count = lax.axis_size("chan")
    _, win_here, samples = traces.shape
    piece = HALF // BLOCKS
    scale = (2.0 / (win_here * chan_count * (samples // 2))) ** 0.5
    dft_rows = dft_rows_table(samples)
    same = selection(2 * LANES, 2 * LANES, [(n, n) for n in range(2 * LANES)])
    tables = [lag_rows_table(samples, scale), same]
    everywhere = tuple(range(BLOCKS))

    def over_sub(rows):
        return lax.ppermute(rows, "sub", [(0, 1), (1, 0)])

    def over_core(rows):
        return lax.ppermute(rows, "rep", [(0, 1), (1, 0)])

    def with_device(share, apart):
        return lax.ppermute(share, "chan", [(z, z ^ apart) for z in range(chan_count)])

    def after(value, *others):
        return lax.optimization_barrier((value,) + others)[0]

    def added(share, arrived):
        return (share.astype(jnp.float32) + arrived.astype(jnp.float32)).astype(jnp.bfloat16)

    def for_two_away(kinds):
        return [(i_other, j_other, there ^ 2) for i_other, j_other, there in kinds]

    mine, mine_far, mine_near = order_rows(traces, channel_slot, [everywhere, FAR, NEAR])
    far = over_sub(mine_far)
    near = over_sub(mine_near)

    own_i, own_j = spectra(mine, over_core(mine), (dft_rows, *own_picks()))
    own_left, own_right = (own_i, 0), (own_j, 0, everywhere)
    own_far, own_near = (0, 0, FAR[0]), (0, piece, NEAR[0])
    (kept_1, sent_far_1, own_1, sent_near_1), kinds_1 = partial_correlations(
        [own_left], [own_right], tables, [((0,), [own_far, own_near])], [(0,), (1,), (2,), (3,)]
    )
    arrived_far_1 = with_device(sent_far_1, 1)

    far, arrived_far_1 = lax.optimization_barrier((far, arrived_far_1))
    far_1 = with_device(added(kept_1, arrived_far_1), 2)
    arrived_near_1 = with_device(sent_near_1, 1)
    far_i, far_j = spectra(far, over_core(far), (dft_rows, *half_picks()))
    far_left, far_right = (far_i, 1), (far_j, 1, FAR)
    other_far = (1, 0, FAR[0])
    (kept_2, sent_far_2, own_2, sent_near_2), kinds_2 = partial_correlations(
        [own_left, far_left],
        [own_right, far_right],
        tables,
        [((0,), [other_far]), ((1,), [own_far, own_near, other_far])],
        [(0,), (1,), (2,), (3,)],
    )
    sent_far_2, far_1, arrived_near_1 = lax.optimization_barrier((sent_far_2, far_1, arrived_near_1))
    arrived_far_2 = with_device(sent_far_2, 1)

    near, arrived_far_2 = lax.optimization_barrier((near, arrived_far_2))
    near_i, near_j = spectra(near, over_core(near), (dft_rows, *half_picks()))
    summed_2 = added(kept_2, arrived_far_2)
    far_2 = with_device(summed_2, 2)
    near_j = after(near_j, summed_2)
    near_left, near_right = (near_i, 1), (near_j, 1, NEAR)
    (kept_3, sent_far_3, own_3, sent_near_3), kinds_3 = partial_correlations(
        [own_left, far_left],
        [near_right],
        tables,
        [((0,), [own_far, other_far, own_near])],
        [(0,), (1,), (2,), (3,)],
    )
    arrived_far_3 = with_device(sent_far_3, 1)
    arrived_near_2 = with_device(sent_near_2, 1)
    near_right = (after(near_j, kept_3, sent_far_3, far_2, arrived_near_2), 1, NEAR)
    (own_4, sent_4), kinds_4 = partial_correlations(
        [near_left], [far_right, near_right], tables, [((0, 1), [(0, 0, NEAR[0])])], [(2,), (3,)]
    )
    arrived_4 = with_device(jnp.concatenate([sent_near_3, sent_4]), 1)
    summed_3 = added(after(kept_3, own_4), arrived_far_3)
    far_3 = with_device(summed_3, 2)
    near_left = (after(near_i, own_4, sent_4, summed_3), 1)
    (own_5, sent_5), kinds_5 = partial_correlations(
        [near_left], [own_right], tables, [((0,), [(0, 0, NEAR[0])])], [(2,), (3,)]
    )
    arrived_5 = with_device(sent_5, 1)
    shares = [
        (own_1, kinds_1[2]),
        (own_2, kinds_2[2]),
        (own_3, kinds_3[2]),
        (own_4, kinds_4[2]),
        (own_5, kinds_5[2]),
        (arrived_near_1, kinds_1[3]),
        (arrived_near_2, kinds_2[3]),
        (arrived_4, kinds_3[3] + kinds_4[3]),
        (arrived_5, kinds_5[3]),
        (far_1, for_two_away(kinds_1[0])),
        (far_2, for_two_away(kinds_2[0])),
        (far_3, for_two_away(kinds_3[0])),
    ]
    return assembled(shares)


def from_behind(shard, axis, by):
    count = lax.axis_size(axis)
    return lax.ppermute(shard, axis, [(i, (i + by) % count) for i in range(count)])


def dft_columns(samples, parts, sub_bins):
    shape = (samples, parts, 2, sub_bins)
    time_pos = lax.broadcasted_iota(jnp.int32, shape, 0)
    range_pos = lax.broadcasted_iota(jnp.int32, shape, 1)
    part_pos = lax.broadcasted_iota(jnp.int32, shape, 2)
    bin_pos = lax.broadcasted_iota(jnp.int32, shape, 3)
    frequency = range_pos * sub_bins + bin_pos
    angles = jnp.mod(time_pos * frequency, samples).astype(jnp.float32) * (2.0 * math.pi / samples)
    entries = jnp.where(part_pos == 0, jnp.cos(angles), -jnp.sin(angles))
    return entries.reshape(samples, parts * 2 * sub_bins).astype(jnp.bfloat16)


def lag_table(sub_bins, first_bin, lag_count, samples):
    frequency = first_bin + lax.broadcasted_iota(jnp.int32, (sub_bins, lag_count), 0)
    lag_offset = lax.broadcasted_iota(jnp.int32, (sub_bins, lag_count), 1) - lag_count // 2
    angles = jnp.mod(frequency * lag_offset, samples).astype(jnp.float32) * (2.0 * math.pi / samples)
    return jnp.stack([jnp.cos(angles), -jnp.sin(angles)], axis=1)


def moved_spectra(traces, channel_slot):
    chan_count = lax.axis_size("chan")
    sub_count = lax.axis_size("sub")
    group_rows, win_here, samples = traces.shape
    bin_count = samples // 2
    sub_bins = bin_count // sub_count
    bin_width = 2 * sub_bins
    piece_len = group_rows // chan_count
    picked = jnp.take(traces, channel_slot, axis=0)
    dft_rows = dft_columns(samples, sub_count, sub_bins)
    spectrum = jnp.dot(picked.reshape(-1, samples), dft_rows, preferred_element_type=jnp.float32)
    energy = jnp.sum(spectrum * spectrum, axis=1, keepdims=True) / bin_count
    whitened = (spectrum * lax.rsqrt(energy + 1e-05)).astype(jnp.bfloat16)
    whitened = whitened.reshape(chan_count, piece_len, win_here, sub_count, bin_width)
    regrouped = lax.all_to_all(whitened, "chan", split_axis=0, concat_axis=0, tiled=True)
    regrouped = lax.all_to_all(regrouped, "sub", split_axis=3, concat_axis=3, tiled=True)
    own_half = regrouped.transpose(3, 1, 0, 2, 4).reshape(sub_count * piece_len, chan_count * win_here, bin_width)
    own_block = lax.all_gather(own_half, "rep", axis=0, tiled=True)
    windows = own_block.shape[1]
    own_split = own_block.reshape(own_block.shape[0], windows, 2, sub_bins)
    lag_rows = lag_table(sub_bins, lax.axis_index("sub") * sub_bins, LAGS, samples)
    lag_scale = (2.0 / (windows * bin_count)) ** 0.5
    results = []
    for step in range(1, ROUNDS + 1):
        partner = from_behind(own_half, "chan", -step)
        partner_split = partner.reshape(partner.shape[0], windows, 2, sub_bins)
        turned = jnp.stack([-partner_split[:, :, 1], partner_split[:, :, 0]], axis=2)
        partner_pair = jnp.stack([partner_split, turned], axis=0)
        cross_spec = jnp.einsum("iwpf,qjwpf->fqij", own_split, partner_pair, preferred_element_type=jnp.float32)
        summed = jnp.einsum("fqij,fql->ijl", cross_spec, lag_rows, precision=lax.Precision.HIGHEST)
        results.append(lax.psum_scatter(lag_scale * summed, "sub", scatter_dimension=0, tiled=True))
    return jnp.stack(results)[:, None]


def solution(mesh):
    sizes = mesh.shape
    in_place = sizes["chan"] == BLOCKS == ROUNDS + 1 and sizes["sub"] == 2 and sizes["rep"] == 2
    return jax.shard_map(
        summed_in_place if in_place else moved_spectra,
        mesh=mesh,
        in_specs=(P(("groups", "sub", "rep"), "chan", None), P(("groups", "sub", "rep"))),
        out_specs=P(None, ("groups", "chan"), "sub", "rep", None),
        check_vma=False,
    )
```

```python
import functools
import math

import jax
import jax.numpy as jnp
import numpy as np
from jax import lax
from jax.experimental import pallas as pl
from jax.experimental.pallas import tpu as pltpu
from jax.sharding import PartitionSpec as P

LAGS = 128
ROUNDS = 3
LANES = 128
HALF = LANES // 2
VMEM_BYTES = 32 * 1024 * 1024
ORDER_VMEM_BYTES = 48 * 1024 * 1024
NT = (((1,), (1,)), ((), ()))
BLOCKS = 4
FAR = (0, 1)
NEAR = (2, 3)
KEPT_AT, OWN_AT = 0, 2


def kernel_call(kernel, name, flops, bytes_accessed, vmem_bytes=VMEM_BYTES, **more):
    return pl.pallas_call(
        kernel,
        name=name,
        compiler_params=pltpu.CompilerParams(vmem_limit_bytes=vmem_bytes),
        cost_estimate=pl.CostEstimate(flops=flops, bytes_accessed=bytes_accessed, transcendentals=0),
        **more,
    )


def in_vmem():
    return pl.BlockSpec(memory_space=pltpu.VMEM)


def dft_rows_table(samples):
    bins = samples // 2
    turns = (np.arange(bins)[:, None] * np.arange(samples)[None, :]) % samples
    angles = turns.astype(np.float32) * np.float32(2.0 * math.pi / samples)
    table = np.concatenate([np.cos(angles), -np.sin(angles)], axis=0)
    return jnp.asarray(table.astype(np.float32)).astype(jnp.bfloat16)


def lag_rows_table(samples, scale):
    bins = samples // 2
    offsets = np.arange(LAGS) - LAGS // 2
    turns = (offsets[:, None] * np.arange(bins)[None, :]) % samples
    angles = turns.astype(np.float32) * np.float32(2.0 * math.pi / samples)
    table = np.concatenate([np.cos(angles), -np.sin(angles)], axis=1) * np.float32(scale)
    return jnp.asarray(table.astype(np.float32)).astype(jnp.bfloat16)


def selection(rows, columns, ones):
    table = np.zeros((rows, columns), np.float32)
    for row, column in ones:
        table[row, column] = 1.0
    return jnp.asarray(table).astype(jnp.bfloat16)


def own_picks():
    piece = HALF // BLOCKS
    to_i = []
    for at in range(BLOCKS):
        for n in range(piece):
            to_i.append((at // 2 * piece + n, at % 2 * LANES + HALF + at * piece + n))
    to_j = [(j, copy * HALF + j) for j in range(HALF) for copy in range(2)]
    return selection(2 * piece, 2 * LANES, to_i), selection(LANES, LANES, to_j)


def half_picks():
    count = HALF // 2
    to_i, to_j = [], []
    for odd in range(2):
        for n in range(count):
            to_i.append((n, odd * LANES + odd * HALF + count + n))
            to_j += [(odd * HALF + n, odd * LANES + copy * count + n) for copy in range(4)]
    return selection(count, 2 * LANES, to_i), selection(LANES, 2 * LANES, to_j)


def order_rows(traces, slots, kinds):
    rows, wins, samples = traces.shape
    tiles = samples // LANES
    piece = rows // BLOCKS
    step_wins = 16
    steps = wins // step_wins
    batch = 4
    used = max(kinds, key=len)
    pitch = len(used) * piece + 1

    def kernel(slots_ref, traces_ref, *refs):
        out_refs, (wide, in_ref, slot_ref, sems) = refs[:-4], refs[-4:]
        slot_copy = pltpu.make_async_copy(slots_ref, slot_ref, sems.at[steps])
        slot_copy.start()
        copies = []
        for step in range(steps):
            here = pl.ds(step * step_wins, step_wins)
            copies.append(
                pltpu.make_async_copy(traces_ref.at[:, here, :], in_ref.at[:, here, :], sems.at[step])
            )
            copies[-1].start()
        slot_copy.wait()
        z = lax.axis_index("chan")
        odd = lax.rem(z, 2)
        pair = jnp.where(z < 2, 2, 0)

        def some_windows(step):
            first_win = step * step_wins
            for at, position in enumerate(used):
                block = pair + position + (odd if position % 2 == 0 else -odd)
                first = lax.rem(block, BLOCKS) * piece

                def move(group, carry, at=at, first=first):
                    js = [group * batch + u for u in range(batch)]
                    picked = [
                        in_ref[slot_ref[first + j], pl.ds(first_win, step_wins), :].astype(jnp.float32) for j in js
                    ]
                    for j, row in zip(js, picked):
                        for tile in range(tiles):
                            wide[tile, pl.ds(at * piece + j, step_wins, stride=pitch), :] = row[
                                :, tile * LANES : (tile + 1) * LANES
                            ]
                    return carry

                lax.fori_loop(0, piece // batch, move, 0)

            def pack(w, carry):
                blocks = [
                    wide[tile, pl.ds(w * pitch, len(used) * piece), :].astype(jnp.bfloat16) for tile in range(tiles)
                ]
                for out_ref, kind in zip(out_refs, kinds):
                    first = used.index(kind[0]) * piece
                    for tile, block in enumerate(blocks):
                        out_ref[first_win + w, :, tile * LANES : (tile + 1) * LANES] = block[
                            first : first + len(kind) * piece
                        ]
                return carry

            lax.fori_loop(0, step_wins, pack, 0, unroll=2)

        for step in range(steps):
            copies[step].wait()
            some_windows(step)

    return kernel_call(
        kernel,
        "order_rows",
        0,
        3 * traces.size * 2,
        vmem_bytes=ORDER_VMEM_BYTES,
        out_shape=[jax.ShapeDtypeStruct((wins, len(kind) * piece, samples), jnp.bfloat16) for kind in kinds],
        in_specs=[pl.BlockSpec(memory_space=pltpu.HBM)] * 2,
        out_specs=[in_vmem()] * len(kinds),
        scratch_shapes=[
            pltpu.VMEM((tiles, (step_wins + 1) * pitch, LANES), jnp.float32),
            pltpu.VMEM(traces.shape, traces.dtype),
            pltpu.SMEM(slots.shape, slots.dtype),
            pltpu.SemaphoreType.DMA((steps + 1,)),
        ],
    )(slots, traces)


def diagonal(values, copies):
    blank = jnp.zeros_like(values)
    rows = [[values if at == copy else blank for at in range(copies)] for copy in range(copies)]
    return jnp.concatenate([jnp.concatenate(row, axis=1) for row in rows], axis=0)


def spectra(rows_j, rows_i, tables):
    wins, given, samples = rows_j.shape
    bins = samples // 2
    pairs = wins // 2
    depth = 2 * wins
    folded = HALF // given
    line = depth // folded
    pitch = line + 1
    per_step = 2 * folded
    batch = 8

    def kernel(j_ref, i_ref, table_ref, to_i_ref, to_j_ref, i_out, j_out, wide):
        same = lax.axis_index("sub") == lax.axis_index("rep")

        def spectrum_of(group):
            stacked = []
            for win in [per_step * group + u for u in range(per_step)]:
                here = j_ref[win]
                stacked += [here, jnp.where(same, here, i_ref[win])]
            wave = jnp.concatenate(stacked, axis=0)
            return [
                lax.dot_general(
                    table_ref[part * bins : (part + 1) * bins], wave, NT, preferred_element_type=jnp.float32
                )
                for part in range(2)
            ]

        def keep(group, spectrum):
            energy = sum(jnp.sum(values * values, axis=0, keepdims=True) for values in spectrum) / bins
            white = [values * lax.rsqrt(energy + 1e-05) for values in spectrum]
            for half in range(2):
                for part in range(2):
                    if folded == 1:
                        row = half * wins + part * pairs + group
                    else:
                        row = part * pairs + 2 * group + half
                    wide[pl.ds(row, bins, stride=pitch), :] = white[part][:, half * LANES : (half + 1) * LANES]

        groups = wins // per_step
        at_once = 4

        def some_windows(step, carry):
            first = step * at_once
            last = spectrum_of(first)
            for group in range(1, at_once):
                now = spectrum_of(first + group)
                keep(first + group - 1, last)
                last = now
            keep(first + at_once - 1, last)
            return carry

        lax.fori_loop(0, groups // at_once, some_windows, 0)

        def moved(fs):
            loaded = [wide[pl.ds(f * pitch, line), :].astype(jnp.bfloat16) for f in fs]
            i_rows = [
                lax.dot_general(to_i_ref[...], diagonal(values, 2), NT, preferred_element_type=jnp.float32)
                for values in loaded
            ]
            if folded == 2:
                i_rows = [jnp.concatenate([rows[: given // 2], rows[given // 2 :]], axis=1) for rows in i_rows]
            j_rows = jnp.dot(jnp.concatenate(loaded, axis=0), to_j_ref[...], preferred_element_type=jnp.float32)
            return fs, i_rows, j_rows

        def store(fs, i_rows, j_rows):
            for at, f in enumerate(fs):
                i_out[f] = i_rows[at].astype(jnp.bfloat16)
                for odd in range(folded):
                    j_out[f, odd * line : (odd + 1) * line] = j_rows[
                        at * line : (at + 1) * line, odd * LANES : (odd + 1) * LANES
                    ].astype(jnp.bfloat16)

        def pack(group, carry):
            first = group * 4 * batch
            waiting = moved([first + u for u in range(batch)])
            for at in range(1, 4):
                following = moved([first + at * batch + u for u in range(batch)])
                store(*waiting)
                waiting = following
            store(*waiting)
            return carry

        lax.fori_loop(0, bins // (4 * batch), pack, 0)

    shapes = [(bins, given // 2, LANES), (bins, depth, LANES)]
    return kernel_call(
        kernel,
        "spectra",
        4 * samples * samples * wins * given,
        4 * wins * given * samples * 2,
        out_shape=[jax.ShapeDtypeStruct(shape, jnp.bfloat16) for shape in shapes],
        in_specs=[in_vmem()] * (2 + len(tables)),
        out_specs=[in_vmem()] * len(shapes),
        scratch_shapes=[pltpu.VMEM(((bins + 1) * pitch, LANES), jnp.float32)],
    )(rows_j, rows_i, *tables)


def partial_correlations(lefts, rights, tables, jobs, outs):
    left_arrays = [array for array, _ in lefts]
    right_arrays = [array for array, _, _ in rights]
    bins, depth, _ = right_arrays[0].shape
    piece = HALF // BLOCKS
    pitch = bins + 1
    step_bins = 32
    groups = []
    slices = {}
    for used, groups_here in jobs:
        js = [(rights[right][1], there) for right in used for there in rights[right][2]]
        for left, _, first in groups_here:
            found = []
            for offset in range(2):
                at = first + offset
                for order, (j_other, there) in enumerate(js):
                    if there != at:
                        kind = (lefts[left][1], j_other, there ^ (at % 2))
                        found.append((at, kind, offset * HALF + order * piece))
                        slices.setdefault(at, []).append(kind)
            groups.append(found)
    for kinds in slices.values():
        kinds.sort()
    total = len(groups) * piece
    batch = 4

    def first_of(at):
        (out,) = [positions for positions in outs if at in positions]
        return outs.index(out), sum(len(slices[before]) for before in out[: out.index(at)])

    def kernel(*refs):
        left_refs, rest = refs[: len(lefts)], refs[len(lefts) :]
        right_refs, rest = rest[: len(rights)], rest[len(rights) :]
        lag_ref, same_ref, out_refs, cross = rest[0], rest[1], rest[2:-1], rest[-1]
        lanes = lax.broadcasted_iota(jnp.int32, (depth, LANES), 1)

        first_half = lanes < HALF
        lower = lanes % HALF < HALF // 2
        blank = jnp.zeros((depth, LANES), jnp.bfloat16)

        def turn(values):
            swapped = []
            for first in range(0, depth, depth // 2):
                middle, last = first + depth // 4, first + depth // 2
                swapped += [-values[middle:last], values[first:middle]]
            return jnp.concatenate(swapped, axis=0)

        def right_hand(used, f):
            values = right_refs[used[0]][f]
            if len(used) == 2:
                values = jnp.where(lower, values, right_refs[used[1]][f])
            turned = turn(values)
            return jnp.concatenate(
                [
                    jnp.concatenate([jnp.where(first_half, part, blank) for part in (values, turned)], axis=1),
                    jnp.concatenate([jnp.where(first_half, blank, part) for part in (values, turned)], axis=1),
                ],
                axis=0,
            )

        def products(first_bin, count):
            found = []
            for f in [first_bin + u for u in range(count)]:
                first = 0
                for used, groups_here in jobs:
                    lhs = [left_refs[left][f, row : row + piece] for left, row, _ in groups_here]
                    lhs = jnp.concatenate(lhs, axis=0) if len(lhs) > 1 else lhs[0]
                    product = jnp.dot(lhs, right_hand(used, f), preferred_element_type=jnp.float32)
                    found.append((first * pitch + f, product))
                    first += lhs.shape[0]
            return found

        def keep(found):
            for here, product in found:
                for part in range(2):
                    cross[pl.ds(part * total * pitch + here, product.shape[0], stride=pitch), :] = product[
                        :, part * LANES : (part + 1) * LANES
                    ]

        def some_bins(step, carry):
            first = step * step_bins
            waiting = products(first, batch)
            for at in range(batch, step_bins, batch):
                following = products(first + at, batch)
                keep(waiting)
                waiting = following
            keep(waiting)
            return carry

        lax.fori_loop(0, bins // step_bins, some_bins, 0)

        for index, found in enumerate(groups):
            targets = []
            for at, kind, lane in found:
                out, first = first_of(at)
                targets.append((out_refs[out], first + slices[at].index(kind), lane))

            def summed(i):
                parts = []
                for part in range(2):
                    start = (part * total + index * piece + i) * pitch
                    parts.append(
                        jnp.concatenate([cross[pl.ds(start, bins), :], cross[pl.ds(start + pitch, bins), :]], axis=1)
                    )
                values = jnp.concatenate(parts, axis=0).astype(jnp.bfloat16)
                return i, jnp.dot(lag_ref[...], values, preferred_element_type=jnp.float32)

            def across(i, lagged):
                lagged = lagged.astype(jnp.bfloat16)
                return i, lax.dot_general(same_ref[...], lagged, NT, preferred_element_type=jnp.float32)

            def store(i, rows):
                for half in range(2):
                    for out, place, lane in targets:
                        row = half * LANES + lane
                        out[place, i + half] = rows[row : row + piece].astype(out.dtype)

            sums, rows = summed(0), None
            for i in range(2, piece, 2):
                more = summed(i)
                if rows is not None:
                    store(*rows)
                rows = across(*sums)
                sums = more
            store(*rows)
            store(*across(*sums))

    shapes = [(sum(len(slices[at]) for at in positions), piece, piece, LAGS) for positions in outs]
    types = [jnp.float32 if positions == (OWN_AT,) else jnp.bfloat16 for positions in outs]
    results = kernel_call(
        kernel,
        "partial_correlations",
        4 * total * bins * depth * LANES + 4 * total * bins * LANES * LAGS,
        2 * sum(array.size for array in left_arrays + right_arrays),
        out_shape=[jax.ShapeDtypeStruct(shape, kind) for shape, kind in zip(shapes, types)],
        in_specs=[in_vmem()] * (len(lefts) + len(rights) + len(tables)),
        out_specs=[in_vmem()] * len(shapes),
        scratch_shapes=[pltpu.VMEM(((2 * total + 1) * pitch, LANES), jnp.float32)],
    )(*left_arrays, *right_arrays, *tables)
    return results, slices


def assembled(shares):
    arrays = [array for array, _ in shares]
    _, piece, _, lags = arrays[0].shape
    width = 2 * piece

    def kernel(*refs):
        out, held, sems = refs[-3:]
        sub = lax.axis_index("sub")
        odd = lax.rem(lax.axis_index("chan"), 2)
        copies = []
        for there, round_at in ((0, 1), (1, 2 - 2 * odd), (3, 2 * odd)):
            for i_other in range(2):
                for j_other in range(2):
                    parts = [
                        refs[at][place].astype(jnp.float32)
                        for at, (_, kinds) in enumerate(shares)
                        for place, kind in enumerate(kinds)
                        if kind == (i_other, j_other, there)
                    ]
                    i_first = jnp.where(sub == 0, i_other, 1 - i_other) * piece
                    j_first = pl.multiple_of(jnp.where(sub == 0, j_other, 1 - j_other) * piece, piece)
                    held[round_at, 0, pl.ds(i_first, piece), pl.ds(j_first, piece), :] = functools.reduce(
                        jnp.add, parts
                    )
            at = len(copies)
            copies.append(pltpu.make_async_copy(held.at[round_at], out.at[round_at], sems.at[at]))
            copies[-1].start()
        for copy in copies:
            copy.wait()

    shape = (ROUNDS, 1, width, width, lags)
    return kernel_call(
        kernel,
        "assembled",
        0,
        sum(array.size for array in arrays) * 2,
        out_shape=jax.ShapeDtypeStruct(shape, jnp.float32),
        in_specs=[in_vmem()] * len(arrays),
        out_specs=pl.BlockSpec(memory_space=pl.ANY),
        scratch_shapes=[pltpu.VMEM(shape, jnp.float32), pltpu.SemaphoreType.DMA((ROUNDS,))],
    )(*arrays)


def summed_in_place(traces, channel_slot):
    chan_count = lax.axis_size("chan")
    _, win_here, samples = traces.shape
    piece = HALF // BLOCKS
    scale = (2.0 / (win_here * chan_count * (samples // 2))) ** 0.5
    dft_rows = dft_rows_table(samples)
    same = selection(2 * LANES, 2 * LANES, [(n, n) for n in range(2 * LANES)])
    tables = [lag_rows_table(samples, scale), same]
    everywhere = tuple(range(BLOCKS))

    def over_sub(rows):
        return lax.ppermute(rows, "sub", [(0, 1), (1, 0)])

    def over_core(rows):
        return lax.ppermute(rows, "rep", [(0, 1), (1, 0)])

    def with_device(share, apart):
        return lax.ppermute(share, "chan", [(z, z ^ apart) for z in range(chan_count)])

    def after(value, *others):
        return lax.optimization_barrier((value,) + others)[0]

    def added(share, arrived):
        return (share.astype(jnp.float32) + arrived.astype(jnp.float32)).astype(jnp.bfloat16)

    def for_two_away(kinds):
        return [(i_other, j_other, there ^ 2) for i_other, j_other, there in kinds]

    mine, mine_far, mine_near = order_rows(traces, channel_slot, [everywhere, FAR, NEAR])
    far = over_sub(mine_far)
    near = over_sub(mine_near)

    own_i, own_j = spectra(mine, over_core(mine), (dft_rows, *own_picks()))
    own_left, own_right = (own_i, 0), (own_j, 0, everywhere)
    own_far, own_near = (0, 0, FAR[0]), (0, piece, NEAR[0])
    (kept_1, sent_far_1, own_1, sent_near_1), kinds_1 = partial_correlations(
        [own_left], [own_right], tables, [((0,), [own_far, own_near])], [(0,), (1,), (2,), (3,)]
    )
    arrived_far_1 = with_device(sent_far_1, 1)

    far, arrived_far_1 = lax.optimization_barrier((far, arrived_far_1))
    far_1 = with_device(added(kept_1, arrived_far_1), 2)
    arrived_near_1 = with_device(sent_near_1, 1)
    far_i, far_j = spectra(far, over_core(far), (dft_rows, *half_picks()))
    far_left, far_right = (far_i, 1), (far_j, 1, FAR)
    other_far = (1, 0, FAR[0])
    (kept_2, sent_far_2, own_2, sent_near_2), kinds_2 = partial_correlations(
        [own_left, far_left],
        [own_right, far_right],
        tables,
        [((0,), [other_far]), ((1,), [own_far, own_near, other_far])],
        [(0,), (1,), (2,), (3,)],
    )
    sent_far_2, far_1, arrived_near_1 = lax.optimization_barrier((sent_far_2, far_1, arrived_near_1))
    arrived_far_2 = with_device(sent_far_2, 1)

    near, arrived_far_2 = lax.optimization_barrier((near, arrived_far_2))
    near_i, near_j = spectra(near, over_core(near), (dft_rows, *half_picks()))
    summed_2 = added(kept_2, arrived_far_2)
    far_2 = with_device(summed_2, 2)
    near_j = after(near_j, summed_2)
    near_left, near_right = (near_i, 1), (near_j, 1, NEAR)
    (kept_3, sent_far_3, own_3, sent_near_3), kinds_3 = partial_correlations(
        [own_left, far_left],
        [near_right],
        tables,
        [((0,), [own_far, other_far, own_near])],
        [(0,), (1,), (2,), (3,)],
    )
    arrived_far_3 = with_device(sent_far_3, 1)
    arrived_near_2 = with_device(sent_near_2, 1)
    near_right = (after(near_j, kept_3, sent_far_3, far_2, arrived_near_2), 1, NEAR)
    (own_4, sent_4), kinds_4 = partial_correlations(
        [near_left], [far_right, near_right], tables, [((0, 1), [(0, 0, NEAR[0])])], [(2,), (3,)]
    )
    arrived_4 = with_device(jnp.concatenate([sent_near_3, sent_4]), 1)
    summed_3 = added(after(kept_3, own_4), arrived_far_3)
    far_3 = with_device(summed_3, 2)
    near_left = (after(near_i, own_4, sent_4, summed_3), 1)
    (own_5, sent_5), kinds_5 = partial_correlations(
        [near_left], [own_right], tables, [((0,), [(0, 0, NEAR[0])])], [(2,), (3,)]
    )
    arrived_5 = with_device(sent_5, 1)
    shares = [
        (own_1, kinds_1[2]),
        (own_2, kinds_2[2]),
        (own_3, kinds_3[2]),
        (own_4, kinds_4[2]),
        (own_5, kinds_5[2]),
        (arrived_near_1, kinds_1[3]),
        (arrived_near_2, kinds_2[3]),
        (arrived_4, kinds_3[3] + kinds_4[3]),
        (arrived_5, kinds_5[3]),
        (far_1, for_two_away(kinds_1[0])),
        (far_2, for_two_away(kinds_2[0])),
        (far_3, for_two_away(kinds_3[0])),
    ]
    return assembled(shares)


def from_behind(shard, axis, by):
    count = lax.axis_size(axis)
    return lax.ppermute(shard, axis, [(i, (i + by) % count) for i in range(count)])


def dft_columns(samples, parts, sub_bins):
    shape = (samples, parts, 2, sub_bins)
    time_pos = lax.broadcasted_iota(jnp.int32, shape, 0)
    range_pos = lax.broadcasted_iota(jnp.int32, shape, 1)
    part_pos = lax.broadcasted_iota(jnp.int32, shape, 2)
    bin_pos = lax.broadcasted_iota(jnp.int32, shape, 3)
    frequency = range_pos * sub_bins + bin_pos
    angles = jnp.mod(time_pos * frequency, samples).astype(jnp.float32) * (2.0 * math.pi / samples)
    entries = jnp.where(part_pos == 0, jnp.cos(angles), -jnp.sin(angles))
    return entries.reshape(samples, parts * 2 * sub_bins).astype(jnp.bfloat16)


def lag_table(sub_bins, first_bin, lag_count, samples):
    frequency = first_bin + lax.broadcasted_iota(jnp.int32, (sub_bins, lag_count), 0)
    lag_offset = lax.broadcasted_iota(jnp.int32, (sub_bins, lag_count), 1) - lag_count // 2
    angles = jnp.mod(frequency * lag_offset, samples).astype(jnp.float32) * (2.0 * math.pi / samples)
    return jnp.stack([jnp.cos(angles), -jnp.sin(angles)], axis=1)


def moved_spectra(traces, channel_slot):
    chan_count = lax.axis_size("chan")
    sub_count = lax.axis_size("sub")
    group_rows, win_here, samples = traces.shape
    bin_count = samples // 2
    sub_bins = bin_count // sub_count
    bin_width = 2 * sub_bins
    piece_len = group_rows // chan_count
    picked = jnp.take(traces, channel_slot, axis=0)
    dft_rows = dft_columns(samples, sub_count, sub_bins)
    spectrum = jnp.dot(picked.reshape(-1, samples), dft_rows, preferred_element_type=jnp.float32)
    energy = jnp.sum(spectrum * spectrum, axis=1, keepdims=True) / bin_count
    whitened = (spectrum * lax.rsqrt(energy + 1e-05)).astype(jnp.bfloat16)
    whitened = whitened.reshape(chan_count, piece_len, win_here, sub_count, bin_width)
    regrouped = lax.all_to_all(whitened, "chan", split_axis=0, concat_axis=0, tiled=True)
    regrouped = lax.all_to_all(regrouped, "sub", split_axis=3, concat_axis=3, tiled=True)
    own_half = regrouped.transpose(3, 1, 0, 2, 4).reshape(sub_count * piece_len, chan_count * win_here, bin_width)
    own_block = lax.all_gather(own_half, "rep", axis=0, tiled=True)
    windows = own_block.shape[1]
    own_split = own_block.reshape(own_block.shape[0], windows, 2, sub_bins)
    lag_rows = lag_table(sub_bins, lax.axis_index("sub") * sub_bins, LAGS, samples)
    lag_scale = (2.0 / (windows * bin_count)) ** 0.5
    results = []
    for step in range(1, ROUNDS + 1):
        partner = from_behind(own_half, "chan", -step)
        partner_split = partner.reshape(partner.shape[0], windows, 2, sub_bins)
        turned = jnp.stack([-partner_split[:, :, 1], partner_split[:, :, 0]], axis=2)
        partner_pair = jnp.stack([partner_split, turned], axis=0)
        cross_spec = jnp.einsum("iwpf,qjwpf->fqij", own_split, partner_pair, preferred_element_type=jnp.float32)
        summed = jnp.einsum("fqij,fql->ijl", cross_spec, lag_rows, precision=lax.Precision.HIGHEST)
        results.append(lax.psum_scatter(lag_scale * summed, "sub", scatter_dimension=0, tiled=True))
    return jnp.stack(results)[:, None]


def solution(mesh):
    sizes = mesh.shape
    in_place = sizes["chan"] == BLOCKS == ROUNDS + 1 and sizes["sub"] == 2 and sizes["rep"] == 2
    return jax.shard_map(
        summed_in_place if in_place else moved_spectra,
        mesh=mesh,
        in_specs=(P(("groups", "sub", "rep"), "chan", None), P(("groups", "sub", "rep"))),
        out_specs=P(None, ("groups", "chan"), "sub", "rep", None),
        check_vma=False,
    )
```

```python
import functools
import math

import jax
import jax.numpy as jnp
import numpy as np
from jax import lax
from jax.experimental import pallas as pl
from jax.experimental.pallas import tpu as pltpu
from jax.sharding import PartitionSpec as P

LAGS = 128
ROUNDS = 3
LANES = 128
HALF = LANES // 2
VMEM_BYTES = 32 * 1024 * 1024
ORDER_VMEM_BYTES = 48 * 1024 * 1024
NT = (((1,), (1,)), ((), ()))
BLOCKS = 4
FAR = (0, 1)
NEAR = (2, 3)
KEPT_AT, OWN_AT = 0, 2


def kernel_call(kernel, name, flops, bytes_accessed, vmem_bytes=VMEM_BYTES, **more):
    return pl.pallas_call(
        kernel,
        name=name,
        compiler_params=pltpu.CompilerParams(vmem_limit_bytes=vmem_bytes),
        cost_estimate=pl.CostEstimate(flops=flops, bytes_accessed=bytes_accessed, transcendentals=0),
        **more,
    )


def in_vmem():
    return pl.BlockSpec(memory_space=pltpu.VMEM)


def bin_order(bins):
    return np.concatenate([np.arange(0, bins, 2), np.arange(1, bins, 2)])


def dft_rows_table(samples):
    bins = samples // 2
    turns = (bin_order(bins)[:, None] * np.arange(samples // 2)[None, :]) % samples
    angles = turns.astype(np.float32) * np.float32(2.0 * math.pi / samples)
    halves = np.split(angles, 2)
    table = np.concatenate([part for half in halves for part in (np.cos(half), -np.sin(half))], axis=0)
    return jnp.asarray(table.astype(np.float32)).astype(jnp.bfloat16)


def lag_rows_table(samples, scale):
    bins = samples // 2
    offsets = np.arange(LAGS) - LAGS // 2
    turns = (offsets[:, None] * bin_order(bins)[None, :]) % samples
    angles = turns.astype(np.float32) * np.float32(2.0 * math.pi / samples)
    table = np.concatenate([np.cos(angles), -np.sin(angles)], axis=1) * np.float32(scale)
    return jnp.asarray(table.astype(np.float32)).astype(jnp.bfloat16)


def selection(rows, columns, ones):
    table = np.zeros((rows, columns), np.float32)
    for row, column in ones:
        table[row, column] = 1.0
    return jnp.asarray(table).astype(jnp.bfloat16)


def own_picks():
    piece = HALF // BLOCKS
    to_i = []
    for at in range(BLOCKS):
        for n in range(piece):
            to_i.append((at // 2 * piece + n, at % 2 * LANES + HALF + at * piece + n))
    to_j = [(j, copy * HALF + j) for j in range(HALF) for copy in range(2)]
    return selection(2 * piece, 2 * LANES, to_i), selection(LANES, LANES, to_j)


def half_picks():
    count = HALF // 2
    to_i, to_j = [], []
    for odd in range(2):
        for n in range(count):
            to_i.append((n, odd * LANES + odd * HALF + count + n))
            to_j += [(odd * HALF + n, odd * LANES + copy * count + n) for copy in range(4)]
    return selection(count, 2 * LANES, to_i), selection(LANES, 2 * LANES, to_j)


def order_rows(traces, slots, kinds):
    rows, wins, samples = traces.shape
    tiles = samples // LANES
    piece = rows // BLOCKS
    step_wins = 16
    steps = wins // step_wins
    batch = 4
    used = max(kinds, key=len)
    pitch = len(used) * piece + 1

    def kernel(slots_ref, traces_ref, *refs):
        out_refs, (wide, in_ref, slot_ref, sems) = refs[:-4], refs[-4:]
        slot_copy = pltpu.make_async_copy(slots_ref, slot_ref, sems.at[steps])
        slot_copy.start()
        copies = []
        for step in range(steps):
            here = pl.ds(step * step_wins, step_wins)
            copies.append(
                pltpu.make_async_copy(traces_ref.at[:, here, :], in_ref.at[:, here, :], sems.at[step])
            )
            copies[-1].start()
        slot_copy.wait()
        z = lax.axis_index("chan")
        odd = lax.rem(z, 2)
        pair = jnp.where(z < 2, 2, 0)

        def some_windows(step):
            first_win = step * step_wins
            for at, position in enumerate(used):
                block = pair + position + (odd if position % 2 == 0 else -odd)
                first = lax.rem(block, BLOCKS) * piece

                def move(group, carry, at=at, first=first):
                    js = [group * batch + u for u in range(batch)]
                    picked = [
                        in_ref[slot_ref[first + j], pl.ds(first_win, step_wins), :].astype(jnp.float32) for j in js
                    ]
                    for j, row in zip(js, picked):
                        for tile in range(tiles):
                            wide[tile, pl.ds(at * piece + j, step_wins, stride=pitch), :] = row[
                                :, tile * LANES : (tile + 1) * LANES
                            ]
                    return carry

                lax.fori_loop(0, piece // batch, move, 0)

            def pack(w, carry):
                blocks = [
                    wide[tile, pl.ds(w * pitch, len(used) * piece), :].astype(jnp.bfloat16) for tile in range(tiles)
                ]
                for out_ref, kind in zip(out_refs, kinds):
                    first = used.index(kind[0]) * piece
                    for tile, block in enumerate(blocks):
                        out_ref[first_win + w, :, tile * LANES : (tile + 1) * LANES] = block[
                            first : first + len(kind) * piece
                        ]
                return carry

            lax.fori_loop(0, step_wins, pack, 0, unroll=2)

        for step in range(steps):
            copies[step].wait()
            some_windows(step)

    return kernel_call(
        kernel,
        "order_rows",
        0,
        3 * traces.size * 2,
        vmem_bytes=ORDER_VMEM_BYTES,
        out_shape=[jax.ShapeDtypeStruct((wins, len(kind) * piece, samples), jnp.bfloat16) for kind in kinds],
        in_specs=[pl.BlockSpec(memory_space=pltpu.HBM)] * 2,
        out_specs=[in_vmem()] * len(kinds),
        scratch_shapes=[
            pltpu.VMEM((tiles, (step_wins + 1) * pitch, LANES), jnp.float32),
            pltpu.VMEM(traces.shape, traces.dtype),
            pltpu.SMEM(slots.shape, slots.dtype),
            pltpu.SemaphoreType.DMA((steps + 1,)),
        ],
    )(slots, traces)


def diagonal(values, copies):
    blank = jnp.zeros_like(values)
    rows = [[values if at == copy else blank for at in range(copies)] for copy in range(copies)]
    return jnp.concatenate([jnp.concatenate(row, axis=1) for row in rows], axis=0)


def spectra(rows_j, rows_i, tables):
    wins, given, samples = rows_j.shape
    bins = samples // 2
    pairs = wins // 2
    depth = 2 * wins
    folded = HALF // given
    line = depth // folded
    pitch = line + 1
    per_step = 2 * folded
    half_bins = bins // 2
    batch = 8

    def kernel(j_ref, i_ref, table_ref, to_i_ref, to_j_ref, i_out, j_out, wide):
        same = lax.axis_index("sub") == lax.axis_index("rep")

        def spectrum_of(group):
            stacked = []
            for win in [per_step * group + u for u in range(per_step)]:
                here = j_ref[win]
                stacked += [here, jnp.where(same, here, i_ref[win])]
            wave = jnp.concatenate(stacked, axis=0)
            first, second = wave[:, :bins].astype(jnp.float32), wave[:, bins:].astype(jnp.float32)
            folds = [(first + second).astype(jnp.bfloat16), (first - second).astype(jnp.bfloat16)]
            return [
                lax.dot_general(
                    table_ref[odd * bins : (odd + 1) * bins], fold, NT, preferred_element_type=jnp.float32
                )
                for odd, fold in enumerate(folds)
            ]

        def keep(group, spectrum):
            energy = sum(jnp.sum(values * values, axis=0, keepdims=True) for values in spectrum) / bins
            white = [values * lax.rsqrt(energy + 1e-05) for values in spectrum]
            for half in range(2):
                for part in range(2):
                    if folded == 1:
                        row = half * wins + part * pairs + group
                    else:
                        row = part * pairs + 2 * group + half
                    for odd in range(2):
                        wide[pl.ds(odd * half_bins * pitch + row, half_bins, stride=pitch), :] = white[odd][
                            part * half_bins : (part + 1) * half_bins, half * LANES : (half + 1) * LANES
                        ]

        groups = wins // per_step
        at_once = 4

        def some_windows(step, carry):
            first = step * at_once
            last = spectrum_of(first)
            for group in range(1, at_once):
                now = spectrum_of(first + group)
                keep(first + group - 1, last)
                last = now
            keep(first + at_once - 1, last)
            return carry

        lax.fori_loop(0, groups // at_once, some_windows, 0)

        def moved(fs):
            loaded = [wide[pl.ds(f * pitch, line), :].astype(jnp.bfloat16) for f in fs]
            i_rows = [
                lax.dot_general(to_i_ref[...], diagonal(values, 2), NT, preferred_element_type=jnp.float32)
                for values in loaded
            ]
            if folded == 2:
                i_rows = [jnp.concatenate([rows[: given // 2], rows[given // 2 :]], axis=1) for rows in i_rows]
            j_rows = jnp.dot(jnp.concatenate(loaded, axis=0), to_j_ref[...], preferred_element_type=jnp.float32)
            return fs, i_rows, j_rows

        def store(fs, i_rows, j_rows):
            for at, f in enumerate(fs):
                i_out[f] = i_rows[at].astype(jnp.bfloat16)
                for odd in range(folded):
                    j_out[f, odd * line : (odd + 1) * line] = j_rows[
                        at * line : (at + 1) * line, odd * LANES : (odd + 1) * LANES
                    ].astype(jnp.bfloat16)

        def pack(group, carry):
            first = group * 4 * batch
            waiting = moved([first + u for u in range(batch)])
            for at in range(1, 4):
                following = moved([first + at * batch + u for u in range(batch)])
                store(*waiting)
                waiting = following
            store(*waiting)
            return carry

        lax.fori_loop(0, bins // (4 * batch), pack, 0)

    shapes = [(bins, given // 2, LANES), (bins, depth, LANES)]
    return kernel_call(
        kernel,
        "spectra",
        4 * samples * samples * wins * given,
        4 * wins * given * samples * 2,
        out_shape=[jax.ShapeDtypeStruct(shape, jnp.bfloat16) for shape in shapes],
        in_specs=[in_vmem()] * (2 + len(tables)),
        out_specs=[in_vmem()] * len(shapes),
        scratch_shapes=[pltpu.VMEM(((bins + 1) * pitch, LANES), jnp.float32)],
    )(rows_j, rows_i, *tables)


def partial_correlations(lefts, rights, tables, jobs, outs):
    left_arrays = [array for array, _ in lefts]
    right_arrays = [array for array, _, _ in rights]
    bins, depth, _ = right_arrays[0].shape
    piece = HALF // BLOCKS
    pitch = bins + 1
    step_bins = 32
    groups = []
    slices = {}
    for used, groups_here in jobs:
        js = [(rights[right][1], there) for right in used for there in rights[right][2]]
        for left, _, first in groups_here:
            found = []
            for offset in range(2):
                at = first + offset
                for order, (j_other, there) in enumerate(js):
                    if there != at:
                        kind = (lefts[left][1], j_other, there ^ (at % 2))
                        found.append((at, kind, offset * HALF + order * piece))
                        slices.setdefault(at, []).append(kind)
            groups.append(found)
    for kinds in slices.values():
        kinds.sort()
    total = len(groups) * piece
    batch = 4

    def first_of(at):
        (out,) = [positions for positions in outs if at in positions]
        return outs.index(out), sum(len(slices[before]) for before in out[: out.index(at)])

    def kernel(*refs):
        left_refs, rest = refs[: len(lefts)], refs[len(lefts) :]
        right_refs, rest = rest[: len(rights)], rest[len(rights) :]
        lag_ref, same_ref, out_refs, cross = rest[0], rest[1], rest[2:-1], rest[-1]
        lanes = lax.broadcasted_iota(jnp.int32, (depth, LANES), 1)

        first_half = lanes < HALF
        lower = lanes % HALF < HALF // 2
        blank = jnp.zeros((depth, LANES), jnp.bfloat16)

        def turn(values):
            swapped = []
            for first in range(0, depth, depth // 2):
                middle, last = first + depth // 4, first + depth // 2
                swapped += [-values[middle:last], values[first:middle]]
            return jnp.concatenate(swapped, axis=0)

        def right_hand(used, f):
            values = right_refs[used[0]][f]
            if len(used) == 2:
                values = jnp.where(lower, values, right_refs[used[1]][f])
            turned = turn(values)
            return jnp.concatenate(
                [
                    jnp.concatenate([jnp.where(first_half, part, blank) for part in (values, turned)], axis=1),
                    jnp.concatenate([jnp.where(first_half, blank, part) for part in (values, turned)], axis=1),
                ],
                axis=0,
            )

        def products(first_bin, count):
            found = []
            for f in [first_bin + u for u in range(count)]:
                first = 0
                for used, groups_here in jobs:
                    lhs = [left_refs[left][f, row : row + piece] for left, row, _ in groups_here]
                    lhs = jnp.concatenate(lhs, axis=0) if len(lhs) > 1 else lhs[0]
                    product = jnp.dot(lhs, right_hand(used, f), preferred_element_type=jnp.float32)
                    found.append((first * pitch + f, product))
                    first += lhs.shape[0]
            return found

        def keep(found):
            for here, product in found:
                for part in range(2):
                    cross[pl.ds(part * total * pitch + here, product.shape[0], stride=pitch), :] = product[
                        :, part * LANES : (part + 1) * LANES
                    ]

        def some_bins(step, carry):
            first = step * step_bins
            waiting = products(first, batch)
            for at in range(batch, step_bins, batch):
                following = products(first + at, batch)
                keep(waiting)
                waiting = following
            keep(waiting)
            return carry

        lax.fori_loop(0, bins // step_bins, some_bins, 0)

        for index, found in enumerate(groups):
            targets = []
            for at, kind, lane in found:
                out, first = first_of(at)
                targets.append((out_refs[out], first + slices[at].index(kind), lane))

            def summed(i):
                parts = []
                for part in range(2):
                    start = (part * total + index * piece + i) * pitch
                    parts.append(
                        jnp.concatenate([cross[pl.ds(start, bins), :], cross[pl.ds(start + pitch, bins), :]], axis=1)
                    )
                values = jnp.concatenate(parts, axis=0).astype(jnp.bfloat16)
                return i, jnp.dot(lag_ref[...], values, preferred_element_type=jnp.float32)

            def across(i, lagged):
                lagged = lagged.astype(jnp.bfloat16)
                return i, lax.dot_general(same_ref[...], lagged, NT, preferred_element_type=jnp.float32)

            def store(i, rows):
                for half in range(2):
                    for out, place, lane in targets:
                        row = half * LANES + lane
                        out[place, i + half] = rows[row : row + piece].astype(out.dtype)

            sums, rows = summed(0), None
            for i in range(2, piece, 2):
                more = summed(i)
                if rows is not None:
                    store(*rows)
                rows = across(*sums)
                sums = more
            store(*rows)
            store(*across(*sums))

    shapes = [(sum(len(slices[at]) for at in positions), piece, piece, LAGS) for positions in outs]
    types = [jnp.float32 if positions == (OWN_AT,) else jnp.bfloat16 for positions in outs]
    results = kernel_call(
        kernel,
        "partial_correlations",
        4 * total * bins * depth * LANES + 4 * total * bins * LANES * LAGS,
        2 * sum(array.size for array in left_arrays + right_arrays),
        out_shape=[jax.ShapeDtypeStruct(shape, kind) for shape, kind in zip(shapes, types)],
        in_specs=[in_vmem()] * (len(lefts) + len(rights) + len(tables)),
        out_specs=[in_vmem()] * len(shapes),
        scratch_shapes=[pltpu.VMEM(((2 * total + 1) * pitch, LANES), jnp.float32)],
    )(*left_arrays, *right_arrays, *tables)
    return results, slices


def assembled(shares):
    arrays = [array for array, _ in shares]
    _, piece, _, lags = arrays[0].shape
    width = 2 * piece

    def kernel(*refs):
        out, held, sems = refs[-3:]
        sub = lax.axis_index("sub")
        odd = lax.rem(lax.axis_index("chan"), 2)
        copies = []
        for there, round_at in ((0, 1), (1, 2 - 2 * odd), (3, 2 * odd)):
            for i_other in range(2):
                for j_other in range(2):
                    parts = [
                        refs[at][place].astype(jnp.float32)
                        for at, (_, kinds) in enumerate(shares)
                        for place, kind in enumerate(kinds)
                        if kind == (i_other, j_other, there)
                    ]
                    i_first = jnp.where(sub == 0, i_other, 1 - i_other) * piece
                    j_first = pl.multiple_of(jnp.where(sub == 0, j_other, 1 - j_other) * piece, piece)
                    held[round_at, 0, pl.ds(i_first, piece), pl.ds(j_first, piece), :] = functools.reduce(
                        jnp.add, parts
                    )
            at = len(copies)
            copies.append(pltpu.make_async_copy(held.at[round_at], out.at[round_at], sems.at[at]))
            copies[-1].start()
        for copy in copies:
            copy.wait()

    shape = (ROUNDS, 1, width, width, lags)
    return kernel_call(
        kernel,
        "assembled",
        0,
        sum(array.size for array in arrays) * 2,
        out_shape=jax.ShapeDtypeStruct(shape, jnp.float32),
        in_specs=[in_vmem()] * len(arrays),
        out_specs=pl.BlockSpec(memory_space=pl.ANY),
        scratch_shapes=[pltpu.VMEM(shape, jnp.float32), pltpu.SemaphoreType.DMA((ROUNDS,))],
    )(*arrays)


def summed_in_place(traces, channel_slot):
    chan_count = lax.axis_size("chan")
    _, win_here, samples = traces.shape
    piece = HALF // BLOCKS
    scale = (2.0 / (win_here * chan_count * (samples // 2))) ** 0.5
    dft_rows = dft_rows_table(samples)
    same = selection(2 * LANES, 2 * LANES, [(n, n) for n in range(2 * LANES)])
    tables = [lag_rows_table(samples, scale), same]
    everywhere = tuple(range(BLOCKS))

    def over_sub(rows):
        return lax.ppermute(rows, "sub", [(0, 1), (1, 0)])

    def over_core(rows):
        return lax.ppermute(rows, "rep", [(0, 1), (1, 0)])

    def with_device(share, apart):
        return lax.ppermute(share, "chan", [(z, z ^ apart) for z in range(chan_count)])

    def after(value, *others):
        return lax.optimization_barrier((value,) + others)[0]

    def added(share, arrived):
        return (share.astype(jnp.float32) + arrived.astype(jnp.float32)).astype(jnp.bfloat16)

    def for_two_away(kinds):
        return [(i_other, j_other, there ^ 2) for i_other, j_other, there in kinds]

    mine, mine_far, mine_near = order_rows(traces, channel_slot, [everywhere, FAR, NEAR])
    far = over_sub(mine_far)
    near = over_sub(mine_near)

    own_i, own_j = spectra(mine, over_core(mine), (dft_rows, *own_picks()))
    own_left, own_right = (own_i, 0), (own_j, 0, everywhere)
    own_far, own_near = (0, 0, FAR[0]), (0, piece, NEAR[0])
    (kept_1, sent_far_1, own_1, sent_near_1), kinds_1 = partial_correlations(
        [own_left], [own_right], tables, [((0,), [own_far, own_near])], [(0,), (1,), (2,), (3,)]
    )
    arrived_far_1 = with_device(sent_far_1, 1)

    far, arrived_far_1 = lax.optimization_barrier((far, arrived_far_1))
    far_1 = with_device(added(kept_1, arrived_far_1), 2)
    arrived_near_1 = with_device(sent_near_1, 1)
    far_i, far_j = spectra(far, over_core(far), (dft_rows, *half_picks()))
    far_left, far_right = (far_i, 1), (far_j, 1, FAR)
    other_far = (1, 0, FAR[0])
    (kept_2, sent_far_2, own_2, sent_near_2), kinds_2 = partial_correlations(
        [own_left, far_left],
        [own_right, far_right],
        tables,
        [((0,), [other_far]), ((1,), [own_far, own_near, other_far])],
        [(0,), (1,), (2,), (3,)],
    )
    sent_far_2, far_1, arrived_near_1 = lax.optimization_barrier((sent_far_2, far_1, arrived_near_1))
    arrived_far_2 = with_device(sent_far_2, 1)

    near, arrived_far_2 = lax.optimization_barrier((near, arrived_far_2))
    near_i, near_j = spectra(near, over_core(near), (dft_rows, *half_picks()))
    summed_2 = added(kept_2, arrived_far_2)
    far_2 = with_device(summed_2, 2)
    near_j = after(near_j, summed_2)
    near_left, near_right = (near_i, 1), (near_j, 1, NEAR)
    (kept_3, sent_far_3, own_3, sent_near_3), kinds_3 = partial_correlations(
        [own_left, far_left],
        [near_right],
        tables,
        [((0,), [own_far, other_far, own_near])],
        [(0,), (1,), (2,), (3,)],
    )
    arrived_far_3 = with_device(sent_far_3, 1)
    arrived_near_2 = with_device(sent_near_2, 1)
    near_right = (after(near_j, kept_3, sent_far_3, far_2, arrived_near_2), 1, NEAR)
    (own_4, sent_4), kinds_4 = partial_correlations(
        [near_left], [far_right, near_right], tables, [((0, 1), [(0, 0, NEAR[0])])], [(2,), (3,)]
    )
    arrived_4 = with_device(jnp.concatenate([sent_near_3, sent_4]), 1)
    summed_3 = added(after(kept_3, own_4), arrived_far_3)
    far_3 = with_device(summed_3, 2)
    near_left = (after(near_i, own_4, sent_4, summed_3), 1)
    (own_5, sent_5), kinds_5 = partial_correlations(
        [near_left], [own_right], tables, [((0,), [(0, 0, NEAR[0])])], [(2,), (3,)]
    )
    arrived_5 = with_device(sent_5, 1)
    shares = [
        (own_1, kinds_1[2]),
        (own_2, kinds_2[2]),
        (own_3, kinds_3[2]),
        (own_4, kinds_4[2]),
        (own_5, kinds_5[2]),
        (arrived_near_1, kinds_1[3]),
        (arrived_near_2, kinds_2[3]),
        (arrived_4, kinds_3[3] + kinds_4[3]),
        (arrived_5, kinds_5[3]),
        (far_1, for_two_away(kinds_1[0])),
        (far_2, for_two_away(kinds_2[0])),
        (far_3, for_two_away(kinds_3[0])),
    ]
    return assembled(shares)


def from_behind(shard, axis, by):
    count = lax.axis_size(axis)
    return lax.ppermute(shard, axis, [(i, (i + by) % count) for i in range(count)])


def dft_columns(samples, parts, sub_bins):
    shape = (samples, parts, 2, sub_bins)
    time_pos = lax.broadcasted_iota(jnp.int32, shape, 0)
    range_pos = lax.broadcasted_iota(jnp.int32, shape, 1)
    part_pos = lax.broadcasted_iota(jnp.int32, shape, 2)
    bin_pos = lax.broadcasted_iota(jnp.int32, shape, 3)
    frequency = range_pos * sub_bins + bin_pos
    angles = jnp.mod(time_pos * frequency, samples).astype(jnp.float32) * (2.0 * math.pi / samples)
    entries = jnp.where(part_pos == 0, jnp.cos(angles), -jnp.sin(angles))
    return entries.reshape(samples, parts * 2 * sub_bins).astype(jnp.bfloat16)


def lag_table(sub_bins, first_bin, lag_count, samples):
    frequency = first_bin + lax.broadcasted_iota(jnp.int32, (sub_bins, lag_count), 0)
    lag_offset = lax.broadcasted_iota(jnp.int32, (sub_bins, lag_count), 1) - lag_count // 2
    angles = jnp.mod(frequency * lag_offset, samples).astype(jnp.float32) * (2.0 * math.pi / samples)
    return jnp.stack([jnp.cos(angles), -jnp.sin(angles)], axis=1)


def moved_spectra(traces, channel_slot):
    chan_count = lax.axis_size("chan")
    sub_count = lax.axis_size("sub")
    group_rows, win_here, samples = traces.shape
    bin_count = samples // 2
    sub_bins = bin_count // sub_count
    bin_width = 2 * sub_bins
    piece_len = group_rows // chan_count
    picked = jnp.take(traces, channel_slot, axis=0)
    dft_rows = dft_columns(samples, sub_count, sub_bins)
    spectrum = jnp.dot(picked.reshape(-1, samples), dft_rows, preferred_element_type=jnp.float32)
    energy = jnp.sum(spectrum * spectrum, axis=1, keepdims=True) / bin_count
    whitened = (spectrum * lax.rsqrt(energy + 1e-05)).astype(jnp.bfloat16)
    whitened = whitened.reshape(chan_count, piece_len, win_here, sub_count, bin_width)
    regrouped = lax.all_to_all(whitened, "chan", split_axis=0, concat_axis=0, tiled=True)
    regrouped = lax.all_to_all(regrouped, "sub", split_axis=3, concat_axis=3, tiled=True)
    own_half = regrouped.transpose(3, 1, 0, 2, 4).reshape(sub_count * piece_len, chan_count * win_here, bin_width)
    own_block = lax.all_gather(own_half, "rep", axis=0, tiled=True)
    windows = own_block.shape[1]
    own_split = own_block.reshape(own_block.shape[0], windows, 2, sub_bins)
    lag_rows = lag_table(sub_bins, lax.axis_index("sub") * sub_bins, LAGS, samples)
    lag_scale = (2.0 / (windows * bin_count)) ** 0.5
    results = []
    for step in range(1, ROUNDS + 1):
        partner = from_behind(own_half, "chan", -step)
        partner_split = partner.reshape(partner.shape[0], windows, 2, sub_bins)
        turned = jnp.stack([-partner_split[:, :, 1], partner_split[:, :, 0]], axis=2)
        partner_pair = jnp.stack([partner_split, turned], axis=0)
        cross_spec = jnp.einsum("iwpf,qjwpf->fqij", own_split, partner_pair, preferred_element_type=jnp.float32)
        summed = jnp.einsum("fqij,fql->ijl", cross_spec, lag_rows, precision=lax.Precision.HIGHEST)
        results.append(lax.psum_scatter(lag_scale * summed, "sub", scatter_dimension=0, tiled=True))
    return jnp.stack(results)[:, None]


def solution(mesh):
    sizes = mesh.shape
    in_place = sizes["chan"] == BLOCKS == ROUNDS + 1 and sizes["sub"] == 2 and sizes["rep"] == 2
    return jax.shard_map(
        summed_in_place if in_place else moved_spectra,
        mesh=mesh,
        in_specs=(P(("groups", "sub", "rep"), "chan", None), P(("groups", "sub", "rep"))),
        out_specs=P(None, ("groups", "chan"), "sub", "rep", None),
        check_vma=False,
    )
```

```python
import functools
import math

import jax
import jax.numpy as jnp
import numpy as np
from jax import lax
from jax.experimental import pallas as pl
from jax.experimental.pallas import tpu as pltpu
from jax.sharding import PartitionSpec as P

LAGS = 128
ROUNDS = 3
LANES = 128
HALF = LANES // 2
VMEM_BYTES = 32 * 1024 * 1024
ORDER_VMEM_BYTES = 48 * 1024 * 1024
NT = (((1,), (1,)), ((), ()))
BLOCKS = 4
FAR = (0, 1)
NEAR = (2, 3)
KEPT_AT, OWN_AT = 0, 2


def kernel_call(kernel, name, flops, bytes_accessed, vmem_bytes=VMEM_BYTES, **more):
    return pl.pallas_call(
        kernel,
        name=name,
        compiler_params=pltpu.CompilerParams(vmem_limit_bytes=vmem_bytes),
        cost_estimate=pl.CostEstimate(flops=flops, bytes_accessed=bytes_accessed, transcendentals=0),
        **more,
    )


def in_vmem():
    return pl.BlockSpec(memory_space=pltpu.VMEM)


def dft_rows_table(samples):
    bins = samples // 2
    turns = (np.arange(bins)[:, None] * np.arange(samples)[None, :]) % samples
    angles = turns.astype(np.float32) * np.float32(2.0 * math.pi / samples)
    table = np.concatenate([np.cos(angles), -np.sin(angles)], axis=0)
    return jnp.asarray(table.astype(np.float32)).astype(jnp.bfloat16)


def lag_rows_table(samples, scale):
    bins = samples // 2
    offsets = np.arange(LAGS) - LAGS // 2
    turns = (offsets[:, None] * np.arange(bins)[None, :]) % samples
    angles = turns.astype(np.float32) * np.float32(2.0 * math.pi / samples)
    table = np.concatenate([np.cos(angles), -np.sin(angles)], axis=1) * np.float32(scale)
    return jnp.asarray(table.astype(np.float32)).astype(jnp.bfloat16)


def selection(rows, columns, ones):
    table = np.zeros((rows, columns), np.float32)
    for row, column in ones:
        table[row, column] = 1.0
    return jnp.asarray(table).astype(jnp.bfloat16)


def own_picks():
    piece = HALF // BLOCKS
    to_i = []
    for at in range(BLOCKS):
        for n in range(piece):
            to_i.append((at // 2 * piece + n, at % 2 * LANES + HALF + at * piece + n))
    to_j = [(j, copy * HALF + j) for j in range(HALF) for copy in range(2)]
    return selection(2 * piece, 2 * LANES, to_i), selection(LANES, LANES, to_j)


def half_picks():
    count = HALF // 2
    to_i, to_j = [], []
    for odd in range(2):
        for n in range(count):
            to_i.append((n, odd * LANES + odd * HALF + count + n))
            to_j += [(odd * HALF + n, odd * LANES + copy * count + n) for copy in range(4)]
    return selection(count, 2 * LANES, to_i), selection(LANES, 2 * LANES, to_j)


def order_rows(traces, slots, kinds):
    rows, wins, samples = traces.shape
    tiles = samples // LANES
    piece = rows // BLOCKS
    step_wins = 16
    steps = wins // step_wins
    batch = 4
    used = max(kinds, key=len)
    pitch = len(used) * piece + 1

    def kernel(slots_ref, traces_ref, *refs):
        out_refs, (wide, in_ref, slot_ref, sems) = refs[:-4], refs[-4:]
        slot_copy = pltpu.make_async_copy(slots_ref, slot_ref, sems.at[steps])
        slot_copy.start()
        copies = []
        for step in range(steps):
            here = pl.ds(step * step_wins, step_wins)
            copies.append(
                pltpu.make_async_copy(traces_ref.at[:, here, :], in_ref.at[:, here, :], sems.at[step])
            )
            copies[-1].start()
        slot_copy.wait()
        z = lax.axis_index("chan")
        odd = lax.rem(z, 2)
        pair = jnp.where(z < 2, 2, 0)

        def some_windows(step):
            first_win = step * step_wins
            for at, position in enumerate(used):
                block = pair + position + (odd if position % 2 == 0 else -odd)
                first = lax.rem(block, BLOCKS) * piece

                def move(group, carry, at=at, first=first):
                    js = [group * batch + u for u in range(batch)]
                    picked = [
                        in_ref[slot_ref[first + j], pl.ds(first_win, step_wins), :].astype(jnp.float32) for j in js
                    ]
                    for j, row in zip(js, picked):
                        for tile in range(tiles):
                            wide[tile, pl.ds(at * piece + j, step_wins, stride=pitch), :] = row[
                                :, tile * LANES : (tile + 1) * LANES
                            ]
                    return carry

                lax.fori_loop(0, piece // batch, move, 0)

            def pack(w, carry):
                blocks = [
                    wide[tile, pl.ds(w * pitch, len(used) * piece), :].astype(jnp.bfloat16) for tile in range(tiles)
                ]
                for out_ref, kind in zip(out_refs, kinds):
                    first = used.index(kind[0]) * piece
                    for tile, block in enumerate(blocks):
                        out_ref[first_win + w, :, tile * LANES : (tile + 1) * LANES] = block[
                            first : first + len(kind) * piece
                        ]
                return carry

            lax.fori_loop(0, step_wins, pack, 0, unroll=2)

        for step in range(steps):
            copies[step].wait()
            some_windows(step)

    return kernel_call(
        kernel,
        "order_rows",
        0,
        3 * traces.size * 2,
        vmem_bytes=ORDER_VMEM_BYTES,
        out_shape=[jax.ShapeDtypeStruct((wins, len(kind) * piece, samples), jnp.bfloat16) for kind in kinds],
        in_specs=[pl.BlockSpec(memory_space=pltpu.HBM)] * 2,
        out_specs=[in_vmem()] * len(kinds),
        scratch_shapes=[
            pltpu.VMEM((tiles, (step_wins + 1) * pitch, LANES), jnp.float32),
            pltpu.VMEM(traces.shape, traces.dtype),
            pltpu.SMEM(slots.shape, slots.dtype),
            pltpu.SemaphoreType.DMA((steps + 1,)),
        ],
    )(slots, traces)


def diagonal(values, copies):
    blank = jnp.zeros_like(values)
    rows = [[values if at == copy else blank for at in range(copies)] for copy in range(copies)]
    return jnp.concatenate([jnp.concatenate(row, axis=1) for row in rows], axis=0)


def spectra(rows_j, rows_i, tables):
    wins, given, samples = rows_j.shape
    bins = samples // 2
    pairs = wins // 2
    depth = 2 * wins
    folded = HALF // given
    line = depth // folded
    pitch = line + 1
    per_step = 2 * folded
    batch = 16

    def kernel(j_ref, i_ref, table_ref, to_i_ref, to_j_ref, i_out, j_out, wide):
        same = lax.axis_index("sub") == lax.axis_index("rep")

        def spectrum_of(group):
            stacked = []
            for win in [per_step * group + u for u in range(per_step)]:
                here = j_ref[win]
                stacked += [here, jnp.where(same, here, i_ref[win])]
            wave = jnp.concatenate(stacked, axis=0)
            return lax.dot_general(table_ref[...], wave, NT, preferred_element_type=jnp.float32)

        def keep(group, spectrum):
            energy = jnp.sum(spectrum * spectrum, axis=0, keepdims=True) / bins
            white = spectrum * lax.rsqrt(energy + 1e-05)
            for half in range(2):
                for part in range(2):
                    if folded == 1:
                        row = half * wins + part * pairs + group
                    else:
                        row = part * pairs + 2 * group + half
                    wide[pl.ds(row, bins, stride=pitch), :] = white[
                        part * bins : (part + 1) * bins, half * LANES : (half + 1) * LANES
                    ]

        groups = wins // per_step
        at_once = 4

        def some_windows(step, carry):
            first = step * at_once
            last = spectrum_of(first)
            for group in range(1, at_once):
                now = spectrum_of(first + group)
                keep(first + group - 1, last)
                last = now
            keep(first + at_once - 1, last)
            return carry

        lax.fori_loop(0, groups // at_once, some_windows, 0)

        def moved(fs):
            loaded = [wide[pl.ds(f * pitch, line), :].astype(jnp.bfloat16) for f in fs]
            i_rows = [
                lax.dot_general(to_i_ref[...], diagonal(values, 2), NT, preferred_element_type=jnp.float32)
                for values in loaded
            ]
            if folded == 2:
                i_rows = [jnp.concatenate([rows[: given // 2], rows[given // 2 :]], axis=1) for rows in i_rows]
            j_rows = jnp.dot(jnp.concatenate(loaded, axis=0), to_j_ref[...], preferred_element_type=jnp.float32)
            return fs, i_rows, j_rows

        def store(fs, i_rows, j_rows):
            for at, f in enumerate(fs):
                i_out[f] = i_rows[at].astype(jnp.bfloat16)
                for odd in range(folded):
                    j_out[f, odd * line : (odd + 1) * line] = j_rows[
                        at * line : (at + 1) * line, odd * LANES : (odd + 1) * LANES
                    ].astype(jnp.bfloat16)

        def pack(group, carry):
            first = group * 4 * batch
            waiting = moved([first + u for u in range(batch)])
            for at in range(1, 4):
                following = moved([first + at * batch + u for u in range(batch)])
                store(*waiting)
                waiting = following
            store(*waiting)
            return carry

        lax.fori_loop(0, bins // (4 * batch), pack, 0)

    shapes = [(bins, given // 2, LANES), (bins, depth, LANES)]
    return kernel_call(
        kernel,
        "spectra",
        4 * samples * samples * wins * given,
        4 * wins * given * samples * 2,
        out_shape=[jax.ShapeDtypeStruct(shape, jnp.bfloat16) for shape in shapes],
        in_specs=[in_vmem()] * (2 + len(tables)),
        out_specs=[in_vmem()] * len(shapes),
        scratch_shapes=[pltpu.VMEM(((bins + 1) * pitch, LANES), jnp.float32)],
    )(rows_j, rows_i, *tables)


def partial_correlations(lefts, rights, tables, jobs, outs):
    left_arrays = [array for array, _ in lefts]
    right_arrays = [array for array, _, _ in rights]
    bins, depth, _ = right_arrays[0].shape
    piece = HALF // BLOCKS
    pitch = bins + 1
    step_bins = 32
    groups = []
    slices = {}
    for used, groups_here in jobs:
        js = [(rights[right][1], there) for right in used for there in rights[right][2]]
        for left, _, first in groups_here:
            found = []
            for offset in range(2):
                at = first + offset
                for order, (j_other, there) in enumerate(js):
                    if there != at:
                        kind = (lefts[left][1], j_other, there ^ (at % 2))
                        found.append((at, kind, offset * HALF + order * piece))
                        slices.setdefault(at, []).append(kind)
            groups.append(found)
    for kinds in slices.values():
        kinds.sort()
    total = len(groups) * piece
    batch = 8 if len(groups) == 1 else 4

    def first_of(at):
        (out,) = [positions for positions in outs if at in positions]
        return outs.index(out), sum(len(slices[before]) for before in out[: out.index(at)])

    def kernel(*refs):
        left_refs, rest = refs[: len(lefts)], refs[len(lefts) :]
        right_refs, rest = rest[: len(rights)], rest[len(rights) :]
        lag_ref, same_ref, out_refs, cross = rest[0], rest[1], rest[2:-1], rest[-1]
        lanes = lax.broadcasted_iota(jnp.int32, (depth, LANES), 1)

        first_half = lanes < HALF
        lower = lanes % HALF < HALF // 2
        blank = jnp.zeros((depth, LANES), jnp.bfloat16)

        def turn(values):
            swapped = []
            for first in range(0, depth, depth // 2):
                middle, last = first + depth // 4, first + depth // 2
                swapped += [-values[middle:last], values[first:middle]]
            return jnp.concatenate(swapped, axis=0)

        def right_hand(used, f):
            values = right_refs[used[0]][f]
            if len(used) == 2:
                values = jnp.where(lower, values, right_refs[used[1]][f])
            turned = turn(values)
            return jnp.concatenate(
                [
                    jnp.concatenate([jnp.where(first_half, part, blank) for part in (values, turned)], axis=1),
                    jnp.concatenate([jnp.where(first_half, blank, part) for part in (values, turned)], axis=1),
                ],
                axis=0,
            )

        def products(first_bin, count):
            found = []
            for f in [first_bin + u for u in range(count)]:
                first = 0
                for used, groups_here in jobs:
                    lhs = [left_refs[left][f, row : row + piece] for left, row, _ in groups_here]
                    lhs = jnp.concatenate(lhs, axis=0) if len(lhs) > 1 else lhs[0]
                    product = jnp.dot(lhs, right_hand(used, f), preferred_element_type=jnp.float32)
                    found.append((first * pitch + f, product))
                    first += lhs.shape[0]
            return found

        def keep(found):
            for here, product in found:
                for part in range(2):
                    cross[pl.ds(part * total * pitch + here, product.shape[0], stride=pitch), :] = product[
                        :, part * LANES : (part + 1) * LANES
                    ]

        def some_bins(step, carry):
            first = step * step_bins
            waiting = products(first, batch)
            for at in range(batch, step_bins, batch):
                following = products(first + at, batch)
                keep(waiting)
                waiting = following
            keep(waiting)
            return carry

        lax.fori_loop(0, bins // step_bins, some_bins, 0)

        for index, found in enumerate(groups):
            targets = []
            for at, kind, lane in found:
                out, first = first_of(at)
                targets.append((out_refs[out], first + slices[at].index(kind), lane))

            def summed(i):
                parts = []
                for part in range(2):
                    start = (part * total + index * piece + i) * pitch
                    parts.append(
                        jnp.concatenate([cross[pl.ds(start, bins), :], cross[pl.ds(start + pitch, bins), :]], axis=1)
                    )
                values = jnp.concatenate(parts, axis=0).astype(jnp.bfloat16)
                return i, jnp.dot(lag_ref[...], values, preferred_element_type=jnp.float32)

            def across(i, lagged):
                lagged = lagged.astype(jnp.bfloat16)
                return i, lax.dot_general(same_ref[...], lagged, NT, preferred_element_type=jnp.float32)

            def store(i, rows):
                for half in range(2):
                    for out, place, lane in targets:
                        row = half * LANES + lane
                        out[place, i + half] = rows[row : row + piece].astype(out.dtype)

            sums, rows = summed(0), None
            for i in range(2, piece, 2):
                more = summed(i)
                if rows is not None:
                    store(*rows)
                rows = across(*sums)
                sums = more
            store(*rows)
            store(*across(*sums))

    shapes = [(sum(len(slices[at]) for at in positions), piece, piece, LAGS) for positions in outs]
    types = [jnp.float32 if positions == (OWN_AT,) else jnp.bfloat16 for positions in outs]
    results = kernel_call(
        kernel,
        "partial_correlations",
        4 * total * bins * depth * LANES + 4 * total * bins * LANES * LAGS,
        2 * sum(array.size for array in left_arrays + right_arrays),
        out_shape=[jax.ShapeDtypeStruct(shape, kind) for shape, kind in zip(shapes, types)],
        in_specs=[in_vmem()] * (len(lefts) + len(rights) + len(tables)),
        out_specs=[in_vmem()] * len(shapes),
        scratch_shapes=[pltpu.VMEM(((2 * total + 1) * pitch, LANES), jnp.float32)],
    )(*left_arrays, *right_arrays, *tables)
    return results, slices


def assembled(shares):
    arrays = [array for array, _ in shares]
    _, piece, _, lags = arrays[0].shape
    width = 2 * piece

    def kernel(*refs):
        out, held, sems = refs[-3:]
        sub = lax.axis_index("sub")
        odd = lax.rem(lax.axis_index("chan"), 2)
        copies = []
        for there, round_at in ((0, 1), (1, 2 - 2 * odd), (3, 2 * odd)):
            for i_other in range(2):
                for j_other in range(2):
                    parts = [
                        refs[at][place].astype(jnp.float32)
                        for at, (_, kinds) in enumerate(shares)
                        for place, kind in enumerate(kinds)
                        if kind == (i_other, j_other, there)
                    ]
                    i_first = jnp.where(sub == 0, i_other, 1 - i_other) * piece
                    j_first = pl.multiple_of(jnp.where(sub == 0, j_other, 1 - j_other) * piece, piece)
                    held[round_at, 0, pl.ds(i_first, piece), pl.ds(j_first, piece), :] = functools.reduce(
                        jnp.add, parts
                    )
            at = len(copies)
            copies.append(pltpu.make_async_copy(held.at[round_at], out.at[round_at], sems.at[at]))
            copies[-1].start()
        for copy in copies:
            copy.wait()

    shape = (ROUNDS, 1, width, width, lags)
    return kernel_call(
        kernel,
        "assembled",
        0,
        sum(array.size for array in arrays) * 2,
        out_shape=jax.ShapeDtypeStruct(shape, jnp.float32),
        in_specs=[in_vmem()] * len(arrays),
        out_specs=pl.BlockSpec(memory_space=pl.ANY),
        scratch_shapes=[pltpu.VMEM(shape, jnp.float32), pltpu.SemaphoreType.DMA((ROUNDS,))],
    )(*arrays)


def summed_in_place(traces, channel_slot):
    chan_count = lax.axis_size("chan")
    _, win_here, samples = traces.shape
    piece = HALF // BLOCKS
    scale = (2.0 / (win_here * chan_count * (samples // 2))) ** 0.5
    dft_rows = dft_rows_table(samples)
    same = selection(2 * LANES, 2 * LANES, [(n, n) for n in range(2 * LANES)])
    tables = [lag_rows_table(samples, scale), same]
    everywhere = tuple(range(BLOCKS))

    def over_sub(rows):
        return lax.ppermute(rows, "sub", [(0, 1), (1, 0)])

    def over_core(rows):
        return lax.ppermute(rows, "rep", [(0, 1), (1, 0)])

    def with_device(share, apart):
        return lax.ppermute(share, "chan", [(z, z ^ apart) for z in range(chan_count)])

    def after(value, *others):
        return lax.optimization_barrier((value,) + others)[0]

    def added(share, arrived):
        return (share.astype(jnp.float32) + arrived.astype(jnp.float32)).astype(jnp.bfloat16)

    def for_two_away(kinds):
        return [(i_other, j_other, there ^ 2) for i_other, j_other, there in kinds]

    mine, mine_far, mine_near = order_rows(traces, channel_slot, [everywhere, FAR, NEAR])
    far = over_sub(mine_far)
    near = over_sub(mine_near)

    own_i, own_j = spectra(mine, over_core(mine), (dft_rows, *own_picks()))
    own_left, own_right = (own_i, 0), (own_j, 0, everywhere)
    own_far, own_near = (0, 0, FAR[0]), (0, piece, NEAR[0])
    (kept_1, sent_far_1, own_1, sent_near_1), kinds_1 = partial_correlations(
        [own_left], [own_right], tables, [((0,), [own_far, own_near])], [(0,), (1,), (2,), (3,)]
    )
    arrived_far_1 = with_device(sent_far_1, 1)

    far, arrived_far_1 = lax.optimization_barrier((far, arrived_far_1))
    far_1 = with_device(added(kept_1, arrived_far_1), 2)
    arrived_near_1 = with_device(sent_near_1, 1)
    far_i, far_j = spectra(far, over_core(far), (dft_rows, *half_picks()))
    far_left, far_right = (far_i, 1), (far_j, 1, FAR)
    other_far = (1, 0, FAR[0])
    (kept_2, sent_far_2, own_2, sent_near_2), kinds_2 = partial_correlations(
        [own_left, far_left],
        [own_right, far_right],
        tables,
        [((0,), [other_far]), ((1,), [own_far, own_near, other_far])],
        [(0,), (1,), (2,), (3,)],
    )
    sent_far_2, far_1, arrived_near_1 = lax.optimization_barrier((sent_far_2, far_1, arrived_near_1))
    arrived_far_2 = with_device(sent_far_2, 1)

    near, arrived_far_2 = lax.optimization_barrier((near, arrived_far_2))
    near_i, near_j = spectra(near, over_core(near), (dft_rows, *half_picks()))
    summed_2 = added(kept_2, arrived_far_2)
    far_2 = with_device(summed_2, 2)
    near_j = after(near_j, summed_2)
    near_left, near_right = (near_i, 1), (near_j, 1, NEAR)
    (kept_3, sent_far_3, own_3, sent_near_3), kinds_3 = partial_correlations(
        [own_left, far_left],
        [near_right],
        tables,
        [((0,), [own_far, other_far, own_near])],
        [(0,), (1,), (2,), (3,)],
    )
    arrived_far_3 = with_device(sent_far_3, 1)
    arrived_near_2 = with_device(sent_near_2, 1)
    near_right = (after(near_j, kept_3, sent_far_3, far_2, arrived_near_2), 1, NEAR)
    (own_4, sent_4), kinds_4 = partial_correlations(
        [near_left], [far_right, near_right], tables, [((0, 1), [(0, 0, NEAR[0])])], [(2,), (3,)]
    )
    arrived_4 = with_device(jnp.concatenate([sent_near_3, sent_4]), 1)
    summed_3 = added(after(kept_3, own_4), arrived_far_3)
    far_3 = with_device(summed_3, 2)
    near_left = (after(near_i, own_4, sent_4, summed_3), 1)
    (own_5, sent_5), kinds_5 = partial_correlations(
        [near_left], [own_right], tables, [((0,), [(0, 0, NEAR[0])])], [(2,), (3,)]
    )
    arrived_5 = with_device(sent_5, 1)
    shares = [
        (own_1, kinds_1[2]),
        (own_2, kinds_2[2]),
        (own_3, kinds_3[2]),
        (own_4, kinds_4[2]),
        (own_5, kinds_5[2]),
        (arrived_near_1, kinds_1[3]),
        (arrived_near_2, kinds_2[3]),
        (arrived_4, kinds_3[3] + kinds_4[3]),
        (arrived_5, kinds_5[3]),
        (far_1, for_two_away(kinds_1[0])),
        (far_2, for_two_away(kinds_2[0])),
        (far_3, for_two_away(kinds_3[0])),
    ]
    return assembled(shares)


def from_behind(shard, axis, by):
    count = lax.axis_size(axis)
    return lax.ppermute(shard, axis, [(i, (i + by) % count) for i in range(count)])


def dft_columns(samples, parts, sub_bins):
    shape = (samples, parts, 2, sub_bins)
    time_pos = lax.broadcasted_iota(jnp.int32, shape, 0)
    range_pos = lax.broadcasted_iota(jnp.int32, shape, 1)
    part_pos = lax.broadcasted_iota(jnp.int32, shape, 2)
    bin_pos = lax.broadcasted_iota(jnp.int32, shape, 3)
    frequency = range_pos * sub_bins + bin_pos
    angles = jnp.mod(time_pos * frequency, samples).astype(jnp.float32) * (2.0 * math.pi / samples)
    entries = jnp.where(part_pos == 0, jnp.cos(angles), -jnp.sin(angles))
    return entries.reshape(samples, parts * 2 * sub_bins).astype(jnp.bfloat16)


def lag_table(sub_bins, first_bin, lag_count, samples):
    frequency = first_bin + lax.broadcasted_iota(jnp.int32, (sub_bins, lag_count), 0)
    lag_offset = lax.broadcasted_iota(jnp.int32, (sub_bins, lag_count), 1) - lag_count // 2
    angles = jnp.mod(frequency * lag_offset, samples).astype(jnp.float32) * (2.0 * math.pi / samples)
    return jnp.stack([jnp.cos(angles), -jnp.sin(angles)], axis=1)


def moved_spectra(traces, channel_slot):
    chan_count = lax.axis_size("chan")
    sub_count = lax.axis_size("sub")
    group_rows, win_here, samples = traces.shape
    bin_count = samples // 2
    sub_bins = bin_count // sub_count
    bin_width = 2 * sub_bins
    piece_len = group_rows // chan_count
    picked = jnp.take(traces, channel_slot, axis=0)
    dft_rows = dft_columns(samples, sub_count, sub_bins)
    spectrum = jnp.dot(picked.reshape(-1, samples), dft_rows, preferred_element_type=jnp.float32)
    energy = jnp.sum(spectrum * spectrum, axis=1, keepdims=True) / bin_count
    whitened = (spectrum * lax.rsqrt(energy + 1e-05)).astype(jnp.bfloat16)
    whitened = whitened.reshape(chan_count, piece_len, win_here, sub_count, bin_width)
    regrouped = lax.all_to_all(whitened, "chan", split_axis=0, concat_axis=0, tiled=True)
    regrouped = lax.all_to_all(regrouped, "sub", split_axis=3, concat_axis=3, tiled=True)
    own_half = regrouped.transpose(3, 1, 0, 2, 4).reshape(sub_count * piece_len, chan_count * win_here, bin_width)
    own_block = lax.all_gather(own_half, "rep", axis=0, tiled=True)
    windows = own_block.shape[1]
    own_split = own_block.reshape(own_block.shape[0], windows, 2, sub_bins)
    lag_rows = lag_table(sub_bins, lax.axis_index("sub") * sub_bins, LAGS, samples)
    lag_scale = (2.0 / (windows * bin_count)) ** 0.5
    results = []
    for step in range(1, ROUNDS + 1):
        partner = from_behind(own_half, "chan", -step)
        partner_split = partner.reshape(partner.shape[0], windows, 2, sub_bins)
        turned = jnp.stack([-partner_split[:, :, 1], partner_split[:, :, 0]], axis=2)
        partner_pair = jnp.stack([partner_split, turned], axis=0)
        cross_spec = jnp.einsum("iwpf,qjwpf->fqij", own_split, partner_pair, preferred_element_type=jnp.float32)
        summed = jnp.einsum("fqij,fql->ijl", cross_spec, lag_rows, precision=lax.Precision.HIGHEST)
        results.append(lax.psum_scatter(lag_scale * summed, "sub", scatter_dimension=0, tiled=True))
    return jnp.stack(results)[:, None]


def solution(mesh):
    sizes = mesh.shape
    in_place = sizes["chan"] == BLOCKS == ROUNDS + 1 and sizes["sub"] == 2 and sizes["rep"] == 2
    return jax.shard_map(
        summed_in_place if in_place else moved_spectra,
        mesh=mesh,
        in_specs=(P(("groups", "sub", "rep"), "chan", None), P(("groups", "sub", "rep"))),
        out_specs=P(None, ("groups", "chan"), "sub", "rep", None),
        check_vma=False,
    )
```

```python
import functools
import math

import jax
import jax.numpy as jnp
import numpy as np
from jax import lax
from jax.experimental import pallas as pl
from jax.experimental.pallas import tpu as pltpu
from jax.sharding import PartitionSpec as P

LAGS = 128
ROUNDS = 3
LANES = 128
HALF = LANES // 2
VMEM_BYTES = 32 * 1024 * 1024
ORDER_VMEM_BYTES = 48 * 1024 * 1024
NT = (((1,), (1,)), ((), ()))
BLOCKS = 4
FAR = (0, 1)
NEAR = (2, 3)
KEPT_AT, OWN_AT = 0, 2


def kernel_call(kernel, name, flops, bytes_accessed, vmem_bytes=VMEM_BYTES, **more):
    return pl.pallas_call(
        kernel,
        name=name,
        compiler_params=pltpu.CompilerParams(vmem_limit_bytes=vmem_bytes),
        cost_estimate=pl.CostEstimate(flops=flops, bytes_accessed=bytes_accessed, transcendentals=0),
        **more,
    )


def in_vmem():
    return pl.BlockSpec(memory_space=pltpu.VMEM)


def dft_rows_table(samples):
    bins = samples // 2
    turns = (np.arange(bins)[:, None] * np.arange(samples)[None, :]) % samples
    angles = turns.astype(np.float32) * np.float32(2.0 * math.pi / samples)
    table = np.concatenate([np.cos(angles), -np.sin(angles)], axis=0)
    return jnp.asarray(table.astype(np.float32)).astype(jnp.bfloat16)


def lag_rows_table(samples, scale):
    bins = samples // 2
    offsets = np.arange(LAGS) - LAGS // 2
    turns = (offsets[:, None] * np.arange(bins)[None, :]) % samples
    angles = turns.astype(np.float32) * np.float32(2.0 * math.pi / samples)
    table = np.concatenate([np.cos(angles), -np.sin(angles)], axis=1) * np.float32(scale)
    return jnp.asarray(table.astype(np.float32)).astype(jnp.bfloat16)


def selection(rows, columns, ones):
    table = np.zeros((rows, columns), np.float32)
    for row, column in ones:
        table[row, column] = 1.0
    return jnp.asarray(table).astype(jnp.bfloat16)


def own_picks():
    piece = HALF // BLOCKS
    to_i = []
    for at in range(BLOCKS):
        for n in range(piece):
            to_i.append((at // 2 * piece + n, at % 2 * LANES + HALF + at * piece + n))
    to_j = [(j, copy * HALF + j) for j in range(HALF) for copy in range(2)]
    return selection(2 * piece, 2 * LANES, to_i), selection(LANES, LANES, to_j)


def half_picks():
    count = HALF // 2
    to_i, to_j = [], []
    for odd in range(2):
        for n in range(count):
            to_i.append((n, odd * LANES + odd * HALF + count + n))
            to_j += [(odd * HALF + n, odd * LANES + copy * count + n) for copy in range(4)]
    return selection(count, 2 * LANES, to_i), selection(LANES, 2 * LANES, to_j)


def order_rows(traces, slots, kinds):
    rows, wins, samples = traces.shape
    tiles = samples // LANES
    piece = rows // BLOCKS
    step_wins = 16
    steps = wins // step_wins
    batch = 4
    used = max(kinds, key=len)
    pitch = len(used) * piece + 1

    def kernel(slots_ref, traces_ref, *refs):
        out_refs, (wide, in_ref, slot_ref, sems) = refs[:-4], refs[-4:]
        slot_copy = pltpu.make_async_copy(slots_ref, slot_ref, sems.at[steps])
        slot_copy.start()
        copies = []
        for step in range(steps):
            here = pl.ds(step * step_wins, step_wins)
            copies.append(
                pltpu.make_async_copy(traces_ref.at[:, here, :], in_ref.at[:, here, :], sems.at[step])
            )
            copies[-1].start()
        slot_copy.wait()
        z = lax.axis_index("chan")
        odd = lax.rem(z, 2)
        pair = jnp.where(z < 2, 2, 0)

        def some_windows(step):
            first_win = step * step_wins
            for at, position in enumerate(used):
                block = pair + position + (odd if position % 2 == 0 else -odd)
                first = lax.rem(block, BLOCKS) * piece

                def move(group, carry, at=at, first=first):
                    js = [group * batch + u for u in range(batch)]
                    picked = [
                        in_ref[slot_ref[first + j], pl.ds(first_win, step_wins), :].astype(jnp.float32) for j in js
                    ]
                    for j, row in zip(js, picked):
                        for tile in range(tiles):
                            wide[tile, pl.ds(at * piece + j, step_wins, stride=pitch), :] = row[
                                :, tile * LANES : (tile + 1) * LANES
                            ]
                    return carry

                lax.fori_loop(0, piece // batch, move, 0)

            def pack(w, carry):
                blocks = [
                    wide[tile, pl.ds(w * pitch, len(used) * piece), :].astype(jnp.bfloat16) for tile in range(tiles)
                ]
                for out_ref, kind in zip(out_refs, kinds):
                    first = used.index(kind[0]) * piece
                    for tile, block in enumerate(blocks):
                        out_ref[first_win + w, :, tile * LANES : (tile + 1) * LANES] = block[
                            first : first + len(kind) * piece
                        ]
                return carry

            lax.fori_loop(0, step_wins, pack, 0, unroll=2)

        for step in range(steps):
            copies[step].wait()
            some_windows(step)

    return kernel_call(
        kernel,
        "order_rows",
        0,
        3 * traces.size * 2,
        vmem_bytes=ORDER_VMEM_BYTES,
        out_shape=[jax.ShapeDtypeStruct((wins, len(kind) * piece, samples), jnp.bfloat16) for kind in kinds],
        in_specs=[pl.BlockSpec(memory_space=pltpu.HBM)] * 2,
        out_specs=[in_vmem()] * len(kinds),
        scratch_shapes=[
            pltpu.VMEM((tiles, (step_wins + 1) * pitch, LANES), jnp.float32),
            pltpu.VMEM(traces.shape, traces.dtype),
            pltpu.SMEM(slots.shape, slots.dtype),
            pltpu.SemaphoreType.DMA((steps + 1,)),
        ],
    )(slots, traces)


def diagonal(values, copies):
    blank = jnp.zeros_like(values)
    rows = [[values if at == copy else blank for at in range(copies)] for copy in range(copies)]
    return jnp.concatenate([jnp.concatenate(row, axis=1) for row in rows], axis=0)


def spectra(rows_j, rows_i, tables):
    wins, given, samples = rows_j.shape
    bins = samples // 2
    pairs = wins // 2
    depth = 2 * wins
    folded = HALF // given
    line = depth // folded
    pitch = line + 1
    per_step = 2 * folded
    batch = 32

    def kernel(j_ref, i_ref, table_ref, to_i_ref, to_j_ref, i_out, j_out, wide):
        same = lax.axis_index("sub") == lax.axis_index("rep")

        def spectrum_of(group):
            stacked = []
            for win in [per_step * group + u for u in range(per_step)]:
                here = j_ref[win]
                stacked += [here, jnp.where(same, here, i_ref[win])]
            wave = jnp.concatenate(stacked, axis=0)
            return lax.dot_general(table_ref[...], wave, NT, preferred_element_type=jnp.float32)

        def keep(group, spectrum):
            energy = jnp.sum(spectrum * spectrum, axis=0, keepdims=True) / bins
            white = spectrum * lax.rsqrt(energy + 1e-05)
            for half in range(2):
                for part in range(2):
                    if folded == 1:
                        row = half * wins + part * pairs + group
                    else:
                        row = part * pairs + 2 * group + half
                    wide[pl.ds(row, bins, stride=pitch), :] = white[
                        part * bins : (part + 1) * bins, half * LANES : (half + 1) * LANES
                    ]

        groups = wins // per_step
        at_once = 8

        def some_windows(step, carry):
            first = step * at_once
            last = spectrum_of(first)
            for group in range(1, at_once):
                now = spectrum_of(first + group)
                keep(first + group - 1, last)
                last = now
            keep(first + at_once - 1, last)
            return carry

        lax.fori_loop(0, groups // at_once, some_windows, 0)

        def moved(fs):
            loaded = [wide[pl.ds(f * pitch, line), :].astype(jnp.bfloat16) for f in fs]
            i_rows = [
                lax.dot_general(to_i_ref[...], diagonal(values, 2), NT, preferred_element_type=jnp.float32)
                for values in loaded
            ]
            if folded == 2:
                i_rows = [jnp.concatenate([rows[: given // 2], rows[given // 2 :]], axis=1) for rows in i_rows]
            j_rows = jnp.dot(jnp.concatenate(loaded, axis=0), to_j_ref[...], preferred_element_type=jnp.float32)
            return fs, i_rows, j_rows

        def store(fs, i_rows, j_rows):
            for at, f in enumerate(fs):
                i_out[f] = i_rows[at].astype(jnp.bfloat16)
                for odd in range(folded):
                    j_out[f, odd * line : (odd + 1) * line] = j_rows[
                        at * line : (at + 1) * line, odd * LANES : (odd + 1) * LANES
                    ].astype(jnp.bfloat16)

        def pack(group, carry):
            first = group * 4 * batch
            waiting = moved([first + u for u in range(batch)])
            for at in range(1, 4):
                following = moved([first + at * batch + u for u in range(batch)])
                store(*waiting)
                waiting = following
            store(*waiting)
            return carry

        lax.fori_loop(0, bins // (4 * batch), pack, 0)

    shapes = [(bins, given // 2, LANES), (bins, depth, LANES)]
    return kernel_call(
        kernel,
        "spectra",
        4 * samples * samples * wins * given,
        4 * wins * given * samples * 2,
        out_shape=[jax.ShapeDtypeStruct(shape, jnp.bfloat16) for shape in shapes],
        in_specs=[in_vmem()] * (2 + len(tables)),
        out_specs=[in_vmem()] * len(shapes),
        scratch_shapes=[pltpu.VMEM(((bins + 1) * pitch, LANES), jnp.float32)],
    )(rows_j, rows_i, *tables)


def partial_correlations(lefts, rights, tables, jobs, outs):
    left_arrays = [array for array, _ in lefts]
    right_arrays = [array for array, _, _ in rights]
    bins, depth, _ = right_arrays[0].shape
    piece = HALF // BLOCKS
    pitch = bins + 1
    step_bins = 128
    groups = []
    slices = {}
    for used, groups_here in jobs:
        js = [(rights[right][1], there) for right in used for there in rights[right][2]]
        for left, _, first in groups_here:
            found = []
            for offset in range(2):
                at = first + offset
                for order, (j_other, there) in enumerate(js):
                    if there != at:
                        kind = (lefts[left][1], j_other, there ^ (at % 2))
                        found.append((at, kind, offset * HALF + order * piece))
                        slices.setdefault(at, []).append(kind)
            groups.append(found)
    for kinds in slices.values():
        kinds.sort()
    total = len(groups) * piece
    batch = 8 if len(groups) == 1 else 4

    def first_of(at):
        (out,) = [positions for positions in outs if at in positions]
        return outs.index(out), sum(len(slices[before]) for before in out[: out.index(at)])

    def kernel(*refs):
        left_refs, rest = refs[: len(lefts)], refs[len(lefts) :]
        right_refs, rest = rest[: len(rights)], rest[len(rights) :]
        lag_ref, same_ref, out_refs, cross = rest[0], rest[1], rest[2:-1], rest[-1]
        lanes = lax.broadcasted_iota(jnp.int32, (depth, LANES), 1)

        first_half = lanes < HALF
        lower = lanes % HALF < HALF // 2
        blank = jnp.zeros((depth, LANES), jnp.bfloat16)

        def turn(values):
            swapped = []
            for first in range(0, depth, depth // 2):
                middle, last = first + depth // 4, first + depth // 2
                swapped += [-values[middle:last], values[first:middle]]
            return jnp.concatenate(swapped, axis=0)

        def right_hand(used, f):
            values = right_refs[used[0]][f]
            if len(used) == 2:
                values = jnp.where(lower, values, right_refs[used[1]][f])
            turned = turn(values)
            return jnp.concatenate(
                [
                    jnp.concatenate([jnp.where(first_half, part, blank) for part in (values, turned)], axis=1),
                    jnp.concatenate([jnp.where(first_half, blank, part) for part in (values, turned)], axis=1),
                ],
                axis=0,
            )

        def products(first_bin, count):
            found = []
            for f in [first_bin + u for u in range(count)]:
                first = 0
                for used, groups_here in jobs:
                    lhs = [left_refs[left][f, row : row + piece] for left, row, _ in groups_here]
                    lhs = jnp.concatenate(lhs, axis=0) if len(lhs) > 1 else lhs[0]
                    product = jnp.dot(lhs, right_hand(used, f), preferred_element_type=jnp.float32)
                    found.append((first * pitch + f, product))
                    first += lhs.shape[0]
            return found

        def keep(found):
            for here, product in found:
                for part in range(2):
                    cross[pl.ds(part * total * pitch + here, product.shape[0], stride=pitch), :] = product[
                        :, part * LANES : (part + 1) * LANES
                    ]

        def some_bins(step, carry):
            first = step * step_bins
            waiting = products(first, batch)
            for at in range(batch, step_bins, batch):
                following = products(first + at, batch)
                keep(waiting)
                waiting = following
            keep(waiting)
            return carry

        lax.fori_loop(0, bins // step_bins, some_bins, 0)

        for index, found in enumerate(groups):
            targets = []
            for at, kind, lane in found:
                out, first = first_of(at)
                targets.append((out_refs[out], first + slices[at].index(kind), lane))

            def summed(i):
                parts = []
                for part in range(2):
                    start = (part * total + index * piece + i) * pitch
                    parts.append(
                        jnp.concatenate([cross[pl.ds(start, bins), :], cross[pl.ds(start + pitch, bins), :]], axis=1)
                    )
                values = jnp.concatenate(parts, axis=0).astype(jnp.bfloat16)
                return i, jnp.dot(lag_ref[...], values, preferred_element_type=jnp.float32)

            def across(i, lagged):
                lagged = lagged.astype(jnp.bfloat16)
                return i, lax.dot_general(same_ref[...], lagged, NT, preferred_element_type=jnp.float32)

            def store(i, rows):
                for half in range(2):
                    for out, place, lane in targets:
                        row = half * LANES + lane
                        out[place, i + half] = rows[row : row + piece].astype(out.dtype)

            sums, rows = summed(0), None
            for i in range(2, piece, 2):
                more = summed(i)
                if rows is not None:
                    store(*rows)
                rows = across(*sums)
                sums = more
            store(*rows)
            store(*across(*sums))

    shapes = [(sum(len(slices[at]) for at in positions), piece, piece, LAGS) for positions in outs]
    types = [jnp.float32 if positions == (OWN_AT,) else jnp.bfloat16 for positions in outs]
    results = kernel_call(
        kernel,
        "partial_correlations",
        4 * total * bins * depth * LANES + 4 * total * bins * LANES * LAGS,
        2 * sum(array.size for array in left_arrays + right_arrays),
        out_shape=[jax.ShapeDtypeStruct(shape, kind) for shape, kind in zip(shapes, types)],
        in_specs=[in_vmem()] * (len(lefts) + len(rights) + len(tables)),
        out_specs=[in_vmem()] * len(shapes),
        scratch_shapes=[pltpu.VMEM(((2 * total + 1) * pitch, LANES), jnp.float32)],
    )(*left_arrays, *right_arrays, *tables)
    return results, slices


def assembled(shares):
    arrays = [array for array, _ in shares]
    _, piece, _, lags = arrays[0].shape
    width = 2 * piece

    def kernel(*refs):
        out, held, sems = refs[-3:]
        sub = lax.axis_index("sub")
        odd = lax.rem(lax.axis_index("chan"), 2)
        copies = []
        for there, round_at in ((0, 1), (1, 2 - 2 * odd), (3, 2 * odd)):
            for i_other in range(2):
                for j_other in range(2):
                    parts = [
                        refs[at][place].astype(jnp.float32)
                        for at, (_, kinds) in enumerate(shares)
                        for place, kind in enumerate(kinds)
                        if kind == (i_other, j_other, there)
                    ]
                    i_first = jnp.where(sub == 0, i_other, 1 - i_other) * piece
                    j_first = pl.multiple_of(jnp.where(sub == 0, j_other, 1 - j_other) * piece, piece)
                    held[round_at, 0, pl.ds(i_first, piece), pl.ds(j_first, piece), :] = functools.reduce(
                        jnp.add, parts
                    )
            at = len(copies)
            copies.append(pltpu.make_async_copy(held.at[round_at], out.at[round_at], sems.at[at]))
            copies[-1].start()
        for copy in copies:
            copy.wait()

    shape = (ROUNDS, 1, width, width, lags)
    return kernel_call(
        kernel,
        "assembled",
        0,
        sum(array.size for array in arrays) * 2,
        out_shape=jax.ShapeDtypeStruct(shape, jnp.float32),
        in_specs=[in_vmem()] * len(arrays),
        out_specs=pl.BlockSpec(memory_space=pl.ANY),
        scratch_shapes=[pltpu.VMEM(shape, jnp.float32), pltpu.SemaphoreType.DMA((ROUNDS,))],
    )(*arrays)


def summed_in_place(traces, channel_slot):
    chan_count = lax.axis_size("chan")
    _, win_here, samples = traces.shape
    piece = HALF // BLOCKS
    scale = (2.0 / (win_here * chan_count * (samples // 2))) ** 0.5
    dft_rows = dft_rows_table(samples)
    same = selection(2 * LANES, 2 * LANES, [(n, n) for n in range(2 * LANES)])
    tables = [lag_rows_table(samples, scale), same]
    everywhere = tuple(range(BLOCKS))

    def over_sub(rows):
        return lax.ppermute(rows, "sub", [(0, 1), (1, 0)])

    def over_core(rows):
        return lax.ppermute(rows, "rep", [(0, 1), (1, 0)])

    def with_device(share, apart):
        return lax.ppermute(share, "chan", [(z, z ^ apart) for z in range(chan_count)])

    def after(value, *others):
        return lax.optimization_barrier((value,) + others)[0]

    def added(share, arrived):
        return (share.astype(jnp.float32) + arrived.astype(jnp.float32)).astype(jnp.bfloat16)

    def for_two_away(kinds):
        return [(i_other, j_other, there ^ 2) for i_other, j_other, there in kinds]

    mine, mine_far, mine_near = order_rows(traces, channel_slot, [everywhere, FAR, NEAR])
    far = over_sub(mine_far)
    near = over_sub(mine_near)

    own_i, own_j = spectra(mine, over_core(mine), (dft_rows, *own_picks()))
    own_left, own_right = (own_i, 0), (own_j, 0, everywhere)
    own_far, own_near = (0, 0, FAR[0]), (0, piece, NEAR[0])
    (kept_1, sent_far_1, own_1, sent_near_1), kinds_1 = partial_correlations(
        [own_left], [own_right], tables, [((0,), [own_far, own_near])], [(0,), (1,), (2,), (3,)]
    )
    arrived_far_1 = with_device(sent_far_1, 1)

    far, arrived_far_1 = lax.optimization_barrier((far, arrived_far_1))
    far_1 = with_device(added(kept_1, arrived_far_1), 2)
    arrived_near_1 = with_device(sent_near_1, 1)
    far_i, far_j = spectra(far, over_core(far), (dft_rows, *half_picks()))
    far_left, far_right = (far_i, 1), (far_j, 1, FAR)
    other_far = (1, 0, FAR[0])
    (kept_2, sent_far_2, own_2, sent_near_2), kinds_2 = partial_correlations(
        [own_left, far_left],
        [own_right, far_right],
        tables,
        [((0,), [other_far]), ((1,), [own_far, own_near, other_far])],
        [(0,), (1,), (2,), (3,)],
    )
    sent_far_2, far_1, arrived_near_1 = lax.optimization_barrier((sent_far_2, far_1, arrived_near_1))
    arrived_far_2 = with_device(sent_far_2, 1)

    near, arrived_far_2 = lax.optimization_barrier((near, arrived_far_2))
    near_i, near_j = spectra(near, over_core(near), (dft_rows, *half_picks()))
    summed_2 = added(kept_2, arrived_far_2)
    far_2 = with_device(summed_2, 2)
    near_j = after(near_j, summed_2)
    near_left, near_right = (near_i, 1), (near_j, 1, NEAR)
    (kept_3, sent_far_3, own_3, sent_near_3), kinds_3 = partial_correlations(
        [own_left, far_left],
        [near_right],
        tables,
        [((0,), [own_far, other_far, own_near])],
        [(0,), (1,), (2,), (3,)],
    )
    arrived_far_3 = with_device(sent_far_3, 1)
    arrived_near_2 = with_device(sent_near_2, 1)
    near_right = (after(near_j, kept_3, sent_far_3, far_2, arrived_near_2), 1, NEAR)
    (own_4, sent_4), kinds_4 = partial_correlations(
        [near_left], [far_right, near_right], tables, [((0, 1), [(0, 0, NEAR[0])])], [(2,), (3,)]
    )
    arrived_4 = with_device(jnp.concatenate([sent_near_3, sent_4]), 1)
    summed_3 = added(after(kept_3, own_4), arrived_far_3)
    far_3 = with_device(summed_3, 2)
    near_left = (after(near_i, own_4, sent_4, summed_3), 1)
    (own_5, sent_5), kinds_5 = partial_correlations(
        [near_left], [own_right], tables, [((0,), [(0, 0, NEAR[0])])], [(2,), (3,)]
    )
    arrived_5 = with_device(sent_5, 1)
    shares = [
        (own_1, kinds_1[2]),
        (own_2, kinds_2[2]),
        (own_3, kinds_3[2]),
        (own_4, kinds_4[2]),
        (own_5, kinds_5[2]),
        (arrived_near_1, kinds_1[3]),
        (arrived_near_2, kinds_2[3]),
        (arrived_4, kinds_3[3] + kinds_4[3]),
        (arrived_5, kinds_5[3]),
        (far_1, for_two_away(kinds_1[0])),
        (far_2, for_two_away(kinds_2[0])),
        (far_3, for_two_away(kinds_3[0])),
    ]
    return assembled(shares)


def from_behind(shard, axis, by):
    count = lax.axis_size(axis)
    return lax.ppermute(shard, axis, [(i, (i + by) % count) for i in range(count)])


def dft_columns(samples, parts, sub_bins):
    shape = (samples, parts, 2, sub_bins)
    time_pos = lax.broadcasted_iota(jnp.int32, shape, 0)
    range_pos = lax.broadcasted_iota(jnp.int32, shape, 1)
    part_pos = lax.broadcasted_iota(jnp.int32, shape, 2)
    bin_pos = lax.broadcasted_iota(jnp.int32, shape, 3)
    frequency = range_pos * sub_bins + bin_pos
    angles = jnp.mod(time_pos * frequency, samples).astype(jnp.float32) * (2.0 * math.pi / samples)
    entries = jnp.where(part_pos == 0, jnp.cos(angles), -jnp.sin(angles))
    return entries.reshape(samples, parts * 2 * sub_bins).astype(jnp.bfloat16)


def lag_table(sub_bins, first_bin, lag_count, samples):
    frequency = first_bin + lax.broadcasted_iota(jnp.int32, (sub_bins, lag_count), 0)
    lag_offset = lax.broadcasted_iota(jnp.int32, (sub_bins, lag_count), 1) - lag_count // 2
    angles = jnp.mod(frequency * lag_offset, samples).astype(jnp.float32) * (2.0 * math.pi / samples)
    return jnp.stack([jnp.cos(angles), -jnp.sin(angles)], axis=1)


def moved_spectra(traces, channel_slot):
    chan_count = lax.axis_size("chan")
    sub_count = lax.axis_size("sub")
    group_rows, win_here, samples = traces.shape
    bin_count = samples // 2
    sub_bins = bin_count // sub_count
    bin_width = 2 * sub_bins
    piece_len = group_rows // chan_count
    picked = jnp.take(traces, channel_slot, axis=0)
    dft_rows = dft_columns(samples, sub_count, sub_bins)
    spectrum = jnp.dot(picked.reshape(-1, samples), dft_rows, preferred_element_type=jnp.float32)
    energy = jnp.sum(spectrum * spectrum, axis=1, keepdims=True) / bin_count
    whitened = (spectrum * lax.rsqrt(energy + 1e-05)).astype(jnp.bfloat16)
    whitened = whitened.reshape(chan_count, piece_len, win_here, sub_count, bin_width)
    regrouped = lax.all_to_all(whitened, "chan", split_axis=0, concat_axis=0, tiled=True)
    regrouped = lax.all_to_all(regrouped, "sub", split_axis=3, concat_axis=3, tiled=True)
    own_half = regrouped.transpose(3, 1, 0, 2, 4).reshape(sub_count * piece_len, chan_count * win_here, bin_width)
    own_block = lax.all_gather(own_half, "rep", axis=0, tiled=True)
    windows = own_block.shape[1]
    own_split = own_block.reshape(own_block.shape[0], windows, 2, sub_bins)
    lag_rows = lag_table(sub_bins, lax.axis_index("sub") * sub_bins, LAGS, samples)
    lag_scale = (2.0 / (windows * bin_count)) ** 0.5
    results = []
    for step in range(1, ROUNDS + 1):
        partner = from_behind(own_half, "chan", -step)
        partner_split = partner.reshape(partner.shape[0], windows, 2, sub_bins)
        turned = jnp.stack([-partner_split[:, :, 1], partner_split[:, :, 0]], axis=2)
        partner_pair = jnp.stack([partner_split, turned], axis=0)
        cross_spec = jnp.einsum("iwpf,qjwpf->fqij", own_split, partner_pair, preferred_element_type=jnp.float32)
        summed = jnp.einsum("fqij,fql->ijl", cross_spec, lag_rows, precision=lax.Precision.HIGHEST)
        results.append(lax.psum_scatter(lag_scale * summed, "sub", scatter_dimension=0, tiled=True))
    return jnp.stack(results)[:, None]


def solution(mesh):
    sizes = mesh.shape
    in_place = sizes["chan"] == BLOCKS == ROUNDS + 1 and sizes["sub"] == 2 and sizes["rep"] == 2
    return jax.shard_map(
        summed_in_place if in_place else moved_spectra,
        mesh=mesh,
        in_specs=(P(("groups", "sub", "rep"), "chan", None), P(("groups", "sub", "rep"))),
        out_specs=P(None, ("groups", "chan"), "sub", "rep", None),
        check_vma=False,
    )
```

```python
import functools
import math

import jax
import jax.numpy as jnp
import numpy as np
from jax import lax
from jax.experimental import pallas as pl
from jax.experimental.pallas import tpu as pltpu
from jax.sharding import PartitionSpec as P

LAGS = 128
ROUNDS = 3
LANES = 128
HALF = LANES // 2
VMEM_BYTES = 32 * 1024 * 1024
ORDER_VMEM_BYTES = 48 * 1024 * 1024
NT = (((1,), (1,)), ((), ()))
BLOCKS = 4
FAR = (0, 1)
NEAR = (2, 3)
KEPT_AT, OWN_AT = 0, 2


def kernel_call(kernel, name, flops, bytes_accessed, vmem_bytes=VMEM_BYTES, **more):
    return pl.pallas_call(
        kernel,
        name=name,
        compiler_params=pltpu.CompilerParams(vmem_limit_bytes=vmem_bytes),
        cost_estimate=pl.CostEstimate(flops=flops, bytes_accessed=bytes_accessed, transcendentals=0),
        **more,
    )


def in_vmem():
    return pl.BlockSpec(memory_space=pltpu.VMEM)


def dft_rows_table(samples):
    bins = samples // 2
    turns = (np.arange(bins)[:, None] * np.arange(samples)[None, :]) % samples
    angles = turns.astype(np.float32) * np.float32(2.0 * math.pi / samples)
    table = np.concatenate([np.cos(angles), -np.sin(angles)], axis=0)
    return jnp.asarray(table.astype(np.float32)).astype(jnp.bfloat16)


def lag_rows_table(samples, scale):
    bins = samples // 2
    offsets = np.arange(LAGS) - LAGS // 2
    turns = (offsets[:, None] * np.arange(bins)[None, :]) % samples
    angles = turns.astype(np.float32) * np.float32(2.0 * math.pi / samples)
    table = np.concatenate([np.cos(angles), -np.sin(angles)], axis=1) * np.float32(scale)
    return jnp.asarray(table.astype(np.float32)).astype(jnp.bfloat16)


def selection(rows, columns, ones):
    table = np.zeros((rows, columns), np.float32)
    for row, column in ones:
        table[row, column] = 1.0
    return jnp.asarray(table).astype(jnp.bfloat16)


def own_picks():
    piece = HALF // BLOCKS
    to_i = []
    for at in range(BLOCKS):
        for n in range(piece):
            to_i.append((at // 2 * piece + n, at % 2 * LANES + HALF + at * piece + n))
    to_j = [(j, copy * HALF + j) for j in range(HALF) for copy in range(2)]
    return selection(2 * piece, 2 * LANES, to_i), selection(LANES, LANES, to_j)


def half_picks():
    count = HALF // 2
    to_i, to_j = [], []
    for odd in range(2):
        for n in range(count):
            to_i.append((n, odd * LANES + odd * HALF + count + n))
            to_j += [(odd * HALF + n, odd * LANES + copy * count + n) for copy in range(4)]
    return selection(count, 2 * LANES, to_i), selection(LANES, 2 * LANES, to_j)


def order_rows(traces, slots, kinds):
    rows, wins, samples = traces.shape
    tiles = samples // LANES
    piece = rows // BLOCKS
    step_wins = 16
    steps = wins // step_wins
    batch = 8
    used = max(kinds, key=len)
    pitch = len(used) * piece + 1

    def kernel(slots_ref, traces_ref, *refs):
        out_refs, (wide, in_ref, slot_ref, sems) = refs[:-4], refs[-4:]
        slot_copy = pltpu.make_async_copy(slots_ref, slot_ref, sems.at[steps])
        slot_copy.start()
        copies = []
        for step in range(steps):
            here = pl.ds(step * step_wins, step_wins)
            copies.append(
                pltpu.make_async_copy(traces_ref.at[:, here, :], in_ref.at[:, here, :], sems.at[step])
            )
            copies[-1].start()
        slot_copy.wait()
        z = lax.axis_index("chan")
        odd = lax.rem(z, 2)
        pair = jnp.where(z < 2, 2, 0)

        def some_windows(step):
            first_win = step * step_wins
            for at, position in enumerate(used):
                block = pair + position + (odd if position % 2 == 0 else -odd)
                first = lax.rem(block, BLOCKS) * piece

                def move(group, carry, at=at, first=first):
                    js = [group * batch + u for u in range(batch)]
                    picked = [
                        in_ref[slot_ref[first + j], pl.ds(first_win, step_wins), :].astype(jnp.float32) for j in js
                    ]
                    for j, row in zip(js, picked):
                        for tile in range(tiles):
                            wide[tile, pl.ds(at * piece + j, step_wins, stride=pitch), :] = row[
                                :, tile * LANES : (tile + 1) * LANES
                            ]
                    return carry

                lax.fori_loop(0, piece // batch, move, 0)

            def pack(w, carry):
                blocks = [
                    wide[tile, pl.ds(w * pitch, len(used) * piece), :].astype(jnp.bfloat16) for tile in range(tiles)
                ]
                for out_ref, kind in zip(out_refs, kinds):
                    first = used.index(kind[0]) * piece
                    for tile, block in enumerate(blocks):
                        out_ref[first_win + w, :, tile * LANES : (tile + 1) * LANES] = block[
                            first : first + len(kind) * piece
                        ]
                return carry

            lax.fori_loop(0, step_wins, pack, 0, unroll=4)

        for step in range(steps):
            copies[step].wait()
            some_windows(step)

    return kernel_call(
        kernel,
        "order_rows",
        0,
        3 * traces.size * 2,
        vmem_bytes=ORDER_VMEM_BYTES,
        out_shape=[jax.ShapeDtypeStruct((wins, len(kind) * piece, samples), jnp.bfloat16) for kind in kinds],
        in_specs=[pl.BlockSpec(memory_space=pltpu.HBM)] * 2,
        out_specs=[in_vmem()] * len(kinds),
        scratch_shapes=[
            pltpu.VMEM((tiles, (step_wins + 1) * pitch, LANES), jnp.float32),
            pltpu.VMEM(traces.shape, traces.dtype),
            pltpu.SMEM(slots.shape, slots.dtype),
            pltpu.SemaphoreType.DMA((steps + 1,)),
        ],
    )(slots, traces)


def diagonal(values, copies):
    blank = jnp.zeros_like(values)
    rows = [[values if at == copy else blank for at in range(copies)] for copy in range(copies)]
    return jnp.concatenate([jnp.concatenate(row, axis=1) for row in rows], axis=0)


def spectra(rows_j, rows_i, tables):
    wins, given, samples = rows_j.shape
    bins = samples // 2
    pairs = wins // 2
    depth = 2 * wins
    folded = HALF // given
    line = depth // folded
    pitch = line + 1
    per_step = 2 * folded
    batch = 32

    def kernel(j_ref, i_ref, table_ref, to_i_ref, to_j_ref, i_out, j_out, wide):
        same = lax.axis_index("sub") == lax.axis_index("rep")

        def spectrum_of(group):
            stacked = []
            for win in [per_step * group + u for u in range(per_step)]:
                here = j_ref[win]
                stacked += [here, jnp.where(same, here, i_ref[win])]
            wave = jnp.concatenate(stacked, axis=0)
            return lax.dot_general(table_ref[...], wave, NT, preferred_element_type=jnp.float32)

        def keep(group, spectrum):
            energy = jnp.sum(spectrum * spectrum, axis=0, keepdims=True) / bins
            white = spectrum * lax.rsqrt(energy + 1e-05)
            for half in range(2):
                for part in range(2):
                    if folded == 1:
                        row = half * wins + part * pairs + group
                    else:
                        row = part * pairs + 2 * group + half
                    wide[pl.ds(row, bins, stride=pitch), :] = white[
                        part * bins : (part + 1) * bins, half * LANES : (half + 1) * LANES
                    ]

        groups = wins // per_step
        at_once = 8

        def some_windows(step, carry):
            first = step * at_once
            last = spectrum_of(first)
            for group in range(1, at_once):
                now = spectrum_of(first + group)
                keep(first + group - 1, last)
                last = now
            keep(first + at_once - 1, last)
            return carry

        lax.fori_loop(0, groups // at_once, some_windows, 0)

        def moved(fs):
            loaded = [wide[pl.ds(f * pitch, line), :].astype(jnp.bfloat16) for f in fs]
            i_rows = [
                lax.dot_general(to_i_ref[...], diagonal(values, 2), NT, preferred_element_type=jnp.float32)
                for values in loaded
            ]
            if folded == 2:
                i_rows = [jnp.concatenate([rows[: given // 2], rows[given // 2 :]], axis=1) for rows in i_rows]
            j_rows = jnp.dot(jnp.concatenate(loaded, axis=0), to_j_ref[...], preferred_element_type=jnp.float32)
            return fs, i_rows, j_rows

        def store(fs, i_rows, j_rows):
            for at, f in enumerate(fs):
                i_out[f] = i_rows[at].astype(jnp.bfloat16)
                for odd in range(folded):
                    j_out[f, odd * line : (odd + 1) * line] = j_rows[
                        at * line : (at + 1) * line, odd * LANES : (odd + 1) * LANES
                    ].astype(jnp.bfloat16)

        def pack(group, carry):
            first = group * 4 * batch
            waiting = moved([first + u for u in range(batch)])
            for at in range(1, 4):
                following = moved([first + at * batch + u for u in range(batch)])
                store(*waiting)
                waiting = following
            store(*waiting)
            return carry

        lax.fori_loop(0, bins // (4 * batch), pack, 0)

    shapes = [(bins, given // 2, LANES), (bins, depth, LANES)]
    return kernel_call(
        kernel,
        "spectra",
        4 * samples * samples * wins * given,
        4 * wins * given * samples * 2,
        out_shape=[jax.ShapeDtypeStruct(shape, jnp.bfloat16) for shape in shapes],
        in_specs=[in_vmem()] * (2 + len(tables)),
        out_specs=[in_vmem()] * len(shapes),
        scratch_shapes=[pltpu.VMEM(((bins + 1) * pitch, LANES), jnp.float32)],
    )(rows_j, rows_i, *tables)


def partial_correlations(lefts, rights, tables, jobs, outs):
    left_arrays = [array for array, _ in lefts]
    right_arrays = [array for array, _, _ in rights]
    bins, depth, _ = right_arrays[0].shape
    piece = HALF // BLOCKS
    pitch = bins + 1
    step_bins = 256
    groups = []
    slices = {}
    for used, groups_here in jobs:
        js = [(rights[right][1], there) for right in used for there in rights[right][2]]
        for left, _, first in groups_here:
            found = []
            for offset in range(2):
                at = first + offset
                for order, (j_other, there) in enumerate(js):
                    if there != at:
                        kind = (lefts[left][1], j_other, there ^ (at % 2))
                        found.append((at, kind, offset * HALF + order * piece))
                        slices.setdefault(at, []).append(kind)
            groups.append(found)
    for kinds in slices.values():
        kinds.sort()
    total = len(groups) * piece
    batch = 8 if len(groups) == 1 else 4

    def first_of(at):
        (out,) = [positions for positions in outs if at in positions]
        return outs.index(out), sum(len(slices[before]) for before in out[: out.index(at)])

    def kernel(*refs):
        left_refs, rest = refs[: len(lefts)], refs[len(lefts) :]
        right_refs, rest = rest[: len(rights)], rest[len(rights) :]
        lag_ref, same_ref, out_refs, cross = rest[0], rest[1], rest[2:-1], rest[-1]
        lanes = lax.broadcasted_iota(jnp.int32, (depth, LANES), 1)

        first_half = lanes < HALF
        lower = lanes % HALF < HALF // 2
        blank = jnp.zeros((depth, LANES), jnp.bfloat16)

        def turn(values):
            swapped = []
            for first in range(0, depth, depth // 2):
                middle, last = first + depth // 4, first + depth // 2
                swapped += [-values[middle:last], values[first:middle]]
            return jnp.concatenate(swapped, axis=0)

        def right_hand(used, f):
            values = right_refs[used[0]][f]
            if len(used) == 2:
                values = jnp.where(lower, values, right_refs[used[1]][f])
            turned = turn(values)
            return jnp.concatenate(
                [
                    jnp.concatenate([jnp.where(first_half, part, blank) for part in (values, turned)], axis=1),
                    jnp.concatenate([jnp.where(first_half, blank, part) for part in (values, turned)], axis=1),
                ],
                axis=0,
            )

        def products(first_bin, count):
            found = []
            for f in [first_bin + u for u in range(count)]:
                first = 0
                for used, groups_here in jobs:
                    lhs = [left_refs[left][f, row : row + piece] for left, row, _ in groups_here]
                    lhs = jnp.concatenate(lhs, axis=0) if len(lhs) > 1 else lhs[0]
                    product = jnp.dot(lhs, right_hand(used, f), preferred_element_type=jnp.float32)
                    found.append((first * pitch + f, product))
                    first += lhs.shape[0]
            return found

        def keep(found):
            for here, product in found:
                for part in range(2):
                    cross[pl.ds(part * total * pitch + here, product.shape[0], stride=pitch), :] = product[
                        :, part * LANES : (part + 1) * LANES
                    ]

        def some_bins(step, carry):
            first = step * step_bins
            waiting = products(first, batch)
            for at in range(batch, step_bins, batch):
                following = products(first + at, batch)
                keep(waiting)
                waiting = following
            keep(waiting)
            return carry

        lax.fori_loop(0, bins // step_bins, some_bins, 0)

        for index, found in enumerate(groups):
            targets = []
            for at, kind, lane in found:
                out, first = first_of(at)
                targets.append((out_refs[out], first + slices[at].index(kind), lane))

            def summed(i):
                parts = []
                for part in range(2):
                    start = (part * total + index * piece + i) * pitch
                    parts.append(
                        jnp.concatenate([cross[pl.ds(start, bins), :], cross[pl.ds(start + pitch, bins), :]], axis=1)
                    )
                values = jnp.concatenate(parts, axis=0).astype(jnp.bfloat16)
                return i, jnp.dot(lag_ref[...], values, preferred_element_type=jnp.float32)

            def across(i, lagged):
                lagged = lagged.astype(jnp.bfloat16)
                return i, lax.dot_general(same_ref[...], lagged, NT, preferred_element_type=jnp.float32)

            def store(i, rows):
                for half in range(2):
                    for out, place, lane in targets:
                        row = half * LANES + lane
                        out[place, i + half] = rows[row : row + piece].astype(out.dtype)

            sums, rows = summed(0), None
            for i in range(2, piece, 2):
                more = summed(i)
                if rows is not None:
                    store(*rows)
                rows = across(*sums)
                sums = more
            store(*rows)
            store(*across(*sums))

    shapes = [(sum(len(slices[at]) for at in positions), piece, piece, LAGS) for positions in outs]
    types = [jnp.float32 if positions == (OWN_AT,) else jnp.bfloat16 for positions in outs]
    results = kernel_call(
        kernel,
        "partial_correlations",
        4 * total * bins * depth * LANES + 4 * total * bins * LANES * LAGS,
        2 * sum(array.size for array in left_arrays + right_arrays),
        out_shape=[jax.ShapeDtypeStruct(shape, kind) for shape, kind in zip(shapes, types)],
        in_specs=[in_vmem()] * (len(lefts) + len(rights) + len(tables)),
        out_specs=[in_vmem()] * len(shapes),
        scratch_shapes=[pltpu.VMEM(((2 * total + 1) * pitch, LANES), jnp.float32)],
    )(*left_arrays, *right_arrays, *tables)
    return results, slices


def assembled(shares):
    arrays = [array for array, _ in shares]
    _, piece, _, lags = arrays[0].shape
    width = 2 * piece

    def kernel(*refs):
        out, held, sems = refs[-3:]
        sub = lax.axis_index("sub")
        odd = lax.rem(lax.axis_index("chan"), 2)
        copies = []
        for there, round_at in ((0, 1), (1, 2 - 2 * odd), (3, 2 * odd)):
            for i_other in range(2):
                for j_other in range(2):
                    parts = [
                        refs[at][place].astype(jnp.float32)
                        for at, (_, kinds) in enumerate(shares)
                        for place, kind in enumerate(kinds)
                        if kind == (i_other, j_other, there)
                    ]
                    i_first = jnp.where(sub == 0, i_other, 1 - i_other) * piece
                    j_first = pl.multiple_of(jnp.where(sub == 0, j_other, 1 - j_other) * piece, piece)
                    held[round_at, 0, pl.ds(i_first, piece), pl.ds(j_first, piece), :] = functools.reduce(
                        jnp.add, parts
                    )
            at = len(copies)
            copies.append(pltpu.make_async_copy(held.at[round_at], out.at[round_at], sems.at[at]))
            copies[-1].start()
        for copy in copies:
            copy.wait()

    shape = (ROUNDS, 1, width, width, lags)
    return kernel_call(
        kernel,
        "assembled",
        0,
        sum(array.size for array in arrays) * 2,
        out_shape=jax.ShapeDtypeStruct(shape, jnp.float32),
        in_specs=[in_vmem()] * len(arrays),
        out_specs=pl.BlockSpec(memory_space=pl.ANY),
        scratch_shapes=[pltpu.VMEM(shape, jnp.float32), pltpu.SemaphoreType.DMA((ROUNDS,))],
    )(*arrays)


def summed_in_place(traces, channel_slot):
    chan_count = lax.axis_size("chan")
    _, win_here, samples = traces.shape
    piece = HALF // BLOCKS
    scale = (2.0 / (win_here * chan_count * (samples // 2))) ** 0.5
    dft_rows = dft_rows_table(samples)
    same = selection(2 * LANES, 2 * LANES, [(n, n) for n in range(2 * LANES)])
    tables = [lag_rows_table(samples, scale), same]
    everywhere = tuple(range(BLOCKS))

    def over_sub(rows):
        return lax.ppermute(rows, "sub", [(0, 1), (1, 0)])

    def over_core(rows):
        return lax.ppermute(rows, "rep", [(0, 1), (1, 0)])

    def with_device(share, apart):
        return lax.ppermute(share, "chan", [(z, z ^ apart) for z in range(chan_count)])

    def after(value, *others):
        return lax.optimization_barrier((value,) + others)[0]

    def added(share, arrived):
        return (share.astype(jnp.float32) + arrived.astype(jnp.float32)).astype(jnp.bfloat16)

    def for_two_away(kinds):
        return [(i_other, j_other, there ^ 2) for i_other, j_other, there in kinds]

    mine, mine_far, mine_near = order_rows(traces, channel_slot, [everywhere, FAR, NEAR])
    far = over_sub(mine_far)
    near = over_sub(mine_near)

    own_i, own_j = spectra(mine, over_core(mine), (dft_rows, *own_picks()))
    own_left, own_right = (own_i, 0), (own_j, 0, everywhere)
    own_far, own_near = (0, 0, FAR[0]), (0, piece, NEAR[0])
    (kept_1, sent_far_1, own_1, sent_near_1), kinds_1 = partial_correlations(
        [own_left], [own_right], tables, [((0,), [own_far, own_near])], [(0,), (1,), (2,), (3,)]
    )
    arrived_far_1 = with_device(sent_far_1, 1)

    far, arrived_far_1 = lax.optimization_barrier((far, arrived_far_1))
    far_1 = with_device(added(kept_1, arrived_far_1), 2)
    arrived_near_1 = with_device(sent_near_1, 1)
    far_i, far_j = spectra(far, over_core(far), (dft_rows, *half_picks()))
    far_left, far_right = (far_i, 1), (far_j, 1, FAR)
    other_far = (1, 0, FAR[0])
    (kept_2, sent_far_2, own_2, sent_near_2), kinds_2 = partial_correlations(
        [own_left, far_left],
        [own_right, far_right],
        tables,
        [((0,), [other_far]), ((1,), [own_far, own_near, other_far])],
        [(0,), (1,), (2,), (3,)],
    )
    sent_far_2, far_1, arrived_near_1 = lax.optimization_barrier((sent_far_2, far_1, arrived_near_1))
    arrived_far_2 = with_device(sent_far_2, 1)

    near, arrived_far_2 = lax.optimization_barrier((near, arrived_far_2))
    near_i, near_j = spectra(near, over_core(near), (dft_rows, *half_picks()))
    summed_2 = added(kept_2, arrived_far_2)
    far_2 = with_device(summed_2, 2)
    near_j = after(near_j, summed_2)
    near_left, near_right = (near_i, 1), (near_j, 1, NEAR)
    (kept_3, sent_far_3, own_3, sent_near_3), kinds_3 = partial_correlations(
        [own_left, far_left],
        [near_right],
        tables,
        [((0,), [own_far, other_far, own_near])],
        [(0,), (1,), (2,), (3,)],
    )
    arrived_far_3 = with_device(sent_far_3, 1)
    arrived_near_2 = with_device(sent_near_2, 1)
    near_right = (after(near_j, kept_3, sent_far_3, far_2, arrived_near_2), 1, NEAR)
    (own_4, sent_4), kinds_4 = partial_correlations(
        [near_left], [far_right, near_right], tables, [((0, 1), [(0, 0, NEAR[0])])], [(2,), (3,)]
    )
    arrived_4 = with_device(jnp.concatenate([sent_near_3, sent_4]), 1)
    summed_3 = added(after(kept_3, own_4), arrived_far_3)
    far_3 = with_device(summed_3, 2)
    near_left = (after(near_i, own_4, sent_4, summed_3), 1)
    (own_5, sent_5), kinds_5 = partial_correlations(
        [near_left], [own_right], tables, [((0,), [(0, 0, NEAR[0])])], [(2,), (3,)]
    )
    arrived_5 = with_device(sent_5, 1)
    shares = [
        (own_1, kinds_1[2]),
        (own_2, kinds_2[2]),
        (own_3, kinds_3[2]),
        (own_4, kinds_4[2]),
        (own_5, kinds_5[2]),
        (arrived_near_1, kinds_1[3]),
        (arrived_near_2, kinds_2[3]),
        (arrived_4, kinds_3[3] + kinds_4[3]),
        (arrived_5, kinds_5[3]),
        (far_1, for_two_away(kinds_1[0])),
        (far_2, for_two_away(kinds_2[0])),
        (far_3, for_two_away(kinds_3[0])),
    ]
    return assembled(shares)


def from_behind(shard, axis, by):
    count = lax.axis_size(axis)
    return lax.ppermute(shard, axis, [(i, (i + by) % count) for i in range(count)])


def dft_columns(samples, parts, sub_bins):
    shape = (samples, parts, 2, sub_bins)
    time_pos = lax.broadcasted_iota(jnp.int32, shape, 0)
    range_pos = lax.broadcasted_iota(jnp.int32, shape, 1)
    part_pos = lax.broadcasted_iota(jnp.int32, shape, 2)
    bin_pos = lax.broadcasted_iota(jnp.int32, shape, 3)
    frequency = range_pos * sub_bins + bin_pos
    angles = jnp.mod(time_pos * frequency, samples).astype(jnp.float32) * (2.0 * math.pi / samples)
    entries = jnp.where(part_pos == 0, jnp.cos(angles), -jnp.sin(angles))
    return entries.reshape(samples, parts * 2 * sub_bins).astype(jnp.bfloat16)


def lag_table(sub_bins, first_bin, lag_count, samples):
    frequency = first_bin + lax.broadcasted_iota(jnp.int32, (sub_bins, lag_count), 0)
    lag_offset = lax.broadcasted_iota(jnp.int32, (sub_bins, lag_count), 1) - lag_count // 2
    angles = jnp.mod(frequency * lag_offset, samples).astype(jnp.float32) * (2.0 * math.pi / samples)
    return jnp.stack([jnp.cos(angles), -jnp.sin(angles)], axis=1)


def moved_spectra(traces, channel_slot):
    chan_count = lax.axis_size("chan")
    sub_count = lax.axis_size("sub")
    group_rows, win_here, samples = traces.shape
    bin_count = samples // 2
    sub_bins = bin_count // sub_count
    bin_width = 2 * sub_bins
    piece_len = group_rows // chan_count
    picked = jnp.take(traces, channel_slot, axis=0)
    dft_rows = dft_columns(samples, sub_count, sub_bins)
    spectrum = jnp.dot(picked.reshape(-1, samples), dft_rows, preferred_element_type=jnp.float32)
    energy = jnp.sum(spectrum * spectrum, axis=1, keepdims=True) / bin_count
    whitened = (spectrum * lax.rsqrt(energy + 1e-05)).astype(jnp.bfloat16)
    whitened = whitened.reshape(chan_count, piece_len, win_here, sub_count, bin_width)
    regrouped = lax.all_to_all(whitened, "chan", split_axis=0, concat_axis=0, tiled=True)
    regrouped = lax.all_to_all(regrouped, "sub", split_axis=3, concat_axis=3, tiled=True)
    own_half = regrouped.transpose(3, 1, 0, 2, 4).reshape(sub_count * piece_len, chan_count * win_here, bin_width)
    own_block = lax.all_gather(own_half, "rep", axis=0, tiled=True)
    windows = own_block.shape[1]
    own_split = own_block.reshape(own_block.shape[0], windows, 2, sub_bins)
    lag_rows = lag_table(sub_bins, lax.axis_index("sub") * sub_bins, LAGS, samples)
    lag_scale = (2.0 / (windows * bin_count)) ** 0.5
    results = []
    for step in range(1, ROUNDS + 1):
        partner = from_behind(own_half, "chan", -step)
        partner_split = partner.reshape(partner.shape[0], windows, 2, sub_bins)
        turned = jnp.stack([-partner_split[:, :, 1], partner_split[:, :, 0]], axis=2)
        partner_pair = jnp.stack([partner_split, turned], axis=0)
        cross_spec = jnp.einsum("iwpf,qjwpf->fqij", own_split, partner_pair, preferred_element_type=jnp.float32)
        summed = jnp.einsum("fqij,fql->ijl", cross_spec, lag_rows, precision=lax.Precision.HIGHEST)
        results.append(lax.psum_scatter(lag_scale * summed, "sub", scatter_dimension=0, tiled=True))
    return jnp.stack(results)[:, None]


def solution(mesh):
    sizes = mesh.shape
    in_place = sizes["chan"] == BLOCKS == ROUNDS + 1 and sizes["sub"] == 2 and sizes["rep"] == 2
    return jax.shard_map(
        summed_in_place if in_place else moved_spectra,
        mesh=mesh,
        in_specs=(P(("groups", "sub", "rep"), "chan", None), P(("groups", "sub", "rep"))),
        out_specs=P(None, ("groups", "chan"), "sub", "rep", None),
        check_vma=False,
    )
```
